128 devices in a mesh: seq: 32 (over x, y, core), fsdp: 4 (over z).
Axes of the slice: x: 4, y: 4, z: 4, core: 2. Of those that a mesh axis runs over, the one named last changes fastest.
Arguments:
- tokens: bfloat16 [4, 4096, 1536], P('fsdp', 'seq'), may hold values from -6 to 6
- cotangent: bfloat16 [4, 4096, 1536], P('fsdp', 'seq'), may hold values from -6 to 6
- lengths: int32 [4], P('fsdp'), may hold values from 1024 to 4096, as said below
- routes: int32 [4, 4096, 6], P('fsdp', 'seq'), may hold values from 0 to 7, all different within a row; in each aligned block of 128 rows (0 to 127, 128 to 255, ..., all dimensions but the last counted through in order) at most 112 rows name the same one
- norm_gain: float32 [1536], replicated, may hold values from 0.5 to 1.5
- w_in: bfloat16 [1536, 6448], P('fsdp'), may hold values from -0.15625 to 0.15625
- conv_weight: float32 [4, 3328], replicated, may hold values from -3 to 3
- conv_bias: float32 [3328], replicated, may hold values from -0.5 to 0.5
- a_log: float32 [48], replicated
- dt_bias: float32 [48], replicated, may hold values from -1 to 1
- skip_scale: float32 [48], replicated, may hold values from 0.5 to 1.5
- gated_gain: float32 [3072], replicated, may hold values from 0.5 to 1.5
- w_out: bfloat16 [3072, 1536], P('fsdp'), may hold values from -0.109375 to 0.109375
- post_gain: float32 [1536], replicated, may hold values from 0.5 to 1.5
- w_router: bfloat16 [1536, 8], P('fsdp'), may hold values from -0.078125 to 0.078125
- shared_in: bfloat16 [1536, 2048], P('fsdp'), may hold values from -0.15625 to 0.15625
- shared_out: bfloat16 [1024, 1536], P('fsdp'), may hold values from -0.1875 to 0.1875
- expert_in: bfloat16 [8, 1536, 1024], P('fsdp'), may hold values from -0.15625 to 0.15625
- expert_out: bfloat16 [8, 512, 1536], P('fsdp'), may hold values from -0.25 to 0.25
Outputs:
- block_out: bfloat16 [4, 4096, 1536], P('fsdp', 'seq')
- grad_tokens: float32 [4, 4096, 1536], P('fsdp', 'seq')
- grad_norm_gain: float32 [1536], P(('seq', 'fsdp'))
- grad_w_in: float32 [1536, 6448], P(('seq', 'fsdp'))
- grad_conv_weight: float32 [4, 3328], P(None, ('seq', 'fsdp'))
- grad_conv_bias: float32 [3328], P(('seq', 'fsdp'))
- grad_a_log: float32 [48], replicated
- grad_dt_bias: float32 [48], replicated
- grad_skip_scale: float32 [48], replicated
- grad_gated_gain: float32 [3072], P(('seq', 'fsdp'))
- grad_w_out: float32 [3072, 1536], P(('seq', 'fsdp'))
- grad_post_gain: float32 [1536], P(('seq', 'fsdp'))
- grad_w_router: float32 [1536, 8], P(('seq', 'fsdp'))
- grad_shared_in: float32 [1536, 2048], P(('seq', 'fsdp'))
- grad_shared_out: float32 [1024, 1536], P(('seq', 'fsdp'))
- grad_expert_in: float32 [8, 1536, 1024], P('fsdp', 'seq')
- grad_expert_out: float32 [8, 512, 1536], P('fsdp', 'seq')
The draws below stay inside these ranges and needn't reach their ends.
Inputs may be any that keep to these rules, and one draw needn't show every extreme that they name: `lengths`: one entry, drawn from the seed, equals 4096. `routes`: each row names 6 different experts. In each aligned block of 128 rows (the slots of one sequence on one device) no expert is named by more than 112 rows, and some block reaches 112.
All inputs are finite; a program needn't handle non-finite values.
Results may differ from the reference program's by a relative error of at most 0.015.
Values may be sent and summed in bfloat16 or wider, within the bound.
A program may use at most 512 MiB of HBM per device.

```python
import math
import jax
import jax.numpy as jnp
import numpy as np
from jax import lax

D = 1536
H = 48
K = 4
FF = 512
SH = 1024
TOP = 6
E = 8
SLOT_DEV = 128
MOST = 112
LEN = 4096
SEQS = 4
INNER = 3072
CONVCH = 3328
DIN = 6448


def draw_lengths(key, part):
    key = jax.random.fold_in(key, 11)
    key_len, key_pick = jax.random.split(key)
    drawn_lengths = jax.random.randint(key_len, (SEQS,), LEN // 4, LEN + 1)
    chosen = jax.random.randint(key_pick, (), 0, SEQS)
    positions = jnp.arange(SEQS)
    return jnp.where(positions == chosen, LEN, drawn_lengths).astype(jnp.int32)


def draw_a_log(key, part):
    key = jax.random.fold_in(key, 23)
    uniform_draw = jax.random.uniform(key, (H,), jnp.float32)
    rate_floor = 0.5
    rate_ceiling = LEN / 20.0
    log_floor = jnp.log(jnp.float32(rate_floor))
    log_ceiling = jnp.log(jnp.float32(rate_ceiling))
    log_rates = log_floor + uniform_draw * (log_ceiling - log_floor)
    return (log_rates - jnp.log(jnp.float32(LEN))).astype(jnp.float32)


def block_scale(key, dims, cuts, smallest, largest):
    factor_of = 1.0
    for axis_at, blocks in cuts:
        heights = jax.random.uniform(jax.random.fold_in(jax.random.fold_in(key, 6), axis_at), (blocks,), jnp.float32, smallest / len(cuts), largest / len(cuts))
        factor_of = factor_of * jnp.repeat(jnp.exp(heights), dims[axis_at] // blocks).reshape((-1,) + (1,) * (len(dims) - 1 - axis_at))
    return factor_of


def routed_block(key, own, number, rows, amount, top, reach, lean):
    sequence = jax.random.permutation(key, amount)
    heavy_load, usual = portions_of(amount, rows * top, reach, lean, True), portions_of(amount, rows * top, reach, lean, False)
    places = jnp.arange(amount)

    def named(sizes, turn):
        used = int((sizes > 0).sum())
        fixed = max(1, used // 4)
        moved = fixed + (places - fixed + turn * (used - fixed)) % max(1, amount - fixed)
        return jnp.zeros((amount,), jnp.int32).at[sequence[jnp.where(places < fixed, places, moved)]].set(jnp.asarray(sizes, jnp.int32))

    sizes = jnp.where(number % 4 == 0, named(heavy_load, number // 4), named(usual, number - number // 4 - 1))
    mixed = jax.random.permutation(jax.random.fold_in(own, 3), amount)
    donor, sink = mixed[0:amount // 2 * 2:2], mixed[1:amount // 2 * 2:2]
    room = jnp.minimum(sizes[donor] - 1, reach - sizes[sink]) // 2
    room = jnp.where((donor == sequence[0]) | (sink == sequence[0]) | (sizes[sink] == 0), 0, jnp.maximum(room, 0))
    moved = jax.random.randint(jax.random.fold_in(own, 4), (amount // 2,), 0, 1 << 20) % (room + 1)
    sizes = sizes.at[donor].add(-moved).at[sink].add(moved)
    items = jnp.searchsorted(jnp.cumsum(sizes), jnp.arange(rows * top), side="right").astype(jnp.int32)
    grid = items.reshape(top, rows).T
    grid = grid[jax.random.permutation(jax.random.fold_in(own, 1), rows)]
    turn = jax.random.randint(jax.random.fold_in(own, 2), (rows, 1), 0, top)
    return jnp.take_along_axis(grid, (jnp.arange(top)[None, :] + turn) % top, axis=1)


def portions_of(amount, total, most, skew, full):
    loads = [(1 << 20) // math.isqrt(rank ** skew) + 1 for rank in range(1, amount + 1)]
    largest = most if full else min(most, max(-(-total // amount), total * loads[0] // sum(loads)))
    least = 1 if total - largest >= amount - 1 else 0
    given, surplus = [largest] + [least] * (amount - 1), total - largest - least * (amount - 1)
    while surplus > 0:
        movable = [i for i in range(1, amount) if given[i] < largest] or [i for i in range(1, amount) if given[i] < most]
        pool, remaining = sum([loads[i] for i in movable]), surplus
        for i in movable:
            extra = min(most - given[i], max(1, remaining * loads[i] // pool), surplus)
            given[i] = given[i] + extra
            surplus = surplus - extra
    return np.array(given)


def noise(stream_key, extent, spread, most, cuts=(), dtype=jnp.bfloat16):
    values = spread * jax.random.normal(stream_key, extent, jnp.float32)
    if cuts:
        values = values * block_scale(stream_key, extent, cuts, -0.22, 0.18)
    return jnp.clip(values, -most, most).astype(dtype)


def setup_inputs(seed: int = 0) -> dict:
    key_of = jax.random.split(jax.random.key(seed), 20)
    tokens = noise(key_of[0], (SEQS, LEN, D), 1.0, 6.0, ((0, 4), (1, 32)))
    cotangent = noise(key_of[1], (SEQS, LEN, D), 1.0, 6.0, ((0, 4), (1, 32)))
    lengths = draw_lengths(jax.random.fold_in(key_of[19], 71), 0)
    routes_keys = jax.random.split(jax.random.fold_in(key_of[3], 1), SEQS * LEN // SLOT_DEV)
    routes_turns = jax.random.permutation(jax.random.fold_in(key_of[3], 3), SEQS * LEN // SLOT_DEV)
    routes = jax.vmap(lambda own, number: routed_block(jax.random.fold_in(key_of[3], 2), own, number, SLOT_DEV, E, TOP, MOST, 1))(routes_keys, routes_turns).reshape((SEQS, LEN, TOP))
    norm_gain = jnp.clip(1.0 + 0.1 * jax.random.normal(key_of[4], (D,), jnp.float32), 0.5, 1.5)
    w_in = noise(key_of[5], (D, DIN), D ** -0.5, 0.15625, ((0, 4),))
    conv_weight = noise(key_of[6], (K, CONVCH), K ** -0.5, 3.0, (), jnp.float32)
    conv_bias = jnp.clip(jax.random.uniform(key_of[7], (CONVCH,), jnp.float32, -0.5, 0.5), -0.5, 0.5)
    a_log = draw_a_log(jax.random.fold_in(key_of[19], 71), 0)
    dt_bias = jnp.clip(jax.random.uniform(key_of[9], (H,), jnp.float32, -1.0, 1.0), -1.0, 1.0)
    skip_scale = jnp.clip(jax.random.uniform(key_of[10], (H,), jnp.float32, 0.5, 1.5), 0.5, 1.5)
    gated_gain = jnp.clip(1.0 + 0.1 * jax.random.normal(key_of[11], (INNER,), jnp.float32), 0.5, 1.5)
    w_out = noise(key_of[12], (INNER, D), INNER ** -0.5, 0.109375, ((0, 4),))
    post_gain = jnp.clip(1.0 + 0.1 * jax.random.normal(key_of[13], (D,), jnp.float32), 0.5, 1.5)
    w_router = noise(key_of[14], (D, E), (4 * D) ** -0.5, 0.078125, ((0, 4),))
    shared_in = noise(key_of[15], (D, 2 * SH), D ** -0.5, 0.15625, ((0, 4),))
    shared_out = noise(key_of[16], (SH, D), SH ** -0.5, 0.1875, ((0, 4),))
    expert_in = noise(key_of[17], (E, D, 2 * FF), D ** -0.5, 0.15625, ((0, 4),))
    expert_out = noise(key_of[18], (E, FF, D), FF ** -0.5, 0.25, ((0, 4),))
    return dict(tokens=tokens, cotangent=cotangent, lengths=lengths, routes=routes, norm_gain=norm_gain, w_in=w_in, conv_weight=conv_weight, conv_bias=conv_bias, a_log=a_log, dt_bias=dt_bias, skip_scale=skip_scale, gated_gain=gated_gain, w_out=w_out, post_gain=post_gain, w_router=w_router, shared_in=shared_in, shared_out=shared_out, expert_in=expert_in, expert_out=expert_out)


NORM_EPS = 1e-05
PRECISE = lax.Precision.HIGHEST

@jax.custom_vjp
def low(v):
    return lax.optimization_barrier(v.astype(jnp.bfloat16)).astype(jnp.float32)

@jax.custom_vjp
def low_back(v):
    return v

def low_keep(v):
    return (low(v), None)

def low_pass(kept, grad):
    return (grad,)

def back_keep(v):
    return (v, None)

def back_low(kept, grad):
    return (low(grad),)
low.defvjp(low_keep, low_pass)
low_back.defvjp(back_keep, back_low)

def scaled_rows(values, gain_vector):
    return values * lax.rsqrt(lax.optimization_barrier(jnp.mean(values * values, -1, keepdims=True)) + NORM_EPS) * gain_vector

def product(left, right):
    return jnp.dot(left, right, precision=PRECISE)

def causal_conv(extended, conv_weight, conv_bias):
    tap_count = conv_weight.shape[0]
    length = extended.shape[0] - tap_count + 1
    summed = conv_bias[None, :]
    for offset in range(tap_count):
        summed = summed + conv_weight[offset][None, :] * extended[offset:offset + length]
    return jax.nn.silu(summed)

def scan_inputs(extended, dt_raw, conv_weight, conv_bias, a_log, dt_bias, inner_width):
    mixed = causal_conv(extended, conv_weight, conv_bias)
    length = mixed.shape[0]
    head_count = a_log.shape[0]
    state_width = (mixed.shape[1] - inner_width) // 2
    values = mixed[:, :inner_width].reshape(length, head_count, inner_width // head_count)
    in_map = mixed[:, inner_width:inner_width + state_width]
    out_map = mixed[:, inner_width + state_width:]
    step_size = jax.nn.softplus(dt_raw + dt_bias)
    log_decay = -jnp.exp(a_log) * step_size
    return (values, in_map, out_map, step_size, log_decay)

def block_scan(carried, values, in_map, out_map, step_size, log_decay):
    length = values.shape[0]
    running = jnp.cumsum(log_decay, 0)
    positions = jnp.arange(length)
    is_lower = (positions[:, None] >= positions[None, :])[:, :, None]
    decays = jnp.where(is_lower, jnp.exp(jnp.minimum(running[:, None, :] - running[None, :, :], 0.0)), 0.0)
    kernel = jnp.dot(out_map, in_map.T, precision=PRECISE)
    weights = kernel[:, :, None] * decays * step_size[None, :, :]
    result = jnp.einsum('tsh,shp->thp', weights, values, precision=PRECISE)
    result = result + jnp.exp(running)[:, :, None] * jnp.einsum('tn,hpn->thp', out_map, carried, precision=PRECISE)
    last_sum = running[-1]
    scaled = jnp.exp(last_sum[None, :] - running) * step_size
    leaving = jnp.einsum('sh,shp,sn->hpn', scaled, values, in_map, precision=PRECISE)
    return (jnp.exp(last_sum), leaving, result)

def one_sequence(residual, valid_rows, routes, params):
    norm_gain, w_in, conv_weight, conv_bias, a_log, dt_bias, skip_scale, gated_gain, w_out, post_gain, w_router, shared_in, shared_out, expert_in, expert_out = params
    inner_width = gated_gain.shape[0]
    conv_width = conv_bias.shape[0]
    tap_count = conv_weight.shape[0]
    first_norm = low(scaled_rows(residual, norm_gain))
    projected = low_back(product(first_norm, w_in))
    gate_raw = projected[:, :inner_width]
    conv_in = projected[:, inner_width:inner_width + conv_width]
    dt_raw = projected[:, inner_width + conv_width:]
    extended = jnp.concatenate([jnp.zeros((tap_count - 1, conv_width), jnp.float32), conv_in], 0)
    values, in_map, out_map, step_size, log_decay = scan_inputs(extended, dt_raw, conv_weight, conv_bias, a_log, dt_bias, inner_width)
    block_count = LEN // SLOT_DEV

    def in_blocks(shaped):
        return shaped.reshape((block_count, SLOT_DEV) + shaped.shape[1:])

    def advance(carried, pieces):
        decay_total, leaving, result = block_scan(carried, pieces[0], pieces[1], pieces[2], pieces[3], pieces[4])
        return (decay_total[:, None, None] * carried + leaving, result)
    initial = jnp.zeros((values.shape[1], values.shape[2], in_map.shape[1]), jnp.float32)
    unused, results = lax.scan(jax.checkpoint(advance), initial, (in_blocks(values), in_blocks(in_map), in_blocks(out_map), in_blocks(step_size), in_blocks(log_decay)))
    scanned = results.reshape(values.shape) + skip_scale[None, :, None] * values
    normed = low(scaled_rows(scanned.reshape(LEN, inner_width) * jax.nn.silu(gate_raw), gated_gain))
    middle = residual + low_back(product(normed, w_out))
    second_norm = low(scaled_rows(middle, post_gain))
    logits = low_back(product(second_norm, w_router))
    gate_values = jax.nn.softmax(jnp.take_along_axis(logits, routes, 1), -1)
    route_hits = (routes[:, :, None] == jnp.arange(E)[None, None, :]).astype(jnp.float32)
    gate_dense = lax.optimization_barrier(jnp.sum(gate_values[:, :, None] * route_hits, 1))
    expert_acts = low_back(jnp.einsum('td,edf->tef', second_norm, expert_in, precision=PRECISE))
    expert_hidden = low(jax.nn.silu(expert_acts[..., :FF]) * expert_acts[..., FF:])
    expert_output = low_back(jnp.einsum('tef,efd->ted', expert_hidden, expert_out, precision=PRECISE))
    expert_sum = lax.optimization_barrier(jnp.sum(gate_dense[:, :, None] * low(expert_output), 1))
    shared_acts = low_back(product(second_norm, shared_in))
    shared_hidden = low(jax.nn.silu(shared_acts[:, :SH]) * shared_acts[:, SH:])
    shared_sum = product(shared_hidden, shared_out)
    return valid_rows[:, None] * (middle + expert_sum + shared_sum)

def reference(tokens, cotangent, lengths, routes, norm_gain, w_in, conv_weight, conv_bias, a_log, dt_bias, skip_scale, gated_gain, w_out, post_gain, w_router, shared_in, shared_out, expert_in, expert_out):
    params = tuple((argument.astype(jnp.float32) for argument in (norm_gain, w_in, conv_weight, conv_bias, a_log, dt_bias, skip_scale, gated_gain, w_out, post_gain, w_router, shared_in, shared_out, expert_in, expert_out)))
    residual = tokens.astype(jnp.float32)
    upstream = cotangent.astype(jnp.float32)
    valid_rows = (jnp.arange(LEN)[None, :] < lengths[:, None]).astype(jnp.float32)

    def forward(residual, params):

        def per_sequence(pieces):
            return one_sequence(pieces[0], pieces[1], pieces[2], params)
        return lax.map(jax.checkpoint(per_sequence), (residual, valid_rows, routes))
    block_out, pullback = jax.vjp(forward, residual, params)
    grad_tokens, weight_grads = pullback(upstream)
    return (block_out.astype(jnp.bfloat16), grad_tokens, weight_grads[0], weight_grads[1], weight_grads[2], weight_grads[3], weight_grads[4], weight_grads[5], weight_grads[6], weight_grads[7], weight_grads[8], weight_grads[9], weight_grads[10], weight_grads[11], weight_grads[12], weight_grads[13], weight_grads[14])
```

```python
import functools

import jax
import jax.numpy as jnp
from jax import lax
from jax.experimental import pallas as pl
from jax.experimental.pallas import tpu as pltpu
from jax.sharding import Mesh
from jax.sharding import PartitionSpec as P

SEQ = ("x", "y", "c")
ALL = ("x", "y", "c", "z")
NORM_EPS = 1e-05
PRECISE = lax.Precision.HIGHEST


def scaled_rows(values, gain_vector):
    return values * lax.rsqrt(jnp.mean(values * values, -1, keepdims=True) + NORM_EPS) * gain_vector


def causal_conv(extended, conv_weight, conv_bias):
    tap_count = conv_weight.shape[0]
    length = extended.shape[0] - tap_count + 1
    summed = conv_bias[None, :]
    for offset in range(tap_count):
        summed = summed + conv_weight[offset][None, :] * extended[offset : offset + length]
    return jax.nn.silu(summed)


def scan_inputs(extended, dt_raw, conv_weight, conv_bias, a_log, dt_bias, inner_width):
    mixed = causal_conv(extended, conv_weight, conv_bias)
    length = mixed.shape[0]
    head_count = a_log.shape[0]
    state_width = (mixed.shape[1] - inner_width) // 2
    values = mixed[:, :inner_width].reshape(length, head_count, inner_width // head_count)
    in_map = mixed[:, inner_width : inner_width + state_width]
    out_map = mixed[:, inner_width + state_width :]
    step_size = jax.nn.softplus(dt_raw + dt_bias)
    log_decay = -jnp.exp(a_log) * step_size
    return (values, in_map, out_map, step_size, log_decay)


def block_scan(carried, values, in_map, out_map, step_size, log_decay):
    length = values.shape[0]
    running = jnp.cumsum(log_decay, 0)
    positions = jnp.arange(length)
    is_lower = (positions[:, None] >= positions[None, :])[:, :, None]
    decays = jnp.where(
        is_lower, jnp.exp(jnp.minimum(running[:, None, :] - running[None, :, :], 0.0)), 0.0
    )
    kernel = jnp.dot(out_map, in_map.T, precision=PRECISE)
    weights = kernel[:, :, None] * decays * step_size[None, :, :]
    result = jnp.einsum("tsh,shp->thp", weights, values, precision=PRECISE)
    result = result + jnp.exp(running)[:, :, None] * jnp.einsum(
        "tn,hpn->thp", out_map, carried, precision=PRECISE
    )
    last_sum = running[-1]
    scaled = jnp.exp(last_sum[None, :] - running) * step_size
    leaving = jnp.einsum("sh,shp,sn->hpn", scaled, values, in_map, precision=PRECISE)
    return (jnp.exp(last_sum), leaving, result)


def mixer_rows(
    extended,
    gate_raw,
    dt_raw,
    conv_weight,
    conv_bias,
    a_log,
    dt_bias,
    skip_scale,
    gated_gain,
    carried,
):
    inner_width = gated_gain.shape[0]
    values, in_map, out_map, step_size, log_decay = scan_inputs(
        extended, dt_raw, conv_weight, conv_bias, a_log, dt_bias, inner_width
    )
    unused_total, unused_state, result = block_scan(
        carried, values, in_map, out_map, step_size, log_decay
    )
    result = result + skip_scale[None, :, None] * values
    gated_rows = result.reshape(values.shape[0], inner_width) * jax.nn.silu(gate_raw)
    return scaled_rows(gated_rows, gated_gain)


def state_rows(extended, dt_raw, conv_weight, conv_bias, a_log, dt_bias, inner_width):
    values, in_map, out_map, step_size, log_decay = scan_inputs(
        extended, dt_raw, conv_weight, conv_bias, a_log, dt_bias, inner_width
    )
    carried = jnp.zeros((values.shape[1], values.shape[2], in_map.shape[1]), jnp.float32)
    decay_total, leaving, unused = block_scan(
        carried, values, in_map, out_map, step_size, log_decay
    )
    return (decay_total, leaving)


def glu_back(acts_pair, hidden_back):
    half_width = acts_pair.shape[-1] // 2
    gate_part = acts_pair[..., :half_width]
    up_part = acts_pair[..., half_width:]
    sigmoid_gate = jax.nn.sigmoid(gate_part)
    gate_grad = hidden_back * up_part * sigmoid_gate * (1.0 + gate_part * (1.0 - sigmoid_gate))
    up_grad = hidden_back * gate_part * sigmoid_gate
    return jnp.concatenate([gate_grad, up_grad], -1).astype(jnp.bfloat16)


MESH_ID = pl.DeviceIdType.MESH
RS_ORDERS = (("x", "y", "z"), ("y", "z", "x"), ("z", "x", "y"))
RS_STEPS = 9
RS_COLS = 512


def ring(axis, offset):
    size = lax.axis_size(axis)
    return lax.rem(lax.axis_index(axis) + offset + size, size)


def greet(targets):
    barrier = pltpu.get_barrier_semaphore()
    for target in targets:
        pl.semaphore_signal(barrier, inc=1, device_id=target, device_id_type=MESH_ID)
    pl.semaphore_wait(barrier, len(targets))


def remote(src, dst, send_sem, recv_sem, target):
    return pltpu.make_async_remote_copy(
        src_ref=src,
        dst_ref=dst,
        send_sem=send_sem,
        recv_sem=recv_sem,
        device_id=target,
        device_id_type=MESH_ID,
    )


def dot32(left, right):
    return jnp.dot(left, right, preferred_element_type=jnp.float32)


def grad_sum_kernel(
    a_ref, b_ref, out_ref,
    core_out, core_in, near, far, second_in, third_out, third_in, lines,
    core_ss, core_rs, near_ss, near_rs, far_ss, far_rs, second_ss, second_rs, third_ss, third_rs,
):
    me_core = lax.axis_index("c")
    other = 1 - me_core
    half = core_out.shape[2]
    block = half // 4
    edge = block // 2
    small = block // 4
    unit = out_ref.shape[0]
    kept = small // 4
    lines[...] = jnp.zeros_like(lines)
    greet(
        [{"c": other}]
        + [{axis: ring(axis, o)} for axis in ("x", "y", "z") for o in (1, 2, 3)]
    )

    def left_of(part, k):
        if part == 0:
            return 0
        if part == 1:
            return 1 + jnp.minimum(k // 4, 1)
        return 3 + k // 3

    def core_copy(part, k):
        slot = part * RS_STEPS + k
        return remote(
            core_out.at[lax.rem(k, 2), part], core_in.at[slot],
            core_ss.at[slot], core_rs.at[slot], {"c": other},
        )

    def near_copies(part, k):
        slot = part * RS_STEPS + k
        axis = RS_ORDERS[part][0]
        after, before, across = ring(axis, 1), ring(axis, -1), ring(axis, 2)
        plan = ((before, 0, before), (after, edge, after), (across, 0, after), (across, edge, before))
        return [
            remote(
                core_in.at[slot, pl.ds(which * block + offset, edge)], near.at[slot, n],
                near_ss.at[slot, n], near_rs.at[slot, n], {axis: target},
            )
            for n, (which, offset, target) in enumerate(plan)
        ]

    def far_copies(part, k):
        slot = part * RS_STEPS + k
        axis = RS_ORDERS[part][0]
        return [
            remote(
                near.at[slot, 2 + n], far.at[slot, n],
                far_ss.at[slot, n], far_rs.at[slot, n], {axis: ring(axis, o)},
            )
            for n, o in enumerate((1, -1))
        ]

    def second_copies(part, k):
        slot = part * RS_STEPS + k
        axis = RS_ORDERS[part][1]
        copies = []
        for o in (1, 2, 3):
            target = ring(axis, o)
            copies.append(
                remote(
                    near.at[slot, target // 2, pl.ds(lax.rem(target, 2) * small, small)],
                    second_in.at[slot, o - 1],
                    second_ss.at[slot, o - 1], second_rs.at[slot, o - 1], {axis: target},
                )
            )
        return copies

    def third_copies(part, k):
        slot = part * RS_STEPS + k
        axis = RS_ORDERS[part][2]
        return [
            remote(
                third_out.at[slot, ring(axis, o)], third_in.at[slot, o - 1],
                third_ss.at[slot, o - 1], third_rs.at[slot, o - 1], {axis: ring(axis, o)},
            )
            for o in (1, 2, 3)
        ]

    def stage_product(part, k):
        slot = part * RS_STEPS + k

        @pl.when(k >= 2)
        def _():
            core_copy(part, k - 2).wait_send()

        def rows_at(j, carry):
            rows = pl.ds(pl.multiple_of(j * block, block), block)
            left = a_ref[left_of(part, k), pl.ds(pl.multiple_of(other * half + j * block, block), block), :]
            for col in range(0, RS_COLS, 256):
                core_out[lax.rem(k, 2), part, rows, col : col + 256] = dot32(
                    left, b_ref[:, pl.ds(pl.multiple_of(slot * RS_COLS + col, 256), 256)]
                ).astype(jnp.bfloat16)
            return carry

        lax.fori_loop(0, 4, rows_at, 0)
        core_copy(part, k).start()

    def stage_near(part, k):
        slot = part * RS_STEPS + k
        core_copy(part, k).wait_recv()

        def rows_at(j, carry):
            rows = pl.ds(pl.multiple_of(j * block, block), block)
            left = a_ref[left_of(part, k), pl.ds(pl.multiple_of(me_core * half + j * block, block), block), :]
            for col in range(0, RS_COLS, 256):
                mine = dot32(left, b_ref[:, pl.ds(pl.multiple_of(slot * RS_COLS + col, 256), 256)])
                theirs = core_in[slot, rows, col : col + 256].astype(jnp.float32)
                core_in[slot, rows, col : col + 256] = (mine + theirs).astype(jnp.bfloat16)
            return carry

        lax.fori_loop(0, 4, rows_at, 0)
        for copy in near_copies(part, k):
            copy.start()

    def load(ref, *where):
        return ref[where].astype(jnp.float32)

    def stage_far(part, k):
        slot = part * RS_STEPS + k
        axis = RS_ORDERS[part][0]
        copies = near_copies(part, k)
        for n, (which, offset) in enumerate(((ring(axis, 1), 0), (ring(axis, -1), edge))):
            copies[2 + n].wait_recv()
            rows = pl.ds(pl.multiple_of(which * block + offset, edge), edge)
            near[slot, 2 + n] = (load(near, slot, 2 + n) + load(core_in, slot, rows)).astype(jnp.bfloat16)
        for copy in far_copies(part, k):
            copy.start()

    def stage_second(part, k):
        slot = part * RS_STEPS + k
        me = lax.axis_index(RS_ORDERS[part][0])
        copies, far_in = near_copies(part, k), far_copies(part, k)
        for n in range(2):
            copies[n].wait_recv()
            far_in[n].wait_recv()
            rows = pl.ds(pl.multiple_of(me * block + n * edge, edge), edge)
            near[slot, n] = (
                load(near, slot, n) + load(far, slot, n) + load(core_in, slot, rows)
            ).astype(jnp.bfloat16)
        for copy in second_copies(part, k):
            copy.start()

    def stage_third(part, k):
        slot = part * RS_STEPS + k
        me = lax.axis_index(RS_ORDERS[part][1])
        for copy in second_copies(part, k):
            copy.wait_recv()
        rows = pl.ds(pl.multiple_of(lax.rem(me, 2) * small, small), small)
        lines[part, :small] = load(near, slot, me // 2, rows) + (
            load(second_in, slot, 0) + load(second_in, slot, 1) + load(second_in, slot, 2)
        )
        for j in range(4):
            third_out[slot, j] = lines[part, kept * j : kept * j + unit].astype(jnp.bfloat16)
        for copy in third_copies(part, k):
            copy.start()

    def stage_last(part, k):
        slot = part * RS_STEPS + k
        for copy in third_copies(part, k):
            copy.wait_recv()
        me = lax.axis_index(RS_ORDERS[part][2])
        out_ref[:, pl.ds(pl.multiple_of(slot * RS_COLS, RS_COLS), RS_COLS)] = load(
            third_out, slot, me
        ) + (load(third_in, slot, 0) + load(third_in, slot, 1) + load(third_in, slot, 2))

    stages = (stage_product, stage_near, stage_far, stage_second, stage_third, stage_last)

    def step(t, carry):
        for lag, stage in enumerate(stages):
            k = t - lag

            @pl.when((k >= 0) & (k < RS_STEPS))
            def _():
                for part in range(3):
                    stage(part, k)

        return carry

    lax.fori_loop(0, RS_STEPS + len(stages) - 1, step, 0)

    def finish(k, carry):
        for part in range(3):
            @pl.when(k >= RS_STEPS - 2)
            def _():
                core_copy(part, k).wait_send()

            for copies in (near_copies, far_copies, second_copies, third_copies):
                for copy in copies(part, k):
                    copy.wait_send()
        return carry

    lax.fori_loop(0, RS_STEPS, finish, 0)


def grad_sum(lefts, rights):
    cols, slots, depth = RS_COLS, rights.shape[1] // RS_COLS, rights.shape[0]
    rows = lefts.shape[1]
    half = rows // 2
    block = half // 4
    low = jnp.bfloat16
    sems = lambda *shape: pltpu.SemaphoreType.DMA(shape)
    return pl.pallas_call(
        grad_sum_kernel,
        out_shape=jax.ShapeDtypeStruct((16, slots * cols), jnp.float32),
        in_specs=[pl.BlockSpec(memory_space=pltpu.VMEM)] * 2,
        out_specs=pl.BlockSpec(memory_space=pltpu.VMEM),
        scratch_shapes=[
            pltpu.VMEM((2, 3, half, cols), low),
            pltpu.VMEM((slots, half, cols), low),
            pltpu.VMEM((slots, 4, block // 2, cols), low),
            pltpu.VMEM((slots, 2, block // 2, cols), low),
            pltpu.VMEM((slots, 3, block // 4, cols), low),
            pltpu.VMEM((slots, 4, 16, cols), low),
            pltpu.VMEM((slots, 3, 16, cols), low),
            pltpu.VMEM((3, block // 4 + 8, cols), jnp.float32),
            sems(slots), sems(slots), sems(slots, 4), sems(slots, 4), sems(slots, 2), sems(slots, 2),
            sems(slots, 3), sems(slots, 3), sems(slots, 3), sems(slots, 3),
        ],
        compiler_params=pltpu.CompilerParams(
            collective_id=0, has_side_effects=True, vmem_limit_bytes=58 * 2**20
        ),
        cost_estimate=pl.CostEstimate(flops=2 * slots * rows * depth * cols, bytes_accessed=8 * 2**20, transcendentals=0),
        name="grad_sum",
    )(lefts, rights)


def plane_spot(position):
    return {"x": position // 8, "y": lax.rem(position // 2, 4), "c": lax.rem(position, 2)}


def state_exchange(reverse, state_ref, totals_ref, out_ref, decays_ref, got, back, ss, rs, ts, tr, bs, br):
    spots = 32
    me = lax.axis_index("x") * 8 + lax.axis_index("y") * 2 + lax.axis_index("c")
    heads = got.shape[1]
    barrier = pltpu.get_barrier_semaphore()

    def spot(o):
        return lax.rem(me + o, spots)

    def share(ref, position):
        return ref.at[pl.ds(heads * (position // 2), heads), lax.rem(position, 2)]

    def knock(o, carry):
        pl.semaphore_signal(barrier, inc=1, device_id=plane_spot(spot(o)), device_id_type=MESH_ID)
        return carry

    lax.fori_loop(1, spots, knock, 0)
    pl.semaphore_wait(barrier, spots - 1)

    def out_copy(o):
        target = spot(o)
        return remote(share(state_ref, target), got.at[me], ss.at[o], rs.at[o], plane_spot(target))

    def total_copy(o):
        return remote(totals_ref, decays_ref.at[me], ts.at[o], tr.at[o], plane_spot(spot(o)))

    def back_copy(o):
        target = spot(o)
        return remote(back.at[target], share(out_ref, me), bs.at[o], br.at[o], plane_spot(target))

    def send(o, carry):
        if not reverse:
            total_copy(o).start()
        out_copy(o).start()
        return carry

    lax.fori_loop(1, spots, send, 0)
    mine = pl.ds(heads * (me // 2), heads)
    got[me] = state_ref[mine, lax.rem(me, 2)]
    if not reverse:
        decays_ref[me] = totals_ref[...]

    def arrive(o, carry):
        if not reverse:
            total_copy(o).wait_recv()
        out_copy(o).wait_recv()
        return carry

    lax.fori_loop(1, spots, arrive, 0)
    source = totals_ref if reverse else decays_ref
    lanes = lax.broadcasted_iota(jnp.int32, (8, 128), 1) - heads * (me // 2)

    def advance(step, carried):
        p = spots - 1 - step if reverse else step
        logs = source[p]
        new = []
        for h in range(heads):
            back[p, h] = carried[h].astype(back.dtype)
            decay = jnp.exp(jnp.sum(jnp.where(lanes == h, logs, 0.0), 1, keepdims=True))[:1]
            new.append(carried[h] * decay + got[p, h].astype(jnp.float32))
        return tuple(new)

    zero = jnp.zeros(got.shape[2:], jnp.float32)
    lax.fori_loop(0, spots, advance, (zero,) * heads)

    def send_back(o, carry):
        back_copy(o).start()
        return carry

    lax.fori_loop(1, spots, send_back, 0)
    out_ref[mine, lax.rem(me, 2)] = back[me]

    def finish(o, carry):
        back_copy(o).wait_recv()
        back_copy(o).wait_send()
        out_copy(o).wait_send()
        if not reverse:
            total_copy(o).wait_send()
        return carry

    lax.fori_loop(1, spots, finish, 0)


def scan_forward_kernel(state_ref, totals_ref, out_ref, decays_ref, *scratch):
    state_exchange(False, state_ref, totals_ref, out_ref, decays_ref, *scratch)


def scan_backward_kernel(state_ref, decays_ref, out_ref, *scratch):
    state_exchange(True, state_ref, decays_ref, out_ref, None, *scratch)


def carried_states(state, logs, reverse):
    heads, size, width = state.shape
    share = (heads // 16, size // 2, width)
    state = state.astype(jnp.bfloat16).reshape(heads, 2, size // 2, width)
    sem = pltpu.SemaphoreType.DMA((32,))
    out_shape = jax.ShapeDtypeStruct(state.shape, jnp.bfloat16)
    space = pl.BlockSpec(memory_space=pltpu.VMEM)
    kept = jax.ShapeDtypeStruct((32, 8, 128), jnp.float32)
    result = pl.pallas_call(
        scan_backward_kernel if reverse else scan_forward_kernel,
        out_shape=out_shape if reverse else (out_shape, kept),
        in_specs=[space] * 2,
        out_specs=space if reverse else (space, space),
        scratch_shapes=[pltpu.VMEM((32, *share), jnp.bfloat16)] * 2 + [sem] * 6,
        compiler_params=pltpu.CompilerParams(
            collective_id=2 if reverse else 1, has_side_effects=True, vmem_limit_bytes=32 * 2**20
        ),
        name="scan_backward" if reverse else "scan_forward",
    )(state, logs)
    if reverse:
        return result.reshape(heads, size, width)
    return result[0].reshape(heads, size, width), result[1]


Z_ALL = [{"z": 1}, {"z": 2}, {"z": 3}]


def z_gather_kernel(count, *refs):
    ins, outs, (ss, rs) = refs[:count], refs[count : 2 * count], refs[2 * count :]
    me = lax.axis_index("z")
    greet([{"z": ring("z", o)} for o in (1, 2, 3)])
    copies = []
    for n in range(count):
        for o in (1, 3, 2):
            copies.append(
                remote(ins[n], outs[n].at[me], ss.at[n, o], rs.at[n, o], {"z": ring("z", o)})
            )
            copies[-1].start()
    for n in range(count):
        outs[n][me] = ins[n][...]
    for copy in copies:
        copy.wait()


def z_gather(arrays, cid, name):
    count = len(arrays)
    space = pl.BlockSpec(memory_space=pltpu.VMEM)
    sem = pltpu.SemaphoreType.DMA((count, 4))
    return pl.pallas_call(
        functools.partial(z_gather_kernel, count),
        out_shape=tuple(jax.ShapeDtypeStruct((4, *a.shape), a.dtype) for a in arrays),
        in_specs=[space] * count,
        out_specs=(space,) * count,
        scratch_shapes=[sem, sem],
        compiler_params=pltpu.CompilerParams(
            collective_id=cid, has_side_effects=True, vmem_limit_bytes=32 * 2**20
        ),
        name=name,
    )(*arrays)


def z_sum_kernel(back_ref, part_ref, picks_ref, back_sum, part_sum, picks_all, got, ss, rs):
    me = lax.axis_index("z")
    greet([{"z": ring("z", o)} for o in (1, 2, 3)])
    copies = []
    for n, ref in enumerate((back_ref, part_ref)):
        for o in (1, 3, 2):
            copies.append(
                remote(ref.at[ring("z", o)], got.at[n, o - 1], ss.at[n, o], rs.at[n, o], {"z": ring("z", o)})
            )
            copies[-1].start()
    for o in (1, 3, 2):
        copies.append(
            remote(picks_ref.at[ring("z", o)], picks_all.at[me], ss.at[2, o], rs.at[2, o], {"z": ring("z", o)})
        )
        copies[-1].start()
    picks_all[me] = picks_ref[me]
    for copy in copies:
        copy.wait()
    for n, (ref, out) in enumerate(((back_ref, back_sum), (part_ref, part_sum))):
        def rows_at(j, carry, ref=ref, out=out, n=n):
            rows = pl.ds(pl.multiple_of(j * 32, 32), 32)
            total = ref[me, rows].astype(jnp.float32)
            for o in range(3):
                total = total + got[n, o, rows].astype(jnp.float32)
            out[rows] = total
            return carry

        lax.fori_loop(0, out.shape[0] // 32, rows_at, 0)


def z_sum(back, part, picks):
    space = pl.BlockSpec(memory_space=pltpu.VMEM)
    sem = pltpu.SemaphoreType.DMA((3, 4))
    total = jax.ShapeDtypeStruct(back.shape[1:], jnp.float32)
    return pl.pallas_call(
        z_sum_kernel,
        out_shape=(total, total, jax.ShapeDtypeStruct(picks.shape, picks.dtype)),
        in_specs=[space] * 3,
        out_specs=(space,) * 3,
        scratch_shapes=[pltpu.VMEM((2, 3, *back.shape[1:]), back.dtype), sem, sem],
        compiler_params=pltpu.CompilerParams(
            collective_id=4, has_side_effects=True, vmem_limit_bytes=32 * 2**20
        ),
        name="z_sum",
    )(back, part, picks)


def from_behind(block, axis, distance):
    devices = range(lax.axis_size(axis))
    route = [(i - distance, i) for i in devices if i - distance in devices]
    return lax.ppermute(block, axis, route)


def side_by_side(arrays, axis, dim, along):
    both = jnp.concatenate(arrays, axis=along)
    out, at, finished = (lax.all_gather(both, axis, axis=dim, tiled=True), 0, [])
    for a in arrays:
        finished.append(lax.slice_in_dim(out, at, at + a.shape[along], axis=along))
        at += a.shape[along]
    return tuple(finished)


def owner_rows(values, order, per_owner):
    depth, columns = values.shape
    grid = values.T.reshape(4, 4, 2, 4, per_owner, depth)
    place = {"x": 0, "y": 1, "c": 2, "z": 3}
    return jnp.transpose(grid, [place[a] for a in ("c", *order)] + [4, 5])


def left_rows(values, order, per_owner=12):
    grid = owner_rows(values, order, per_owner)
    if per_owner == 24:
        return [grid[..., :12, :].reshape(1536, -1), grid[..., 12:, :].reshape(1536, -1)]
    grid = jnp.pad(grid, ((0, 0),) * 4 + ((0, 12 - per_owner), (0, 0)))
    return [grid.reshape(1536, -1)]


def local(
    tokens,
    cotangent,
    lengths,
    routes,
    norm_gain,
    w_in,
    conv_weight,
    conv_bias,
    a_log,
    dt_bias,
    skip_scale,
    gated_gain,
    w_out,
    post_gain,
    w_router,
    shared_in,
    shared_out,
    expert_in,
    expert_out,
):
    low = jnp.bfloat16
    full_in, full_out, full_router, full_shared_in, full_shared_out = (
        lax.all_gather(w_in, "z", axis=0, tiled=True),
        lax.all_gather(w_out, "z", axis=0, tiled=True),
        *side_by_side((w_router, shared_in), "z", 0, 1),
        lax.all_gather(shared_out, "z", axis=0, tiled=True),
    )
    tokens, cotangent, routes = tokens[0], cotangent[0], routes[0]
    slot_count, model_width = tokens.shape
    inner_width = gated_gain.shape[0]
    conv_width = conv_bias.shape[0]
    head_count = a_log.shape[0]
    tap_count = conv_weight.shape[0]
    expert_count = w_router.shape[1]
    residual = tokens.astype(jnp.float32)
    positions = lax.axis_index(SEQ) * slot_count + jnp.arange(slot_count)
    valid = positions < lengths[0]
    upstream_low = jnp.where(valid[:, None], cotangent, jnp.zeros_like(cotangent))
    upstream = upstream_low.astype(jnp.float32)
    (all_upstream,) = z_gather((upstream_low,), 3, "gather_upstream")

    first_norm = scaled_rows(residual, norm_gain).astype(low)
    projected = dot32(first_norm, full_in)
    gate_raw = projected[:, :inner_width]
    conv_in = projected[:, inner_width : inner_width + conv_width]
    dt_raw = projected[:, inner_width + conv_width :]
    rim_rows = from_behind(conv_in[slot_count - tap_count + 1 :, :], SEQ, 1)
    extended = jnp.concatenate([rim_rows, conv_in], 0)
    state_fn = functools.partial(state_rows, inner_width=inner_width)
    (decay_total, leaving), state_pull = jax.vjp(
        state_fn, extended, dt_raw, conv_weight, conv_bias, a_log, dt_bias
    )
    log_total = jnp.sum(-jnp.exp(a_log) * jax.nn.softplus(dt_raw + dt_bias), 0)
    totals = jnp.broadcast_to(jnp.pad(log_total, (0, 128 - head_count))[None], (8, 128))
    carried, decays = carried_states(leaving, totals, False)
    carried = carried.astype(jnp.float32)
    normed, mixer_pull = jax.vjp(
        mixer_rows,
        extended,
        gate_raw,
        dt_raw,
        conv_weight,
        conv_bias,
        a_log,
        dt_bias,
        skip_scale,
        gated_gain,
        carried,
    )
    normed_low = normed.astype(low)
    middle = residual + dot32(normed_low, full_out)
    second_norm = scaled_rows(middle, post_gain).astype(low)
    logits = dot32(second_norm, full_router)
    gate_values = jax.nn.softmax(jnp.take_along_axis(logits, routes, 1), -1)
    hits = (routes[:, :, None] == jnp.arange(expert_count)[None, None, :]).astype(jnp.float32)
    gate_dense = jnp.sum(gate_values[..., None] * hits, 1)

    all_rows, all_gates = z_gather((second_norm, gate_dense.T), 5, "gather_rows")
    rows = all_rows.reshape(-1, model_width)
    back_rows = all_upstream.reshape(-1, model_width)
    owned = expert_in.shape[0]
    first_owned = lax.axis_index("z") * owned
    gates = lax.dynamic_slice_in_dim(all_gates, first_owned, owned, 1)
    gates = jnp.swapaxes(gates, 0, 1).reshape(owned, -1)
    hidden_width = expert_out.shape[1]
    acts = jnp.einsum("td,edf->etf", rows, expert_in, preferred_element_type=jnp.float32)
    hidden = (jax.nn.silu(acts[..., :hidden_width]) * acts[..., hidden_width:]).astype(low)
    output = jnp.einsum("etf,efd->etd", hidden, expert_out, preferred_element_type=jnp.float32)
    output = output.astype(low).astype(jnp.float32)
    part = jnp.sum(gates[..., None] * output, 0).astype(low)
    back_wide = back_rows.astype(jnp.float32)
    picks = jnp.sum(output * back_wide[None], -1)
    out_grad = (gates[..., None] * back_wide[None]).astype(low)
    hidden_back = jnp.einsum("etd,efd->etf", out_grad, expert_out, preferred_element_type=jnp.float32)
    act_grad = glu_back(acts, hidden_back)
    back = jnp.einsum("etf,edf->td", act_grad, expert_in, preferred_element_type=jnp.float32).astype(low)
    picks = jnp.swapaxes(picks.reshape(owned, 4, slot_count), 0, 1)
    picks = jnp.pad(picks, ((0, 0), (0, 8 - owned), (0, 0)))
    back_sum, expert_sum, all_picks = z_sum(
        back.reshape(4, slot_count, model_width), part.reshape(4, slot_count, model_width), picks
    )
    grad_expert_in = jnp.einsum("td,etf->edf", rows, act_grad, preferred_element_type=jnp.float32)
    grad_expert_out = jnp.einsum("etf,etd->efd", hidden, out_grad, preferred_element_type=jnp.float32)
    grad_expert_in = lax.psum_scatter(
        grad_expert_in.astype(low), SEQ, scatter_dimension=1, tiled=True
    ).astype(jnp.float32)
    grad_expert_out = lax.psum_scatter(
        grad_expert_out.astype(low), SEQ, scatter_dimension=1, tiled=True
    ).astype(jnp.float32)

    shared_width = full_shared_out.shape[0]
    shared_acts = dot32(second_norm, full_shared_in)
    shared_hidden = (
        jax.nn.silu(shared_acts[:, :shared_width]) * shared_acts[:, shared_width:]
    ).astype(low)
    shared_sum = dot32(shared_hidden, full_shared_out)
    block_out = jnp.where(valid[:, None], middle + expert_sum + shared_sum, 0.0).astype(low)
    shared_back = jnp.einsum("td,hd->th", upstream_low, full_shared_out, preferred_element_type=jnp.float32)
    shared_act_grad = glu_back(shared_acts, shared_back)
    second_back = jnp.einsum("tf,df->td", shared_act_grad, full_shared_in, preferred_element_type=jnp.float32)
    gate_grads = all_picks[:, :owned].reshape(expert_count, slot_count).T
    pick_grads = gate_dense * (gate_grads - jnp.sum(gate_dense * gate_grads, -1, keepdims=True))
    logit_grads = pick_grads.astype(low)
    second_back = second_back + back_sum + jnp.einsum(
        "te,de->td", logit_grads, full_router, preferred_element_type=jnp.float32
    )
    unused_second, second_pull = jax.vjp(scaled_rows, middle, post_gain)
    middle_back, grad_post_gain = second_pull(second_back)
    middle_back = middle_back + upstream
    mix_low = middle_back.astype(low)
    normed_back = jnp.einsum("td,kd->tk", mix_low, full_out, preferred_element_type=jnp.float32)
    (
        ext_mixer,
        gate_back,
        dt_mixer,
        conv_w_mixer,
        conv_b_mixer,
        decay_mixer,
        bias_mixer,
        grad_skip_scale,
        grad_gated_gain,
        incoming_back,
    ) = mixer_pull(normed_back)
    leaving_back = carried_states(incoming_back, decays, True).astype(jnp.float32)
    decay_back = jnp.sum(leaving_back * carried, (1, 2))
    ext_state, dt_state, conv_w_state, conv_b_state, decay_state, bias_state = state_pull(
        (decay_back, leaving_back)
    )
    ext_back = ext_mixer + ext_state
    rim_back = from_behind(ext_back[: tap_count - 1, :].astype(low), SEQ, -1).astype(jnp.float32)
    conv_back = ext_back[tap_count - 1 :, :] + jnp.pad(
        rim_back, ((slot_count - tap_count + 1, 0), (0, 0))
    )
    proj_back = jnp.concatenate([gate_back, conv_back, dt_mixer + dt_state], -1).astype(low)
    first_back = jnp.einsum("tk,dk->td", proj_back, full_in, preferred_element_type=jnp.float32)
    unused_first, first_pull = jax.vjp(scaled_rows, residual, norm_gain)
    input_back, grad_norm_gain = first_pull(first_back)
    grad_tokens = middle_back + input_back

    first, second, third = RS_ORDERS
    lefts = jnp.stack(
        left_rows(first_norm, first)
        + left_rows(first_norm, second)
        + left_rows(second_norm, second)
        + left_rows(normed_low, third, 24)
        + left_rows(shared_hidden, third, 8)
    )
    width_in = proj_back.shape[1]
    zeros = lambda columns: jnp.zeros((slot_count, columns), low)
    rights = jnp.concatenate(
        [
            proj_back,
            zeros(13 * RS_COLS - width_in),
            shared_act_grad,
            logit_grads,
            zeros(RS_COLS - expert_count),
            mix_low,
            mix_low,
            upstream_low,
        ],
        1,
    )
    summed = grad_sum(lefts, rights)
    at = 13 * RS_COLS
    w_in_part = summed[:12, :width_in]
    shared_in_part = summed[:12, at : at + 2 * shared_width]
    at = at + 4 * RS_COLS
    router_part = summed[:12, at : at + expert_count]
    at = at + RS_COLS
    w_out_part = jnp.concatenate(
        [summed[:12, at : at + model_width], summed[:12, at + model_width : at + 2 * model_width]], 0
    )
    at = at + 2 * model_width
    shared_out_part = summed[:8, at : at + model_width]

    smalls = [
        grad_norm_gain,
        (conv_w_mixer + conv_w_state).reshape(-1),
        conv_b_mixer + conv_b_state,
        grad_gated_gain,
        grad_post_gain,
        decay_mixer + decay_state,
        bias_mixer + bias_state,
        grad_skip_scale,
    ]
    sizes = [s.shape[0] for s in smalls]
    packed = jnp.concatenate(smalls)
    packed = lax.psum(jnp.pad(packed, (0, -packed.shape[0] % 1024)).reshape(-1, 128), ALL).reshape(-1)
    pieces, at = [], 0
    for size in sizes:
        pieces.append(packed[at : at + size])
        at += size
    owner = lax.axis_index(ALL)

    def owned_part(values):
        size = values.shape[-1] // 128
        return lax.dynamic_slice_in_dim(values, owner * size, size, values.ndim - 1)

    return (
        block_out[None],
        grad_tokens[None],
        owned_part(pieces[0]),
        w_in_part,
        owned_part(pieces[1].reshape(tap_count, conv_width)),
        owned_part(pieces[2]),
        pieces[5],
        pieces[6],
        pieces[7],
        owned_part(pieces[3]),
        w_out_part,
        owned_part(pieces[4]),
        router_part,
        shared_in_part,
        shared_out_part,
        grad_expert_in,
        grad_expert_out,
    )


def solution(mesh):
    split = Mesh(mesh.devices.reshape(4, 4, 2, 4), ALL)
    placed = (
        P("z", SEQ, None),
        P("z", SEQ, None),
        P("z"),
        P("z", SEQ, None),
        P(),
        P("z", None),
        P(),
        P(),
        P(),
        P(),
        P(),
        P(),
        P("z", None),
        P(),
        P("z", None),
        P("z", None),
        P("z", None),
        P("z", None, None),
        P("z", None, None),
    )
    return jax.shard_map(
        local,
        mesh=split,
        in_specs=placed,
        out_specs=(
            P("z", SEQ, None),
            P("z", SEQ, None),
            P(ALL),
            P(ALL, None),
            P(None, ALL),
            P(ALL),
            P(),
            P(),
            P(),
            P(ALL),
            P(ALL, None),
            P(ALL),
            P(ALL, None),
            P(ALL, None),
            P(ALL, None),
            P("z", SEQ, None),
            P("z", SEQ, None),
        ),
        check_vma=False,
    )
```

```python
import functools

import jax
import jax.numpy as jnp
from jax import lax
from jax.experimental import pallas as pl
from jax.experimental.pallas import tpu as pltpu
from jax.sharding import Mesh
from jax.sharding import PartitionSpec as P

SEQ = ("x", "y", "c")
ALL = ("x", "y", "c", "z")
NORM_EPS = 1e-05
HEADS = 48
INNER = 3072
CONV = 3328


def scaled_rows(values, gain_vector):
    return values * lax.rsqrt(jnp.mean(values * values, -1, keepdims=True) + NORM_EPS) * gain_vector


def glu_back(acts_pair, hidden_back):
    half_width = acts_pair.shape[-1] // 2
    gate_part = acts_pair[..., :half_width]
    up_part = acts_pair[..., half_width:]
    sigmoid_gate = jax.nn.sigmoid(gate_part)
    gate_grad = hidden_back * up_part * sigmoid_gate * (1.0 + gate_part * (1.0 - sigmoid_gate))
    up_grad = hidden_back * gate_part * sigmoid_gate
    return jnp.concatenate([gate_grad, up_grad], -1).astype(jnp.bfloat16)


MESH_ID = pl.DeviceIdType.MESH
RS_ORDERS = (("x", "y", "z"), ("y", "z", "x"), ("z", "x", "y"))
RS_STEPS = 9
RS_COLS = 512


def ring(axis, offset):
    size = lax.axis_size(axis)
    return lax.rem(lax.axis_index(axis) + offset + size, size)


def greet(targets):
    barrier = pltpu.get_barrier_semaphore()
    for target in targets:
        pl.semaphore_signal(barrier, inc=1, device_id=target, device_id_type=MESH_ID)
    pl.semaphore_wait(barrier, len(targets))


def remote(src, dst, send_sem, recv_sem, target):
    return pltpu.make_async_remote_copy(
        src_ref=src,
        dst_ref=dst,
        send_sem=send_sem,
        recv_sem=recv_sem,
        device_id=target,
        device_id_type=MESH_ID,
    )


def dot32(left, right):
    return jnp.dot(left, right, preferred_element_type=jnp.float32)


def grad_sum_kernel(
    a_ref, b_ref, taps_ref, gain_ref, norm_ref, post_ref, heads_ref, router_ref, out_ref, small_ref,
    core_out, core_in, near, far, second_in, third_out, third_in, lines,
    core_ss, core_rs, near_ss, near_rs, far_ss, far_rs, second_ss, second_rs, third_ss, third_rs,
    pack, pack_in, pack_work, pack_others, pack_ss, pack_rs,
):
    me_core = lax.axis_index("c")
    other = 1 - me_core
    half = core_out.shape[2]
    block = half // 4
    edge = block // 2
    small = block // 4
    unit = out_ref.shape[0]
    kept = small // 4
    lines[...] = jnp.zeros_like(lines)
    greet(
        [{"c": other}]
        + [{axis: ring(axis, o)} for axis in ("x", "y", "z") for o in (1, 2, 3)]
    )

    taps_width, wide = taps_ref.shape[1], pack.shape[1] // 2
    pack[:, :taps_width] = taps_ref[...]
    pack[5:6, : gain_ref.shape[1]] = gain_ref[0:1]
    pack[6:7, : norm_ref.shape[1]] = norm_ref[...]
    pack[6:7, norm_ref.shape[1] : 2 * norm_ref.shape[1]] = post_ref[...]
    for i in range(3):
        pack[7:8, TILE * i : TILE * (i + 1)] = heads_ref[i : i + 1]
    pack[:, taps_width:] = router_ref[...]

    def pack_half(ref, which):
        return ref.at[:, pl.ds(pl.multiple_of(which * wide, 128), wide)]

    def pack_core(last):
        if last:
            return remote(pack_work.at[3], pack_half(small_ref, me_core), pack_ss.at[4, 0], pack_rs.at[4, 0], {"c": other})
        return remote(pack_half(pack, other), pack_in, pack_ss.at[0, 0], pack_rs.at[0, 0], {"c": other})

    def pack_copies(s):
        axis = ("x", "y", "z")[s - 1]
        return [
            remote(pack_work.at[s - 1], pack_others.at[s - 1, o - 1], pack_ss.at[s, o], pack_rs.at[s, o], {axis: ring(axis, o)})
            for o in (1, 2, 3)
        ]

    def pack_step(s):
        if s == 0:
            pack_core(False).start()
        if s == 1:
            pack_core(False).wait_recv()
            pack_work[0] = pack[:, pl.ds(pl.multiple_of(me_core * wide, 128), wide)] + pack_in[...]
        if s in (2, 3, 4):
            for copy in pack_copies(s - 1):
                copy.wait_recv()
            pack_work[s - 1] = pack_work[s - 2] + (
                pack_others[s - 2, 0] + pack_others[s - 2, 1] + pack_others[s - 2, 2]
            )
        if s in (1, 2, 3):
            for copy in pack_copies(s):
                copy.start()
        if s == 4:
            pack_core(True).start()
            small_ref[:, pl.ds(pl.multiple_of(me_core * wide, 128), wide)] = pack_work[3]
        if s == 5:
            pack_core(True).wait_recv()
            pack_core(True).wait_send()
            pack_core(False).wait_send()
            for n in (1, 2, 3):
                for copy in pack_copies(n):
                    copy.wait_send()

    def left_of(part, k):
        if part == 0:
            return 0
        if part == 1:
            return 1 + k // 4
        return 4 + k // 3

    def core_copy(part, k):
        slot = part * RS_STEPS + k
        return remote(
            core_out.at[lax.rem(k, 2), part], core_in.at[slot],
            core_ss.at[slot], core_rs.at[slot], {"c": other},
        )

    def near_copies(part, k):
        slot = part * RS_STEPS + k
        axis = RS_ORDERS[part][0]
        after, before, across = ring(axis, 1), ring(axis, -1), ring(axis, 2)
        plan = ((before, 0, before), (after, edge, after), (across, 0, after), (across, edge, before))
        return [
            remote(
                core_in.at[slot, pl.ds(which * block + offset, edge)], near.at[slot, n],
                near_ss.at[slot, n], near_rs.at[slot, n], {axis: target},
            )
            for n, (which, offset, target) in enumerate(plan)
        ]

    def far_copies(part, k):
        slot = part * RS_STEPS + k
        axis = RS_ORDERS[part][0]
        return [
            remote(
                near.at[slot, 2 + n], far.at[slot, n],
                far_ss.at[slot, n], far_rs.at[slot, n], {axis: ring(axis, o)},
            )
            for n, o in enumerate((1, -1))
        ]

    def second_copies(part, k):
        slot = part * RS_STEPS + k
        axis = RS_ORDERS[part][1]
        copies = []
        for o in (1, 2, 3):
            target = ring(axis, o)
            copies.append(
                remote(
                    near.at[slot, target // 2, pl.ds(lax.rem(target, 2) * small, small)],
                    second_in.at[slot, o - 1],
                    second_ss.at[slot, o - 1], second_rs.at[slot, o - 1], {axis: target},
                )
            )
        return copies

    def third_copies(part, k):
        slot = part * RS_STEPS + k
        axis = RS_ORDERS[part][2]
        return [
            remote(
                third_out.at[slot, ring(axis, o)], third_in.at[slot, o - 1],
                third_ss.at[slot, o - 1], third_rs.at[slot, o - 1], {axis: ring(axis, o)},
            )
            for o in (1, 2, 3)
        ]

    def stage_product(part, k):
        slot = part * RS_STEPS + k

        @pl.when(k >= 2)
        def _():
            core_copy(part, k - 2).wait_send()

        left = a_ref[left_of(part, k), pl.ds(pl.multiple_of(other * half, half), half), :]
        for col in range(0, RS_COLS, 256):
            core_out[lax.rem(k, 2), part, :, col : col + 256] = dot32(
                left, b_ref[:, pl.ds(pl.multiple_of(slot * RS_COLS + col, 256), 256)]
            ).astype(jnp.bfloat16)
        core_copy(part, k).start()

    def stage_near(part, k):
        slot = part * RS_STEPS + k
        core_copy(part, k).wait_recv()

        left = a_ref[left_of(part, k), pl.ds(pl.multiple_of(me_core * half, half), half), :]
        for col in range(0, RS_COLS, 256):
            mine = dot32(left, b_ref[:, pl.ds(pl.multiple_of(slot * RS_COLS + col, 256), 256)])
            theirs = core_in[slot, :, col : col + 256].astype(jnp.float32)
            core_in[slot, :, col : col + 256] = (mine + theirs).astype(jnp.bfloat16)
        for copy in near_copies(part, k):
            copy.start()

    def load(ref, *where):
        return ref[where].astype(jnp.float32)

    def stage_far(part, k):
        slot = part * RS_STEPS + k
        axis = RS_ORDERS[part][0]
        copies = near_copies(part, k)
        for n, (which, offset) in enumerate(((ring(axis, 1), 0), (ring(axis, -1), edge))):
            copies[2 + n].wait_recv()
            rows = pl.ds(pl.multiple_of(which * block + offset, edge), edge)
            near[slot, 2 + n] = (load(near, slot, 2 + n) + load(core_in, slot, rows)).astype(jnp.bfloat16)
        for copy in far_copies(part, k):
            copy.start()

    def stage_second(part, k):
        slot = part * RS_STEPS + k
        me = lax.axis_index(RS_ORDERS[part][0])
        copies, far_in = near_copies(part, k), far_copies(part, k)
        for n in range(2):
            copies[n].wait_recv()
            far_in[n].wait_recv()
            rows = pl.ds(pl.multiple_of(me * block + n * edge, edge), edge)
            near[slot, n] = (
                load(near, slot, n) + load(far, slot, n) + load(core_in, slot, rows)
            ).astype(jnp.bfloat16)
        for copy in second_copies(part, k):
            copy.start()

    def stage_third(part, k):
        slot = part * RS_STEPS + k
        me = lax.axis_index(RS_ORDERS[part][1])
        for copy in second_copies(part, k):
            copy.wait_recv()
        rows = pl.ds(pl.multiple_of(lax.rem(me, 2) * small, small), small)
        lines[part, :small] = load(near, slot, me // 2, rows) + (
            load(second_in, slot, 0) + load(second_in, slot, 1) + load(second_in, slot, 2)
        )
        for j in range(4):
            third_out[slot, j] = lines[part, kept * j : kept * j + unit].astype(jnp.bfloat16)
        for copy in third_copies(part, k):
            copy.start()

    def stage_last(part, k):
        slot = part * RS_STEPS + k
        for copy in third_copies(part, k):
            copy.wait_recv()
        me = lax.axis_index(RS_ORDERS[part][2])
        out_ref[:, pl.ds(pl.multiple_of(slot * RS_COLS, RS_COLS), RS_COLS)] = load(
            third_out, slot, me
        ) + (load(third_in, slot, 0) + load(third_in, slot, 1) + load(third_in, slot, 2))

    stages = (stage_product, stage_near, stage_far, stage_second, stage_third, stage_last)

    def step(t, carry):
        for s in range(6):
            @pl.when(t == s)
            def _():
                pack_step(s)

        for lag, stage in enumerate(stages):
            k = t - lag

            @pl.when((k >= 0) & (k < RS_STEPS))
            def _():
                for part in range(3):
                    stage(part, k)

        return carry

    lax.fori_loop(0, RS_STEPS + len(stages) - 1, step, 0)

    def finish(k, carry):
        for part in range(3):
            @pl.when(k >= RS_STEPS - 2)
            def _():
                core_copy(part, k).wait_send()

            for copies in (near_copies, far_copies, second_copies, third_copies):
                for copy in copies(part, k):
                    copy.wait_send()
        return carry

    lax.fori_loop(0, RS_STEPS, finish, 0)


def grad_sum(lefts, rights, taps, gain, norm, post, heads, router):
    cols, slots, depth = RS_COLS, rights.shape[1] // RS_COLS, rights.shape[0]
    rows = lefts.shape[1]
    half = rows // 2
    block = half // 4
    low = jnp.bfloat16
    wide = taps.shape[1] + router.shape[1]
    space = pl.BlockSpec(memory_space=pltpu.VMEM)
    sems = lambda *shape: pltpu.SemaphoreType.DMA(shape)
    return pl.pallas_call(
        grad_sum_kernel,
        out_shape=(
            jax.ShapeDtypeStruct((16, slots * cols), jnp.float32),
            jax.ShapeDtypeStruct((8, wide), jnp.float32),
        ),
        in_specs=[space] * 8,
        out_specs=(space, space),
        scratch_shapes=[
            pltpu.VMEM((2, 3, half, cols), low),
            pltpu.VMEM((slots, half, cols), low),
            pltpu.VMEM((slots, 4, block // 2, cols), low),
            pltpu.VMEM((slots, 2, block // 2, cols), low),
            pltpu.VMEM((slots, 3, block // 4, cols), low),
            pltpu.VMEM((slots, 4, 16, cols), low),
            pltpu.VMEM((slots, 3, 16, cols), low),
            pltpu.VMEM((3, block // 4 + 8, cols), jnp.float32),
            sems(slots), sems(slots), sems(slots, 4), sems(slots, 4), sems(slots, 2), sems(slots, 2),
            sems(slots, 3), sems(slots, 3), sems(slots, 3), sems(slots, 3),
            pltpu.VMEM((8, wide), jnp.float32),
            pltpu.VMEM((8, wide // 2), jnp.float32),
            pltpu.VMEM((4, 8, wide // 2), jnp.float32),
            pltpu.VMEM((3, 3, 8, wide // 2), jnp.float32),
            sems(5, 4), sems(5, 4),
        ],
        compiler_params=pltpu.CompilerParams(
            collective_id=0, has_side_effects=True, vmem_limit_bytes=61 * 2**20
        ),
        cost_estimate=pl.CostEstimate(flops=2 * slots * rows * depth * cols, bytes_accessed=8 * 2**20, transcendentals=0),
        name="grad_sum",
    )(lefts, rights, taps, gain, norm, post, heads, router)


def plane_spot(position):
    return {"x": position // 8, "y": lax.rem(position // 2, 4), "c": lax.rem(position, 2)}


def state_exchange(
    reverse, state_ref, totals_ref, rows_ref, out_ref, decays_ref, all_rows, rows_sum, got, back, ss, rs, ts, tr, bs, br
):
    spots = 32
    me = lax.axis_index("x") * 8 + lax.axis_index("y") * 2 + lax.axis_index("c")
    heads = got.shape[1]
    barrier = pltpu.get_barrier_semaphore()

    def spot(o):
        return lax.rem(me + o, spots)

    def share(ref, position):
        return ref.at[pl.ds(heads * (position // 2), heads), lax.rem(position, 2)]

    def knock(o, carry):
        pl.semaphore_signal(barrier, inc=1, device_id=plane_spot(spot(o)), device_id_type=MESH_ID)
        return carry

    lax.fori_loop(1, spots, knock, 0)
    sides = (1, 3, 2)
    for o in sides:
        pl.semaphore_signal(barrier, inc=1, device_id={"z": ring("z", o)}, device_id_type=MESH_ID)
    pl.semaphore_wait(barrier, spots - 1 + len(sides))
    me_z = lax.axis_index("z")
    row_copies = []
    for o in sides:
        source = rows_ref.at[ring("z", o)] if reverse else rows_ref
        target = all_rows.at[o - 1] if reverse else all_rows.at[me_z]
        row_copies.append(remote(source, target, ts.at[o + 32], tr.at[o + 32], {"z": ring("z", o)}))

    def out_copy(o):
        target = spot(o)
        return remote(share(state_ref, target), got.at[me], ss.at[o], rs.at[o], plane_spot(target))

    def total_copy(o):
        return remote(totals_ref, decays_ref.at[me], ts.at[o], tr.at[o], plane_spot(spot(o)))

    def back_copy(o):
        target = spot(o)
        return remote(back.at[target], share(out_ref, me), bs.at[o], br.at[o], plane_spot(target))

    def send(o, carry):
        if not reverse:
            total_copy(o).start()
        out_copy(o).start()
        return carry

    lax.fori_loop(1, spots, send, 0)
    for copy in row_copies:
        copy.start()
    if not reverse:
        all_rows[me_z] = rows_ref[...]
    mine = pl.ds(heads * (me // 2), heads)
    got[me] = state_ref[mine, lax.rem(me, 2)]
    if not reverse:
        decays_ref[me] = totals_ref[...]

    def arrive(o, carry):
        if not reverse:
            total_copy(o).wait_recv()
        out_copy(o).wait_recv()
        return carry

    lax.fori_loop(1, spots, arrive, 0)
    source = totals_ref if reverse else decays_ref
    lanes = lax.broadcasted_iota(jnp.int32, (8, 128), 1) - heads * (me // 2)

    def advance(step, carried):
        p = spots - 1 - step if reverse else step
        logs = source[p]
        new = []
        for h in range(heads):
            back[p, h] = carried[h].astype(back.dtype)
            decay = jnp.exp(jnp.sum(jnp.where(lanes == h, logs, 0.0), 1, keepdims=True))[:1]
            new.append(carried[h] * decay + got[p, h].astype(jnp.float32))
        return tuple(new)

    zero = jnp.zeros(got.shape[2:], jnp.float32)
    lax.fori_loop(0, spots, advance, (zero,) * heads)

    def send_back(o, carry):
        back_copy(o).start()
        return carry

    lax.fori_loop(1, spots, send_back, 0)
    out_ref[mine, lax.rem(me, 2)] = back[me]

    def finish(o, carry):
        back_copy(o).wait_recv()
        back_copy(o).wait_send()
        out_copy(o).wait_send()
        if not reverse:
            total_copy(o).wait_send()
        return carry

    lax.fori_loop(1, spots, finish, 0)
    for copy in row_copies:
        copy.wait()
    if reverse:
        add_parts(rows_ref, me_z, all_rows, rows_sum)


def scan_forward_kernel(state_ref, totals_ref, rows_ref, out_ref, decays_ref, all_rows, *scratch):
    state_exchange(False, state_ref, totals_ref, rows_ref, out_ref, decays_ref, all_rows, None, *scratch)


def scan_backward_kernel(state_ref, decays_ref, parts_ref, out_ref, rows_sum, got_parts, *scratch):
    state_exchange(True, state_ref, decays_ref, parts_ref, out_ref, None, got_parts, rows_sum, *scratch)


def carried_states(state, logs, rows):
    reverse = rows.ndim == 3
    heads, size, width = state.shape
    share = (heads // 16, size // 2, width)
    state = state.astype(jnp.bfloat16).reshape(heads, 2, size // 2, width)
    sem = pltpu.SemaphoreType.DMA((32,))
    out_shape = jax.ShapeDtypeStruct(state.shape, jnp.bfloat16)
    space = pl.BlockSpec(memory_space=pltpu.VMEM)
    kept = jax.ShapeDtypeStruct((32, 8, 128), jnp.float32)
    args = (state, logs, rows)
    if reverse:
        outs = [out_shape, jax.ShapeDtypeStruct(rows.shape[1:], jnp.float32)]
        extra = [pltpu.VMEM((3, *rows.shape[1:]), rows.dtype)]
    else:
        outs = [out_shape, kept, jax.ShapeDtypeStruct((4, *rows.shape), rows.dtype)]
        extra = []
    result = pl.pallas_call(
        scan_backward_kernel if reverse else scan_forward_kernel,
        out_shape=tuple(outs),
        in_specs=[space] * len(args),
        out_specs=(space,) * len(outs),
        scratch_shapes=extra
        + [pltpu.VMEM((32, *share), jnp.bfloat16)] * 2
        + [sem] * 2
        + [pltpu.SemaphoreType.DMA((36,))] * 2
        + [sem] * 2,
        compiler_params=pltpu.CompilerParams(
            collective_id=2 if reverse else 1, has_side_effects=True, vmem_limit_bytes=32 * 2**20
        ),
        name="scan_backward" if reverse else "scan_forward",
    )(*args)
    return (result[0].reshape(heads, size, width), *result[1:])


def z_gather_kernel(count, *refs):
    ins, outs, (ss, rs) = refs[:count], refs[count : 2 * count], refs[2 * count :]
    me = lax.axis_index("z")
    greet([{"z": ring("z", o)} for o in (1, 2, 3)])
    copies = []
    for n in range(count):
        for o in (1, 3, 2):
            copies.append(
                remote(ins[n], outs[n].at[me], ss.at[n, o], rs.at[n, o], {"z": ring("z", o)})
            )
            copies[-1].start()
    for n in range(count):
        outs[n][me] = ins[n][...]
    for copy in copies:
        copy.wait()


def z_gather(arrays, cid, name):
    count = len(arrays)
    space = pl.BlockSpec(memory_space=pltpu.VMEM)
    sem = pltpu.SemaphoreType.DMA((count, 4))
    return pl.pallas_call(
        functools.partial(z_gather_kernel, count),
        out_shape=tuple(jax.ShapeDtypeStruct((4, *a.shape), a.dtype) for a in arrays),
        in_specs=[space] * count,
        out_specs=(space,) * count,
        scratch_shapes=[sem, sem],
        compiler_params=pltpu.CompilerParams(
            collective_id=cid, has_side_effects=True, vmem_limit_bytes=32 * 2**20
        ),
        name=name,
    )(*arrays)


EXPERT_ORDERS = (("x", "y"), ("y", "x"))
EXPERT_STEPS = 6
EXPERT_COLS = 256


def add_parts(ref, me, got, out):
    def rows_at(j, carry):
        rows = pl.ds(pl.multiple_of(j * 32, 32), 32)
        total = ref[me, rows].astype(jnp.float32)
        for o in range(3):
            total = total + got[o, rows].astype(jnp.float32)
        out[rows] = total
        return carry

    lax.fori_loop(0, out.shape[0] // 32, rows_at, 0)


def expert_sum_kernel(
    rows_ref, acts_ref, hidden_ref, grads_ref, back_ref, picks_ref,
    out_ref, back_sum, picks_all,
    core_out, core_in, near, far, second_in, got,
    core_ss, core_rs, near_ss, near_rs, far_ss, far_rs, second_ss, second_rs, zs, zr,
):
    me_core = lax.axis_index("c")
    me_z = lax.axis_index("z")
    other = 1 - me_core
    half = core_out.shape[2]
    block = half // 4
    edge = block // 2
    small = block // 4
    third = small // 3
    cols = EXPERT_COLS
    greet(
        [{"c": other}]
        + [{axis: ring(axis, o)} for axis in ("x", "y", "z") for o in (1, 2, 3)]
    )

    sums = []
    for n, ref in enumerate((back_ref,)):
        for o in (1, 3, 2):
            sums.append(
                remote(ref.at[ring("z", o)], got.at[n, o - 1], zs.at[n, o], zr.at[n, o], {"z": ring("z", o)})
            )
    for o in (1, 3, 2):
        sums.append(
            remote(picks_ref.at[ring("z", o)], picks_all.at[me_z], zs.at[2, o], zr.at[2, o], {"z": ring("z", o)})
        )
    for copy in sums:
        copy.start()
    picks_all[me_z] = picks_ref[me_z]

    def core_copy(part, k):
        slot = part * EXPERT_STEPS + k
        return remote(
            core_out.at[lax.rem(k, 2), part], core_in.at[slot],
            core_ss.at[slot], core_rs.at[slot], {"c": other},
        )

    def near_copies(part, k):
        slot = part * EXPERT_STEPS + k
        axis = EXPERT_ORDERS[part][0]
        after, before, across = ring(axis, 1), ring(axis, -1), ring(axis, 2)
        plan = ((before, 0, before), (after, edge, after), (across, 0, after), (across, edge, before))
        return [
            remote(
                core_in.at[slot, pl.ds(which * block + offset, edge)], near.at[slot, n],
                near_ss.at[slot, n], near_rs.at[slot, n], {axis: target},
            )
            for n, (which, offset, target) in enumerate(plan)
        ]

    def far_copies(part, k):
        slot = part * EXPERT_STEPS + k
        axis = EXPERT_ORDERS[part][0]
        return [
            remote(
                near.at[slot, 2 + n], far.at[slot, n],
                far_ss.at[slot, n], far_rs.at[slot, n], {axis: ring(axis, o)},
            )
            for n, o in enumerate((1, -1))
        ]

    def second_copies(part, k):
        slot = part * EXPERT_STEPS + k
        axis = EXPERT_ORDERS[part][1]
        copies = []
        for o in (1, 2, 3):
            target = ring(axis, o)
            copies.append(
                remote(
                    near.at[slot, target // 2, pl.ds(lax.rem(target, 2) * small, small)],
                    second_in.at[slot, o - 1],
                    second_ss.at[slot, o - 1], second_rs.at[slot, o - 1], {axis: target},
                )
            )
        return copies

    def load(ref, *where):
        return ref[where].astype(jnp.float32)

    def products(part, k, which_half, store):
        @pl.when(k < 4)
        def _():
            right = acts_ref[part, :, pl.ds(pl.multiple_of(k * cols, cols), cols)]

            at = pl.multiple_of(which_half * half, half)
            store(0, half, dot32(rows_ref[part, pl.ds(at, half), :], right))

        @pl.when(k >= 4)
        def _():
            at = pl.multiple_of(which_half * (half // 3), half // 3)
            left = hidden_ref[part, pl.ds(at, half // 3), :]
            for t in range(3):
                right = grads_ref[part, :, pl.ds(pl.multiple_of(t * 2 * cols + (k - 4) * cols, cols), cols)]
                product = dot32(left, right)
                for i in range(16):
                    store(i * small + t * third, third, product[i * third : (i + 1) * third])

    def stage_product(part, k):
        @pl.when(k >= 2)
        def _():
            core_copy(part, k - 2).wait_send()

        def store(at, size, value):
            core_out[lax.rem(k, 2), part, pl.ds(at, size), :] = value.astype(jnp.bfloat16)

        products(part, k, other, store)
        core_copy(part, k).start()

    def stage_near(part, k):
        slot = part * EXPERT_STEPS + k
        core_copy(part, k).wait_recv()

        def store(at, size, value):
            rows = pl.ds(at, size)
            core_in[slot, rows, :] = (value + load(core_in, slot, rows)).astype(jnp.bfloat16)

        products(part, k, me_core, store)
        for copy in near_copies(part, k):
            copy.start()

    def stage_far(part, k):
        slot = part * EXPERT_STEPS + k
        axis = EXPERT_ORDERS[part][0]
        copies = near_copies(part, k)
        for n, (which, offset) in enumerate(((ring(axis, 1), 0), (ring(axis, -1), edge))):
            copies[2 + n].wait_recv()
            rows = pl.ds(pl.multiple_of(which * block + offset, edge), edge)
            near[slot, 2 + n] = (load(near, slot, 2 + n) + load(core_in, slot, rows)).astype(jnp.bfloat16)
        for copy in far_copies(part, k):
            copy.start()

    def stage_second(part, k):
        slot = part * EXPERT_STEPS + k
        me = lax.axis_index(EXPERT_ORDERS[part][0])
        copies, far_in = near_copies(part, k), far_copies(part, k)
        for n in range(2):
            copies[n].wait_recv()
            far_in[n].wait_recv()
            rows = pl.ds(pl.multiple_of(me * block + n * edge, edge), edge)
            near[slot, n] = (
                load(near, slot, n) + load(far, slot, n) + load(core_in, slot, rows)
            ).astype(jnp.bfloat16)
        for copy in second_copies(part, k):
            copy.start()

    def stage_last(part, k):
        slot = part * EXPERT_STEPS + k
        me = lax.axis_index(EXPERT_ORDERS[part][1])
        for copy in second_copies(part, k):
            copy.wait_recv()
        rows = pl.ds(pl.multiple_of(lax.rem(me, 2) * small, small), small)
        out_ref[part, :, pl.ds(pl.multiple_of(k * cols, cols), cols)] = load(near, slot, me // 2, rows) + (
            load(second_in, slot, 0) + load(second_in, slot, 1) + load(second_in, slot, 2)
        )

    stages = (stage_product, stage_near, stage_far, stage_second, stage_last)

    def step(t, carry):
        for lag, stage in enumerate(stages):
            k = t - lag

            @pl.when((k >= 0) & (k < EXPERT_STEPS))
            def _():
                for part in range(2):
                    stage(part, k)

        return carry

    lax.fori_loop(0, EXPERT_STEPS + len(stages) - 1, step, 0)

    for copy in sums:
        copy.wait()
    add_parts(back_ref, me_z, got.at[0], back_sum)

    def finish(k, carry):
        for part in range(2):
            @pl.when(k >= EXPERT_STEPS - 2)
            def _():
                core_copy(part, k).wait_send()

            for copies in (near_copies, far_copies, second_copies):
                for copy in copies(part, k):
                    copy.wait_send()
        return carry

    lax.fori_loop(0, EXPERT_STEPS, finish, 0)


def expert_sum(rows, acts, hidden, grads, back, picks):
    slots, cols, half = 2 * EXPERT_STEPS, EXPERT_COLS, rows.shape[1] // 2
    block = half // 4
    low = jnp.bfloat16
    sems = lambda *shape: pltpu.SemaphoreType.DMA(shape)
    space = pl.BlockSpec(memory_space=pltpu.VMEM)
    total = jax.ShapeDtypeStruct(back.shape[1:], jnp.float32)
    return pl.pallas_call(
        expert_sum_kernel,
        out_shape=(
            jax.ShapeDtypeStruct((2, block // 4, EXPERT_STEPS * cols), jnp.float32),
            total,
            jax.ShapeDtypeStruct(picks.shape, picks.dtype),
        ),
        in_specs=[space] * 6,
        out_specs=(space,) * 3,
        scratch_shapes=[
            pltpu.VMEM((2, 2, half, cols), low),
            pltpu.VMEM((slots, half, cols), low),
            pltpu.VMEM((slots, 4, block // 2, cols), low),
            pltpu.VMEM((slots, 2, block // 2, cols), low),
            pltpu.VMEM((slots, 3, block // 4, cols), low),
            pltpu.VMEM((1, 3, *back.shape[1:]), low),
            sems(slots), sems(slots), sems(slots, 4), sems(slots, 4), sems(slots, 2), sems(slots, 2),
            sems(slots, 3), sems(slots, 3), sems(3, 4), sems(3, 4),
        ],
        compiler_params=pltpu.CompilerParams(
            collective_id=4, has_side_effects=True, vmem_limit_bytes=52 * 2**20
        ),
        name="expert_sum",
    )(rows, acts, hidden, grads, back, picks)


def gather_kernel(count, *refs):
    shards, plain_in = refs[:count], refs[count : count + 1]
    fulls, plain_out = refs[count + 1 : 2 * count + 1], refs[2 * count + 1 : 2 * count + 2]
    load_sem, own_sem, unit_ss, unit_rs, deep_ss, deep_rs, first_ss, first_rs, second_ss, second_rs, core_ss, core_rs, row_ss, row_rs, *staged = refs[2 * count + 2 :]
    x, y, c, z = (lax.axis_index(a) for a in ALL)
    first_at = (1 - c) * x + c * y
    second_at = c * x + (1 - c) * y

    def along_first(o):
        return {"x": lax.rem(x + (1 - c) * o, 4), "y": lax.rem(y + c * o, 4)}

    def along_second(o):
        return {"x": lax.rem(x + c * o, 4), "y": lax.rem(y + (1 - c) * o, 4)}

    greet(
        [{"c": 1 - c}]
        + [{axis: ring(axis, o)} for axis in ("x", "y", "z") for o in (1, 2, 3)]
    )

    by_rows = (0, 1)

    def sizes(n):
        if n == 0:
            total = fulls[0].shape[1]
            spread = total * 16 // 25
            return total // 2, spread // 2, spread // 32
        total = shards[n].shape[0]
        spread = total if total % 384 else total * 2 // 3
        if n in by_rows:
            return total // 2, spread // 2, spread // 32
        return total, spread, spread // 16

    def place(n, deep, offset):
        total, spread, unit = sizes(n)
        if n in by_rows:
            return (2 * spread + c * (total - spread) if deep else c * spread) + offset
        return (spread if deep else 0) + offset

    def window(n, shard, deep, offset, length):
        rows, width = shards[n].shape
        at = place(n, deep, offset)
        if n == 0:
            return fulls[0].at[shard, pl.ds(pl.multiple_of(at, 16), length)]
        rows = pl.ds(pl.multiple_of(at + shard * rows, 16), length)
        if n in by_rows:
            return fulls[n].at[rows]
        return fulls[n].at[rows, pl.ds(pl.multiple_of(c * (width // 2), 128), width // 2)]

    def own_window(n, deep, offset, length):
        width = shards[n].shape[1]
        rows = pl.ds(pl.multiple_of(place(n, deep, offset), 16), length)
        if n in by_rows:
            return shards[n].at[rows]
        return shards[n].at[rows, pl.ds(pl.multiple_of(c * (width // 2), 128), width // 2)]

    def own_rows(n):
        return fulls[0].shape[1] if n == 0 else shards[n].shape[0]

    def own_load(n):
        return pltpu.make_async_copy(shards[n].at[pl.ds(0, own_rows(n))], staged[n], load_sem.at[n])

    def own_copy(n):
        if n == 0:
            return pltpu.make_async_copy(staged[0], fulls[0].at[z], own_sem.at[0])
        total = shards[n].shape[0]
        return pltpu.make_async_copy(
            staged[n], fulls[n].at[pl.ds(pl.multiple_of(z * total, 16), total)], own_sem.at[n]
        )

    def came_from(o):
        return lax.rem(z - o + 4, 4)

    def unit_copy(n, o):
        unit = sizes(n)[2]
        at = (second_at * 4 + first_at) * unit
        return remote(
            own_window(n, False, at, unit), window(n, z, False, at, unit), unit_ss.at[n, o], unit_rs.at[n, o], {"z": ring("z", o)}
        )

    def deep_copy(n, o):
        total, spread, unit = sizes(n)
        return remote(
            own_window(n, True, 0, total - spread), window(n, z, True, 0, total - spread),
            deep_ss.at[n, o], deep_rs.at[n, o], {"z": ring("z", o)},
        )

    def deep_forward(n, o):
        total, spread, unit = sizes(n)
        edge = (total - spread) // 2
        block = window(n, came_from(o), True, 0 if o == 1 else edge, edge)
        return remote(block, block, deep_ss.at[n, 3 + o], deep_rs.at[n, 3 + o], {"z": ring("z", o)})

    def first_copy(n, o, step):
        unit = sizes(n)[2]
        block = window(n, came_from(o), False, (second_at * 4 + first_at) * unit, unit)
        return remote(block, block, first_ss.at[n, o, step], first_rs.at[n, o, step], along_first(step))

    def second_copy(n, o, step):
        unit = sizes(n)[2]
        block = window(n, came_from(o), False, second_at * 4 * unit, 4 * unit)
        return remote(block, block, second_ss.at[n, o, step], second_rs.at[n, o, step], along_second(step))

    def second_forward(n, o, step):
        unit = sizes(n)[2]
        source = lax.rem(second_at + 4 - step, 4)
        at = source * 4 * unit + (0 if step == 1 else 2 * unit)
        block = window(n, came_from(o), False, at, 2 * unit)
        return remote(block, block, second_ss.at[n, o, 4 + step], second_rs.at[n, o, 4 + step], along_second(step))

    def core_copies(n, o):
        total, spread, unit = sizes(n)
        shard = came_from(o)
        blocks = [window(n, shard, False, 0, spread)]
        if spread < total:
            blocks.append(window(n, shard, True, 0, total - spread))
        return [
            remote(block, block, core_ss.at[n, o, i], core_rs.at[n, o, i], {"c": 1 - c})
            for i, block in enumerate(blocks)
        ]

    def plain_copy(i, o):
        return remote(plain_in[i], plain_out[i].at[z], row_ss.at[i, o], row_rs.at[i, o], {"z": ring("z", o)})

    arrays = range(count)
    deep = [n for n in arrays if sizes(n)[0] > sizes(n)[1]]
    sides, offsets = (1, 3), (1, 3, 2)
    for n in arrays:
        for o in offsets:
            unit_copy(n, o).start()
    for n in deep:
        for o in sides:
            deep_copy(n, o).start()
    for i in range(1):
        for o in offsets:
            plain_copy(i, o).start()
    for n in arrays:
        own_load(n).start()
    own_plain = [pltpu.make_async_copy(plain_in[i], plain_out[i].at[z], own_sem.at[count + i]) for i in range(1)]
    for copy in own_plain:
        copy.start()
    for n in arrays:
        for o in offsets:
            unit_copy(n, o).wait_recv()
            for step in offsets:
                first_copy(n, o, step).start()
    for n in arrays:
        own_load(n).wait()
        own_copy(n).start()
    for n in arrays:
        for o in offsets:
            for step in offsets:
                first_copy(n, o, step).wait_recv()
            for step in sides:
                second_copy(n, o, step).start()
    for n in arrays:
        if n in deep:
            for o in sides:
                deep_copy(n, o).wait_recv()
                deep_forward(n, o).start()
                core_copies(n, o)[1].start()
        for o in offsets:
            for step in sides:
                second_copy(n, o, step).wait_recv()
                second_forward(n, o, step).start()
    for n in arrays:
        for o in offsets:
            for step in sides:
                second_forward(n, o, step).wait_recv()
            core_copies(n, o)[0].start()
        if n in deep:
            for o in sides:
                deep_forward(n, o).wait_recv()
            core_copies(n, 2)[1].start()
    for i in range(1):
        for o in offsets:
            plain_copy(i, o).wait()
        own_plain[i].wait()
    for n in arrays:
        own_copy(n).wait()
        for o in offsets:
            for copy in core_copies(n, o):
                copy.wait()
            unit_copy(n, o).wait_send()
            for step in offsets:
                first_copy(n, o, step).wait_send()
            for step in sides:
                second_copy(n, o, step).wait_send()
                second_forward(n, o, step).wait_send()
        if n in deep:
            for o in sides:
                deep_copy(n, o).wait_send()
                deep_forward(n, o).wait_send()


def gather_weights(shards, plain, main_rows):
    count = len(shards)
    space = pl.BlockSpec(memory_space=pl.ANY)
    sem = lambda *shape: pltpu.SemaphoreType.DMA(shape)
    fulls = [(4, main_rows, shards[0].shape[1])] + [(4 * s.shape[0], s.shape[1]) for s in shards[1:]]
    return pl.pallas_call(
        functools.partial(gather_kernel, count),
        out_shape=tuple(jax.ShapeDtypeStruct(f, jnp.bfloat16) for f in fulls)
        + tuple(jax.ShapeDtypeStruct((4, *p.shape), p.dtype) for p in plain),
        in_specs=[space] * (count + 1),
        out_specs=(space,) * (count + 1),
        scratch_shapes=[
            sem(count),
            sem(count + 1),
            sem(count, 4), sem(count, 4), sem(count, 8), sem(count, 8),
            sem(count, 4, 4), sem(count, 4, 4), sem(count, 4, 8), sem(count, 4, 8),
            sem(count, 4, 2), sem(count, 4, 2), sem(1, 4), sem(1, 4),
            pltpu.VMEM((main_rows, shards[0].shape[1]), jnp.bfloat16),
        ]
        + [pltpu.VMEM(s.shape, s.dtype) for s in shards[1:]],
        compiler_params=pltpu.CompilerParams(
            collective_id=6, has_side_effects=True, vmem_limit_bytes=60 * 2**20
        ),
        name="gather_weights",
    )(*shards, *plain)


TILE = 128
HIGH = lax.Precision.HIGHEST


def tile_at(j):
    return pl.ds(pl.multiple_of(j * TILE, TILE), TILE)


def dot_nt(left, right):
    return lax.dot_general(left, right, (((1,), (1,)), ((), ())), preferred_element_type=jnp.float32)


def short(values):
    return values.astype(jnp.bfloat16)


def lane_ids():
    return lax.broadcasted_iota(jnp.int32, (TILE, TILE), 1)


def row_ids():
    return lax.broadcasted_iota(jnp.int32, (TILE, TILE), 0)


def head_steps(tail_ref, heads_ref):
    raw = tail_ref[...] + heads_ref[1:2]
    used = lane_ids() < HEADS
    small = jnp.exp(-jnp.abs(raw))
    tail = jnp.where(small < 1e-3, small * (1.0 - small * (0.5 - small / 3.0)), jnp.log(1.0 + small))
    soft = jnp.maximum(raw, 0.0) + tail
    step = jnp.where(used, soft, 0.0)
    return raw, step, jnp.where(used, -jnp.exp(heads_ref[0:1]) * step, 0.0)


def head_columns(values, pair):
    moved = pltpu.roll(values, lax.rem(TILE - 2 * pair, TILE), 1)
    return moved[:, 0:1], moved[:, 1:2]


def both_heads(columns):
    return jnp.where(lane_ids() < TILE // 2, columns[0], columns[1])


def taps_of(ext, cw_ref, lanes):
    summed = cw_ref[4:5, lanes]
    for k in range(4):
        summed = summed + cw_ref[k : k + 1, lanes] * ext[5 + k : 5 + k + TILE]
    return summed


def fill_ext(ext, halo_ref, proj_ref, j):
    ext[0:8] = halo_ref[:, tile_at(j)]
    ext[8 : 8 + TILE] = proj_ref[:, pl.ds(pl.multiple_of(INNER + j * TILE, TILE), TILE)]


def mixer_in_kernel(proj_ref, tail_ref, halo_ref, cw_ref, heads_ref, mixed_ref, state_ref, totals_ref, run_ref, step_ref, ext):
    unused_raw, step, log_decay = head_steps(tail_ref, heads_ref)
    lower = (row_ids() >= lane_ids()).astype(jnp.float32)
    run = jnp.dot(lower, log_decay, precision=HIGH, preferred_element_type=jnp.float32)
    run_ref[...] = run
    step_ref[...] = step
    last = run[TILE - 1 : TILE]
    totals_ref[...] = jnp.broadcast_to(last, totals_ref.shape)
    weight = jnp.exp(last - run) * step

    def conv(j, carry):
        fill_ext(ext, halo_ref, proj_ref, j)
        u = taps_of(ext, cw_ref, tile_at(j))
        mixed_ref[:, tile_at(j)] = u * jax.nn.sigmoid(u)
        return carry

    lax.fori_loop(0, CONV // TILE, conv, 0)
    in_map = short(mixed_ref[:, INNER : INNER + TILE])

    def state(p, carry):
        scaled = mixed_ref[:, tile_at(p)] * both_heads(head_columns(weight, p))
        state_ref[p] = short(dot32(short(scaled.T), in_map))
        return carry

    lax.fori_loop(0, HEADS // 2, state, 0, unroll=2)


def decays_of(column, row, lower):
    return jnp.where(lower, jnp.exp(jnp.minimum(column - row, 0.0)), 0.0)


def mixer_out_kernel(proj_ref, mixed_ref, run_ref, step_ref, carried_ref, wide_ref, normed_ref, scanned_ref, gated, rows, ):
    run = run_ref[...]
    rows[0] = run.T
    rows[1] = step_ref[...].T
    lower = row_ids() >= lane_ids()
    in_map = mixed_ref[:, INNER : INNER + TILE]
    out_map = mixed_ref[:, INNER + TILE : INNER + 2 * TILE]
    kernel = lax.dot_general(out_map, in_map, (((1,), (1,)), ((), ())), precision=HIGH, preferred_element_type=jnp.float32)
    out_low = short(out_map)

    def pair(p, squares):
        values = mixed_ref[:, tile_at(p)]
        values_low = short(values)
        columns = head_columns(run, p)
        parts = []
        for h in range(2):
            decays = decays_of(columns[h], rows[0, pl.ds(2 * p + h, 1)], lower)
            weights = kernel * decays * rows[1, pl.ds(2 * p + h, 1)]
            parts.append(dot32(short(weights), values_low))
        result = jnp.where(lane_ids() < TILE // 2, parts[0], parts[1])
        result = result + jnp.exp(both_heads(columns)) * dot_nt(out_low, carried_ref[p])
        result = result + wide_ref[0:1, tile_at(p)] * values
        scanned_ref[:, tile_at(p)] = result
        gate = proj_ref[:, tile_at(p)]
        g = result * (gate * jax.nn.sigmoid(gate))
        gated[:, tile_at(p)] = g
        return squares + g * g

    squares = lax.fori_loop(0, HEADS // 2, pair, jnp.zeros((TILE, TILE), jnp.float32), unroll=2)
    scale = lax.rsqrt(jnp.sum(squares, 1, keepdims=True) / INNER + NORM_EPS)

    def norm(p, carry):
        normed_ref[:, tile_at(p)] = short(gated[:, tile_at(p)] * scale * wide_ref[1:2, tile_at(p)])
        return carry

    lax.fori_loop(0, HEADS // 2, norm, 0, unroll=2)


def gate_back_kernel(proj_ref, mixed_ref, scanned_ref, back_ref, run_ref, wide_ref, result_ref, gate_ref, gain_ref, state_ref, gated):
    run = run_ref[...]
    out_map = short(mixed_ref[:, INNER + TILE : INNER + 2 * TILE])

    def first(p, sums):
        gate = proj_ref[:, tile_at(p)]
        g = scanned_ref[:, tile_at(p)] * (gate * jax.nn.sigmoid(gate))
        gated[:, tile_at(p)] = g
        back = back_ref[:, tile_at(p)] * wide_ref[1:2, tile_at(p)]
        return sums[0] + g * g, sums[1] + g * back

    zero = jnp.zeros((TILE, TILE), jnp.float32)
    squares, products = lax.fori_loop(0, HEADS // 2, first, (zero, zero), unroll=2)
    scale = lax.rsqrt(jnp.sum(squares, 1, keepdims=True) / INNER + NORM_EPS)
    shift = jnp.sum(products, 1, keepdims=True) * scale * scale * scale / INNER

    def second(p, carry):
        lanes = tile_at(p)
        gate = proj_ref[:, lanes]
        sig = jax.nn.sigmoid(gate)
        g = gated[:, lanes]
        back = back_ref[:, lanes]
        gain_ref[:, lanes] = jnp.broadcast_to(jnp.sum(back * g * scale, 0, keepdims=True), (8, TILE))
        g_back = back * wide_ref[1:2, lanes] * scale - g * shift
        result_back = g_back * (gate * sig)
        result_ref[:, lanes] = result_back
        gate_ref[:, lanes] = short(g_back * scanned_ref[:, lanes] * sig * (1.0 + gate * (1.0 - sig)))
        moved = result_back * jnp.exp(both_heads(head_columns(run, p)))
        state_ref[p] = short(dot32(short(moved.T), out_map))
        return carry

    lax.fori_loop(0, HEADS // 2, second, 0, unroll=2)


def mixer_back_kernel(
    proj_ref, tail_ref, halo_ref, cw_ref, heads_ref, mixed_ref, run_ref, step_ref, wide_ref,
    carried_ref, result_ref, leaving_ref,
    conv_ref, rim_ref, taps_ref, step_back_ref, heads_back_ref,
    rows, column_sums, row_sums, kernel_back, maps_back, mixed_back, ext, padded,
):
    run, step = run_ref[...], step_ref[...]
    rows[0] = run.T
    rows[1] = step.T
    lanes_id, rows_id = lane_ids(), row_ids()
    lower = rows_id >= lanes_id
    left_half = lanes_id < TILE // 2
    half_line = lax.broadcasted_iota(jnp.int32, (1, TILE), 1) // (TILE // 2)
    in_map = mixed_ref[:, INNER : INNER + TILE]
    out_map = mixed_ref[:, INNER + TILE : INNER + 2 * TILE]
    kernel = lax.dot_general(out_map, in_map, (((1,), (1,)), ((), ())), precision=HIGH, preferred_element_type=jnp.float32)
    in_low, out_low = short(in_map), short(out_map)
    last = run[TILE - 1 : TILE]
    fade = jnp.exp(last - run)
    weight = fade * step
    column_sums[...] = jnp.zeros_like(column_sums)
    row_sums[...] = jnp.zeros_like(row_sums)
    kernel_back[...] = jnp.zeros_like(kernel_back)
    maps_back[...] = jnp.zeros_like(maps_back)

    def pair(p, carry):
        lanes = tile_at(p)
        values, back = mixed_ref[:, lanes], result_ref[:, lanes]
        values_low, back_low = short(values), short(back)
        columns = head_columns(run, p)
        which = 2 * p + (rows_id >= TILE // 2).astype(jnp.int32)
        spread = (lanes_id == which).astype(jnp.bfloat16)
        parts = []
        for h in range(2):
            at = pl.ds(2 * p + h, 1)
            decays = decays_of(columns[h], rows[0, at], lower)
            plain = kernel * decays
            steps = rows[1, at]
            weights = plain * steps
            mine = jnp.where(left_half, back, 0.0) if h == 0 else jnp.where(left_half, 0.0, back)
            weights_back = dot_nt(short(mine), values_low)
            kernel_back[...] += weights_back * (decays * steps)
            loose = weights_back * plain
            pulled = short(loose * steps)
            column_sums[0] += dot32(pulled, (lanes_id == 2 * p + h).astype(jnp.bfloat16))
            row_sums[0, at] = jnp.sum(pulled.astype(jnp.float32), 0, keepdims=True)
            row_sums[1, at] = jnp.sum(loose, 0, keepdims=True)
            parts.append(dot32(short(weights.T), back_low))
        values_back = jnp.where(left_half, parts[0], parts[1]) + wide_ref[0:1, lanes] * back
        carried, leaving = carried_ref[p], leaving_ref[p]
        moved = back * jnp.exp(both_heads(columns))
        moved_low = short(moved)
        seen = dot_nt(out_low, carried)
        column_sums[0] += dot32(short(moved * seen), spread)
        maps_back[1] += dot32(moved_low, carried)
        weight_pair = both_heads(head_columns(weight, p))
        pulled_state = dot_nt(in_low, leaving)
        values_back = values_back + weight_pair * pulled_state
        maps_back[0] += dot32(short(values * weight_pair), leaving)
        column_sums[1] += dot32(short(values * pulled_state), spread)
        mixed_back[:, lanes] = values_back
        skip_part = jnp.sum(back * values, 0, keepdims=True)
        kept = jnp.sum(carried.astype(jnp.float32) * leaving.astype(jnp.float32), 1, keepdims=True)
        for h in range(2):
            half = slice(h * TILE // 2, (h + 1) * TILE // 2)
            row_sums[2, pl.ds(2 * p + h, 1)] = jnp.broadcast_to(
                jnp.sum(jnp.where(half_line == h, skip_part, 0.0), 1, keepdims=True), (1, TILE)
            )
            row_sums[3, pl.ds(2 * p + h, 1)] = jnp.broadcast_to(
                jnp.sum(kept[half], 0, keepdims=True), (1, TILE)
            )
        return carry

    lax.fori_loop(0, HEADS // 2, pair, 0)

    used = lanes_id < HEADS
    loose_columns = row_sums[1].T
    weight_back = column_sums[1]
    run_back = column_sums[0] - row_sums[0].T - weight * weight_back
    skip_back, decay_back = row_sums[2].T, row_sums[3].T
    last_back = jnp.sum(weight * weight_back, 0, keepdims=True) + jnp.exp(last) * decay_back[0:1]
    run_back = run_back + jnp.where(rows_id == TILE - 1, last_back, 0.0)
    upper = (lanes_id >= rows_id).astype(jnp.float32)
    log_back = jnp.dot(upper, run_back, precision=HIGH, preferred_element_type=jnp.float32)
    raw, unused_step, log_decay = head_steps(tail_ref, heads_ref)
    rate = jnp.exp(heads_ref[0:1])
    step_back = loose_columns + fade * weight_back - rate * log_back
    raw_back = jnp.where(used, step_back * jax.nn.sigmoid(raw), 0.0)
    step_back_ref[...] = raw_back
    rate_back = jnp.sum(jnp.where(used, log_back * log_decay, 0.0), 0, keepdims=True)
    bias_back = jnp.sum(raw_back, 0, keepdims=True)
    at_row = lax.broadcasted_iota(jnp.int32, (8, TILE), 0)
    heads_back_ref[...] = jnp.where(
        at_row == 0, rate_back, jnp.where(at_row == 1, bias_back, jnp.where(at_row == 2, skip_back[0:1], 0.0))
    )
    both = kernel_back[...]
    mixed_back[:, INNER : INNER + TILE] = maps_back[0] + dot32(short(both.T), out_low)
    mixed_back[:, INNER + TILE : INNER + 2 * TILE] = maps_back[1] + dot32(short(both), in_low)
    padded[0:8] = jnp.zeros((8, TILE), jnp.float32)
    padded[8 + TILE : 16 + TILE] = jnp.zeros((8, TILE), jnp.float32)

    def conv(j, carry):
        lanes = tile_at(j)
        fill_ext(ext, halo_ref, proj_ref, j)
        u = taps_of(ext, cw_ref, lanes)
        sig = jax.nn.sigmoid(u)
        back = mixed_back[:, lanes] * sig * (1.0 + u * (1.0 - sig))
        padded[8 : 8 + TILE] = back
        taps_ref[4:5, lanes] = jnp.sum(back, 0, keepdims=True)
        total = jnp.zeros((TILE, TILE), jnp.float32)
        rim = jnp.zeros((8, TILE), jnp.float32)
        for k in range(4):
            tap = cw_ref[k : k + 1, lanes]
            taps_ref[k : k + 1, lanes] = jnp.sum(back * ext[5 + k : 5 + k + TILE], 0, keepdims=True)
            total = total + tap * padded[11 - k : 11 - k + TILE]
            rim = rim + tap * padded[3 - k : 11 - k]
        conv_ref[:, lanes] = total
        rim_ref[:, lanes] = rim
        return carry

    lax.fori_loop(0, CONV // TILE, conv, 0)


def tile_call(kernel, outs, scratch, name, *args):
    space = pl.BlockSpec(memory_space=pltpu.VMEM)
    return pl.pallas_call(
        kernel,
        out_shape=tuple(jax.ShapeDtypeStruct(s, d) for s, d in outs),
        in_specs=[space] * len(args),
        out_specs=(space,) * len(outs),
        scratch_shapes=[pltpu.VMEM(s, jnp.float32) for s in scratch],
        compiler_params=pltpu.CompilerParams(vmem_limit_bytes=40 * 2**20),
        name=name,
    )(*args)


PROJ_BLOCK = 640


def project_kernel(tokens_ref, gain_ref, *refs):
    *mains, tail_ref, norm_ref, proj_ref, tail_out, kept = refs
    width = mains[0].shape[2]

    def product(weights):
        total = dot32(weights[0], kept[:width])
        for i in range(1, len(weights)):
            total = total + dot32(weights[i], kept[i * width : (i + 1) * width])
        return total.T

    @pl.when(pl.program_id(0) == 0)
    def _():
        values = tokens_ref[...].astype(jnp.float32)
        scale = lax.rsqrt(jnp.mean(values * values, 1, keepdims=True) + NORM_EPS)
        normed = values * scale * gain_ref[...]
        norm_ref[...] = short(normed)
        kept[...] = short(normed.T)
        tail_out[...] = product([tail_ref[i] for i in range(len(mains))])

    proj_ref[...] = product([m[0] for m in mains])


def project(tokens, gain, main, tail):
    parts, rows, width = main.shape
    slots, model = tokens.shape
    whole = lambda shape: pl.BlockSpec(shape, lambda j: (0,) * len(shape))
    return pl.pallas_call(
        project_kernel,
        grid=(rows // PROJ_BLOCK,),
        out_shape=(
            jax.ShapeDtypeStruct((slots, model), jnp.bfloat16),
            jax.ShapeDtypeStruct((slots, rows), jnp.float32),
            jax.ShapeDtypeStruct((slots, tail.shape[1]), jnp.float32),
        ),
        in_specs=[
            whole((slots, model)),
            whole((1, model)),
            *[pl.BlockSpec((1, PROJ_BLOCK, width), lambda j, i=i: (i, j, 0)) for i in range(parts)],
            whole(tail.shape),
        ],
        out_specs=(
            whole((slots, model)),
            pl.BlockSpec((slots, PROJ_BLOCK), lambda j: (0, j)),
            whole((slots, tail.shape[1])),
        ),
        scratch_shapes=[pltpu.VMEM((model, slots), jnp.bfloat16)],
        compiler_params=pltpu.CompilerParams(vmem_limit_bytes=56 * 2**20),
        name="project",
    )(tokens, gain, *[main] * parts, tail)


def project_back_kernel(back_ref, tail_back_ref, *refs):
    *mains, tail_ref, tokens_ref, gain_ref, middle_ref, tokens_back_ref, gain_back_ref, total = refs
    parts, width = len(mains), mains[0].shape[2]
    step = pl.program_id(0)

    @pl.when(step == 0)
    def _():
        for i in range(parts):
            total[:, i * width : (i + 1) * width] = dot32(tail_back_ref[...], tail_ref[i])

    for i in range(parts):
        total[:, i * width : (i + 1) * width] += dot32(back_ref[...], mains[i][0])

    @pl.when(step == pl.num_programs(0) - 1)
    def _():
        values = tokens_ref[...].astype(jnp.float32)
        scale = lax.rsqrt(jnp.mean(values * values, 1, keepdims=True) + NORM_EPS)
        back = total[...]
        gain_back_ref[...] = jnp.sum(back * values * scale, 0, keepdims=True)
        spread = back * gain_ref[...]
        shift = jnp.mean(spread * values, 1, keepdims=True) * scale * scale * scale
        tokens_back_ref[...] = middle_ref[...] + spread * scale - values * shift


def project_back(back, tail_back, main, tail, tokens, gain, middle_back):
    parts, rows, width = main.shape
    slots, model = tokens.shape
    whole = lambda shape: pl.BlockSpec(shape, lambda j: (0,) * len(shape))
    return pl.pallas_call(
        project_back_kernel,
        grid=(rows // PROJ_BLOCK,),
        out_shape=(
            jax.ShapeDtypeStruct((slots, model), jnp.float32),
            jax.ShapeDtypeStruct((1, model), jnp.float32),
        ),
        in_specs=[
            pl.BlockSpec((slots, PROJ_BLOCK), lambda j: (0, j)),
            whole(tail_back.shape),
            *[pl.BlockSpec((1, PROJ_BLOCK, width), lambda j, i=i: (i, j, 0)) for i in range(parts)],
            whole(tail.shape),
            whole((slots, model)),
            whole((1, model)),
            whole((slots, model)),
        ],
        out_specs=(whole((slots, model)), whole((1, model))),
        scratch_shapes=[pltpu.VMEM((slots, model), jnp.float32)],
        compiler_params=pltpu.CompilerParams(vmem_limit_bytes=56 * 2**20),
        name="project_back",
    )(back, tail_back, *[main] * parts, tail, tokens, gain, middle_back)


def from_behind(block, axis, distance):
    devices = range(lax.axis_size(axis))
    route = [(i - distance, i) for i in devices if i - distance in devices]
    return lax.ppermute(block, axis, route)


def owner_rows(values, order, per_owner):
    depth, columns = values.shape
    grid = values.T.reshape(4, 4, 2, 4, per_owner, depth)
    place = {"x": 0, "y": 1, "c": 2, "z": 3}
    return jnp.transpose(grid, [place[a] for a in ("c", *order)] + [4, 5])


def plane_rows(values, order):
    depth, columns = values.shape
    grid = values.T.reshape(4, 4, 2, columns // 32, depth)
    place = {"x": 0, "y": 1, "c": 2}
    return jnp.transpose(grid, [place[a] for a in ("c", *order)] + [3, 4]).reshape(columns, depth)


def left_rows(values, order, per_owner=12):
    grid = owner_rows(values, order, per_owner)
    if per_owner == 24:
        return [grid[..., :12, :].reshape(1536, -1), grid[..., 12:, :].reshape(1536, -1)]
    grid = jnp.pad(grid, ((0, 0),) * 4 + ((0, 12 - per_owner), (0, 0)))
    return [grid.reshape(1536, -1)]


def local(
    tokens,
    cotangent,
    lengths,
    routes,
    norm_gain,
    w_in,
    conv_weight,
    conv_bias,
    a_log,
    dt_bias,
    skip_scale,
    gated_gain,
    w_out,
    post_gain,
    w_router,
    shared_in,
    shared_out,
    expert_in,
    expert_out,
):
    low = jnp.bfloat16
    tokens, cotangent, routes = tokens[0], cotangent[0], routes[0]
    slot_count, model_width = tokens.shape
    inner_width = gated_gain.shape[0]
    conv_width = conv_bias.shape[0]
    head_count = a_log.shape[0]
    tap_count = conv_weight.shape[0]
    expert_count = w_router.shape[1]
    residual = tokens.astype(jnp.float32)
    positions = lax.axis_index(SEQ) * slot_count + jnp.arange(slot_count)
    valid = positions < lengths[0]
    upstream_low = jnp.where(valid[:, None], cotangent, jnp.zeros_like(cotangent))
    upstream = upstream_low.astype(jnp.float32)
    main_rows = inner_width + conv_width
    turned = w_in.T
    tail_shard = jnp.concatenate(
        [
            turned[main_rows:],
            w_router.T,
            jnp.zeros((TILE - head_count - expert_count, turned.shape[1]), low),
        ],
        0,
    )
    full_in, full_out, full_shared_in, full_shared_out, tails = gather_weights(
        [turned, w_out, shared_in, shared_out], [tail_shard], main_rows
    )
    full_router = jnp.swapaxes(tails[:, head_count : head_count + expert_count], 0, 1)
    full_router = full_router.reshape(expert_count, model_width)

    first_norm, projected, tail_values = project(tokens, norm_gain[None], full_in, tails)
    halo = from_behind(projected[slot_count - 8 :, inner_width:], SEQ, 1)
    taps = jnp.concatenate([conv_weight, conv_bias[None], jnp.zeros((3, conv_width), jnp.float32)], 0)
    heads = jnp.pad(jnp.stack([a_log, dt_bias]), ((0, 6), (0, TILE - head_count)))
    wide = jnp.stack([jnp.repeat(skip_scale, inner_width // head_count), gated_gain])
    square, pairs = (TILE, TILE), (head_count // 2, TILE, TILE)
    mixed, leaving, totals, running, steps = tile_call(
        mixer_in_kernel,
        [((TILE, conv_width), jnp.float32), (pairs, low), ((8, TILE), jnp.float32), (square, jnp.float32), (square, jnp.float32)],
        [(TILE + 8, TILE)],
        "mixer_in",
        projected, tail_values, halo, taps, heads,
    )
    states = (head_count, inner_width // head_count, TILE)
    carried, decays, all_upstream = carried_states(leaving.reshape(states), totals, upstream_low)
    carried = carried.reshape(pairs)
    normed_low, scanned = tile_call(
        mixer_out_kernel,
        [((TILE, inner_width), low), ((TILE, inner_width), jnp.float32)],
        [(TILE, inner_width), (2, *square)],
        "mixer_out",
        projected, mixed, running, steps, carried, wide,
    )
    middle = residual + dot32(normed_low, full_out)
    second_norm = scaled_rows(middle, post_gain).astype(low)
    logits = dot_nt(second_norm, full_router)
    chosen = jnp.any(routes[:, :, None] == jnp.arange(expert_count)[None, None, :], 1)
    masked = jnp.where(chosen, logits, -jnp.inf)
    powers = jnp.exp(masked - jnp.max(masked, -1, keepdims=True))
    gate_dense = powers / jnp.sum(powers, -1, keepdims=True)

    all_rows, all_gates = z_gather((second_norm, gate_dense.T), 5, "gather_rows")
    rows = all_rows.reshape(-1, model_width)
    back_rows = all_upstream.reshape(-1, model_width)
    owned = expert_in.shape[0]
    first_owned = lax.axis_index("z") * owned
    gates = lax.dynamic_slice_in_dim(all_gates, first_owned, owned, 1)
    gates = jnp.swapaxes(gates, 0, 1).reshape(owned, -1)
    hidden_width = expert_out.shape[1]
    acts = jnp.einsum("td,edf->etf", rows, expert_in, preferred_element_type=jnp.float32)
    hidden = (jax.nn.silu(acts[..., :hidden_width]) * acts[..., hidden_width:]).astype(low)
    output = jnp.einsum("etf,efd->etd", hidden, expert_out, preferred_element_type=jnp.float32)
    output = output.astype(low).astype(jnp.float32)
    part = jnp.sum(gates[..., None] * output, 0).astype(low)
    back_wide = back_rows.astype(jnp.float32)
    picks = jnp.sum(output * back_wide[None], -1)
    out_grad = (gates[..., None] * back_wide[None]).astype(low)
    hidden_back = jnp.einsum("etd,efd->etf", out_grad, expert_out, preferred_element_type=jnp.float32)
    act_grad = glu_back(acts, hidden_back)
    back = jnp.einsum("etf,edf->td", act_grad, expert_in, preferred_element_type=jnp.float32).astype(low)
    picks = jnp.swapaxes(picks.reshape(owned, 4, slot_count), 0, 1)
    picks = jnp.pad(picks, ((0, 0), (0, 8 - owned), (0, 0)))
    expert_parts, back_sum, all_picks = expert_sum(
        jnp.stack([plane_rows(rows, order) for order in EXPERT_ORDERS]),
        act_grad,
        jnp.stack([plane_rows(hidden[e], EXPERT_ORDERS[e]) for e in range(owned)]),
        out_grad,
        back.reshape(4, slot_count, model_width),
        picks,
    )
    act_width = act_grad.shape[2]
    grad_expert_in = expert_parts[:, :, :act_width]
    grad_expert_out = expert_parts[:, :, act_width:].reshape(owned, 3, -1, model_width // 3)
    grad_expert_out = jnp.swapaxes(grad_expert_out, 1, 2).reshape(owned, -1, model_width)

    shared_width = full_shared_out.shape[0]
    shared_acts = dot32(second_norm, full_shared_in)
    shared_hidden = (
        jax.nn.silu(shared_acts[:, :shared_width]) * shared_acts[:, shared_width:]
    ).astype(low)
    shared_sum = dot32(shared_hidden, full_shared_out)
    shared_back = jnp.einsum("td,hd->th", upstream_low, full_shared_out, preferred_element_type=jnp.float32)
    shared_act_grad = glu_back(shared_acts, shared_back)
    second_back = jnp.einsum("tf,df->td", shared_act_grad, full_shared_in, preferred_element_type=jnp.float32)
    gate_grads = all_picks[:, :owned].reshape(expert_count, slot_count).T
    pick_grads = gate_dense * (gate_grads - jnp.sum(gate_dense * gate_grads, -1, keepdims=True))
    logit_grads = pick_grads.astype(low)
    second_back = second_back + back_sum + jnp.einsum(
        "te,ed->td", logit_grads, full_router, preferred_element_type=jnp.float32
    )
    unused_second, second_pull = jax.vjp(scaled_rows, middle, post_gain)
    middle_back, grad_post_gain = second_pull(second_back)
    middle_back = middle_back + upstream
    mix_low = middle_back.astype(low)
    normed_back = jnp.einsum("td,kd->tk", mix_low, full_out, preferred_element_type=jnp.float32)
    result_back, gate_back, gain_back, incoming_back = tile_call(
        gate_back_kernel,
        [((TILE, inner_width), jnp.float32), ((TILE, inner_width), low), ((8, inner_width), jnp.float32), (pairs, low)],
        [(TILE, inner_width)],
        "gate_back",
        projected, mixed, scanned, normed_back, running, wide,
    )
    leaving_back, expert_total = carried_states(
        incoming_back.reshape(states), decays, part.reshape(4, slot_count, model_width)
    )
    leaving_back = leaving_back.reshape(pairs)
    block_out = jnp.where(valid[:, None], middle + expert_total + shared_sum, 0.0).astype(low)
    conv_part, rim_part, taps_back, steps_back, heads_back = tile_call(
        mixer_back_kernel,
        [
            ((TILE, conv_width), jnp.float32), ((8, conv_width), jnp.float32), ((8, conv_width), jnp.float32),
            (square, jnp.float32), ((8, TILE), jnp.float32),
        ],
        [
            (2, *square), (2, *square), (4, *square), square, (2, *square),
            (TILE, conv_width), (TILE + 8, TILE), (TILE + 16, TILE),
        ],
        "mixer_back",
        projected, tail_values, halo, taps, heads, mixed, running, steps, wide, carried, result_back, leaving_back,
    )
    rim_back = from_behind(rim_part.astype(low), SEQ, -1).astype(jnp.float32)
    conv_back = conv_part + jnp.pad(rim_back, ((slot_count - 8, 0), (0, 0)))
    proj_back = jnp.concatenate([gate_back, conv_back.astype(low)], 1)
    tail_back = steps_back.astype(low)
    grad_tokens, grad_norm_gain = project_back(
        proj_back, tail_back, full_in, tails, tokens, norm_gain[None], middle_back
    )

    first, second, third = RS_ORDERS
    lefts = jnp.stack(
        left_rows(first_norm, first)
        + left_rows(first_norm, second)
        + left_rows(second_norm, second) * 2
        + left_rows(normed_low, third, 24)
        + left_rows(shared_hidden, third, 8)
    )
    zeros = lambda columns: jnp.zeros((slot_count, columns), low)
    rights = jnp.concatenate(
        [
            proj_back,
            tail_back,
            zeros(13 * RS_COLS - main_rows - TILE),
            shared_act_grad,
            zeros(RS_COLS),
            mix_low,
            mix_low,
            upstream_low,
        ],
        1,
    )
    router_back = jnp.einsum("te,td->ed", logit_grads, second_norm, preferred_element_type=jnp.float32)
    summed, small = grad_sum(
        lefts, rights, taps_back, gain_back, grad_norm_gain, grad_post_gain[None], heads_back, router_back
    )
    at = 13 * RS_COLS
    w_in_part = summed[:12, : w_in.shape[1]]
    shared_in_part = summed[:12, at : at + 2 * shared_width]
    at = at + 5 * RS_COLS
    w_out_part = jnp.concatenate(
        [summed[:12, at : at + model_width], summed[:12, at + model_width : at + 2 * model_width]], 0
    )
    at = at + 2 * model_width
    shared_out_part = summed[:8, at : at + model_width]
    owner = lax.axis_index(ALL)

    def owned_part(values):
        size = values.shape[-1] // 128
        return lax.dynamic_slice_in_dim(values, owner * size, size, values.ndim - 1)

    return (
        block_out[None],
        grad_tokens[None],
        owned_part(small[6, :model_width]),
        w_in_part,
        owned_part(small[:4, :conv_width]),
        owned_part(small[4, :conv_width]),
        small[7, :head_count],
        small[7, TILE : TILE + head_count],
        small[7, 2 * TILE : 2 * TILE + head_count],
        owned_part(small[5, :inner_width]),
        w_out_part,
        owned_part(small[6, model_width : 2 * model_width]),
        owned_part(small[:, conv_width:]).T,
        shared_in_part,
        shared_out_part,
        grad_expert_in,
        grad_expert_out,
    )


def solution(mesh):
    split = Mesh(mesh.devices.reshape(4, 4, 2, 4), ALL)
    placed = (
        P("z", SEQ, None),
        P("z", SEQ, None),
        P("z"),
        P("z", SEQ, None),
        P(),
        P("z", None),
        P(),
        P(),
        P(),
        P(),
        P(),
        P(),
        P("z", None),
        P(),
        P("z", None),
        P("z", None),
        P("z", None),
        P("z", None, None),
        P("z", None, None),
    )
    return jax.shard_map(
        local,
        mesh=split,
        in_specs=placed,
        out_specs=(
            P("z", SEQ, None),
            P("z", SEQ, None),
            P(ALL),
            P(ALL, None),
            P(None, ALL),
            P(ALL),
            P(),
            P(),
            P(),
            P(ALL),
            P(ALL, None),
            P(ALL),
            P(ALL, None),
            P(ALL, None),
            P(ALL, None),
            P("z", SEQ, None),
            P("z", SEQ, None),
        ),
        check_vma=False,
    )
```

```python
import functools

import jax
import jax.numpy as jnp
from jax import lax
from jax.experimental import pallas as pl
from jax.experimental.pallas import tpu as pltpu
from jax.sharding import Mesh
from jax.sharding import PartitionSpec as P

SEQ = ("x", "y", "c")
ALL = ("x", "y", "c", "z")
NORM_EPS = 1e-05
HEADS = 48
INNER = 3072
CONV = 3328


def scaled_rows(values, gain_vector):
    return values * lax.rsqrt(jnp.mean(values * values, -1, keepdims=True) + NORM_EPS) * gain_vector


def glu_back(acts_pair, hidden_back):
    half_width = acts_pair.shape[-1] // 2
    gate_part = acts_pair[..., :half_width]
    up_part = acts_pair[..., half_width:]
    sigmoid_gate = jax.nn.sigmoid(gate_part)
    gate_grad = hidden_back * up_part * sigmoid_gate * (1.0 + gate_part * (1.0 - sigmoid_gate))
    up_grad = hidden_back * gate_part * sigmoid_gate
    return jnp.concatenate([gate_grad, up_grad], -1).astype(jnp.bfloat16)


MESH_ID = pl.DeviceIdType.MESH
RS_ORDERS = (("x", "y", "z"), ("y", "z", "x"), ("z", "x", "y"))
RS_COUNTS = (5, 4, 4)
RS_FIRST = (0, 5, 9)
RS_SLOTS = 13
RS_COLS = 512
RS_LAGS = 6
RS_TIMES = max(RS_COUNTS) + RS_LAGS - 1
NEIGHBOURS = [("c", 1)] + [(axis, o) for axis in ("x", "y", "z") for o in (1, 2, 3)]


def ring(axis, offset):
    size = lax.axis_size(axis)
    return lax.rem(lax.axis_index(axis) + offset + size, size)


def greet(targets):
    barrier = pltpu.get_barrier_semaphore()
    for target in targets:
        pl.semaphore_signal(barrier, inc=1, device_id=target, device_id_type=MESH_ID)
    pl.semaphore_wait(barrier, len(targets))


def greet_neighbours():
    greet([{axis: ring(axis, o)} for axis, o in NEIGHBOURS])


def remote(src, dst, send_sem, recv_sem, target):
    return pltpu.make_async_remote_copy(
        src_ref=src,
        dst_ref=dst,
        send_sem=send_sem,
        recv_sem=recv_sem,
        device_id=target,
        device_id_type=MESH_ID,
    )


def dot32(left, right):
    return jnp.dot(left, right, preferred_element_type=jnp.float32)


def grad_sum_scratch(rows):
    half, block, low = rows // 2, rows // 8, jnp.bfloat16
    sems = lambda *shape: [pltpu.SemaphoreType.DMA(shape)] * 2
    return [
        pltpu.VMEM((2, 3, half, RS_COLS), low),
        pltpu.VMEM((RS_SLOTS, half, RS_COLS), low),
        pltpu.VMEM((RS_SLOTS, 4, block // 2, RS_COLS), low),
        pltpu.VMEM((RS_SLOTS, 2, block // 2, RS_COLS), low),
        pltpu.VMEM((RS_SLOTS, 3, block // 4, RS_COLS), low),
        pltpu.VMEM((RS_SLOTS, 4, 16, RS_COLS), low),
        pltpu.VMEM((RS_SLOTS, 3, 16, RS_COLS), low),
        pltpu.VMEM((3, block // 4 + 8, RS_COLS), jnp.float32),
        *sems(RS_SLOTS), *sems(RS_SLOTS, 4), *sems(RS_SLOTS, 2), *sems(RS_SLOTS, 3), *sems(RS_SLOTS, 3),
    ]


def grad_sum_steps(scratch, left_of, right_of, store):
    core_out, core_in, near, far, second_in, third_out, third_in, lines = scratch[:8]
    core_ss, core_rs, near_ss, near_rs, far_ss, far_rs, second_ss, second_rs, third_ss, third_rs = scratch[8:]
    me_core = lax.axis_index("c")
    other = 1 - me_core
    half = core_out.shape[2]
    block = half // 4
    edge = block // 2
    small = block // 4
    unit = third_out.shape[2]
    kept = small // 4
    lines[...] = jnp.zeros_like(lines)

    def core_copy(part, k):
        slot = RS_FIRST[part] + k
        return remote(
            core_out.at[lax.rem(k, 2), part], core_in.at[slot],
            core_ss.at[slot], core_rs.at[slot], {"c": other},
        )

    def near_copies(part, k):
        slot = RS_FIRST[part] + k
        axis = RS_ORDERS[part][0]
        after, before, across = ring(axis, 1), ring(axis, -1), ring(axis, 2)
        plan = ((before, 0, before), (after, edge, after), (across, 0, after), (across, edge, before))
        return [
            remote(
                core_in.at[slot, pl.ds(which * block + offset, edge)], near.at[slot, n],
                near_ss.at[slot, n], near_rs.at[slot, n], {axis: target},
            )
            for n, (which, offset, target) in enumerate(plan)
        ]

    def far_copies(part, k):
        slot = RS_FIRST[part] + k
        axis = RS_ORDERS[part][0]
        return [
            remote(
                near.at[slot, 2 + n], far.at[slot, n],
                far_ss.at[slot, n], far_rs.at[slot, n], {axis: ring(axis, o)},
            )
            for n, o in enumerate((1, -1))
        ]

    def second_copies(part, k):
        slot = RS_FIRST[part] + k
        axis = RS_ORDERS[part][1]
        copies = []
        for o in (1, 2, 3):
            target = ring(axis, o)
            copies.append(
                remote(
                    near.at[slot, target // 2, pl.ds(lax.rem(target, 2) * small, small)],
                    second_in.at[slot, o - 1],
                    second_ss.at[slot, o - 1], second_rs.at[slot, o - 1], {axis: target},
                )
            )
        return copies

    def third_copies(part, k):
        slot = RS_FIRST[part] + k
        axis = RS_ORDERS[part][2]
        return [
            remote(
                third_out.at[slot, ring(axis, o)], third_in.at[slot, o - 1],
                third_ss.at[slot, o - 1], third_rs.at[slot, o - 1], {axis: ring(axis, o)},
            )
            for o in (1, 2, 3)
        ]

    def stage_product(part, k):
        @pl.when(k >= 2)
        def _():
            core_copy(part, k - 2).wait_send()

        left = left_of(part, k, other)
        for col in range(0, RS_COLS, 256):
            core_out[lax.rem(k, 2), part, :, col : col + 256] = dot32(left, right_of(part, k, col)).astype(jnp.bfloat16)
        core_copy(part, k).start()

    def stage_near(part, k):
        slot = RS_FIRST[part] + k
        core_copy(part, k).wait_recv()
        left = left_of(part, k, me_core)
        for col in range(0, RS_COLS, 256):
            mine = dot32(left, right_of(part, k, col))
            theirs = core_in[slot, :, col : col + 256].astype(jnp.float32)
            core_in[slot, :, col : col + 256] = (mine + theirs).astype(jnp.bfloat16)
        for copy in near_copies(part, k):
            copy.start()

    def load(ref, *where):
        return ref[where].astype(jnp.float32)

    def stage_far(part, k):
        slot = RS_FIRST[part] + k
        axis = RS_ORDERS[part][0]
        copies = near_copies(part, k)
        for n, (which, offset) in enumerate(((ring(axis, 1), 0), (ring(axis, -1), edge))):
            copies[2 + n].wait_recv()
            rows = pl.ds(pl.multiple_of(which * block + offset, edge), edge)
            near[slot, 2 + n] = (load(near, slot, 2 + n) + load(core_in, slot, rows)).astype(jnp.bfloat16)
        for copy in far_copies(part, k):
            copy.start()

    def stage_second(part, k):
        slot = RS_FIRST[part] + k
        me = lax.axis_index(RS_ORDERS[part][0])
        copies, far_in = near_copies(part, k), far_copies(part, k)
        for n in range(2):
            copies[n].wait_recv()
            far_in[n].wait_recv()
            rows = pl.ds(pl.multiple_of(me * block + n * edge, edge), edge)
            near[slot, n] = (
                load(near, slot, n) + load(far, slot, n) + load(core_in, slot, rows)
            ).astype(jnp.bfloat16)
        for copy in second_copies(part, k):
            copy.start()

    def stage_third(part, k):
        slot = RS_FIRST[part] + k
        me = lax.axis_index(RS_ORDERS[part][1])
        for copy in second_copies(part, k):
            copy.wait_recv()
        rows = pl.ds(pl.multiple_of(lax.rem(me, 2) * small, small), small)
        lines[part, :small] = load(near, slot, me // 2, rows) + (
            load(second_in, slot, 0) + load(second_in, slot, 1) + load(second_in, slot, 2)
        )
        for j in range(4):
            third_out[slot, j] = lines[part, kept * j : kept * j + unit].astype(jnp.bfloat16)
        for copy in third_copies(part, k):
            copy.start()

    def stage_last(part, k):
        slot = RS_FIRST[part] + k
        for copy in third_copies(part, k):
            copy.wait_recv()
        me = lax.axis_index(RS_ORDERS[part][2])
        total = load(third_out, slot, me) + (
            load(third_in, slot, 0) + load(third_in, slot, 1) + load(third_in, slot, 2)
        )
        store(part, k, total)

    stages = (stage_product, stage_near, stage_far, stage_second, stage_third, stage_last)

    def step(t):
        for lag, stage in enumerate(stages):
            k = t - lag
            for count in sorted(set(RS_COUNTS)):
                @pl.when((k >= 0) & (k < count))
                def _():
                    for part in range(3):
                        if RS_COUNTS[part] == count:
                            stage(part, k)

    def finish():
        for part in range(3):
            def wait_sent(k, carry, part=part):
                @pl.when(k >= RS_COUNTS[part] - 2)
                def _():
                    core_copy(part, k).wait_send()

                for copies in (near_copies, far_copies, second_copies, third_copies):
                    for copy in copies(part, k):
                        copy.wait_send()
                return carry

            lax.fori_loop(0, RS_COUNTS[part], wait_sent, 0)

    return step, finish


def grad_sum_kernel(
    lefts_ref, rights_ref, taps_ref, gain_ref, norm_ref, post_ref, heads_ref, router_ref, out_ref, small_ref, *scratch
):
    *sum_scratch, pack, pack_in, pack_work, pack_others, pack_ss, pack_rs = scratch
    me_core = lax.axis_index("c")
    other = 1 - me_core
    half = lefts_ref.shape[1] // 2
    greet_neighbours()

    taps_width, wide = taps_ref.shape[1], pack.shape[1] // 2
    pack[:, :taps_width] = taps_ref[...]
    pack[5:6, : gain_ref.shape[1]] = gain_ref[0:1]
    pack[6:7, : norm_ref.shape[1]] = norm_ref[...]
    pack[6:7, norm_ref.shape[1] : 2 * norm_ref.shape[1]] = post_ref[...]
    for i in range(3):
        pack[7:8, TILE * i : TILE * (i + 1)] = heads_ref[i : i + 1]
    pack[:, taps_width:] = router_ref[...]

    def pack_half(ref, which):
        return ref.at[:, pl.ds(pl.multiple_of(which * wide, 128), wide)]

    def pack_core(last):
        if last:
            return remote(pack_work.at[3], pack_half(small_ref, me_core), pack_ss.at[4, 0], pack_rs.at[4, 0], {"c": other})
        return remote(pack_half(pack, other), pack_in, pack_ss.at[0, 0], pack_rs.at[0, 0], {"c": other})

    def pack_copies(s):
        axis = ("x", "y", "z")[s - 1]
        return [
            remote(pack_work.at[s - 1], pack_others.at[s - 1, o - 1], pack_ss.at[s, o], pack_rs.at[s, o], {axis: ring(axis, o)})
            for o in (1, 2, 3)
        ]

    def pack_step(s):
        if s == 0:
            pack_core(False).start()
        if s == 1:
            pack_core(False).wait_recv()
            pack_work[0] = pack[:, pl.ds(pl.multiple_of(me_core * wide, 128), wide)] + pack_in[...]
        if s in (2, 3, 4):
            for copy in pack_copies(s - 1):
                copy.wait_recv()
            pack_work[s - 1] = pack_work[s - 2] + (
                pack_others[s - 2, 0] + pack_others[s - 2, 1] + pack_others[s - 2, 2]
            )
        if s in (1, 2, 3):
            for copy in pack_copies(s):
                copy.start()
        if s == 4:
            pack_core(True).start()
            small_ref[:, pl.ds(pl.multiple_of(me_core * wide, 128), wide)] = pack_work[3]
        if s == 5:
            pack_core(True).wait_recv()
            pack_core(True).wait_send()
            pack_core(False).wait_send()
            for n in (1, 2, 3):
                for copy in pack_copies(n):
                    copy.wait_send()

    def left_of(part, k, which):
        return lefts_ref[part, pl.ds(pl.multiple_of(which * half, half), half), :]

    def right_of(part, k, col):
        return rights_ref[:, pl.ds(pl.multiple_of((RS_FIRST[part] + k) * RS_COLS + col, 256), 256)]

    whole = out_ref.shape[1] // RS_COLS
    rows = out_ref.shape[0]

    def store(part, k, total):
        chunk = RS_FIRST[part] + k

        @pl.when(chunk < whole)
        def _():
            out_ref[:, pl.ds(pl.multiple_of(chunk * RS_COLS, RS_COLS), RS_COLS)] = total[:rows]

        if part == 2:
            @pl.when(chunk == whole)
            def _():
                out_ref[:, whole * RS_COLS :] = total[:rows, : out_ref.shape[1] - whole * RS_COLS]

    step, finish = grad_sum_steps(sum_scratch, left_of, right_of, store)

    def run(t, carry):
        for s in range(6):
            @pl.when(t == s)
            def _():
                pack_step(s)

        step(t)
        return carry

    lax.fori_loop(0, RS_TIMES, run, 0)
    finish()


def grad_sum(lefts, rights, columns, taps, gain, norm, post, heads, router):
    rows = lefts.shape[1]
    wide = taps.shape[1] + router.shape[1]
    space = pl.BlockSpec(memory_space=pltpu.VMEM)
    return pl.pallas_call(
        grad_sum_kernel,
        out_shape=(
            jax.ShapeDtypeStruct((rows // 128, columns), jnp.float32),
            jax.ShapeDtypeStruct((8, wide), jnp.float32),
        ),
        in_specs=[space] * 8,
        out_specs=(space, space),
        scratch_shapes=grad_sum_scratch(rows)
        + [
            pltpu.VMEM((8, wide), jnp.float32),
            pltpu.VMEM((8, wide // 2), jnp.float32),
            pltpu.VMEM((4, 8, wide // 2), jnp.float32),
            pltpu.VMEM((3, 3, 8, wide // 2), jnp.float32),
            pltpu.SemaphoreType.DMA((5, 4)),
            pltpu.SemaphoreType.DMA((5, 4)),
        ],
        compiler_params=pltpu.CompilerParams(
            collective_id=0, has_side_effects=True, vmem_limit_bytes=58 * 2**20
        ),
        name="grad_sum",
    )(lefts, rights, taps, gain, norm, post, heads, router)


LEFT_SOURCES = (("shared", 0), ("hidden", 0), ("gated_0", 1), ("hidden", 1), ("gated_1", 2), ("hidden", 2))


def owner_moves(order, stride, offset, rows):
    moves = []
    for to in range(128):
        digits = {"c": to // 64}
        for axis, at in zip(order, (to // 16 % 4, to // 4 % 4, to % 4)):
            digits[axis] = at
        owner = ((digits["x"] * 4 + digits["y"]) * 2 + digits["c"]) * 4 + digits["z"]
        source, target = owner * stride + offset, to * 12
        if moves and moves[-1][0] + moves[-1][2] == source and moves[-1][1] + moves[-1][2] == target:
            moves[-1][2] += rows
        else:
            moves.append([source, target, rows])
    return moves


def lefts_kernel(first_ref, second_ref, gated_ref, hidden_ref, early_ref, late_ref, turned, sorted_rows):
    def turn(ref):
        for j in range(ref.shape[1] // TILE):
            turned[j * TILE : (j + 1) * TILE] = ref[:, j * TILE : (j + 1) * TILE].astype(jnp.float32).T

    def place(out_ref, at, order, stride, offset, rows):
        if rows < 12:
            sorted_rows[...] = jnp.zeros_like(sorted_rows)
        for source, target, size in owner_moves(order, stride, offset, rows):
            sorted_rows[target : target + size] = turned[source : source + size]
        out_ref[at] = sorted_rows[...].astype(jnp.bfloat16)

    turn(first_ref)
    for part in range(3):
        place(late_ref, part, RS_ORDERS[part], 12, 0, 12)
    turn(second_ref)
    place(early_ref, 0, RS_ORDERS[0], 12, 0, 12)
    turn(hidden_ref)
    for at, part in ((1, 0), (3, 1), (5, 2)):
        place(early_ref, at, RS_ORDERS[part], 8, 0, 8)
    turn(gated_ref)
    place(early_ref, 2, RS_ORDERS[1], 24, 0, 12)
    place(early_ref, 4, RS_ORDERS[2], 24, 12, 12)


def state_exchange(reverse, state_ref, totals_ref, rows_ref, out_ref, *refs):
    if reverse:
        rows_sum, all_rows, *refs = refs
    else:
        all_rows, *refs = refs
    pair_in, pair_totals, outgoing, got, back, mine, hand, ps, pr, ss, rs, bs, br, zs, zr = refs
    x, y, c, z = (lax.axis_index(a) for a in ALL)
    chip = x * 4 + y
    half = pair_in.shape[0]
    groups, size = back.shape[1:3]
    others = [(dx, dy) for dx in range(4) for dy in range(4) if dx + dy]

    def far(dx, dy):
        tx, ty = lax.rem(x + dx, 4), lax.rem(y + dy, 4)
        return tx * 4 + ty, {"x": tx, "y": ty}

    greet([{"c": 1 - c}] + [{"z": ring("z", o)} for o in (1, 2, 3)] + [far(*d)[1] for d in others])
    mine_at, theirs_at = c * half, (1 - c) * half

    def pair_copies():
        return [
            remote(state_ref.at[pl.ds(theirs_at, half)], pair_in, ps.at[0], pr.at[0], {"c": 1 - c}),
            remote(totals_ref, pair_totals, ps.at[1], pr.at[1], {"c": 1 - c}),
        ]

    def out_copy(dx, dy):
        target, where = far(dx, dy)
        at = dx * 4 + dy
        return remote(outgoing.at[target], got.at[chip], ss.at[at], rs.at[at], where)

    def back_copy(dx, dy):
        target, where = far(dx, dy)
        at = dx * 4 + dy
        return remote(back.at[target], mine.at[pl.ds(groups * chip, groups)], bs.at[at], br.at[at], where)

    def hand_copy():
        return remote(hand, out_ref.at[pl.ds(mine_at, half)], ps.at[2], pr.at[2], {"c": 1 - c})

    row_copies = []
    for o in (1, 3, 2):
        source = rows_ref.at[ring("z", o)] if reverse else rows_ref
        target = all_rows.at[o - 1] if reverse else all_rows.at[z]
        row_copies.append(remote(source, target, zs.at[o], zr.at[o], {"z": ring("z", o)}))
    for copy in pair_copies():
        copy.start()
    for copy in row_copies:
        copy.start()
    if not reverse:
        all_rows[z] = rows_ref[...]
    for copy in pair_copies():
        copy.wait_recv()
    first = jnp.where(c == 0, totals_ref[...], pair_totals[...])
    second = jnp.where(c == 0, pair_totals[...], totals_ref[...])
    inner, outer = (first, second) if reverse else (second, first)
    lanes = lax.broadcasted_iota(jnp.int32, (8, TILE), 1) - c * (half // 2)

    def decay(logs, head):
        return jnp.exp(jnp.sum(jnp.where(lanes[: logs.shape[0]] == head, logs, 0.0), 1, keepdims=True))[:1]

    def states(g):
        own, other = state_ref[mine_at + g].astype(jnp.float32), pair_in[g].astype(jnp.float32)
        return jnp.where(c == 0, own, other), jnp.where(c == 0, other, own)

    total = (first + second)[:1]
    high = total.astype(jnp.bfloat16).astype(jnp.float32)
    middle = (total - high).astype(jnp.bfloat16).astype(jnp.float32)
    row = lax.broadcasted_iota(jnp.int32, (16, TILE), 0)
    split = jnp.where(row == 0, high, jnp.where(row == 1, middle, jnp.where(row == 2, total - high - middle, 0.0)))
    split = split.astype(jnp.bfloat16)

    def combine(m, carry):
        for i in range(groups):
            g = groups * m + i
            early, late = states(g)
            rate = decay(inner, g // 2)
            pair = early + rate * late if reverse else rate * early + late
            outgoing[m, i * size : (i + 1) * size] = pair.astype(jnp.bfloat16)
        outgoing[m, groups * size :] = split
        return carry

    lax.fori_loop(0, 16, combine, 0)
    for d in others:
        out_copy(*d).start()
    got[chip] = outgoing[chip]
    for d in others:
        out_copy(*d).wait_recv()

    def advance(step, carried):
        p = 15 - step if reverse else step
        logs = jnp.sum(got[p, groups * size :].astype(jnp.float32), 0, keepdims=True)
        new = []
        for i in range(groups):
            back[p, i] = carried[i].astype(back.dtype)
            here = got[p, i * size : (i + 1) * size].astype(jnp.float32)
            new.append(carried[i] * decay(logs, (groups * chip + i) // 2) + here)
        return tuple(new)

    lax.fori_loop(0, 16, advance, (jnp.zeros((size, TILE), jnp.float32),) * groups)
    for d in others:
        back_copy(*d).start()
    mine[pl.ds(groups * chip, groups)] = back[chip]
    for d in others:
        back_copy(*d).wait_recv()

    def spread(h, carry):
        rate = decay(outer, h)
        for i in range(2):
            g = 2 * h + i
            early, late = states(g)
            near = mine[g].astype(jnp.float32)
            beyond = rate * near + (late if reverse else early)
            swap = (c == 1) if reverse else (c == 0)
            out_ref[mine_at + g] = jnp.where(swap, near, beyond).astype(out_ref.dtype)
            hand[g] = jnp.where(swap, beyond, near).astype(hand.dtype)
        return carry

    lax.fori_loop(0, half // 2, spread, 0)
    hand_copy().start()
    for copy in row_copies:
        copy.wait()
    if reverse:
        add_parts(rows_ref, z, all_rows, rows_sum)
    hand_copy().wait()
    for copy in pair_copies():
        copy.wait_send()
    for d in others:
        out_copy(*d).wait_send()
        back_copy(*d).wait_send()


def add_parts(ref, me, got, out):
    def rows_at(j, carry):
        rows = pl.ds(pl.multiple_of(j * 32, 32), 32)
        total = ref[me, rows].astype(jnp.float32)
        for o in range(3):
            total = total + got[o, rows].astype(jnp.float32)
        out[rows] = total
        return carry

    lax.fori_loop(0, out.shape[0] // 32, rows_at, 0)


def scan_forward_kernel(*refs):
    state_exchange(False, *refs)


def scan_backward_kernel(*refs):
    state_exchange(True, *refs)


def carried_states(state, totals, rows):
    reverse = rows.ndim == 3
    low = jnp.bfloat16
    pairs = state.shape
    state = state.reshape(96, 32, TILE)
    space = pl.BlockSpec(memory_space=pltpu.VMEM)
    outs = [jax.ShapeDtypeStruct(state.shape, low)]
    extra = []
    if reverse:
        outs.append(jax.ShapeDtypeStruct(rows.shape[1:], jnp.float32))
        extra.append(pltpu.VMEM((3, *rows.shape[1:]), rows.dtype))
    else:
        outs.append(jax.ShapeDtypeStruct((4, *rows.shape), rows.dtype))
    sem = pltpu.SemaphoreType.DMA
    result = pl.pallas_call(
        scan_backward_kernel if reverse else scan_forward_kernel,
        out_shape=tuple(outs),
        in_specs=[space] * 3,
        out_specs=(space,) * 2,
        scratch_shapes=extra
        + [
            pltpu.VMEM((48, 32, TILE), low),
            pltpu.VMEM((8, TILE), jnp.float32),
            pltpu.VMEM((16, 112, TILE), low),
            pltpu.VMEM((16, 112, TILE), low),
            pltpu.VMEM((16, 3, 32, TILE), low),
            pltpu.VMEM((48, 32, TILE), low),
            pltpu.VMEM((48, 32, TILE), low),
            sem((3,)), sem((3,)), sem((16,)), sem((16,)), sem((16,)), sem((16,)), sem((4,)), sem((4,)),
        ],
        compiler_params=pltpu.CompilerParams(
            collective_id=2 if reverse else 1, has_side_effects=True, vmem_limit_bytes=32 * 2**20
        ),
        name="scan_backward" if reverse else "scan_forward",
    )(state, totals, rows)
    return result[0].reshape(pairs), result[1]


def z_gather_kernel(count, *refs):
    ins, outs, (ss, rs) = refs[:count], refs[count : 2 * count], refs[2 * count :]
    me = lax.axis_index("z")
    greet([{"z": ring("z", o)} for o in (1, 2, 3)])
    copies = []
    for n in range(count):
        for o in (1, 3, 2):
            copies.append(
                remote(ins[n], outs[n].at[me], ss.at[n, o], rs.at[n, o], {"z": ring("z", o)})
            )
            copies[-1].start()
    for n in range(count):
        outs[n][me] = ins[n][...]
    for copy in copies:
        copy.wait()


def z_gather(arrays, cid, name):
    count = len(arrays)
    space = pl.BlockSpec(memory_space=pltpu.VMEM)
    sem = pltpu.SemaphoreType.DMA((count, 4))
    return pl.pallas_call(
        functools.partial(z_gather_kernel, count),
        out_shape=tuple(jax.ShapeDtypeStruct((4, *a.shape), a.dtype) for a in arrays),
        in_specs=[space] * count,
        out_specs=(space,) * count,
        scratch_shapes=[sem, sem],
        compiler_params=pltpu.CompilerParams(
            collective_id=cid, has_side_effects=True, vmem_limit_bytes=32 * 2**20
        ),
        name=name,
    )(*arrays)


EXPERT_ORDERS = (("x", "y"), ("y", "x"))
EXPERT_STEPS = 6
EXPERT_COLS = 256


def expert_sum_kernel(
    rows_ref, acts_ref, hidden_ref, grads_ref, back_ref, picks_ref,
    out_ref, back_sum, picks_all,
    core_out, core_in, near, far, second_in, got, turned_rows, turned_hidden,
    core_ss, core_rs, near_ss, near_rs, far_ss, far_rs, second_ss, second_rs, zs, zr,
):
    me_core = lax.axis_index("c")
    me_z = lax.axis_index("z")
    other = 1 - me_core
    half = core_out.shape[2]
    block = half // 4
    edge = block // 2
    small = block // 4
    third = small // 3
    cols = EXPERT_COLS
    greet(
        [{"c": other}]
        + [{axis: ring(axis, o)} for axis in ("x", "y", "z") for o in (1, 2, 3)]
    )

    sums = []
    for n, ref in enumerate((back_ref,)):
        for o in (1, 3, 2):
            sums.append(
                remote(ref.at[ring("z", o)], got.at[n, o - 1], zs.at[n, o], zr.at[n, o], {"z": ring("z", o)})
            )
    for o in (1, 3, 2):
        sums.append(
            remote(picks_ref.at[ring("z", o)], picks_all.at[me_z], zs.at[2, o], zr.at[2, o], {"z": ring("z", o)})
        )
    for copy in sums:
        copy.start()
    picks_all[me_z] = picks_ref[me_z]
    for j in range(rows_ref.shape[1] // TILE):
        turned_rows[j * TILE : (j + 1) * TILE] = rows_ref[:, j * TILE : (j + 1) * TILE].T
    for part in range(2):
        for j in range(hidden_ref.shape[2] // TILE):
            turned_hidden[part, j * TILE : (j + 1) * TILE] = hidden_ref[part, :, j * TILE : (j + 1) * TILE].T

    def plane_rows(part, which, load, size):
        blocks = []
        for j in range(4):
            for i in range(4):
                spot = (j * 4 + i if part == 0 else i * 4 + j) * 2 + which
                blocks.append(load(pl.ds(pl.multiple_of(spot * size, 16), size)))
        return jnp.concatenate(blocks, 0)

    def core_copy(part, k):
        slot = part * EXPERT_STEPS + k
        return remote(
            core_out.at[lax.rem(k, 2), part], core_in.at[slot],
            core_ss.at[slot], core_rs.at[slot], {"c": other},
        )

    def near_copies(part, k):
        slot = part * EXPERT_STEPS + k
        axis = EXPERT_ORDERS[part][0]
        after, before, across = ring(axis, 1), ring(axis, -1), ring(axis, 2)
        plan = ((before, 0, before), (after, edge, after), (across, 0, after), (across, edge, before))
        return [
            remote(
                core_in.at[slot, pl.ds(which * block + offset, edge)], near.at[slot, n],
                near_ss.at[slot, n], near_rs.at[slot, n], {axis: target},
            )
            for n, (which, offset, target) in enumerate(plan)
        ]

    def far_copies(part, k):
        slot = part * EXPERT_STEPS + k
        axis = EXPERT_ORDERS[part][0]
        return [
            remote(
                near.at[slot, 2 + n], far.at[slot, n],
                far_ss.at[slot, n], far_rs.at[slot, n], {axis: ring(axis, o)},
            )
            for n, o in enumerate((1, -1))
        ]

    def second_copies(part, k):
        slot = part * EXPERT_STEPS + k
        axis = EXPERT_ORDERS[part][1]
        copies = []
        for o in (1, 2, 3):
            target = ring(axis, o)
            copies.append(
                remote(
                    near.at[slot, target // 2, pl.ds(lax.rem(target, 2) * small, small)],
                    second_in.at[slot, o - 1],
                    second_ss.at[slot, o - 1], second_rs.at[slot, o - 1], {axis: target},
                )
            )
        return copies

    def load(ref, *where):
        return ref[where].astype(jnp.float32)

    def products(part, k, which_half, store):
        @pl.when(k < 4)
        def _():
            right = acts_ref[part, :, pl.ds(pl.multiple_of(k * cols, cols), cols)]

            left = plane_rows(part, which_half, lambda rows: turned_rows[rows], small)
            store(0, half, dot32(left, right))

        @pl.when(k >= 4)
        def _():
            left = plane_rows(part, which_half, lambda rows: turned_hidden[part, rows], third)
            for t in range(3):
                right = grads_ref[part, :, pl.ds(pl.multiple_of(t * 2 * cols + (k - 4) * cols, cols), cols)]
                product = dot32(left, right)
                for i in range(16):
                    store(i * small + t * third, third, product[i * third : (i + 1) * third])

    def stage_product(part, k):
        @pl.when(k >= 2)
        def _():
            core_copy(part, k - 2).wait_send()

        def store(at, size, value):
            core_out[lax.rem(k, 2), part, pl.ds(at, size), :] = value.astype(jnp.bfloat16)

        products(part, k, other, store)
        core_copy(part, k).start()

    def stage_near(part, k):
        slot = part * EXPERT_STEPS + k
        core_copy(part, k).wait_recv()

        def store(at, size, value):
            rows = pl.ds(at, size)
            core_in[slot, rows, :] = (value + load(core_in, slot, rows)).astype(jnp.bfloat16)

        products(part, k, me_core, store)
        for copy in near_copies(part, k):
            copy.start()

    def stage_far(part, k):
        slot = part * EXPERT_STEPS + k
        axis = EXPERT_ORDERS[part][0]
        copies = near_copies(part, k)
        for n, (which, offset) in enumerate(((ring(axis, 1), 0), (ring(axis, -1), edge))):
            copies[2 + n].wait_recv()
            rows = pl.ds(pl.multiple_of(which * block + offset, edge), edge)
            near[slot, 2 + n] = (load(near, slot, 2 + n) + load(core_in, slot, rows)).astype(jnp.bfloat16)
        for copy in far_copies(part, k):
            copy.start()

    def stage_second(part, k):
        slot = part * EXPERT_STEPS + k
        me = lax.axis_index(EXPERT_ORDERS[part][0])
        copies, far_in = near_copies(part, k), far_copies(part, k)
        for n in range(2):
            copies[n].wait_recv()
            far_in[n].wait_recv()
            rows = pl.ds(pl.multiple_of(me * block + n * edge, edge), edge)
            near[slot, n] = (
                load(near, slot, n) + load(far, slot, n) + load(core_in, slot, rows)
            ).astype(jnp.bfloat16)
        for copy in second_copies(part, k):
            copy.start()

    def stage_last(part, k):
        slot = part * EXPERT_STEPS + k
        me = lax.axis_index(EXPERT_ORDERS[part][1])
        for copy in second_copies(part, k):
            copy.wait_recv()
        rows = pl.ds(pl.multiple_of(lax.rem(me, 2) * small, small), small)
        out_ref[part, :, pl.ds(pl.multiple_of(k * cols, cols), cols)] = load(near, slot, me // 2, rows) + (
            load(second_in, slot, 0) + load(second_in, slot, 1) + load(second_in, slot, 2)
        )

    stages = (stage_product, stage_near, stage_far, stage_second, stage_last)

    def step(t, carry):
        for lag, stage in enumerate(stages):
            k = t - lag

            @pl.when((k >= 0) & (k < EXPERT_STEPS))
            def _():
                for part in range(2):
                    stage(part, k)

        return carry

    lax.fori_loop(0, EXPERT_STEPS + len(stages) - 1, step, 0)

    for copy in sums:
        copy.wait()
    add_parts(back_ref, me_z, got.at[0], back_sum)

    def finish(k, carry):
        for part in range(2):
            @pl.when(k >= EXPERT_STEPS - 2)
            def _():
                core_copy(part, k).wait_send()

            for copies in (near_copies, far_copies, second_copies):
                for copy in copies(part, k):
                    copy.wait_send()
        return carry

    lax.fori_loop(0, EXPERT_STEPS, finish, 0)


def expert_sum(rows, acts, hidden, grads, back, picks):
    slots, cols, half = 2 * EXPERT_STEPS, EXPERT_COLS, rows.shape[1] // 2
    block = half // 4
    low = jnp.bfloat16
    sems = lambda *shape: pltpu.SemaphoreType.DMA(shape)
    space = pl.BlockSpec(memory_space=pltpu.VMEM)
    total = jax.ShapeDtypeStruct(back.shape[1:], jnp.float32)
    return pl.pallas_call(
        expert_sum_kernel,
        out_shape=(
            jax.ShapeDtypeStruct((2, block // 4, EXPERT_STEPS * cols), jnp.float32),
            total,
            jax.ShapeDtypeStruct(picks.shape, picks.dtype),
        ),
        in_specs=[space] * 6,
        out_specs=(space,) * 3,
        scratch_shapes=[
            pltpu.VMEM((2, 2, half, cols), low),
            pltpu.VMEM((slots, half, cols), low),
            pltpu.VMEM((slots, 4, block // 2, cols), low),
            pltpu.VMEM((slots, 2, block // 2, cols), low),
            pltpu.VMEM((slots, 3, block // 4, cols), low),
            pltpu.VMEM((1, 3, *back.shape[1:]), low),
            pltpu.VMEM(rows.shape[::-1], low),
            pltpu.VMEM((2, *hidden.shape[:0:-1]), low),
            sems(slots), sems(slots), sems(slots, 4), sems(slots, 4), sems(slots, 2), sems(slots, 2),
            sems(slots, 3), sems(slots, 3), sems(3, 4), sems(3, 4),
        ],
        compiler_params=pltpu.CompilerParams(
            collective_id=4, has_side_effects=True, vmem_limit_bytes=52 * 2**20
        ),
        name="expert_sum",
    )(rows, acts, hidden, grads, back, picks)


def gather_kernel(count, *refs):
    shards, plain_in = refs[:count], refs[count : count + 1]
    fulls, plain_out = refs[count + 1 : 2 * count + 1], refs[2 * count + 1 : 2 * count + 2]
    load_sem, own_sem, unit_ss, unit_rs, deep_ss, deep_rs, first_ss, first_rs, second_ss, second_rs, core_ss, core_rs, row_ss, row_rs, *staged = refs[2 * count + 2 :]
    x, y, c, z = (lax.axis_index(a) for a in ALL)
    first_at = (1 - c) * x + c * y
    second_at = c * x + (1 - c) * y

    def along_first(o):
        return {"x": lax.rem(x + (1 - c) * o, 4), "y": lax.rem(y + c * o, 4)}

    def along_second(o):
        return {"x": lax.rem(x + c * o, 4), "y": lax.rem(y + (1 - c) * o, 4)}

    greet(
        [{"c": 1 - c}]
        + [{axis: ring(axis, o)} for axis in ("x", "y", "z") for o in (1, 2, 3)]
    )

    by_rows = (0, 1)

    def sizes(n):
        if n == 0:
            total = fulls[0].shape[1]
            spread = total * 16 // 25
            return total // 2, spread // 2, spread // 32
        total = shards[n].shape[0]
        spread = total if total % 384 else total * 2 // 3
        if n in by_rows:
            return total // 2, spread // 2, spread // 32
        return total, spread, spread // 16

    def place(n, deep, offset):
        total, spread, unit = sizes(n)
        if n in by_rows:
            return (2 * spread + c * (total - spread) if deep else c * spread) + offset
        return (spread if deep else 0) + offset

    def window(n, shard, deep, offset, length):
        rows, width = shards[n].shape
        at = place(n, deep, offset)
        if n == 0:
            return fulls[0].at[shard, pl.ds(pl.multiple_of(at, 16), length)]
        rows = pl.ds(pl.multiple_of(at + shard * rows, 16), length)
        if n in by_rows:
            return fulls[n].at[rows]
        return fulls[n].at[rows, pl.ds(pl.multiple_of(c * (width // 2), 128), width // 2)]

    def own_window(n, deep, offset, length):
        width = shards[n].shape[1]
        rows = pl.ds(pl.multiple_of(place(n, deep, offset), 16), length)
        if n in by_rows:
            return shards[n].at[rows]
        return shards[n].at[rows, pl.ds(pl.multiple_of(c * (width // 2), 128), width // 2)]

    def own_rows(n):
        return fulls[0].shape[1] if n == 0 else shards[n].shape[0]

    def own_load(n):
        return pltpu.make_async_copy(shards[n].at[pl.ds(0, own_rows(n))], staged[n], load_sem.at[n])

    def own_copy(n):
        if n == 0:
            return pltpu.make_async_copy(staged[0], fulls[0].at[z], own_sem.at[0])
        total = shards[n].shape[0]
        return pltpu.make_async_copy(
            staged[n], fulls[n].at[pl.ds(pl.multiple_of(z * total, 16), total)], own_sem.at[n]
        )

    def came_from(o):
        return lax.rem(z - o + 4, 4)

    def unit_copy(n, o):
        unit = sizes(n)[2]
        at = (second_at * 4 + first_at) * unit
        return remote(
            own_window(n, False, at, unit), window(n, z, False, at, unit), unit_ss.at[n, o], unit_rs.at[n, o], {"z": ring("z", o)}
        )

    def deep_copy(n, o):
        total, spread, unit = sizes(n)
        return remote(
            own_window(n, True, 0, total - spread), window(n, z, True, 0, total - spread),
            deep_ss.at[n, o], deep_rs.at[n, o], {"z": ring("z", o)},
        )

    def deep_forward(n, o):
        total, spread, unit = sizes(n)
        edge = (total - spread) // 2
        block = window(n, came_from(o), True, 0 if o == 1 else edge, edge)
        return remote(block, block, deep_ss.at[n, 3 + o], deep_rs.at[n, 3 + o], {"z": ring("z", o)})

    def first_copy(n, o, step):
        unit = sizes(n)[2]
        block = window(n, came_from(o), False, (second_at * 4 + first_at) * unit, unit)
        return remote(block, block, first_ss.at[n, o, step], first_rs.at[n, o, step], along_first(step))

    def second_copy(n, o, step):
        unit = sizes(n)[2]
        block = window(n, came_from(o), False, second_at * 4 * unit, 4 * unit)
        return remote(block, block, second_ss.at[n, o, step], second_rs.at[n, o, step], along_second(step))

    def second_forward(n, o, step):
        unit = sizes(n)[2]
        source = lax.rem(second_at + 4 - step, 4)
        at = source * 4 * unit + (0 if step == 1 else 2 * unit)
        block = window(n, came_from(o), False, at, 2 * unit)
        return remote(block, block, second_ss.at[n, o, 4 + step], second_rs.at[n, o, 4 + step], along_second(step))

    def core_copies(n, o):
        total, spread, unit = sizes(n)
        shard = came_from(o)
        blocks = [window(n, shard, False, 0, spread)]
        if spread < total:
            blocks.append(window(n, shard, True, 0, total - spread))
        return [
            remote(block, block, core_ss.at[n, o, i], core_rs.at[n, o, i], {"c": 1 - c})
            for i, block in enumerate(blocks)
        ]

    def plain_copy(i, o):
        return remote(plain_in[i], plain_out[i].at[z], row_ss.at[i, o], row_rs.at[i, o], {"z": ring("z", o)})

    arrays = range(count)
    deep = [n for n in arrays if sizes(n)[0] > sizes(n)[1]]
    sides, offsets = (1, 3), (1, 3, 2)
    for n in arrays:
        for o in offsets:
            unit_copy(n, o).start()
    for n in deep:
        for o in sides:
            deep_copy(n, o).start()
    for i in range(1):
        for o in offsets:
            plain_copy(i, o).start()
    for n in arrays:
        own_load(n).start()
    own_plain = [pltpu.make_async_copy(plain_in[i], plain_out[i].at[z], own_sem.at[count + i]) for i in range(1)]
    for copy in own_plain:
        copy.start()
    for n in arrays:
        for o in offsets:
            unit_copy(n, o).wait_recv()
            for step in offsets:
                first_copy(n, o, step).start()
    for n in arrays:
        own_load(n).wait()
        own_copy(n).start()
    for n in arrays:
        for o in offsets:
            for step in offsets:
                first_copy(n, o, step).wait_recv()
            for step in sides:
                second_copy(n, o, step).start()
    for n in arrays:
        if n in deep:
            for o in sides:
                deep_copy(n, o).wait_recv()
                deep_forward(n, o).start()
                core_copies(n, o)[1].start()
        for o in offsets:
            for step in sides:
                second_copy(n, o, step).wait_recv()
                second_forward(n, o, step).start()
    for n in arrays:
        for o in offsets:
            for step in sides:
                second_forward(n, o, step).wait_recv()
            core_copies(n, o)[0].start()
        if n in deep:
            for o in sides:
                deep_forward(n, o).wait_recv()
            core_copies(n, 2)[1].start()
    for i in range(1):
        for o in offsets:
            plain_copy(i, o).wait()
        own_plain[i].wait()
    for n in arrays:
        own_copy(n).wait()
        for o in offsets:
            for copy in core_copies(n, o):
                copy.wait()
            unit_copy(n, o).wait_send()
            for step in offsets:
                first_copy(n, o, step).wait_send()
            for step in sides:
                second_copy(n, o, step).wait_send()
                second_forward(n, o, step).wait_send()
        if n in deep:
            for o in sides:
                deep_copy(n, o).wait_send()
                deep_forward(n, o).wait_send()


def gather_weights(shards, plain, main_rows):
    count = len(shards)
    space = pl.BlockSpec(memory_space=pl.ANY)
    sem = lambda *shape: pltpu.SemaphoreType.DMA(shape)
    fulls = [(4, main_rows, shards[0].shape[1])] + [(4 * s.shape[0], s.shape[1]) for s in shards[1:]]
    return pl.pallas_call(
        functools.partial(gather_kernel, count),
        out_shape=tuple(jax.ShapeDtypeStruct(f, jnp.bfloat16) for f in fulls)
        + tuple(jax.ShapeDtypeStruct((4, *p.shape), p.dtype) for p in plain),
        in_specs=[space] * (count + 1),
        out_specs=(space,) * (count + 1),
        scratch_shapes=[
            sem(count),
            sem(count + 1),
            sem(count, 4), sem(count, 4), sem(count, 8), sem(count, 8),
            sem(count, 4, 4), sem(count, 4, 4), sem(count, 4, 8), sem(count, 4, 8),
            sem(count, 4, 2), sem(count, 4, 2), sem(1, 4), sem(1, 4),
            pltpu.VMEM((main_rows, shards[0].shape[1]), jnp.bfloat16),
        ]
        + [pltpu.VMEM(s.shape, s.dtype) for s in shards[1:]],
        compiler_params=pltpu.CompilerParams(
            collective_id=6, has_side_effects=True, vmem_limit_bytes=60 * 2**20
        ),
        name="gather_weights",
    )(*shards, *plain)


TILE = 128
HIGH = lax.Precision.HIGHEST


def tile_at(j):
    return pl.ds(pl.multiple_of(j * TILE, TILE), TILE)


def dot_nt(left, right):
    return lax.dot_general(left, right, (((1,), (1,)), ((), ())), preferred_element_type=jnp.float32)


def short(values):
    return values.astype(jnp.bfloat16)


def lane_ids():
    return lax.broadcasted_iota(jnp.int32, (TILE, TILE), 1)


def row_ids():
    return lax.broadcasted_iota(jnp.int32, (TILE, TILE), 0)


def head_steps(tail_ref, heads_ref):
    raw = tail_ref[...] + heads_ref[1:2]
    used = lane_ids() < HEADS
    small = jnp.exp(-jnp.abs(raw))
    tail = jnp.where(small < 1e-3, small * (1.0 - small * (0.5 - small / 3.0)), jnp.log(1.0 + small))
    soft = jnp.maximum(raw, 0.0) + tail
    step = jnp.where(used, soft, 0.0)
    return raw, step, jnp.where(used, -jnp.exp(heads_ref[0:1]) * step, 0.0)


def head_columns(values, pair):
    moved = pltpu.roll(values, lax.rem(TILE - 2 * pair, TILE), 1)
    return moved[:, 0:1], moved[:, 1:2]


def both_heads(columns):
    return jnp.where(lane_ids() < TILE // 2, columns[0], columns[1])


def taps_of(ext, cw_ref, lanes):
    summed = cw_ref[4:5, lanes]
    for k in range(4):
        summed = summed + cw_ref[k : k + 1, lanes] * ext[5 + k : 5 + k + TILE]
    return summed


def fill_ext(ext, halo_ref, proj_ref, j):
    ext[0:8] = halo_ref[:, tile_at(j)]
    ext[8 : 8 + TILE] = proj_ref[:, pl.ds(pl.multiple_of(INNER + j * TILE, TILE), TILE)]


def mixer_in_kernel(proj_ref, tail_ref, halo_ref, cw_ref, heads_ref, mixed_ref, state_ref, totals_ref, run_ref, step_ref, ext):
    unused_raw, step, log_decay = head_steps(tail_ref, heads_ref)
    lower = (row_ids() >= lane_ids()).astype(jnp.float32)
    run = jnp.dot(lower, log_decay, precision=HIGH, preferred_element_type=jnp.float32)
    run_ref[...] = run
    step_ref[...] = step
    last = run[TILE - 1 : TILE]
    totals_ref[...] = jnp.broadcast_to(last, totals_ref.shape)
    weight = jnp.exp(last - run) * step

    def conv(j, carry):
        fill_ext(ext, halo_ref, proj_ref, j)
        u = taps_of(ext, cw_ref, tile_at(j))
        mixed_ref[:, tile_at(j)] = u * jax.nn.sigmoid(u)
        return carry

    lax.fori_loop(0, CONV // TILE, conv, 0)
    in_map = short(mixed_ref[:, INNER : INNER + TILE])

    def state(p, carry):
        scaled = mixed_ref[:, tile_at(p)] * both_heads(head_columns(weight, p))
        state_ref[p] = short(dot32(short(scaled.T), in_map))
        return carry

    lax.fori_loop(0, HEADS // 2, state, 0, unroll=2)


def decays_of(column, row, lower):
    return jnp.where(lower, jnp.exp(jnp.minimum(column - row, 0.0)), 0.0)


def mixer_out_kernel(proj_ref, mixed_ref, run_ref, step_ref, carried_ref, wide_ref, normed_ref, scanned_ref, gated, rows, ):
    run = run_ref[...]
    rows[0] = run.T
    rows[1] = step_ref[...].T
    lower = row_ids() >= lane_ids()
    in_map = mixed_ref[:, INNER : INNER + TILE]
    out_map = mixed_ref[:, INNER + TILE : INNER + 2 * TILE]
    kernel = lax.dot_general(out_map, in_map, (((1,), (1,)), ((), ())), precision=HIGH, preferred_element_type=jnp.float32)
    out_low = short(out_map)

    def pair(p, squares):
        values = mixed_ref[:, tile_at(p)]
        values_low = short(values)
        columns = head_columns(run, p)
        parts = []
        for h in range(2):
            decays = decays_of(columns[h], rows[0, pl.ds(2 * p + h, 1)], lower)
            weights = kernel * decays * rows[1, pl.ds(2 * p + h, 1)]
            parts.append(dot32(short(weights), values_low))
        result = jnp.where(lane_ids() < TILE // 2, parts[0], parts[1])
        result = result + jnp.exp(both_heads(columns)) * dot_nt(out_low, carried_ref[p])
        result = result + wide_ref[0:1, tile_at(p)] * values
        scanned_ref[:, tile_at(p)] = result
        gate = proj_ref[:, tile_at(p)]
        g = result * (gate * jax.nn.sigmoid(gate))
        gated[:, tile_at(p)] = g
        return squares + g * g

    squares = lax.fori_loop(0, HEADS // 2, pair, jnp.zeros((TILE, TILE), jnp.float32), unroll=2)
    scale = lax.rsqrt(jnp.sum(squares, 1, keepdims=True) / INNER + NORM_EPS)

    def norm(p, carry):
        normed_ref[:, tile_at(p)] = short(gated[:, tile_at(p)] * scale * wide_ref[1:2, tile_at(p)])
        return carry

    lax.fori_loop(0, HEADS // 2, norm, 0, unroll=2)


def gate_back_kernel(proj_ref, mixed_ref, scanned_ref, back_ref, run_ref, wide_ref, result_ref, gate_ref, gain_ref, state_ref, gated):
    run = run_ref[...]
    out_map = short(mixed_ref[:, INNER + TILE : INNER + 2 * TILE])

    def first(p, sums):
        gate = proj_ref[:, tile_at(p)]
        g = scanned_ref[:, tile_at(p)] * (gate * jax.nn.sigmoid(gate))
        gated[:, tile_at(p)] = g
        back = back_ref[:, tile_at(p)] * wide_ref[1:2, tile_at(p)]
        return sums[0] + g * g, sums[1] + g * back

    zero = jnp.zeros((TILE, TILE), jnp.float32)
    squares, products = lax.fori_loop(0, HEADS // 2, first, (zero, zero), unroll=2)
    scale = lax.rsqrt(jnp.sum(squares, 1, keepdims=True) / INNER + NORM_EPS)
    shift = jnp.sum(products, 1, keepdims=True) * scale * scale * scale / INNER

    def second(p, carry):
        lanes = tile_at(p)
        gate = proj_ref[:, lanes]
        sig = jax.nn.sigmoid(gate)
        g = gated[:, lanes]
        back = back_ref[:, lanes]
        gain_ref[:, lanes] = jnp.broadcast_to(jnp.sum(back * g * scale, 0, keepdims=True), (8, TILE))
        g_back = back * wide_ref[1:2, lanes] * scale - g * shift
        result_back = g_back * (gate * sig)
        result_ref[:, lanes] = result_back
        gate_ref[:, lanes] = short(g_back * scanned_ref[:, lanes] * sig * (1.0 + gate * (1.0 - sig)))
        moved = result_back * jnp.exp(both_heads(head_columns(run, p)))
        state_ref[p] = short(dot32(short(moved.T), out_map))
        return carry

    lax.fori_loop(0, HEADS // 2, second, 0, unroll=2)


def mixer_back_kernel(
    proj_ref, tail_ref, halo_ref, cw_ref, heads_ref, mixed_ref, run_ref, step_ref, wide_ref,
    carried_ref, result_ref, leaving_ref, lefts_ref, acts_ref, mix_ref, up_ref,
    conv_ref, rim_ref, taps_ref, step_back_ref, heads_back_ref, shared_in_ref, out_ref, shared_out_ref,
    rows, column_sums, row_sums, kernel_back, maps_back, mixed_back, ext, padded, rights, *sum_scratch,
):
    greet_neighbours()
    model = mix_ref.shape[1]
    rights[:, : 4 * RS_COLS] = acts_ref[...]
    for part in range(3):
        at = (RS_FIRST[part] + RS_COUNTS[part] - 1) * RS_COLS
        rights[:, at : at + RS_COLS] = up_ref[:, part * RS_COLS : (part + 1) * RS_COLS]
        if part:
            rights[:, at - model : at] = mix_ref[...]
    share = lefts_ref.shape[1] // 2

    def left_of(part, k, which):
        n = k // 4 if part == 0 else 2 * part + k // 3
        return lefts_ref[n, pl.ds(pl.multiple_of(which * share, share), share), :]

    def right_of(part, k, col):
        return rights[:, pl.ds(pl.multiple_of((RS_FIRST[part] + k) * RS_COLS + col, 256), 256)]

    def store(part, k, total):
        plain = RS_COUNTS[part] - 1

        @pl.when(k < plain)
        def _():
            lanes = pl.ds(pl.multiple_of(k * RS_COLS, RS_COLS), RS_COLS)
            if part == 0:
                shared_in_ref[:, lanes] = total[:12]
            else:
                out_ref[12 * part - 12 : 12 * part, lanes] = total[:12]

        @pl.when(k == plain)
        def _():
            shared_out_ref[:, part * RS_COLS : (part + 1) * RS_COLS] = total[:8]

    sum_step, sum_finish = grad_sum_steps(sum_scratch, left_of, right_of, store)
    run, step = run_ref[...], step_ref[...]
    rows[0] = run.T
    rows[1] = step.T
    lanes_id, rows_id = lane_ids(), row_ids()
    lower = rows_id >= lanes_id
    left_half = lanes_id < TILE // 2
    half_line = lax.broadcasted_iota(jnp.int32, (1, TILE), 1) // (TILE // 2)
    in_map = mixed_ref[:, INNER : INNER + TILE]
    out_map = mixed_ref[:, INNER + TILE : INNER + 2 * TILE]
    kernel = lax.dot_general(out_map, in_map, (((1,), (1,)), ((), ())), precision=HIGH, preferred_element_type=jnp.float32)
    in_low, out_low = short(in_map), short(out_map)
    last = run[TILE - 1 : TILE]
    fade = jnp.exp(last - run)
    weight = fade * step
    column_sums[...] = jnp.zeros_like(column_sums)
    row_sums[...] = jnp.zeros_like(row_sums)
    kernel_back[...] = jnp.zeros_like(kernel_back)
    maps_back[...] = jnp.zeros_like(maps_back)

    def pair(p, carry):
        @pl.when(lax.rem(p, 3) == 0)
        def _():
            sum_step(p // 3)

        lanes = tile_at(p)
        values, back = mixed_ref[:, lanes], result_ref[:, lanes]
        values_low, back_low = short(values), short(back)
        columns = head_columns(run, p)
        which = 2 * p + (rows_id >= TILE // 2).astype(jnp.int32)
        spread = (lanes_id == which).astype(jnp.bfloat16)
        parts = []
        for h in range(2):
            at = pl.ds(2 * p + h, 1)
            decays = decays_of(columns[h], rows[0, at], lower)
            plain = kernel * decays
            steps = rows[1, at]
            weights = plain * steps
            mine = jnp.where(left_half, back, 0.0) if h == 0 else jnp.where(left_half, 0.0, back)
            weights_back = dot_nt(short(mine), values_low)
            kernel_back[...] += weights_back * (decays * steps)
            loose = weights_back * plain
            pulled = short(loose * steps)
            column_sums[0] += dot32(pulled, (lanes_id == 2 * p + h).astype(jnp.bfloat16))
            row_sums[0, at] = jnp.sum(pulled.astype(jnp.float32), 0, keepdims=True)
            row_sums[1, at] = jnp.sum(loose, 0, keepdims=True)
            parts.append(dot32(short(weights.T), back_low))
        values_back = jnp.where(left_half, parts[0], parts[1]) + wide_ref[0:1, lanes] * back
        carried, leaving = carried_ref[p], leaving_ref[p]
        moved = back * jnp.exp(both_heads(columns))
        moved_low = short(moved)
        seen = dot_nt(out_low, carried)
        column_sums[0] += dot32(short(moved * seen), spread)
        maps_back[1] += dot32(moved_low, carried)
        weight_pair = both_heads(head_columns(weight, p))
        pulled_state = dot_nt(in_low, leaving)
        values_back = values_back + weight_pair * pulled_state
        maps_back[0] += dot32(short(values * weight_pair), leaving)
        column_sums[1] += dot32(short(values * pulled_state), spread)
        mixed_back[:, lanes] = values_back
        skip_part = jnp.sum(back * values, 0, keepdims=True)
        kept = jnp.sum(carried.astype(jnp.float32) * leaving.astype(jnp.float32), 1, keepdims=True)
        for h in range(2):
            half = slice(h * TILE // 2, (h + 1) * TILE // 2)
            row_sums[2, pl.ds(2 * p + h, 1)] = jnp.broadcast_to(
                jnp.sum(jnp.where(half_line == h, skip_part, 0.0), 1, keepdims=True), (1, TILE)
            )
            row_sums[3, pl.ds(2 * p + h, 1)] = jnp.broadcast_to(
                jnp.sum(kept[half], 0, keepdims=True), (1, TILE)
            )
        return carry

    lax.fori_loop(0, HEADS // 2, pair, 0)

    used = lanes_id < HEADS
    loose_columns = row_sums[1].T
    weight_back = column_sums[1]
    run_back = column_sums[0] - row_sums[0].T - weight * weight_back
    skip_back, decay_back = row_sums[2].T, row_sums[3].T
    last_back = jnp.sum(weight * weight_back, 0, keepdims=True) + jnp.exp(last) * decay_back[0:1]
    run_back = run_back + jnp.where(rows_id == TILE - 1, last_back, 0.0)
    upper = (lanes_id >= rows_id).astype(jnp.float32)
    log_back = jnp.dot(upper, run_back, precision=HIGH, preferred_element_type=jnp.float32)
    raw, unused_step, log_decay = head_steps(tail_ref, heads_ref)
    rate = jnp.exp(heads_ref[0:1])
    step_back = loose_columns + fade * weight_back - rate * log_back
    raw_back = jnp.where(used, step_back * jax.nn.sigmoid(raw), 0.0)
    step_back_ref[...] = raw_back
    rate_back = jnp.sum(jnp.where(used, log_back * log_decay, 0.0), 0, keepdims=True)
    bias_back = jnp.sum(raw_back, 0, keepdims=True)
    at_row = lax.broadcasted_iota(jnp.int32, (8, TILE), 0)
    heads_back_ref[...] = jnp.where(
        at_row == 0, rate_back, jnp.where(at_row == 1, bias_back, jnp.where(at_row == 2, skip_back[0:1], 0.0))
    )
    both = kernel_back[...]
    mixed_back[:, INNER : INNER + TILE] = maps_back[0] + dot32(short(both.T), out_low)
    mixed_back[:, INNER + TILE : INNER + 2 * TILE] = maps_back[1] + dot32(short(both), in_low)
    padded[0:8] = jnp.zeros((8, TILE), jnp.float32)
    padded[8 + TILE : 16 + TILE] = jnp.zeros((8, TILE), jnp.float32)

    def conv(j, carry):
        @pl.when(lax.rem(j, 13) == 0)
        def _():
            sum_step(8 + j // 13)

        lanes = tile_at(j)
        fill_ext(ext, halo_ref, proj_ref, j)
        u = taps_of(ext, cw_ref, lanes)
        sig = jax.nn.sigmoid(u)
        back = mixed_back[:, lanes] * sig * (1.0 + u * (1.0 - sig))
        padded[8 : 8 + TILE] = back
        taps_ref[4:5, lanes] = jnp.sum(back, 0, keepdims=True)
        total = jnp.zeros((TILE, TILE), jnp.float32)
        rim = jnp.zeros((8, TILE), jnp.float32)
        for k in range(4):
            tap = cw_ref[k : k + 1, lanes]
            taps_ref[k : k + 1, lanes] = jnp.sum(back * ext[5 + k : 5 + k + TILE], 0, keepdims=True)
            total = total + tap * padded[11 - k : 11 - k + TILE]
            rim = rim + tap * padded[3 - k : 11 - k]
        conv_ref[:, lanes] = total
        rim_ref[:, lanes] = rim
        return carry

    lax.fori_loop(0, CONV // TILE, conv, 0)
    sum_finish()


def tile_call(kernel, outs, scratch, name, *args, collective=None):
    space = pl.BlockSpec(memory_space=pltpu.VMEM)
    params = dict(vmem_limit_bytes=40 * 2**20)
    if collective is not None:
        params = dict(vmem_limit_bytes=58 * 2**20, collective_id=collective, has_side_effects=True)
    return pl.pallas_call(
        kernel,
        out_shape=tuple(jax.ShapeDtypeStruct(s, d) for s, d in outs),
        in_specs=[space] * len(args),
        out_specs=(space,) * len(outs),
        scratch_shapes=[pltpu.VMEM(s, jnp.float32) if isinstance(s, tuple) else s for s in scratch],
        compiler_params=pltpu.CompilerParams(**params),
        name=name,
    )(*args)


PROJ_BLOCK = 640


def project_kernel(tokens_ref, gain_ref, *refs):
    *mains, tail_ref, norm_ref, proj_ref, tail_out, kept = refs
    width = mains[0].shape[2]

    def product(weights):
        total = dot32(weights[0], kept[:width])
        for i in range(1, len(weights)):
            total = total + dot32(weights[i], kept[i * width : (i + 1) * width])
        return total.T

    @pl.when(pl.program_id(0) == 0)
    def _():
        values = tokens_ref[...].astype(jnp.float32)
        scale = lax.rsqrt(jnp.mean(values * values, 1, keepdims=True) + NORM_EPS)
        normed = values * scale * gain_ref[...]
        norm_ref[...] = short(normed)
        kept[...] = short(normed.T)
        tail_out[...] = product([tail_ref[i] for i in range(len(mains))])

    proj_ref[...] = product([m[0] for m in mains])


def project(tokens, gain, main, tail):
    parts, rows, width = main.shape
    slots, model = tokens.shape
    whole = lambda shape: pl.BlockSpec(shape, lambda j: (0,) * len(shape))
    return pl.pallas_call(
        project_kernel,
        grid=(rows // PROJ_BLOCK,),
        out_shape=(
            jax.ShapeDtypeStruct((slots, model), jnp.bfloat16),
            jax.ShapeDtypeStruct((slots, rows), jnp.float32),
            jax.ShapeDtypeStruct((slots, tail.shape[1]), jnp.float32),
        ),
        in_specs=[
            whole((slots, model)),
            whole((1, model)),
            *[pl.BlockSpec((1, PROJ_BLOCK, width), lambda j, i=i: (i, j, 0)) for i in range(parts)],
            whole(tail.shape),
        ],
        out_specs=(
            whole((slots, model)),
            pl.BlockSpec((slots, PROJ_BLOCK), lambda j: (0, j)),
            whole((slots, tail.shape[1])),
        ),
        scratch_shapes=[pltpu.VMEM((model, slots), jnp.bfloat16)],
        compiler_params=pltpu.CompilerParams(vmem_limit_bytes=56 * 2**20),
        name="project",
    )(tokens, gain, *[main] * parts, tail)


def project_back_kernel(gate_ref, conv_ref, tail_back_ref, rim_ref, *refs):
    *mains, tail_ref, tokens_ref, gain_ref, middle_ref, tokens_back_ref, gain_back_ref, back_ref, total = refs
    parts, width = len(mains), mains[0].shape[2]
    step = pl.program_id(0)

    @pl.when(step == 0)
    def _():
        for i in range(parts):
            total[:, i * width : (i + 1) * width] = dot32(short(tail_back_ref[...]), tail_ref[i])
        inner, conv = gate_ref.shape[1], conv_ref.shape[1]
        back_ref[:, :inner] = gate_ref[...]
        back_ref[:, inner : inner + conv] = short(conv_ref[...])
        rim = jnp.concatenate([jnp.zeros((8, conv), jnp.float32), rim_ref[...]], 0)
        back_ref[TILE - 16 :, inner : inner + conv] = short(conv_ref[TILE - 16 :] + rim)
        back_ref[:, inner + conv : inner + conv + TILE] = short(tail_back_ref[...])
        rest = back_ref.shape[1] - inner - conv - TILE
        back_ref[:, inner + conv + TILE :] = jnp.zeros((TILE, rest), jnp.bfloat16)

    block = mains[0].shape[1]
    here = back_ref[:, pl.ds(pl.multiple_of(step * block, TILE), block)]
    for i in range(parts):
        total[:, i * width : (i + 1) * width] += dot32(here, mains[i][0])

    @pl.when(step == pl.num_programs(0) - 1)
    def _():
        values = tokens_ref[...].astype(jnp.float32)
        scale = lax.rsqrt(jnp.mean(values * values, 1, keepdims=True) + NORM_EPS)
        back = total[...]
        gain_back_ref[...] = jnp.sum(back * values * scale, 0, keepdims=True)
        spread = back * gain_ref[...]
        shift = jnp.mean(spread * values, 1, keepdims=True) * scale * scale * scale
        tokens_back_ref[...] = middle_ref[...] + spread * scale - values * shift


def project_back(gate, conv, tail_back, rim, main, tail, tokens, gain, middle_back):
    parts, rows, width = main.shape
    slots, model = tokens.shape
    whole = lambda shape: pl.BlockSpec(shape, lambda j: (0,) * len(shape))
    return pl.pallas_call(
        project_back_kernel,
        grid=(rows // PROJ_BLOCK,),
        out_shape=(
            jax.ShapeDtypeStruct((slots, model), jnp.float32),
            jax.ShapeDtypeStruct((1, model), jnp.float32),
            jax.ShapeDtypeStruct((slots, RS_SLOTS * RS_COLS), jnp.bfloat16),
        ),
        in_specs=[
            whole(gate.shape),
            whole(conv.shape),
            whole(tail_back.shape),
            whole(rim.shape),
            *[pl.BlockSpec((1, PROJ_BLOCK, width), lambda j, i=i: (i, j, 0)) for i in range(parts)],
            whole(tail.shape),
            whole((slots, model)),
            whole((1, model)),
            whole((slots, model)),
        ],
        out_specs=(whole((slots, model)), whole((1, model)), whole((slots, RS_SLOTS * RS_COLS))),
        scratch_shapes=[pltpu.VMEM((slots, model), jnp.float32)],
        compiler_params=pltpu.CompilerParams(vmem_limit_bytes=56 * 2**20),
        name="project_back",
    )(gate, conv, tail_back, rim, *[main] * parts, tail, tokens, gain, middle_back)


def from_behind(block, axis, distance):
    devices = range(lax.axis_size(axis))
    route = [(i - distance, i) for i in devices if i - distance in devices]
    return lax.ppermute(block, axis, route)


def local(
    tokens,
    cotangent,
    lengths,
    routes,
    norm_gain,
    w_in,
    conv_weight,
    conv_bias,
    a_log,
    dt_bias,
    skip_scale,
    gated_gain,
    w_out,
    post_gain,
    w_router,
    shared_in,
    shared_out,
    expert_in,
    expert_out,
):
    low = jnp.bfloat16
    tokens, cotangent, routes = tokens[0], cotangent[0], routes[0]
    slot_count, model_width = tokens.shape
    inner_width = gated_gain.shape[0]
    conv_width = conv_bias.shape[0]
    head_count = a_log.shape[0]
    tap_count = conv_weight.shape[0]
    expert_count = w_router.shape[1]
    residual = tokens.astype(jnp.float32)
    positions = lax.axis_index(SEQ) * slot_count + jnp.arange(slot_count)
    valid = positions < lengths[0]
    upstream_low = jnp.where(valid[:, None], cotangent, jnp.zeros_like(cotangent))
    upstream = upstream_low.astype(jnp.float32)
    main_rows = inner_width + conv_width
    turned = w_in.T
    tail_shard = jnp.concatenate(
        [
            turned[main_rows:],
            w_router.T,
            jnp.zeros((TILE - head_count - expert_count, turned.shape[1]), low),
        ],
        0,
    )
    full_in, full_out, full_shared_in, full_shared_out, tails = gather_weights(
        [turned, w_out, shared_in, shared_out], [tail_shard], main_rows
    )
    full_router = jnp.swapaxes(tails[:, head_count : head_count + expert_count], 0, 1)
    full_router = full_router.reshape(expert_count, model_width)

    first_norm, projected, tail_values = project(tokens, norm_gain[None], full_in, tails)
    halo = from_behind(projected[slot_count - 8 :, inner_width:], SEQ, 1)
    taps = jnp.concatenate([conv_weight, conv_bias[None], jnp.zeros((3, conv_width), jnp.float32)], 0)
    heads = jnp.pad(jnp.stack([a_log, dt_bias]), ((0, 6), (0, TILE - head_count)))
    wide = jnp.stack([jnp.repeat(skip_scale, inner_width // head_count), gated_gain])
    square, pairs = (TILE, TILE), (head_count // 2, TILE, TILE)
    mixed, leaving, totals, running, steps = tile_call(
        mixer_in_kernel,
        [((TILE, conv_width), jnp.float32), (pairs, low), ((8, TILE), jnp.float32), (square, jnp.float32), (square, jnp.float32)],
        [(TILE + 8, TILE)],
        "mixer_in",
        projected, tail_values, halo, taps, heads,
    )
    carried, all_upstream = carried_states(leaving, totals, upstream_low)
    normed_low, scanned = tile_call(
        mixer_out_kernel,
        [((TILE, inner_width), low), ((TILE, inner_width), jnp.float32)],
        [(TILE, inner_width), (2, *square)],
        "mixer_out",
        projected, mixed, running, steps, carried, wide,
    )
    middle = residual + dot32(normed_low, full_out)
    second_norm = scaled_rows(middle, post_gain).astype(low)
    logits = dot_nt(second_norm, full_router)
    chosen = jnp.any(routes[:, :, None] == jnp.arange(expert_count)[None, None, :], 1)
    masked = jnp.where(chosen, logits, -jnp.inf)
    powers = jnp.exp(masked - jnp.max(masked, -1, keepdims=True))
    gate_dense = powers / jnp.sum(powers, -1, keepdims=True)

    all_rows, all_gates = z_gather((second_norm, gate_dense.T), 5, "gather_rows")
    rows = all_rows.reshape(-1, model_width)
    back_rows = all_upstream.reshape(-1, model_width)
    owned = expert_in.shape[0]
    first_owned = lax.axis_index("z") * owned
    gates = lax.dynamic_slice_in_dim(all_gates, first_owned, owned, 1)
    gates = jnp.swapaxes(gates, 0, 1).reshape(owned, -1)
    hidden_width = expert_out.shape[1]
    acts = jnp.einsum("td,edf->etf", rows, expert_in, preferred_element_type=jnp.float32)
    hidden = (jax.nn.silu(acts[..., :hidden_width]) * acts[..., hidden_width:]).astype(low)
    output = jnp.einsum("etf,efd->etd", hidden, expert_out, preferred_element_type=jnp.float32)
    output = output.astype(low).astype(jnp.float32)
    part = jnp.sum(gates[..., None] * output, 0).astype(low)
    back_wide = back_rows.astype(jnp.float32)
    picks = jnp.sum(output * back_wide[None], -1)
    out_grad = (gates[..., None] * back_wide[None]).astype(low)
    hidden_back = jnp.einsum("etd,efd->etf", out_grad, expert_out, preferred_element_type=jnp.float32)
    act_grad = glu_back(acts, hidden_back)
    back = jnp.einsum("etf,edf->td", act_grad, expert_in, preferred_element_type=jnp.float32).astype(low)
    picks = jnp.swapaxes(picks.reshape(owned, 4, slot_count), 0, 1)
    picks = jnp.pad(picks, ((0, 0), (0, 8 - owned), (0, 0)))
    expert_parts, back_sum, all_picks = expert_sum(
        rows,
        act_grad,
        hidden,
        out_grad,
        back.reshape(4, slot_count, model_width),
        picks,
    )
    act_width = act_grad.shape[2]
    grad_expert_in = expert_parts[:, :, :act_width]
    grad_expert_out = expert_parts[:, :, act_width:].reshape(owned, 3, -1, model_width // 3)
    grad_expert_out = jnp.swapaxes(grad_expert_out, 1, 2).reshape(owned, -1, model_width)

    shared_width = full_shared_out.shape[0]
    shared_acts = dot32(second_norm, full_shared_in)
    shared_hidden = (
        jax.nn.silu(shared_acts[:, :shared_width]) * shared_acts[:, shared_width:]
    ).astype(low)
    shared_sum = dot32(shared_hidden, full_shared_out)
    shared_back = jnp.einsum("td,hd->th", upstream_low, full_shared_out, preferred_element_type=jnp.float32)
    shared_act_grad = glu_back(shared_acts, shared_back)
    second_back = jnp.einsum("tf,df->td", shared_act_grad, full_shared_in, preferred_element_type=jnp.float32)
    gate_grads = all_picks[:, :owned].reshape(expert_count, slot_count).T
    pick_grads = gate_dense * (gate_grads - jnp.sum(gate_dense * gate_grads, -1, keepdims=True))
    logit_grads = pick_grads.astype(low)
    second_back = second_back + back_sum + jnp.einsum(
        "te,ed->td", logit_grads, full_router, preferred_element_type=jnp.float32
    )
    unused_second, second_pull = jax.vjp(scaled_rows, middle, post_gain)
    middle_back, grad_post_gain = second_pull(second_back)
    middle_back = middle_back + upstream
    mix_low = middle_back.astype(low)
    normed_back = jnp.einsum("td,kd->tk", mix_low, full_out, preferred_element_type=jnp.float32)
    result_back, gate_back, gain_back, incoming_back = tile_call(
        gate_back_kernel,
        [((TILE, inner_width), jnp.float32), ((TILE, inner_width), low), ((8, inner_width), jnp.float32), (pairs, low)],
        [(TILE, inner_width)],
        "gate_back",
        projected, mixed, scanned, normed_back, running, wide,
    )
    early_lefts, late_lefts = tile_call(
        lefts_kernel,
        [((6, model_width, TILE), low), ((3, model_width, TILE), low)],
        [(inner_width, TILE), (model_width, TILE)],
        "lefts",
        first_norm, second_norm, normed_low, shared_hidden,
    )
    leaving_back, expert_total = carried_states(
        incoming_back, totals, part.reshape(4, slot_count, model_width)
    )
    block_out = jnp.where(valid[:, None], middle + expert_total + shared_sum, 0.0).astype(low)
    conv_part, rim_part, taps_back, steps_back, heads_back, shared_in_part, w_out_part, shared_out_part = tile_call(
        mixer_back_kernel,
        [
            ((TILE, conv_width), jnp.float32), ((8, conv_width), jnp.float32), ((8, conv_width), jnp.float32),
            (square, jnp.float32), ((8, TILE), jnp.float32), ((12, 2 * shared_width), jnp.float32),
            ((24, model_width), jnp.float32), ((8, model_width), jnp.float32),
        ],
        [
            (2, *square), (2, *square), (4, *square), square, (2, *square),
            (TILE, conv_width), (TILE + 8, TILE), (TILE + 16, TILE),
            pltpu.VMEM((TILE, RS_SLOTS * RS_COLS), low),
        ]
        + grad_sum_scratch(model_width),
        "mixer_back",
        projected, tail_values, halo, taps, heads, mixed, running, steps, wide, carried, result_back, leaving_back,
        early_lefts, shared_act_grad, mix_low, upstream_low,
        collective=7,
    )
    rim_back = from_behind(rim_part.astype(low), SEQ, -1).astype(jnp.float32)
    grad_tokens, grad_norm_gain, proj_back = project_back(
        gate_back, conv_part, steps_back, rim_back, full_in, tails, tokens, norm_gain[None], middle_back
    )
    router_back = jnp.einsum("te,td->ed", logit_grads, second_norm, preferred_element_type=jnp.float32)
    w_in_part, small = grad_sum(
        late_lefts, proj_back, w_in.shape[1], taps_back, gain_back, grad_norm_gain, grad_post_gain[None], heads_back, router_back
    )
    owner = lax.axis_index(ALL)

    def owned_part(values):
        size = values.shape[-1] // 128
        return lax.dynamic_slice_in_dim(values, owner * size, size, values.ndim - 1)

    return (
        block_out[None],
        grad_tokens[None],
        owned_part(small[6, :model_width]),
        w_in_part,
        owned_part(small[:4, :conv_width]),
        owned_part(small[4, :conv_width]),
        small[7, :head_count],
        small[7, TILE : TILE + head_count],
        small[7, 2 * TILE : 2 * TILE + head_count],
        owned_part(small[5, :inner_width]),
        w_out_part,
        owned_part(small[6, model_width : 2 * model_width]),
        owned_part(small[:, conv_width:]).T,
        shared_in_part,
        shared_out_part,
        grad_expert_in,
        grad_expert_out,
    )


def solution(mesh):
    split = Mesh(mesh.devices.reshape(4, 4, 2, 4), ALL)
    placed = (
        P("z", SEQ, None),
        P("z", SEQ, None),
        P("z"),
        P("z", SEQ, None),
        P(),
        P("z", None),
        P(),
        P(),
        P(),
        P(),
        P(),
        P(),
        P("z", None),
        P(),
        P("z", None),
        P("z", None),
        P("z", None),
        P("z", None, None),
        P("z", None, None),
    )
    return jax.shard_map(
        local,
        mesh=split,
        in_specs=placed,
        out_specs=(
            P("z", SEQ, None),
            P("z", SEQ, None),
            P(ALL),
            P(ALL, None),
            P(None, ALL),
            P(ALL),
            P(),
            P(),
            P(),
            P(ALL),
            P(ALL, None),
            P(ALL),
            P(ALL, None),
            P(ALL, None),
            P(ALL, None),
            P("z", SEQ, None),
            P("z", SEQ, None),
        ),
        check_vma=False,
    )
```

```python
import functools

import jax
import jax.numpy as jnp
from jax import lax
from jax.experimental import pallas as pl
from jax.experimental.pallas import tpu as pltpu
from jax.sharding import Mesh
from jax.sharding import PartitionSpec as P

SEQ = ("x", "y", "c")
ALL = ("x", "y", "c", "z")
NORM_EPS = 1e-05
HEADS = 48
INNER = 3072
CONV = 3328


def scaled_rows(values, gain_vector):
    return values * lax.rsqrt(jnp.mean(values * values, -1, keepdims=True) + NORM_EPS) * gain_vector


def glu_back(acts_pair, hidden_back):
    half_width = acts_pair.shape[-1] // 2
    gate_part = acts_pair[..., :half_width]
    up_part = acts_pair[..., half_width:]
    sigmoid_gate = jax.nn.sigmoid(gate_part)
    gate_grad = hidden_back * up_part * sigmoid_gate * (1.0 + gate_part * (1.0 - sigmoid_gate))
    up_grad = hidden_back * gate_part * sigmoid_gate
    return jnp.concatenate([gate_grad, up_grad], -1).astype(jnp.bfloat16)


MESH_ID = pl.DeviceIdType.MESH
RS_ORDERS = (("x", "y", "z"), ("y", "z", "x"), ("z", "x", "y"))
RS_COUNTS = (9, 9, 8)
RS_FIRST = (0, 9, 18)
RS_SLOTS = 26
RS_COLS = 256
RS_LAGS = 6
RS_TIMES = max(RS_COUNTS) + RS_LAGS - 1
NEIGHBOURS = [("c", 1)] + [(axis, o) for axis in ("x", "y", "z") for o in (1, 2, 3)]


def ring(axis, offset):
    size = lax.axis_size(axis)
    return lax.rem(lax.axis_index(axis) + offset + size, size)


def greet(targets):
    barrier = pltpu.get_barrier_semaphore()
    for target in targets:
        pl.semaphore_signal(barrier, inc=1, device_id=target, device_id_type=MESH_ID)
    pl.semaphore_wait(barrier, len(targets))


def greet_neighbours():
    greet([{axis: ring(axis, o)} for axis, o in NEIGHBOURS])


def remote(src, dst, send_sem, recv_sem, target):
    return pltpu.make_async_remote_copy(
        src_ref=src,
        dst_ref=dst,
        send_sem=send_sem,
        recv_sem=recv_sem,
        device_id=target,
        device_id_type=MESH_ID,
    )


def dot32(left, right):
    return jnp.dot(left, right, preferred_element_type=jnp.float32)


def grad_sum_scratch(rows):
    half, block, low = rows // 2, rows // 8, jnp.bfloat16
    sems = lambda *shape: [pltpu.SemaphoreType.DMA(shape)] * 2
    return [
        pltpu.VMEM((2, 3, half, RS_COLS), low),
        pltpu.VMEM((RS_SLOTS, half, RS_COLS), low),
        pltpu.VMEM((RS_SLOTS, 4, block // 2, RS_COLS), low),
        pltpu.VMEM((RS_SLOTS, 2, block // 2, RS_COLS), low),
        pltpu.VMEM((RS_SLOTS, 3, block // 4, RS_COLS), low),
        pltpu.VMEM((RS_SLOTS, 4, 16, RS_COLS), low),
        pltpu.VMEM((RS_SLOTS, 3, 16, RS_COLS), low),
        pltpu.VMEM((3, block // 4 + 8, RS_COLS), jnp.float32),
        *sems(RS_SLOTS), *sems(RS_SLOTS, 4), *sems(RS_SLOTS, 2), *sems(RS_SLOTS, 3), *sems(RS_SLOTS, 3),
    ]


def grad_sum_steps(scratch, left_of, right_of, store):
    core_out, core_in, near, far, second_in, third_out, third_in, lines = scratch[:8]
    core_ss, core_rs, near_ss, near_rs, far_ss, far_rs, second_ss, second_rs, third_ss, third_rs = scratch[8:]
    me_core = lax.axis_index("c")
    other = 1 - me_core
    half = core_out.shape[2]
    block = half // 4
    edge = block // 2
    small = block // 4
    unit = third_out.shape[2]
    kept = small // 4
    lines[...] = jnp.zeros_like(lines)

    def core_copy(part, k):
        slot = RS_FIRST[part] + k
        return remote(
            core_out.at[lax.rem(k, 2), part], core_in.at[slot],
            core_ss.at[slot], core_rs.at[slot], {"c": other},
        )

    def near_copies(part, k):
        slot = RS_FIRST[part] + k
        axis = RS_ORDERS[part][0]
        after, before, across = ring(axis, 1), ring(axis, -1), ring(axis, 2)
        plan = ((before, 0, before), (after, edge, after), (across, 0, after), (across, edge, before))
        return [
            remote(
                core_in.at[slot, pl.ds(which * block + offset, edge)], near.at[slot, n],
                near_ss.at[slot, n], near_rs.at[slot, n], {axis: target},
            )
            for n, (which, offset, target) in enumerate(plan)
        ]

    def far_copies(part, k):
        slot = RS_FIRST[part] + k
        axis = RS_ORDERS[part][0]
        return [
            remote(
                near.at[slot, 2 + n], far.at[slot, n],
                far_ss.at[slot, n], far_rs.at[slot, n], {axis: ring(axis, o)},
            )
            for n, o in enumerate((1, -1))
        ]

    def second_copies(part, k):
        slot = RS_FIRST[part] + k
        axis = RS_ORDERS[part][1]
        copies = []
        for o in (1, 2, 3):
            target = ring(axis, o)
            copies.append(
                remote(
                    near.at[slot, target // 2, pl.ds(lax.rem(target, 2) * small, small)],
                    second_in.at[slot, o - 1],
                    second_ss.at[slot, o - 1], second_rs.at[slot, o - 1], {axis: target},
                )
            )
        return copies

    def third_copies(part, k):
        slot = RS_FIRST[part] + k
        axis = RS_ORDERS[part][2]
        return [
            remote(
                third_out.at[slot, ring(axis, o)], third_in.at[slot, o - 1],
                third_ss.at[slot, o - 1], third_rs.at[slot, o - 1], {axis: ring(axis, o)},
            )
            for o in (1, 2, 3)
        ]

    def stage_product(part, k):
        @pl.when(k >= 2)
        def _():
            core_copy(part, k - 2).wait_send()

        left = left_of(part, k, other)
        for col in range(0, RS_COLS, 256):
            core_out[lax.rem(k, 2), part, :, col : col + 256] = dot32(left, right_of(part, k, col)).astype(jnp.bfloat16)
        core_copy(part, k).start()

    def stage_near(part, k):
        slot = RS_FIRST[part] + k
        core_copy(part, k).wait_recv()
        left = left_of(part, k, me_core)
        for col in range(0, RS_COLS, 256):
            mine = dot32(left, right_of(part, k, col))
            theirs = core_in[slot, :, col : col + 256].astype(jnp.float32)
            core_in[slot, :, col : col + 256] = (mine + theirs).astype(jnp.bfloat16)
        for copy in near_copies(part, k):
            copy.start()

    def load(ref, *where):
        return ref[where].astype(jnp.float32)

    def stage_far(part, k):
        slot = RS_FIRST[part] + k
        axis = RS_ORDERS[part][0]
        copies = near_copies(part, k)
        for n, (which, offset) in enumerate(((ring(axis, 1), 0), (ring(axis, -1), edge))):
            copies[2 + n].wait_recv()
            rows = pl.ds(pl.multiple_of(which * block + offset, edge), edge)
            near[slot, 2 + n] = (load(near, slot, 2 + n) + load(core_in, slot, rows)).astype(jnp.bfloat16)
        for copy in far_copies(part, k):
            copy.start()

    def stage_second(part, k):
        slot = RS_FIRST[part] + k
        me = lax.axis_index(RS_ORDERS[part][0])
        copies, far_in = near_copies(part, k), far_copies(part, k)
        for n in range(2):
            copies[n].wait_recv()
            far_in[n].wait_recv()
            rows = pl.ds(pl.multiple_of(me * block + n * edge, edge), edge)
            near[slot, n] = (
                load(near, slot, n) + load(far, slot, n) + load(core_in, slot, rows)
            ).astype(jnp.bfloat16)
        for copy in second_copies(part, k):
            copy.start()

    def stage_third(part, k):
        slot = RS_FIRST[part] + k
        me = lax.axis_index(RS_ORDERS[part][1])
        for copy in second_copies(part, k):
            copy.wait_recv()
        rows = pl.ds(pl.multiple_of(lax.rem(me, 2) * small, small), small)
        lines[part, :small] = load(near, slot, me // 2, rows) + (
            load(second_in, slot, 0) + load(second_in, slot, 1) + load(second_in, slot, 2)
        )
        for j in range(4):
            third_out[slot, j] = lines[part, kept * j : kept * j + unit].astype(jnp.bfloat16)
        for copy in third_copies(part, k):
            copy.start()

    def stage_last(part, k):
        slot = RS_FIRST[part] + k
        for copy in third_copies(part, k):
            copy.wait_recv()
        me = lax.axis_index(RS_ORDERS[part][2])
        total = load(third_out, slot, me) + (
            load(third_in, slot, 0) + load(third_in, slot, 1) + load(third_in, slot, 2)
        )
        store(part, k, total)

    stages = (stage_product, stage_near, stage_far, stage_second, stage_third, stage_last)

    def step(t):
        for lag, stage in enumerate(stages):
            k = t - lag
            for count in sorted(set(RS_COUNTS)):
                @pl.when((k >= 0) & (k < count))
                def _():
                    for part in range(3):
                        if RS_COUNTS[part] == count:
                            stage(part, k)

    def finish():
        for part in range(3):
            def wait_sent(k, carry, part=part):
                @pl.when(k >= RS_COUNTS[part] - 2)
                def _():
                    core_copy(part, k).wait_send()

                for copies in (near_copies, far_copies, second_copies, third_copies):
                    for copy in copies(part, k):
                        copy.wait_send()
                return carry

            lax.fori_loop(0, RS_COUNTS[part], wait_sent, 0)

    return step, finish


def grad_sum_kernel(
    tail_back_ref, rim_ref, gain_ref, tail_ref, taps_ref, gated_gain_ref, post_ref, heads_ref, router_ref,
    main_ref, gate_far, conv_far, lefts_far, tokens_far, middle_far,
    out_ref, small_ref, tokens_back_far, *scratch
):
    gate_ref, conv_ref, lefts_ref, tokens_ref, middle_ref, load_sem, tokens_back_ref, save_sem, *scratch = scratch
    save = pltpu.make_async_copy(tokens_back_ref, tokens_back_far, save_sem.at[0])
    loads = [
        pltpu.make_async_copy(far, near, load_sem.at[i])
        for i, (far, near) in enumerate(
            zip((gate_far, conv_far, lefts_far, tokens_far, middle_far), (gate_ref, conv_ref, lefts_ref, tokens_ref, middle_ref))
        )
    ]
    for copy in loads:
        copy.start()
    *sum_scratch, back_ref, total, weights, weight_sem, pack, pack_in, pack_work, pack_others, pack_ss, pack_rs = scratch
    me_core = lax.axis_index("c")
    other = 1 - me_core
    half = lefts_ref.shape[1] // 2
    blocks = main_ref.shape[1] // weights.shape[2]

    def fetch(j):
        rows = weights.shape[2]
        return [
            pltpu.make_async_copy(
                main_ref.at[i, pl.ds(pl.multiple_of(j * rows, 16), rows)],
                weights.at[lax.rem(j, 2), i],
                weight_sem.at[lax.rem(j, 2), i],
            )
            for i in range(4)
        ]

    for copy in fetch(0) + fetch(1):
        copy.start()
    greet_neighbours()
    inner, conv = gate_ref.shape[1], conv_ref.shape[1]
    for copy in loads[:3]:
        copy.wait()
    back_ref[:, :inner] = gate_ref[...]
    back_ref[:, inner : inner + conv] = short(conv_ref[...])
    rim = jnp.concatenate([jnp.zeros((8, conv), jnp.float32), rim_ref[...]], 0)
    back_ref[TILE - 16 :, inner : inner + conv] = short(conv_ref[TILE - 16 :] + rim)
    back_ref[:, inner + conv : inner + conv + TILE] = short(tail_back_ref[...])
    rest = back_ref.shape[1] - inner - conv - TILE
    back_ref[:, inner + conv + TILE :] = jnp.zeros((TILE, rest), jnp.bfloat16)
    taps_width, wide = taps_ref.shape[1], pack.shape[1] // 2

    def project_step(j):
        for copy in fetch(j):
            copy.wait()
        rows, width = weights.shape[2:]
        here = back_ref[:, pl.ds(pl.multiple_of(j * rows, TILE), rows)]
        for i in range(4):
            total[:, i * width : (i + 1) * width] += dot32(here, weights[lax.rem(j, 2), i])

        @pl.when(j + 2 < blocks)
        def _():
            for copy in fetch(j + 2):
                copy.start()

    def project_end():
        for copy in loads[3:]:
            copy.wait()
        values = tokens_ref[...].astype(jnp.float32)
        scale = lax.rsqrt(jnp.mean(values * values, 1, keepdims=True) + NORM_EPS)
        back = total[...]
        spread = back * gain_ref[...]
        shift = jnp.mean(spread * values, 1, keepdims=True) * scale * scale * scale
        tokens_back_ref[...] = middle_ref[...] + spread * scale - values * shift
        save.start()
        model = tokens_ref.shape[1]
        pack[:, :taps_width] = taps_ref[...]
        pack[5:6, : gated_gain_ref.shape[1]] = gated_gain_ref[0:1]
        pack[6:7, :model] = jnp.sum(back * values * scale, 0, keepdims=True)
        pack[6:7, model : 2 * model] = post_ref[...]
        for i in range(3):
            pack[7:8, TILE * i : TILE * (i + 1)] = heads_ref[i : i + 1]
        pack[:, taps_width:] = router_ref[...]

    width = weights.shape[3]
    for i in range(4):
        total[:, i * width : (i + 1) * width] = dot32(short(tail_back_ref[...]), tail_ref[i])

    def pack_half(ref, which):
        return ref.at[:, pl.ds(pl.multiple_of(which * wide, 128), wide)]

    def pack_core(last):
        if last:
            return remote(pack_work.at[3], pack_half(small_ref, me_core), pack_ss.at[4, 0], pack_rs.at[4, 0], {"c": other})
        return remote(pack_half(pack, other), pack_in, pack_ss.at[0, 0], pack_rs.at[0, 0], {"c": other})

    def pack_copies(s):
        axis = ("x", "y", "z")[s - 1]
        return [
            remote(pack_work.at[s - 1], pack_others.at[s - 1, o - 1], pack_ss.at[s, o], pack_rs.at[s, o], {axis: ring(axis, o)})
            for o in (1, 2, 3)
        ]

    def pack_step(s):
        if s == 0:
            project_end()
            pack_core(False).start()
        if s == 1:
            pack_core(False).wait_recv()
            pack_work[0] = pack[:, pl.ds(pl.multiple_of(me_core * wide, 128), wide)] + pack_in[...]
        if s in (2, 3, 4):
            for copy in pack_copies(s - 1):
                copy.wait_recv()
            pack_work[s - 1] = pack_work[s - 2] + (
                pack_others[s - 2, 0] + pack_others[s - 2, 1] + pack_others[s - 2, 2]
            )
        if s in (1, 2, 3):
            for copy in pack_copies(s):
                copy.start()
        if s == 4:
            pack_core(True).start()
            small_ref[:, pl.ds(pl.multiple_of(me_core * wide, 128), wide)] = pack_work[3]
        if s == 5:
            pack_core(True).wait_recv()
            pack_core(True).wait_send()
            pack_core(False).wait_send()
            for n in (1, 2, 3):
                for copy in pack_copies(n):
                    copy.wait_send()

    def left_of(part, k, which):
        return lefts_ref[part, pl.ds(pl.multiple_of(which * half, half), half), :]

    def right_of(part, k, col):
        return back_ref[:, pl.ds(pl.multiple_of((RS_FIRST[part] + k) * RS_COLS + col, 256), 256)]

    whole = out_ref.shape[1] // RS_COLS
    rows = out_ref.shape[0]

    def store(part, k, total):
        chunk = RS_FIRST[part] + k

        @pl.when(chunk < whole)
        def _():
            out_ref[:, pl.ds(pl.multiple_of(chunk * RS_COLS, RS_COLS), RS_COLS)] = total[:rows]

        if part == 2:
            @pl.when(chunk == whole)
            def _():
                out_ref[:, whole * RS_COLS :] = total[:rows, : out_ref.shape[1] - whole * RS_COLS]

    step, finish = grad_sum_steps(sum_scratch, left_of, right_of, store)

    def run(t, carry):
        step(t)

        @pl.when(t < blocks)
        def _():
            project_step(t)

        for s in range(6):
            @pl.when(t == blocks + s)
            def _():
                pack_step(s)

        return carry

    lax.fori_loop(0, RS_TIMES, run, 0)
    finish()
    save.wait()


def grad_sum(lefts, gate, conv, tail_back, rim, tokens, gain, middle, tails, taps, gated_gain, post, heads, router, main, columns):
    rows = lefts.shape[1]
    wide = taps.shape[1] + router.shape[1]
    slots, model = tokens.shape
    space = pl.BlockSpec(memory_space=pltpu.VMEM)
    block = main.shape[1] // 5
    return pl.pallas_call(
        grad_sum_kernel,
        out_shape=(
            jax.ShapeDtypeStruct((rows // 128, columns), jnp.float32),
            jax.ShapeDtypeStruct((8, wide), jnp.float32),
            jax.ShapeDtypeStruct((slots, model), jnp.float32),
        ),
        in_specs=[space] * 9 + [pl.BlockSpec(memory_space=pl.ANY)] * 6,
        out_specs=(space, space, pl.BlockSpec(memory_space=pl.ANY)),
        scratch_shapes=[pltpu.VMEM(a.shape, a.dtype) for a in (gate, conv, lefts, tokens, middle)]
        + [pltpu.SemaphoreType.DMA((5,)), pltpu.VMEM((slots, model), jnp.float32), pltpu.SemaphoreType.DMA((1,))]
        + grad_sum_scratch(rows)
        + [
            pltpu.VMEM((slots, RS_SLOTS * RS_COLS), jnp.bfloat16),
            pltpu.VMEM((slots, model), jnp.float32),
            pltpu.VMEM((2, 4, block, main.shape[2]), jnp.bfloat16),
            pltpu.SemaphoreType.DMA((2, 4)),
            pltpu.VMEM((8, wide), jnp.float32),
            pltpu.VMEM((8, wide // 2), jnp.float32),
            pltpu.VMEM((4, 8, wide // 2), jnp.float32),
            pltpu.VMEM((3, 3, 8, wide // 2), jnp.float32),
            pltpu.SemaphoreType.DMA((5, 4)),
            pltpu.SemaphoreType.DMA((5, 4)),
        ],
        compiler_params=pltpu.CompilerParams(
            collective_id=0, has_side_effects=True, vmem_limit_bytes=60 * 2**20
        ),
        name="grad_sum",
    )(tail_back, rim, gain, tails, taps, gated_gain, post, heads, router, main, gate, conv, lefts, tokens, middle)


def owner_moves(order, stride, offset, rows):
    moves = []
    for to in range(128):
        digits = {"c": to // 64}
        for axis, at in zip(order, (to // 16 % 4, to // 4 % 4, to % 4)):
            digits[axis] = at
        owner = ((digits["x"] * 4 + digits["y"]) * 2 + digits["c"]) * 4 + digits["z"]
        source, target = owner * stride + offset, to * 12
        if moves and moves[-1][0] + moves[-1][2] == source and moves[-1][1] + moves[-1][2] == target:
            moves[-1][2] += rows
        else:
            moves.append([source, target, rows])
    return moves


def lefts_kernel(first_ref, second_ref, gated_ref, hidden_ref, early_ref, late_ref, turned, sorted_rows):
    def turn(ref):
        for j in range(ref.shape[1] // TILE):
            turned[j * TILE : (j + 1) * TILE] = ref[:, j * TILE : (j + 1) * TILE].astype(jnp.float32).T

    def place(out_ref, at, order, stride, offset, rows):
        if rows < 12:
            sorted_rows[...] = jnp.zeros_like(sorted_rows)
        for source, target, size in owner_moves(order, stride, offset, rows):
            sorted_rows[target : target + size] = turned[source : source + size]
        out_ref[at] = sorted_rows[...].astype(jnp.bfloat16)

    turn(first_ref)
    for part in range(3):
        place(late_ref, part, RS_ORDERS[part], 12, 0, 12)
    turn(second_ref)
    place(early_ref, 0, RS_ORDERS[0], 12, 0, 12)
    turn(hidden_ref)
    for at, part in ((1, 0), (3, 1), (5, 2)):
        place(early_ref, at, RS_ORDERS[part], 8, 0, 8)
    turn(gated_ref)
    place(early_ref, 2, RS_ORDERS[1], 24, 0, 12)
    place(early_ref, 4, RS_ORDERS[2], 24, 12, 12)


def plane_others():
    x, y = lax.axis_index("x"), lax.axis_index("y")
    found = []
    for dx in range(4):
        for dy in range(4):
            if dx + dy:
                tx, ty = lax.rem(x + dx, 4), lax.rem(y + dy, 4)
                found.append((dx * 4 + dy, tx * 4 + ty, {"x": tx, "y": ty}))
    return found


def line_neighbour(ahead):
    x, y, c = lax.axis_index("x"), lax.axis_index("y"), lax.axis_index("c")
    chip = lax.rem(x * 4 + y + (c if ahead else c + 15), 16)
    return {"x": chip // 4, "y": lax.rem(chip, 4), "c": 1 - c}


def greet_plane():
    c = lax.axis_index("c")
    chip = lax.rem(lax.axis_index("x") * 4 + lax.axis_index("y") + 2 * c + 15, 16)
    greet(
        [{"c": 1 - c}, {"x": chip // 4, "y": lax.rem(chip, 4), "c": 1 - c}]
        + [{"z": ring("z", o)} for o in (1, 2, 3)]
        + [where for unused, unused_too, where in plane_others()]
    )


def state_exchange(reverse, state_ref, totals_ref, rows_ref, out_ref, all_rows, rows_sum, tick, *refs):
    pair_in, pair_totals, outgoing, got, back, mine, hand, ps, pr, ss, rs, bs, br, zs, zr = refs
    x, y, c, z = (lax.axis_index(a) for a in ALL)
    chip = x * 4 + y
    half = pair_in.shape[0]
    groups, size = back.shape[1:3]
    others = plane_others()
    mine_at, theirs_at = c * half, (1 - c) * half

    def pair_copies():
        return [
            remote(state_ref.at[pl.ds(theirs_at, half)], pair_in, ps.at[0], pr.at[0], {"c": 1 - c}),
            remote(totals_ref, pair_totals, ps.at[1], pr.at[1], {"c": 1 - c}),
        ]

    def out_copy(at, target, where):
        return remote(outgoing.at[target], got.at[chip], ss.at[at], rs.at[at], where)

    def back_copy(at, target, where):
        return remote(back.at[target], mine.at[pl.ds(groups * chip, groups)], bs.at[at], br.at[at], where)

    def hand_copy():
        return remote(hand, out_ref.at[pl.ds(mine_at, half)], ps.at[2], pr.at[2], {"c": 1 - c})

    row_copies = []
    for o in (1, 3, 2):
        source = rows_ref.at[ring("z", o)] if reverse else rows_ref
        target = all_rows.at[o - 1] if reverse else all_rows.at[z]
        row_copies.append(remote(source, target, zs.at[o], zr.at[o], {"z": ring("z", o)}))
    for copy in pair_copies():
        copy.start()
    for copy in row_copies:
        copy.start()
    own_rows = None if reverse else pltpu.make_async_copy(rows_ref, all_rows.at[z], zs.at[0])
    if not reverse:
        own_rows.start()
    tick(0)
    for copy in pair_copies():
        copy.wait_recv()
    first = jnp.where(c == 0, totals_ref[...], pair_totals[...])
    second = jnp.where(c == 0, pair_totals[...], totals_ref[...])
    inner, outer = (first, second) if reverse else (second, first)
    lanes = lax.broadcasted_iota(jnp.int32, (8, TILE), 1) - c * (half // 2)

    def decay(logs, head):
        return jnp.exp(jnp.sum(jnp.where(lanes[: logs.shape[0]] == head, logs, 0.0), 1, keepdims=True))[:1]

    def states(g):
        own, other = state_ref[mine_at + g].astype(jnp.float32), pair_in[g].astype(jnp.float32)
        return jnp.where(c == 0, own, other), jnp.where(c == 0, other, own)

    total = (first + second)[:1]
    high = total.astype(jnp.bfloat16).astype(jnp.float32)
    middle = (total - high).astype(jnp.bfloat16).astype(jnp.float32)
    row = lax.broadcasted_iota(jnp.int32, (16, TILE), 0)
    split = jnp.where(row == 0, high, jnp.where(row == 1, middle, jnp.where(row == 2, total - high - middle, 0.0)))
    split = split.astype(jnp.bfloat16)

    def combine(m, carry):
        for i in range(groups):
            g = groups * m + i
            early, late = states(g)
            rate = decay(inner, g // 2)
            pair = early + rate * late if reverse else rate * early + late
            outgoing[m, i * size : (i + 1) * size] = pair.astype(jnp.bfloat16)
        outgoing[m, groups * size :] = split
        return carry

    lax.fori_loop(0, 16, combine, 0)
    for d in others:
        out_copy(*d).start()
    got[chip] = outgoing[chip]
    tick(1)
    for d in others:
        out_copy(*d).wait_recv()

    def advance(step, carried):
        p = 15 - step if reverse else step
        logs = jnp.sum(got[p, groups * size :].astype(jnp.float32), 0, keepdims=True)
        new = []
        for i in range(groups):
            back[p, i] = carried[i].astype(back.dtype)
            here = got[p, i * size : (i + 1) * size].astype(jnp.float32)
            new.append(carried[i] * decay(logs, (groups * chip + i) // 2) + here)
        return tuple(new)

    lax.fori_loop(0, 16, advance, (jnp.zeros((size, TILE), jnp.float32),) * groups)
    for d in others:
        back_copy(*d).start()
    mine[pl.ds(groups * chip, groups)] = back[chip]
    tick(2)
    for d in others:
        back_copy(*d).wait_recv()

    def spread(h, carry):
        rate = decay(outer, h)
        for i in range(2):
            g = 2 * h + i
            early, late = states(g)
            near = mine[g].astype(jnp.float32)
            beyond = rate * near + (late if reverse else early)
            swap = (c == 1) if reverse else (c == 0)
            out_ref[mine_at + g] = jnp.where(swap, near, beyond).astype(out_ref.dtype)
            hand[g] = jnp.where(swap, beyond, near).astype(hand.dtype)
        return carry

    lax.fori_loop(0, half // 2, spread, 0)
    hand_copy().start()
    tick(3)
    for copy in row_copies:
        copy.wait()
    if not reverse:
        own_rows.wait()
    if reverse:
        add_parts(rows_ref, z, all_rows, rows_sum)
    hand_copy().wait()
    for copy in pair_copies():
        copy.wait_send()
    for d in others:
        out_copy(*d).wait_send()
        back_copy(*d).wait_send()


def add_parts(ref, me, got, out):
    def rows_at(j, carry):
        rows = pl.ds(pl.multiple_of(j * 32, 32), 32)
        total = ref[me, rows].astype(jnp.float32)
        for o in range(3):
            total = total + got[o, rows].astype(jnp.float32)
        out[rows] = total
        return carry

    lax.fori_loop(0, out.shape[0] // 32, rows_at, 0)


def scan_scratch():
    low, sem = jnp.bfloat16, pltpu.SemaphoreType.DMA
    return [
        pltpu.VMEM((48, 32, TILE), low),
        pltpu.VMEM((8, TILE), jnp.float32),
        pltpu.VMEM((16, 112, TILE), low),
        pltpu.VMEM((16, 112, TILE), low),
        pltpu.VMEM((16, 3, 32, TILE), low),
        pltpu.VMEM((48, 32, TILE), low),
        pltpu.VMEM((48, 32, TILE), low),
        sem((3,)), sem((3,)), sem((16,)), sem((16,)), sem((16,)), sem((16,)), sem((4,)), sem((4,)),
    ]


def middle_kernel(
    normed_ref, tokens_ref, gain_ref, router_ref, chosen_ref, up_ref, out_far, in_far, down_far,
    *refs
):
    outs, refs = refs[:6], refs[6:]
    all_rows, all_gates, out_w, in_w, down_w, *refs = refs
    inside, refs = refs[:6], refs[6:]
    middle_ref, second_ref, base_ref, back_ref, hidden_ref, acts_ref = inside
    save_sem, load_sem, row_ss, row_rs, gate_ss, gate_rs = refs
    saves = [pltpu.make_async_copy(near, far, save_sem.at[i]) for i, (near, far) in enumerate(zip(inside, outs))]
    z = lax.axis_index("z")
    own_rows = pltpu.make_async_copy(second_ref, all_rows.at[z], save_sem.at[6])
    loads = []
    for far, near, parts in ((out_far, out_w, 4), (in_far, in_w, 3), (down_far, down_w, 2)):
        rows = near.shape[0] // parts
        for i in range(parts):
            here = pl.ds(i * rows, rows)
            loads.append(pltpu.make_async_copy(far.at[here], near.at[here], load_sem.at[len(loads)]))
    for copy in loads:
        copy.start()
    greet([{"z": ring("z", o)} for o in (1, 2, 3)])
    depth = normed_ref.shape[1] // 4
    middle = tokens_ref[...].astype(jnp.float32)
    for i in range(4):
        loads[i].wait()
        here = slice(i * depth, (i + 1) * depth)
        middle = middle + dot32(normed_ref[:, here], out_w[here])
    middle_ref[...] = middle
    saves[0].start()
    scale = lax.rsqrt(jnp.mean(middle * middle, 1, keepdims=True) + NORM_EPS)
    second_ref[...] = short(middle * scale * gain_ref[...])
    saves[1].start()
    own_rows.start()

    def row_copy(o):
        return remote(second_ref, all_rows.at[z], row_ss.at[o], row_rs.at[o], {"z": ring("z", o)})

    def row_forward(o):
        half = all_rows.shape[1] // 2
        block = all_rows.at[lax.rem(z + 4 - o, 4), pl.ds(0 if o == 1 else half, half)]
        return remote(block, block, row_ss.at[3 + o], row_rs.at[3 + o], {"z": ring("z", o)})

    def gate_copy(o):
        return remote(all_gates.at[z], all_gates.at[z], gate_ss.at[o], gate_rs.at[o], {"z": ring("z", o)})

    for o in (1, 3):
        row_copy(o).start()
    logits = dot_nt(router_ref[...], second_ref[...])
    masked = jnp.where(chosen_ref[...] > 0.0, logits, -jnp.inf)
    powers = jnp.exp(masked - jnp.max(masked, 0, keepdims=True))
    all_gates[z] = powers / jnp.sum(powers, 0, keepdims=True)
    for o in (1, 3, 2):
        gate_copy(o).start()
    width = hidden_ref.shape[1]
    block = 256
    for copy in loads[4:]:
        copy.wait()
    second = second_ref[...]
    for j in range(0, width, block):
        gate = dot32(second, in_w[:, j : j + block])
        up = dot32(second, in_w[:, width + j : width + j + block])
        sig = jax.nn.sigmoid(gate)
        hidden_ref[:, j : j + block] = short(gate * sig * up)
        back = dot_nt(up_ref[...], down_w[j : j + block])
        acts_ref[:, j : j + block] = short(back * up * sig * (1.0 + gate * (1.0 - sig)))
        acts_ref[:, width + j : width + j + block] = short(back * gate * sig)
    saves[4].start()
    saves[5].start()
    for o in (1, 3):
        row_copy(o).wait_recv()
        row_forward(o).start()
    model = middle_ref.shape[1]
    for j in range(0, model, 2 * block):
        here = slice(j, j + 2 * block)
        base_ref[:, here] = middle_ref[:, here] + dot32(hidden_ref[...], down_w[:, here])
        back_ref[:, here] = dot_nt(acts_ref[...], in_w[here])
    saves[2].start()
    saves[3].start()
    for o in (1, 3):
        row_copy(o).wait_send()
        row_forward(o).wait()
    for o in (1, 3, 2):
        gate_copy(o).wait()
    for copy in saves:
        copy.wait()
    own_rows.wait()


def middle_part(normed, tokens, gain, router, chosen, upstream, out_w, in_w, down_w):
    space, away = pl.BlockSpec(memory_space=pltpu.VMEM), pl.BlockSpec(memory_space=pl.ANY)
    slots, model = tokens.shape
    f32, low, sem = jnp.float32, jnp.bfloat16, pltpu.SemaphoreType.DMA
    outs = [
        ((slots, model), f32), ((slots, model), low), ((slots, model), f32), ((slots, model), f32),
        ((slots, down_w.shape[0]), low), ((slots, in_w.shape[1]), low), ((4, slots, model), low), ((4, *chosen.shape), f32),
    ]
    return pl.pallas_call(
        middle_kernel,
        out_shape=tuple(jax.ShapeDtypeStruct(s, d) for s, d in outs),
        in_specs=[space] * 6 + [away] * 3,
        out_specs=(away,) * 7 + (space,),
        scratch_shapes=[pltpu.VMEM(w.shape, w.dtype) for w in (out_w, in_w, down_w)]
        + [pltpu.VMEM(s, d) for s, d in outs[:6]]
        + [sem((7,)), sem((9,)), sem((7,)), sem((7,)), sem((4,)), sem((4,))],
        compiler_params=pltpu.CompilerParams(
            collective_id=5, has_side_effects=True, vmem_limit_bytes=60 * 2**20
        ),
        name="middle",
    )(normed, tokens, gain, router, chosen, upstream, out_w, in_w, down_w)


EXPERT_ORDERS = (("x", "y"), ("y", "x"))
EXPERT_STEPS = 6
EXPERT_COLS = 256


def expert_sum_kernel(
    picks_ref, gates_ref, gain_ref, back_far, *refs
):
    far, refs = refs[:9], refs[9:]
    weights_far, out_ref, middle_out, mix_out, post_back, router_back, normed_out, *refs = refs
    (middle_back, mix_ref, normed_back, back_ref), refs = refs[:4], refs[4:]
    near_refs, refs = refs[:9], refs[9:]
    rows_ref, acts_ref, hidden_ref, grads_ref, middle_ref, shared_ref, up_ref, second_ref, router_ref = near_refs
    expert_sum_body(
        list(zip(far, near_refs)),
        rows_ref, acts_ref, hidden_ref, grads_ref, back_ref, picks_ref,
        middle_ref, shared_ref, up_ref, second_ref, gates_ref, router_ref, gain_ref, weights_far,
        out_ref, middle_back, mix_ref, post_back, router_back, normed_back, back_far, middle_out, mix_out, normed_out, *refs,
    )


def expert_sum_body(
    far_near,
    rows_ref, acts_ref, hidden_ref, grads_ref, back_ref, picks_ref,
    middle_ref, shared_ref, up_ref, second_ref, gates_ref, router_ref, gain_ref, weights_far,
    out_ref, middle_back, mix_ref, post_back, router_back, normed_back, back_far, middle_out, mix_out, normed_out,
    stage_sem, save_sem, weights, load_sem, back_sum, picks_all,
    core_out, core_in, near, far, second_in, got, turned_rows, turned_hidden,
    core_ss, core_rs, near_ss, near_rs, far_ss, far_rs, second_ss, second_rs, zs, zr,
):
    me_core = lax.axis_index("c")
    me_z = lax.axis_index("z")
    other = 1 - me_core
    half = core_out.shape[2]
    block = half // 4
    edge = block // 2
    small = block // 4
    third = small // 3
    cols = EXPERT_COLS
    quarter = weights.shape[0] // 4
    loads = [
        pltpu.make_async_copy(weights_far.at[pl.ds(i * quarter, quarter)], weights.at[pl.ds(i * quarter, quarter)], load_sem.at[i])
        for i in range(4)
    ]
    staged = [pltpu.make_async_copy(far, here, stage_sem.at[i]) for i, (far, here) in enumerate(far_near)]
    staged.append(pltpu.make_async_copy(back_far, back_ref, stage_sem.at[9]))
    saves = [
        pltpu.make_async_copy(here, far, save_sem.at[i])
        for i, (here, far) in enumerate(((middle_back, middle_out), (mix_ref, mix_out), (normed_back, normed_out)))
    ]
    for copy in staged + loads:
        copy.start()
    greet_neighbours()

    sums = []
    for n, ref in enumerate((back_far,)):
        for o in (1, 3, 2):
            sums.append(
                remote(ref.at[ring("z", o)], got.at[n, o - 1], zs.at[n, o], zr.at[n, o], {"z": ring("z", o)})
            )
    for o in (1, 3, 2):
        sums.append(
            remote(picks_ref.at[ring("z", o)], picks_all.at[me_z], zs.at[2, o], zr.at[2, o], {"z": ring("z", o)})
        )
    for copy in sums:
        copy.start()
    picks_all[me_z] = picks_ref[me_z]
    for copy in staged[:4]:
        copy.wait()
    for j in range(rows_ref.shape[1] // TILE):
        turned_rows[j * TILE : (j + 1) * TILE] = rows_ref[:, j * TILE : (j + 1) * TILE].T
    for part in range(2):
        for j in range(hidden_ref.shape[2] // TILE):
            turned_hidden[part, j * TILE : (j + 1) * TILE] = hidden_ref[part, :, j * TILE : (j + 1) * TILE].T

    def plane_rows(part, which, load, size):
        blocks = []
        for j in range(4):
            for i in range(4):
                spot = (j * 4 + i if part == 0 else i * 4 + j) * 2 + which
                blocks.append(load(pl.ds(pl.multiple_of(spot * size, 16), size)))
        return jnp.concatenate(blocks, 0)

    def core_copy(part, k):
        slot = part * EXPERT_STEPS + k
        return remote(
            core_out.at[lax.rem(k, 2), part], core_in.at[slot],
            core_ss.at[slot], core_rs.at[slot], {"c": other},
        )

    def near_copies(part, k):
        slot = part * EXPERT_STEPS + k
        axis = EXPERT_ORDERS[part][0]
        after, before, across = ring(axis, 1), ring(axis, -1), ring(axis, 2)
        plan = ((before, 0, before), (after, edge, after), (across, 0, after), (across, edge, before))
        return [
            remote(
                core_in.at[slot, pl.ds(which * block + offset, edge)], near.at[slot, n],
                near_ss.at[slot, n], near_rs.at[slot, n], {axis: target},
            )
            for n, (which, offset, target) in enumerate(plan)
        ]

    def far_copies(part, k):
        slot = part * EXPERT_STEPS + k
        axis = EXPERT_ORDERS[part][0]
        return [
            remote(
                near.at[slot, 2 + n], far.at[slot, n],
                far_ss.at[slot, n], far_rs.at[slot, n], {axis: ring(axis, o)},
            )
            for n, o in enumerate((1, -1))
        ]

    def second_copies(part, k):
        slot = part * EXPERT_STEPS + k
        axis = EXPERT_ORDERS[part][1]
        copies = []
        for o in (1, 2, 3):
            target = ring(axis, o)
            copies.append(
                remote(
                    near.at[slot, target // 2, pl.ds(lax.rem(target, 2) * small, small)],
                    second_in.at[slot, o - 1],
                    second_ss.at[slot, o - 1], second_rs.at[slot, o - 1], {axis: target},
                )
            )
        return copies

    def load(ref, *where):
        return ref[where].astype(jnp.float32)

    def products(part, k, which_half, store):
        @pl.when(k < 4)
        def _():
            right = acts_ref[part, :, pl.ds(pl.multiple_of(k * cols, cols), cols)]

            left = plane_rows(part, which_half, lambda rows: turned_rows[rows], small)
            store(0, half, dot32(left, right))

        @pl.when(k >= 4)
        def _():
            left = plane_rows(part, which_half, lambda rows: turned_hidden[part, rows], third)
            for t in range(3):
                right = grads_ref[part, :, pl.ds(pl.multiple_of(t * 2 * cols + (k - 4) * cols, cols), cols)]
                product = dot32(left, right)
                for i in range(16):
                    store(i * small + t * third, third, product[i * third : (i + 1) * third])

    def stage_product(part, k):
        @pl.when(k >= 2)
        def _():
            core_copy(part, k - 2).wait_send()

        def store(at, size, value):
            core_out[lax.rem(k, 2), part, pl.ds(at, size), :] = value.astype(jnp.bfloat16)

        products(part, k, other, store)
        core_copy(part, k).start()

    def stage_near(part, k):
        slot = part * EXPERT_STEPS + k
        core_copy(part, k).wait_recv()

        def store(at, size, value):
            rows = pl.ds(at, size)
            core_in[slot, rows, :] = (value + load(core_in, slot, rows)).astype(jnp.bfloat16)

        products(part, k, me_core, store)
        for copy in near_copies(part, k):
            copy.start()

    def stage_far(part, k):
        slot = part * EXPERT_STEPS + k
        axis = EXPERT_ORDERS[part][0]
        copies = near_copies(part, k)
        for n, (which, offset) in enumerate(((ring(axis, 1), 0), (ring(axis, -1), edge))):
            copies[2 + n].wait_recv()
            rows = pl.ds(pl.multiple_of(which * block + offset, edge), edge)
            near[slot, 2 + n] = (load(near, slot, 2 + n) + load(core_in, slot, rows)).astype(jnp.bfloat16)
        for copy in far_copies(part, k):
            copy.start()

    def stage_second(part, k):
        slot = part * EXPERT_STEPS + k
        me = lax.axis_index(EXPERT_ORDERS[part][0])
        copies, far_in = near_copies(part, k), far_copies(part, k)
        for n in range(2):
            copies[n].wait_recv()
            far_in[n].wait_recv()
            rows = pl.ds(pl.multiple_of(me * block + n * edge, edge), edge)
            near[slot, n] = (
                load(near, slot, n) + load(far, slot, n) + load(core_in, slot, rows)
            ).astype(jnp.bfloat16)
        for copy in second_copies(part, k):
            copy.start()

    def stage_last(part, k):
        slot = part * EXPERT_STEPS + k
        me = lax.axis_index(EXPERT_ORDERS[part][1])
        for copy in second_copies(part, k):
            copy.wait_recv()
        rows = pl.ds(pl.multiple_of(lax.rem(me, 2) * small, small), small)
        out_ref[part, :, pl.ds(pl.multiple_of(k * cols, cols), cols)] = load(near, slot, me // 2, rows) + (
            load(second_in, slot, 0) + load(second_in, slot, 1) + load(second_in, slot, 2)
        )

    stages = (stage_product, stage_near, stage_far, stage_second, stage_last)

    def way_back():
        for copy in sums + staged[4:]:
            copy.wait()
        add_parts(back_ref, me_z, got.at[0], back_sum)
        gates = gates_ref[me_z]
        picked = jnp.concatenate([picks_all[i, 0:2] for i in range(4)], 0)
        logits_back = gates * (picked - jnp.sum(gates * picked, 0, keepdims=True))
        padded = jnp.concatenate([logits_back, jnp.zeros((TILE - 8, TILE), jnp.float32)], 0)
        router_back[...] = dot32(short(padded), second_ref[...])[:8]
        middle = middle_ref[...]
        scale = lax.rsqrt(jnp.mean(middle * middle, 1, keepdims=True) + NORM_EPS)
        back = shared_ref[...] + back_sum[...] + dot32(short(padded.T), router_ref[...])
        post_back[...] = jnp.sum(back * middle * scale, 0, keepdims=True)
        spread = back * gain_ref[...]
        shift = jnp.mean(spread * middle, 1, keepdims=True) * scale * scale * scale
        total = spread * scale - middle * shift + up_ref[...].astype(jnp.float32)
        middle_back[...] = total
        mix_ref[...] = short(total)
        saves[0].start()
        saves[1].start()
        turned = short(total.T)
        for i in range(4):
            loads[i].wait()
            here = slice(i * quarter, (i + 1) * quarter)
            normed_back[:, here] = dot32(weights[here], turned).T
        saves[2].start()

    def step(t, carry):
        @pl.when(t == 5)
        def _():
            way_back()

        for lag, stage in enumerate(stages):
            k = t - lag

            @pl.when((k >= 0) & (k < EXPERT_STEPS))
            def _():
                for part in range(2):
                    stage(part, k)

        return carry

    lax.fori_loop(0, EXPERT_STEPS + len(stages) - 1, step, 0)

    def finish(k, carry):
        for part in range(2):
            @pl.when(k >= EXPERT_STEPS - 2)
            def _():
                core_copy(part, k).wait_send()

            for copies in (near_copies, far_copies, second_copies):
                for copy in copies(part, k):
                    copy.wait_send()
        return carry

    lax.fori_loop(0, EXPERT_STEPS, finish, 0)
    for copy in saves:
        copy.wait()


def expert_sum(rows, acts, hidden, grads, back, picks, middle, shared, upstream, second, gates, router, gain, weights):
    slots, cols, half = 2 * EXPERT_STEPS, EXPERT_COLS, rows.shape[1] // 2
    block = half // 4
    low, f32 = jnp.bfloat16, jnp.float32
    sem = pltpu.SemaphoreType.DMA
    sems = lambda *shape: [sem(shape)] * 2
    space, away = pl.BlockSpec(memory_space=pltpu.VMEM), pl.BlockSpec(memory_space=pl.ANY)
    depth, model = middle.shape
    staged = [rows, acts, hidden, grads, middle, shared, upstream, second, router]
    outs = [
        ((2, block // 4, EXPERT_STEPS * cols), f32), ((depth, model), f32), ((depth, model), low),
        ((1, model), f32), ((8, model), f32), ((depth, weights.shape[0]), f32),
    ]
    return pl.pallas_call(
        expert_sum_kernel,
        out_shape=tuple(jax.ShapeDtypeStruct(s, d) for s, d in outs),
        in_specs=[space] * 3 + [away] * 11,
        out_specs=(space, away, away, space, space, away),
        scratch_shapes=[
            *[pltpu.VMEM(*outs[i]) for i in (1, 2, 5)],
            pltpu.VMEM(back.shape, back.dtype),
            *[pltpu.VMEM(a.shape, a.dtype) for a in staged],
            sem((10,)),
            sem((3,)),
            pltpu.VMEM(weights.shape, low),
            sem((4,)),
            pltpu.VMEM((depth, model), f32),
            pltpu.VMEM(picks.shape, f32),
            pltpu.VMEM((2, 2, half, cols), low),
            pltpu.VMEM((slots, half, cols), low),
            pltpu.VMEM((slots, 4, block // 2, cols), low),
            pltpu.VMEM((slots, 2, block // 2, cols), low),
            pltpu.VMEM((slots, 3, block // 4, cols), low),
            pltpu.VMEM((1, 3, *back.shape[1:]), low),
            pltpu.VMEM(rows.shape[::-1], low),
            pltpu.VMEM((2, *hidden.shape[:0:-1]), low),
            *sems(slots), *sems(slots, 4), *sems(slots, 2), *sems(slots, 3), *sems(3, 4),
        ],
        compiler_params=pltpu.CompilerParams(
            collective_id=4, has_side_effects=True, vmem_limit_bytes=60 * 2**20
        ),
        name="expert_sum",
    )(picks, gates, gain, back, *staged, weights)


def gather_sems(count):
    sem = lambda *shape: [pltpu.SemaphoreType.DMA(shape)] * 2
    return sem(count, 4) + sem(count, 8) + sem(count, 4, 4) + sem(count, 4, 8) + sem(count, 4, 5)


def gather_steps(shards, fulls, by_rows, main, sems):
    unit_ss, unit_rs, deep_ss, deep_rs, first_ss, first_rs, second_ss, second_rs, core_ss, core_rs = sems
    x, y, c, z = (lax.axis_index(a) for a in ALL)
    first_at = (1 - c) * x + c * y
    second_at = c * x + (1 - c) * y

    def along_first(o):
        return {"x": lax.rem(x + (1 - c) * o, 4), "y": lax.rem(y + c * o, 4)}

    def along_second(o):
        return {"x": lax.rem(x + c * o, 4), "y": lax.rem(y + (1 - c) * o, 4)}

    def sizes(n):
        if main and n == 0:
            total = fulls[0].shape[1]
            spread = total * 16 // 25
            return total // 2, spread // 2, spread // 32
        total = shards[n].shape[0]
        spread = total if total % 384 else total * 2 // 3
        if n in by_rows:
            return total // 2, spread // 2, spread // 32
        return total, spread, spread // 16

    def place(n, deep, offset):
        total, spread, unit = sizes(n)
        if n in by_rows:
            return (2 * spread + c * (total - spread) if deep else c * spread) + offset
        return (spread if deep else 0) + offset

    def window(n, shard, deep, offset, length):
        rows, width = shards[n].shape
        at = place(n, deep, offset)
        if main and n == 0:
            return fulls[0].at[shard, pl.ds(pl.multiple_of(at, 16), length)]
        rows = pl.ds(pl.multiple_of(at + shard * rows, 16), length)
        if n in by_rows:
            return fulls[n].at[rows]
        return fulls[n].at[rows, pl.ds(pl.multiple_of(c * (width // 2), 128), width // 2)]

    def own_window(n, deep, offset, length):
        width = shards[n].shape[1]
        rows = pl.ds(pl.multiple_of(place(n, deep, offset), 16), length)
        if n in by_rows:
            return shards[n].at[rows]
        return shards[n].at[rows, pl.ds(pl.multiple_of(c * (width // 2), 128), width // 2)]

    def came_from(o):
        return lax.rem(z - o + 4, 4)

    def unit_copy(n, o):
        unit = sizes(n)[2]
        at = (second_at * 4 + first_at) * unit
        return remote(
            own_window(n, False, at, unit), window(n, z, False, at, unit), unit_ss.at[n, o], unit_rs.at[n, o], {"z": ring("z", o)}
        )

    def deep_copy(n, o):
        total, spread, unit = sizes(n)
        return remote(
            own_window(n, True, 0, total - spread), window(n, z, True, 0, total - spread),
            deep_ss.at[n, o], deep_rs.at[n, o], {"z": ring("z", o)},
        )

    def deep_forward(n, o):
        total, spread, unit = sizes(n)
        edge = (total - spread) // 2
        block = window(n, came_from(o), True, 0 if o == 1 else edge, edge)
        return remote(block, block, deep_ss.at[n, 3 + o], deep_rs.at[n, 3 + o], {"z": ring("z", o)})

    def first_copy(n, o, step):
        unit = sizes(n)[2]
        block = window(n, came_from(o), False, (second_at * 4 + first_at) * unit, unit)
        return remote(block, block, first_ss.at[n, o, step], first_rs.at[n, o, step], along_first(step))

    def second_copy(n, o, step):
        unit = sizes(n)[2]
        block = window(n, came_from(o), False, second_at * 4 * unit, 4 * unit)
        return remote(block, block, second_ss.at[n, o, step], second_rs.at[n, o, step], along_second(step))

    def second_forward(n, o, step):
        unit = sizes(n)[2]
        source = lax.rem(second_at + 4 - step, 4)
        at = source * 4 * unit + (0 if step == 1 else 2 * unit)
        block = window(n, came_from(o), False, at, 2 * unit)
        return remote(block, block, second_ss.at[n, o, 4 + step], second_rs.at[n, o, 4 + step], along_second(step))

    def core_copy(n, o, which):
        total, spread, unit = sizes(n)
        shard = came_from(o)
        if which == 4:
            block = window(n, shard, True, 0, total - spread)
        else:
            block = window(n, shard, False, lax.rem(second_at + 4 - which, 4) * 4 * unit, 4 * unit)
        return remote(block, block, core_ss.at[n, o, which], core_rs.at[n, o, which], {"c": 1 - c})

    def core_copies(n, o):
        return [core_copy(n, o, which) for which in ((0, 1, 3, 2, 4) if n in deep else (0, 1, 3, 2))]

    arrays = range(len(shards))
    deep = [n for n in arrays if sizes(n)[0] > sizes(n)[1]]
    sides, offsets = (1, 3), (1, 3, 2)

    def begin():
        for n in arrays:
            for o in offsets:
                unit_copy(n, o).start()
        for n in deep:
            for o in sides:
                deep_copy(n, o).start()

    def go_first():
        for n in arrays:
            for o in offsets:
                unit_copy(n, o).wait_recv()
                for step in offsets:
                    first_copy(n, o, step).start()

    def go_second():
        for n in arrays:
            for o in offsets:
                for step in offsets:
                    first_copy(n, o, step).wait_recv()
                for step in sides:
                    second_copy(n, o, step).start()
                core_copy(n, o, 0).start()

    def go_deep():
        for n in deep:
            for o in sides:
                deep_copy(n, o).wait_recv()
                deep_forward(n, o).start()
                core_copy(n, o, 4).start()

    def go_forward():
        for n in arrays:
            for o in offsets:
                for step in sides:
                    second_copy(n, o, step).wait_recv()
                    second_forward(n, o, step).start()
                    core_copy(n, o, step).start()

    def go_core():
        for n in arrays:
            for o in offsets:
                for step in sides:
                    second_forward(n, o, step).wait_recv()
                core_copy(n, o, 2).start()
            if n in deep:
                for o in sides:
                    deep_forward(n, o).wait_recv()
                core_copy(n, 2, 4).start()

    def arrived(n, o):
        for copy in core_copies(n, o):
            copy.wait_recv()

    def finish():
        for n in arrays:
            for o in offsets:
                for copy in core_copies(n, o):
                    copy.wait_send()
                unit_copy(n, o).wait_send()
                for step in offsets:
                    first_copy(n, o, step).wait_send()
                for step in sides:
                    second_copy(n, o, step).wait_send()
                    second_forward(n, o, step).wait_send()
            if n in deep:
                for o in sides:
                    deep_copy(n, o).wait_send()
                    deep_forward(n, o).wait_send()

    return dict(
        begin=begin, first=go_first, second=go_second, deep=go_deep, forward=go_forward, core=go_core,
        arrived=arrived, finish=finish, came_from=came_from,
    )


def project_kernel(
    tokens_ref, gain_ref, tail_ref, shard_ref, main_out, norm_far, proj_far, tail_out, tails_ref,
    kept, main, turned, norm_ref, proj_ref, out_sem, save_sem, load_sem, tail_ss, tail_rs, *sems
):
    z = lax.axis_index("z")
    rows, width = main.shape[1:]
    load = pltpu.make_async_copy(shard_ref.at[pl.ds(0, rows)], main.at[z], load_sem.at[0])
    load.start()
    greet_neighbours()
    steps = gather_steps([shard_ref], [main], (0,), True, sems)
    steps["begin"]()
    tails = [
        remote(tail_ref, tails_ref.at[z], tail_ss.at[o], tail_rs.at[o], {"z": ring("z", o)}) for o in (1, 3, 2)
    ]
    for copy in tails:
        copy.start()
    tails_ref[z] = tail_ref[...]

    def save(shard):
        return pltpu.make_async_copy(main.at[shard], main_out.at[shard], save_sem.at[shard])

    values = tokens_ref[...].astype(jnp.float32)
    scale = lax.rsqrt(jnp.mean(values * values, 1, keepdims=True) + NORM_EPS)
    normed = values * scale * gain_ref[...]
    norm_ref[...] = short(normed)
    save_norm = pltpu.make_async_copy(norm_ref, norm_far, out_sem.at[0])
    save_norm.start()
    kept[...] = short(normed.T)
    steps["first"]()
    block = PROJ_BLOCK

    def add(shard, fresh):
        right = kept[pl.ds(pl.multiple_of(shard * width, TILE), width)]

        def rows_at(j, carry):
            here = pl.ds(pl.multiple_of(j * block, block), block)
            product = dot32(main[shard, here], right)
            turned[here] = product if fresh else turned[here] + product
            return carry

        lax.fori_loop(0, rows // block, rows_at, 0)

    load.wait()
    add(z, True)
    save(z).start()
    steps["second"]()
    steps["deep"]()
    for copy in tails:
        copy.wait()
    total = dot32(tails_ref[0], kept[:width])
    for i in range(1, 4):
        total = total + dot32(tails_ref[i], kept[i * width : (i + 1) * width])
    tail_out[...] = total.T
    steps["forward"]()
    steps["core"]()
    for o in (1, 3):
        steps["arrived"](0, o)
        shard = steps["came_from"](o)
        save(shard).start()
        add(shard, False)
    steps["arrived"](0, 2)
    shard = steps["came_from"](2)
    save(shard).start()
    right = kept[pl.ds(pl.multiple_of(shard * width, TILE), width)]

    def save_block(j):
        here = pl.ds(pl.multiple_of(j * block, block), block)
        return pltpu.make_async_copy(proj_ref.at[:, here], proj_far.at[:, here], out_sem.at[1 + j])

    def last(j, carry):
        here = pl.ds(pl.multiple_of(j * block, block), block)
        proj_ref[:, here] = (turned[here] + dot32(main[shard, here], right)).T
        save_block(j).start()
        return carry

    lax.fori_loop(0, rows // block, last, 0)
    save_norm.wait()
    for j in range(rows // block):
        save_block(j).wait()
    steps["finish"]()
    for i in range(4):
        save(i).wait()


def project(tokens, gain, tail, shard, main_rows):
    slots, model = tokens.shape
    width = shard.shape[1]
    space, away = pl.BlockSpec(memory_space=pltpu.VMEM), pl.BlockSpec(memory_space=pl.ANY)
    sem = pltpu.SemaphoreType.DMA
    return pl.pallas_call(
        project_kernel,
        out_shape=(
            jax.ShapeDtypeStruct((4, main_rows, width), jnp.bfloat16),
            jax.ShapeDtypeStruct((slots, model), jnp.bfloat16),
            jax.ShapeDtypeStruct((slots, main_rows), jnp.float32),
            jax.ShapeDtypeStruct((slots, tail.shape[0]), jnp.float32),
            jax.ShapeDtypeStruct((4, *tail.shape), jnp.bfloat16),
        ),
        in_specs=[space, space, space, away],
        out_specs=(away, away, away, space, space),
        scratch_shapes=[
            pltpu.VMEM((model, slots), jnp.bfloat16),
            pltpu.VMEM((4, main_rows, width), jnp.bfloat16),
            pltpu.VMEM((main_rows, slots), jnp.float32),
            pltpu.VMEM((slots, model), jnp.bfloat16),
            pltpu.VMEM((slots, main_rows), jnp.float32),
            sem((1 + main_rows // PROJ_BLOCK,)),
            sem((4,)), sem((1,)), sem((4,)), sem((4,)),
        ]
        + gather_sems(1),
        compiler_params=pltpu.CompilerParams(
            collective_id=6, has_side_effects=True, vmem_limit_bytes=60 * 2**20
        ),
        name="project",
    )(tokens, gain, tail, shard)


TILE = 128
HIGH = lax.Precision.HIGHEST


def tile_at(j):
    return pl.ds(pl.multiple_of(j * TILE, TILE), TILE)


def dot_nt(left, right):
    return lax.dot_general(left, right, (((1,), (1,)), ((), ())), preferred_element_type=jnp.float32)


def short(values):
    return values.astype(jnp.bfloat16)


def lane_ids():
    return lax.broadcasted_iota(jnp.int32, (TILE, TILE), 1)


def row_ids():
    return lax.broadcasted_iota(jnp.int32, (TILE, TILE), 0)


def head_steps(tail_ref, heads_ref):
    raw = tail_ref[...] + heads_ref[1:2]
    used = lane_ids() < HEADS
    small = jnp.exp(-jnp.abs(raw))
    tail = jnp.where(small < 1e-3, small * (1.0 - small * (0.5 - small / 3.0)), jnp.log(1.0 + small))
    soft = jnp.maximum(raw, 0.0) + tail
    step = jnp.where(used, soft, 0.0)
    return raw, step, jnp.where(used, -jnp.exp(heads_ref[0:1]) * step, 0.0)


def head_columns(values, pair):
    moved = pltpu.roll(values, lax.rem(TILE - 2 * pair, TILE), 1)
    return moved[:, 0:1], moved[:, 1:2]


def both_heads(columns):
    return jnp.where(lane_ids() < TILE // 2, columns[0], columns[1])


def taps_of(ext, cw_ref, lanes):
    summed = cw_ref[4:5, lanes]
    for k in range(4):
        summed = summed + cw_ref[k : k + 1, lanes] * ext[5 + k : 5 + k + TILE]
    return summed


def fill_ext(ext, halo_ref, proj_ref, j):
    ext[0:8] = halo_ref[:, tile_at(j)]
    ext[8 : 8 + TILE] = proj_ref[:, pl.ds(pl.multiple_of(INNER + j * TILE, TILE), TILE)]


def mixer_in_part(tick, halo_copy, proj_ref, tail_ref, halo_ref, cw_ref, heads_ref, mixed_ref, state_ref, totals_ref, run_ref, step_ref, ext):
    unused_raw, step, log_decay = head_steps(tail_ref, heads_ref)
    lower = (row_ids() >= lane_ids()).astype(jnp.float32)
    run = jnp.dot(lower, log_decay, precision=HIGH, preferred_element_type=jnp.float32)
    run_ref[...] = run
    step_ref[...] = step
    last = run[TILE - 1 : TILE]
    totals_ref[...] = jnp.broadcast_to(last, totals_ref.shape)
    weight = jnp.exp(last - run) * step

    halo_copy.wait()
    spot = lax.axis_index("x") * 8 + lax.axis_index("y") * 2 + lax.axis_index("c")

    @pl.when(spot == 0)
    def _():
        halo_ref[...] = jnp.zeros_like(halo_ref)

    def conv(j, carry):
        fill_ext(ext, halo_ref, proj_ref, j)
        u = taps_of(ext, cw_ref, tile_at(j))
        mixed_ref[:, tile_at(j)] = u * jax.nn.sigmoid(u)
        return carry

    lax.fori_loop(0, CONV // TILE, conv, 0)
    tick()
    in_map = short(mixed_ref[:, INNER : INNER + TILE])

    def state(p, carry):
        scaled = mixed_ref[:, tile_at(p)] * both_heads(head_columns(weight, p))
        state_ref[pl.ds(4 * p, 4)] = short(dot32(short(scaled.T), in_map)).reshape(4, 32, TILE)
        return carry

    lax.fori_loop(0, HEADS // 2, state, 0, unroll=2)


def decays_of(column, row, lower):
    return jnp.where(lower, jnp.exp(jnp.minimum(column - row, 0.0)), 0.0)


def mixer_out_part(proj_ref, mixed_ref, run_ref, step_ref, carried_ref, wide_ref, normed_ref, scanned_ref, gated, rows):
    run = run_ref[...]
    rows[0] = run.T
    rows[1] = step_ref[...].T
    lower = row_ids() >= lane_ids()
    in_map = mixed_ref[:, INNER : INNER + TILE]
    out_map = mixed_ref[:, INNER + TILE : INNER + 2 * TILE]
    kernel = lax.dot_general(out_map, in_map, (((1,), (1,)), ((), ())), precision=HIGH, preferred_element_type=jnp.float32)
    out_low = short(out_map)

    def pair(p, squares):
        values = mixed_ref[:, tile_at(p)]
        values_low = short(values)
        columns = head_columns(run, p)
        parts = []
        for h in range(2):
            decays = decays_of(columns[h], rows[0, pl.ds(2 * p + h, 1)], lower)
            weights = kernel * decays * rows[1, pl.ds(2 * p + h, 1)]
            parts.append(dot32(short(weights), values_low))
        result = jnp.where(lane_ids() < TILE // 2, parts[0], parts[1])
        result = result + jnp.exp(both_heads(columns)) * dot_nt(out_low, carried_ref[pl.ds(4 * p, 4)].reshape(TILE, TILE))
        result = result + wide_ref[0:1, tile_at(p)] * values
        scanned_ref[:, tile_at(p)] = result
        gate = proj_ref[:, tile_at(p)]
        g = result * (gate * jax.nn.sigmoid(gate))
        gated[:, tile_at(p)] = g
        return squares + g * g

    squares = lax.fori_loop(0, HEADS // 2, pair, jnp.zeros((TILE, TILE), jnp.float32), unroll=2)
    scale = lax.rsqrt(jnp.sum(squares, 1, keepdims=True) / INNER + NORM_EPS)

    def norm(p, carry):
        normed_ref[:, tile_at(p)] = short(gated[:, tile_at(p)] * scale * wide_ref[1:2, tile_at(p)])
        return carry

    lax.fori_loop(0, HEADS // 2, norm, 0, unroll=2)


def mixer_kernel(
    tail_ref, cw_ref, heads_ref, wide_ref, rows_ref, proj_far, *refs
):
    shards, refs = refs[:3], refs[3:]
    (mixed_far, totals_ref, run_ref, step_ref, halo_ref, carried_far, normed_ref, scanned_far, all_rows), refs = refs[:9], refs[9:]
    fulls, refs = refs[:3], refs[3:]
    edge, state_ref, ext, gated, rows, mixed_ref, scanned_ref, carried_ref, proj_ref, proj_sem, halo_ss, halo_rs, load_sem, save_sem, out_sem, *refs = refs
    staged, refs = refs[:3], refs[3:]
    scan_refs, sems = refs[: len(scan_scratch())], refs[len(scan_scratch()) :]
    z = lax.axis_index("z")
    loads = [pltpu.make_async_copy(shards[n], staged[n], load_sem.at[n]) for n in range(3)]
    views = [
        ref.at[at : at + 64, columns]
        for columns in (slice(INNER, INNER + CONV), slice(0, INNER))
        for at in (0, 64)
        for ref in (proj_far, proj_ref)
    ]
    proj_loads = [pltpu.make_async_copy(views[2 * i], views[2 * i + 1], proj_sem.at[i]) for i in range(4)]
    for copy in proj_loads + loads:
        copy.start()
    greet_plane()
    proj_loads[0].wait()
    proj_loads[1].wait()
    edge[...] = proj_ref[TILE - 8 :, INNER : INNER + CONV]
    halo_copy = remote(edge, halo_ref, halo_ss.at[0], halo_rs.at[0], line_neighbour(True))
    halo_copy.start()
    steps = gather_steps(shards, fulls, (0,), False, sems)
    steps["begin"]()
    mixer_in_part(steps["first"], halo_copy, proj_ref, tail_ref, halo_ref, cw_ref, heads_ref, mixed_ref, state_ref, totals_ref, run_ref, step_ref, ext)
    save_mixed = pltpu.make_async_copy(mixed_ref, mixed_far, out_sem.at[0])
    save_mixed.start()
    steps["second"]()
    saves = []
    for n in range(3):
        loads[n].wait()
        total = shards[n].shape[0]
        saves.append(
            pltpu.make_async_copy(
                staged[n], fulls[n].at[pl.ds(pl.multiple_of(z * total, 16), total)], save_sem.at[n]
            )
        )
        saves[-1].start()

    def tick(n):
        if n == 0:
            steps["deep"]()
        if n == 2:
            steps["forward"]()
        if n == 3:
            steps["core"]()

    state_exchange(False, state_ref, totals_ref, rows_ref, carried_ref, all_rows, None, tick, *scan_refs)
    save_carried = pltpu.make_async_copy(carried_ref, carried_far, out_sem.at[2])
    save_carried.start()
    proj_loads[2].wait()
    proj_loads[3].wait()
    mixer_out_part(proj_ref, mixed_ref, run_ref, step_ref, carried_ref, wide_ref, normed_ref, scanned_ref, gated, rows)
    save_scanned = pltpu.make_async_copy(scanned_ref, scanned_far, out_sem.at[1])
    save_scanned.start()
    for n in range(3):
        saves[n].wait()
        for o in (1, 3, 2):
            steps["arrived"](n, o)
    steps["finish"]()
    save_mixed.wait()
    save_scanned.wait()
    save_carried.wait()


def mixer(projected, tail_values, taps, heads, wide, rows, shards):
    space, away = pl.BlockSpec(memory_space=pltpu.VMEM), pl.BlockSpec(memory_space=pl.ANY)
    f32, low, sem = jnp.float32, jnp.bfloat16, pltpu.SemaphoreType.DMA
    square = (TILE, TILE)
    outs = [
        ((TILE, CONV), f32), ((8, TILE), f32), (square, f32), (square, f32), ((8, CONV), f32),
        ((96, 32, TILE), low), ((TILE, INNER), low), ((TILE, INNER), f32), ((4, *rows.shape), low),
    ]
    fulls = [((4 * s.shape[0], s.shape[1]), low) for s in shards]
    return pl.pallas_call(
        mixer_kernel,
        out_shape=tuple(jax.ShapeDtypeStruct(s, d) for s, d in outs + fulls),
        in_specs=[space] * 5 + [away] * 4,
        out_specs=tuple(away if i in (0, 5, 7, 8) else space for i in range(len(outs))) + (away,) * 3,
        scratch_shapes=[
            pltpu.VMEM((8, CONV), f32),
            pltpu.VMEM((96, 32, TILE), low),
            pltpu.VMEM((TILE + 8, TILE), f32),
            pltpu.VMEM((TILE, INNER), f32),
            pltpu.VMEM((2, *square), f32),
            pltpu.VMEM((TILE, CONV), f32),
            pltpu.VMEM((TILE, INNER), f32),
            pltpu.VMEM((96, 32, TILE), low),
            pltpu.VMEM(projected.shape, f32),
            sem((4,)),
            sem((1,)), sem((1,)), sem((3,)), sem((3,)), sem((3,)),
            *[pltpu.VMEM(s.shape, s.dtype) for s in shards],
        ]
        + scan_scratch()
        + gather_sems(3),
        compiler_params=pltpu.CompilerParams(
            collective_id=1, has_side_effects=True, vmem_limit_bytes=60 * 2**20
        ),
        name="mixer",
    )(tail_values, taps, heads, wide, rows, projected, *shards)


def gate_back_part(tick, proj_ref, mixed_ref, scanned_ref, back_ref, run_ref, wide_ref, result_ref, gate_ref, gain_ref, state_ref, gated):
    run = run_ref[...]
    out_map = short(mixed_ref[:, INNER + TILE : INNER + 2 * TILE])

    def first(p, sums):
        gate = proj_ref[:, tile_at(p)]
        g = scanned_ref[:, tile_at(p)] * (gate * jax.nn.sigmoid(gate))
        gated[:, tile_at(p)] = g
        back = back_ref[:, tile_at(p)] * wide_ref[1:2, tile_at(p)]
        return sums[0] + g * g, sums[1] + g * back

    zero = jnp.zeros((TILE, TILE), jnp.float32)
    squares, products = lax.fori_loop(0, HEADS // 2, first, (zero, zero), unroll=2)
    scale = lax.rsqrt(jnp.sum(squares, 1, keepdims=True) / INNER + NORM_EPS)
    shift = jnp.sum(products, 1, keepdims=True) * scale * scale * scale / INNER

    tick()

    def second(p, carry):
        lanes = tile_at(p)
        gate = proj_ref[:, lanes]
        sig = jax.nn.sigmoid(gate)
        g = gated[:, lanes]
        back = back_ref[:, lanes]
        gain_ref[:, lanes] = jnp.broadcast_to(jnp.sum(back * g * scale, 0, keepdims=True), (8, TILE))
        g_back = back * wide_ref[1:2, lanes] * scale - g * shift
        result_back = g_back * (gate * sig)
        result_ref[:, lanes] = result_back
        gate_ref[:, lanes] = short(g_back * scanned_ref[:, lanes] * sig * (1.0 + gate * (1.0 - sig)))
        moved = result_back * jnp.exp(both_heads(head_columns(run, p)))
        state_ref[pl.ds(4 * p, 4)] = short(dot32(short(moved.T), out_map)).reshape(4, 32, TILE)
        return carry

    lax.fori_loop(0, HEADS // 2, second, 0, unroll=2)


def mixer_back_kernel(
    tail_ref, halo_ref, cw_ref, heads_ref, run_ref, step_ref, wide_ref, totals_ref, valid_ref, *refs
):
    away, refs = refs[:11], refs[11:]
    (rim_in_ref, taps_ref, step_back_ref, heads_back_ref, shared_in_ref, out_ref, shared_out_ref,
    gate_far, gain_ref, block_ref, conv_far,
    gate_ref, parts_sum, save_sem, result_ref, gated, rim_ref, rows, column_sums, row_sums, kernel_back, maps_back, mixed_back, ext, padded, rights,
    state_ref, leaving_ref, parts_in, rim_ss, rim_rs, load_sem, conv_ref), refs = refs[:33], refs[33:]
    here, refs = refs[:11], refs[11:]
    scan_refs, sum_scratch = refs[: len(scan_scratch())], refs[len(scan_scratch()) :]
    loads = [pltpu.make_async_copy(far, near, load_sem.at[i]) for i, (far, near) in enumerate(zip(away, here))]
    for copy in loads:
        copy.start()
    lefts_ref, acts_ref, mix_ref, up_ref, proj_ref, scanned_ref, back_ref, mixed_ref, parts_ref, carried_ref, base_ref = here
    greet_plane()
    for copy in loads[:4]:
        copy.wait()
    model = mix_ref.shape[1]
    plain = [acts_ref.shape[1] // RS_COLS, model // RS_COLS, model // RS_COLS]
    up_at = [0, RS_COUNTS[0] - plain[0], RS_COUNTS[0] + RS_COUNTS[1] - plain[0] - plain[1]]
    for part, ref in enumerate((acts_ref, mix_ref, mix_ref)):
        at, end = RS_FIRST[part] * RS_COLS, (RS_FIRST[part] + RS_COUNTS[part]) * RS_COLS
        rights[:, at : at + ref.shape[1]] = ref[...]
        at = at + ref.shape[1]
        rights[:, at:end] = up_ref[:, up_at[part] * RS_COLS : up_at[part] * RS_COLS + end - at]
    share = lefts_ref.shape[1] // 2

    def left_of(part, k, which):
        n = 2 * part + k // plain[part]
        return lefts_ref[n, pl.ds(pl.multiple_of(which * share, share), share), :]

    def right_of(part, k, col):
        return rights[:, pl.ds(pl.multiple_of((RS_FIRST[part] + k) * RS_COLS + col, 256), 256)]

    def store(part, k, total):
        @pl.when(k < plain[part])
        def _():
            lanes = pl.ds(pl.multiple_of(k * RS_COLS, RS_COLS), RS_COLS)
            if part == 0:
                shared_in_ref[:, lanes] = total[:12]
            else:
                out_ref[12 * part - 12 : 12 * part, lanes] = total[:12]

        @pl.when(k >= plain[part])
        def _():
            lanes = pl.ds(pl.multiple_of((k - plain[part] + up_at[part]) * RS_COLS, RS_COLS), RS_COLS)
            shared_out_ref[:, lanes] = total[:8]

    sum_step, sum_finish = grad_sum_steps(sum_scratch, left_of, right_of, store)

    sum_step(0)
    for copy in loads[4:8]:
        copy.wait()
    gate_back_part(
        lambda: sum_step(1), proj_ref, mixed_ref, scanned_ref, back_ref, run_ref, wide_ref, result_ref, gate_ref, gain_ref,
        state_ref, gated,
    )
    save_gate = pltpu.make_async_copy(gate_ref, gate_far, save_sem.at[0])
    save_gate.start()
    sum_step(2)
    loads[8].wait()
    state_exchange(
        True, state_ref, totals_ref, parts_ref, leaving_ref, parts_in, parts_sum, lambda n: sum_step(3 + n), *scan_refs
    )
    run, step = run_ref[...], step_ref[...]
    rows[0] = run.T
    rows[1] = step.T
    lanes_id, rows_id = lane_ids(), row_ids()
    lower = rows_id >= lanes_id
    left_half = lanes_id < TILE // 2
    half_line = lax.broadcasted_iota(jnp.int32, (1, TILE), 1) // (TILE // 2)
    in_map = mixed_ref[:, INNER : INNER + TILE]
    out_map = mixed_ref[:, INNER + TILE : INNER + 2 * TILE]
    kernel = lax.dot_general(out_map, in_map, (((1,), (1,)), ((), ())), precision=HIGH, preferred_element_type=jnp.float32)
    in_low, out_low = short(in_map), short(out_map)
    last = run[TILE - 1 : TILE]
    fade = jnp.exp(last - run)
    weight = fade * step
    column_sums[...] = jnp.zeros_like(column_sums)
    row_sums[...] = jnp.zeros_like(row_sums)
    kernel_back[...] = jnp.zeros_like(kernel_back)
    maps_back[...] = jnp.zeros_like(maps_back)

    loads[9].wait()
    loads[10].wait()
    block_ref[...] = short(jnp.where(valid_ref[...] > 0.0, base_ref[...] + parts_sum[...], 0.0))

    def pair(p, carry):
        @pl.when(lax.rem(p, 4) == 0)
        def _():
            sum_step(7 + p // 4)

        lanes = tile_at(p)
        values, back = mixed_ref[:, lanes], result_ref[:, lanes]
        values_low, back_low = short(values), short(back)
        columns = head_columns(run, p)
        which = 2 * p + (rows_id >= TILE // 2).astype(jnp.int32)
        spread = (lanes_id == which).astype(jnp.bfloat16)
        parts = []
        for h in range(2):
            at = pl.ds(2 * p + h, 1)
            decays = decays_of(columns[h], rows[0, at], lower)
            plain = kernel * decays
            steps = rows[1, at]
            weights = plain * steps
            mine = jnp.where(left_half, back, 0.0) if h == 0 else jnp.where(left_half, 0.0, back)
            weights_back = dot_nt(short(mine), values_low)
            kernel_back[...] += weights_back * (decays * steps)
            loose = weights_back * plain
            pulled = short(loose * steps)
            column_sums[0] += dot32(pulled, (lanes_id == 2 * p + h).astype(jnp.bfloat16))
            row_sums[0, at] = jnp.sum(pulled.astype(jnp.float32), 0, keepdims=True)
            row_sums[1, at] = jnp.sum(loose, 0, keepdims=True)
            parts.append(dot32(short(weights.T), back_low))
        values_back = jnp.where(left_half, parts[0], parts[1]) + wide_ref[0:1, lanes] * back
        carried = carried_ref[pl.ds(4 * p, 4)].reshape(TILE, TILE)
        leaving = leaving_ref[pl.ds(4 * p, 4)].reshape(TILE, TILE)
        moved = back * jnp.exp(both_heads(columns))
        moved_low = short(moved)
        seen = dot_nt(out_low, carried)
        column_sums[0] += dot32(short(moved * seen), spread)
        maps_back[1] += dot32(moved_low, carried)
        weight_pair = both_heads(head_columns(weight, p))
        pulled_state = dot_nt(in_low, leaving)
        values_back = values_back + weight_pair * pulled_state
        maps_back[0] += dot32(short(values * weight_pair), leaving)
        column_sums[1] += dot32(short(values * pulled_state), spread)
        mixed_back[:, lanes] = values_back
        skip_part = jnp.sum(back * values, 0, keepdims=True)
        kept = jnp.sum(carried.astype(jnp.float32) * leaving.astype(jnp.float32), 1, keepdims=True)
        for h in range(2):
            half = slice(h * TILE // 2, (h + 1) * TILE // 2)
            row_sums[2, pl.ds(2 * p + h, 1)] = jnp.broadcast_to(
                jnp.sum(jnp.where(half_line == h, skip_part, 0.0), 1, keepdims=True), (1, TILE)
            )
            row_sums[3, pl.ds(2 * p + h, 1)] = jnp.broadcast_to(
                jnp.sum(kept[half], 0, keepdims=True), (1, TILE)
            )
        return carry

    lax.fori_loop(0, HEADS // 2, pair, 0)

    used = lanes_id < HEADS
    loose_columns = row_sums[1].T
    weight_back = column_sums[1]
    run_back = column_sums[0] - row_sums[0].T - weight * weight_back
    skip_back, decay_back = row_sums[2].T, row_sums[3].T
    last_back = jnp.sum(weight * weight_back, 0, keepdims=True) + jnp.exp(last) * decay_back[0:1]
    run_back = run_back + jnp.where(rows_id == TILE - 1, last_back, 0.0)
    upper = (lanes_id >= rows_id).astype(jnp.float32)
    log_back = jnp.dot(upper, run_back, precision=HIGH, preferred_element_type=jnp.float32)
    raw, unused_step, log_decay = head_steps(tail_ref, heads_ref)
    rate = jnp.exp(heads_ref[0:1])
    step_back = loose_columns + fade * weight_back - rate * log_back
    raw_back = jnp.where(used, step_back * jax.nn.sigmoid(raw), 0.0)
    step_back_ref[...] = raw_back
    rate_back = jnp.sum(jnp.where(used, log_back * log_decay, 0.0), 0, keepdims=True)
    bias_back = jnp.sum(raw_back, 0, keepdims=True)
    at_row = lax.broadcasted_iota(jnp.int32, (8, TILE), 0)
    heads_back_ref[...] = jnp.where(
        at_row == 0, rate_back, jnp.where(at_row == 1, bias_back, jnp.where(at_row == 2, skip_back[0:1], 0.0))
    )
    both = kernel_back[...]
    mixed_back[:, INNER : INNER + TILE] = maps_back[0] + dot32(short(both.T), out_low)
    mixed_back[:, INNER + TILE : INNER + 2 * TILE] = maps_back[1] + dot32(short(both), in_low)
    padded[0:8] = jnp.zeros((8, TILE), jnp.float32)
    sum_step(13)
    padded[8 + TILE : 16 + TILE] = jnp.zeros((8, TILE), jnp.float32)

    def conv(j, carry):
        lanes = tile_at(j)
        fill_ext(ext, halo_ref, proj_ref, j)
        u = taps_of(ext, cw_ref, lanes)
        sig = jax.nn.sigmoid(u)
        back = mixed_back[:, lanes] * sig * (1.0 + u * (1.0 - sig))
        padded[8 : 8 + TILE] = back
        taps_ref[4:5, lanes] = jnp.sum(back, 0, keepdims=True)
        total = jnp.zeros((TILE, TILE), jnp.float32)
        rim = jnp.zeros((8, TILE), jnp.float32)
        for k in range(4):
            tap = cw_ref[k : k + 1, lanes]
            taps_ref[k : k + 1, lanes] = jnp.sum(back * ext[5 + k : 5 + k + TILE], 0, keepdims=True)
            total = total + tap * padded[11 - k : 11 - k + TILE]
            rim = rim + tap * padded[3 - k : 11 - k]
        conv_ref[:, lanes] = total
        rim_ref[:, lanes] = rim
        return carry

    lax.fori_loop(0, CONV // TILE, conv, 0)
    rim_copy = remote(rim_ref, rim_in_ref, rim_ss.at[0], rim_rs.at[0], line_neighbour(False))
    rim_copy.start()
    save_conv = pltpu.make_async_copy(conv_ref, conv_far, save_sem.at[1])
    save_conv.start()
    sum_finish()
    rim_copy.wait()
    save_gate.wait()
    save_conv.wait()
    spot = lax.axis_index("x") * 8 + lax.axis_index("y") * 2 + lax.axis_index("c")

    @pl.when(spot == 31)
    def _():
        rim_in_ref[...] = jnp.zeros_like(rim_in_ref)


def tile_call(kernel, outs, scratch, name, *args, collective=None, away=0, away_outs=()):
    space = pl.BlockSpec(memory_space=pltpu.VMEM)
    far = pl.BlockSpec(memory_space=pl.ANY)
    params = dict(vmem_limit_bytes=40 * 2**20)
    if collective is not None:
        params = dict(vmem_limit_bytes=60 * 2**20, collective_id=collective, has_side_effects=True)
    return pl.pallas_call(
        kernel,
        out_shape=tuple(jax.ShapeDtypeStruct(s, d) for s, d in outs),
        in_specs=[space] * (len(args) - away) + [far] * away,
        out_specs=tuple(far if i in away_outs else space for i in range(len(outs))),
        scratch_shapes=[pltpu.VMEM(s, jnp.float32) if isinstance(s, tuple) else s for s in scratch],
        compiler_params=pltpu.CompilerParams(**params),
        name=name,
    )(*args)


PROJ_BLOCK = 640


def local(
    tokens,
    cotangent,
    lengths,
    routes,
    norm_gain,
    w_in,
    conv_weight,
    conv_bias,
    a_log,
    dt_bias,
    skip_scale,
    gated_gain,
    w_out,
    post_gain,
    w_router,
    shared_in,
    shared_out,
    expert_in,
    expert_out,
):
    low = jnp.bfloat16
    tokens, cotangent, routes = tokens[0], cotangent[0], routes[0]
    slot_count, model_width = tokens.shape
    inner_width = gated_gain.shape[0]
    conv_width = conv_bias.shape[0]
    head_count = a_log.shape[0]
    tap_count = conv_weight.shape[0]
    expert_count = w_router.shape[1]
    residual = tokens.astype(jnp.float32)
    positions = lax.axis_index(SEQ) * slot_count + jnp.arange(slot_count)
    valid = positions < lengths[0]
    upstream_low = jnp.where(valid[:, None], cotangent, jnp.zeros_like(cotangent))
    upstream = upstream_low.astype(jnp.float32)
    main_rows = inner_width + conv_width
    turned = w_in.T
    tail_shard = jnp.concatenate(
        [
            turned[main_rows:],
            w_router.T,
            jnp.zeros((TILE - head_count - expert_count, turned.shape[1]), low),
        ],
        0,
    )
    full_in, first_norm, projected, tail_values, tails = project(
        tokens, norm_gain[None], tail_shard, turned, main_rows
    )
    full_router = jnp.swapaxes(tails[:, head_count : head_count + expert_count], 0, 1)
    full_router = full_router.reshape(expert_count, model_width)

    taps = jnp.concatenate([conv_weight, conv_bias[None], jnp.zeros((3, conv_width), jnp.float32)], 0)
    heads = jnp.pad(jnp.stack([a_log, dt_bias]), ((0, 6), (0, TILE - head_count)))
    wide = jnp.stack([jnp.repeat(skip_scale, inner_width // head_count), gated_gain])
    square = (TILE, TILE)
    mixed, totals, running, steps, halo, carried, normed_low, scanned, all_upstream, full_out, full_shared_in, full_shared_out = mixer(
        projected, tail_values, taps, heads, wide, upstream_low, [w_out, shared_in, shared_out]
    )
    chosen = jnp.any(routes[:, :, None] == jnp.arange(expert_count)[None, None, :], 1)
    middle, second_norm, base_out, shared_second, shared_hidden, shared_act_grad, all_rows, all_gates = middle_part(
        normed_low, tokens, post_gain[None], full_router, chosen.T.astype(jnp.float32), upstream_low,
        full_out, full_shared_in, full_shared_out,
    )
    rows = all_rows.reshape(-1, model_width)
    back_rows = all_upstream.reshape(-1, model_width)
    owned = expert_in.shape[0]
    first_owned = lax.axis_index("z") * owned
    gates = lax.dynamic_slice_in_dim(all_gates, first_owned, owned, 1)
    gates = jnp.swapaxes(gates, 0, 1).reshape(owned, -1)
    hidden_width = expert_out.shape[1]
    acts = jnp.einsum("td,edf->etf", rows, expert_in, preferred_element_type=jnp.float32)
    hidden = (jax.nn.silu(acts[..., :hidden_width]) * acts[..., hidden_width:]).astype(low)
    output = jnp.einsum("etf,efd->etd", hidden, expert_out, preferred_element_type=jnp.float32)
    output = output.astype(low).astype(jnp.float32)
    part = jnp.sum(gates[..., None] * output, 0).astype(low)
    back_wide = back_rows.astype(jnp.float32)
    picks = jnp.sum(output * back_wide[None], -1)
    out_grad = (gates[..., None] * back_wide[None]).astype(low)
    hidden_back = jnp.einsum("etd,efd->etf", out_grad, expert_out, preferred_element_type=jnp.float32)
    act_grad = glu_back(acts, hidden_back)
    back = jnp.einsum("etf,edf->td", act_grad, expert_in, preferred_element_type=jnp.float32).astype(low)
    picks = jnp.swapaxes(picks.reshape(owned, 4, slot_count), 0, 1)
    picks = jnp.pad(picks, ((0, 0), (0, 8 - owned), (0, 0)))
    expert_parts, middle_back, mix_low, grad_post_gain, router_back, normed_back = expert_sum(
        rows,
        act_grad,
        hidden,
        out_grad,
        back.reshape(4, slot_count, model_width),
        picks,
        middle,
        shared_second,
        upstream_low,
        second_norm,
        all_gates,
        jnp.pad(full_router, ((0, TILE - expert_count), (0, 0))),
        post_gain[None],
        full_out,
    )
    act_width = act_grad.shape[2]
    grad_expert_in = expert_parts[:, :, :act_width]
    grad_expert_out = expert_parts[:, :, act_width:].reshape(owned, 3, -1, model_width // 3)
    grad_expert_out = jnp.swapaxes(grad_expert_out, 1, 2).reshape(owned, -1, model_width)

    shared_width = full_shared_out.shape[0]
    early_lefts, late_lefts = tile_call(
        lefts_kernel,
        [((6, model_width, TILE), low), ((3, model_width, TILE), low)],
        [(inner_width, TILE), (model_width, TILE)],
        "lefts",
        first_norm, second_norm, normed_low, shared_hidden,
    )
    large = [
        early_lefts, shared_act_grad, mix_low, upstream_low, projected, scanned, normed_back, mixed,
        part.reshape(4, slot_count, model_width), carried, base_out,
    ]
    (
        rim_back, taps_back, steps_back, heads_back, shared_in_part, w_out_part, shared_out_part,
        gate_back, gain_back, block_out, conv_part,
    ) = tile_call(
        mixer_back_kernel,
        [
            ((8, conv_width), jnp.float32), ((8, conv_width), jnp.float32),
            (square, jnp.float32), ((8, TILE), jnp.float32), ((12, 2 * shared_width), jnp.float32),
            ((24, model_width), jnp.float32), ((8, model_width), jnp.float32),
            ((TILE, inner_width), low), ((8, inner_width), jnp.float32), ((TILE, model_width), low),
            ((TILE, conv_width), jnp.float32),
        ],
        [
            pltpu.VMEM((TILE, inner_width), low), (TILE, model_width), pltpu.SemaphoreType.DMA((2,)),
            (TILE, inner_width), (TILE, inner_width), (8, conv_width),
            (2, *square), (2, *square), (4, *square), square, (2, *square),
            (TILE, conv_width), (TILE + 8, TILE), (TILE + 16, TILE),
            pltpu.VMEM((TILE, RS_SLOTS * RS_COLS), low),
            pltpu.VMEM((96, 32, TILE), low),
            pltpu.VMEM((96, 32, TILE), low),
            pltpu.VMEM((3, TILE, model_width), low),
            pltpu.SemaphoreType.DMA((1,)),
            pltpu.SemaphoreType.DMA((1,)),
            pltpu.SemaphoreType.DMA((11,)),
            (TILE, conv_width),
        ]
        + [pltpu.VMEM(a.shape, a.dtype) for a in large]
        + scan_scratch()
        + grad_sum_scratch(model_width),
        "mixer_back",
        tail_values, halo, taps, heads, running, steps, wide, totals,
        valid[:, None].astype(jnp.float32), *large,
        collective=7,
        away=len(large),
        away_outs=(7, 10),
    )
    w_in_part, small, grad_tokens = grad_sum(
        late_lefts, gate_back, conv_part, steps_back, rim_back, tokens, norm_gain[None], middle_back, tails,
        taps_back, gain_back, grad_post_gain, heads_back, router_back, full_in, w_in.shape[1]
    )
    owner = lax.axis_index(ALL)

    def owned_part(values):
        size = values.shape[-1] // 128
        return lax.dynamic_slice_in_dim(values, owner * size, size, values.ndim - 1)

    return (
        block_out[None],
        grad_tokens[None],
        owned_part(small[6, :model_width]),
        w_in_part,
        owned_part(small[:4, :conv_width]),
        owned_part(small[4, :conv_width]),
        small[7, :head_count],
        small[7, TILE : TILE + head_count],
        small[7, 2 * TILE : 2 * TILE + head_count],
        owned_part(small[5, :inner_width]),
        w_out_part,
        owned_part(small[6, model_width : 2 * model_width]),
        owned_part(small[:, conv_width:]).T,
        shared_in_part,
        shared_out_part,
        grad_expert_in,
        grad_expert_out,
    )


def solution(mesh):
    split = Mesh(mesh.devices.reshape(4, 4, 2, 4), ALL)
    placed = (
        P("z", SEQ, None),
        P("z", SEQ, None),
        P("z"),
        P("z", SEQ, None),
        P(),
        P("z", None),
        P(),
        P(),
        P(),
        P(),
        P(),
        P(),
        P("z", None),
        P(),
        P("z", None),
        P("z", None),
        P("z", None),
        P("z", None, None),
        P("z", None, None),
    )
    return jax.shard_map(
        local,
        mesh=split,
        in_specs=placed,
        out_specs=(
            P("z", SEQ, None),
            P("z", SEQ, None),
            P(ALL),
            P(ALL, None),
            P(None, ALL),
            P(ALL),
            P(),
            P(),
            P(),
            P(ALL),
            P(ALL, None),
            P(ALL),
            P(ALL, None),
            P(ALL, None),
            P(ALL, None),
            P("z", SEQ, None),
            P("z", SEQ, None),
        ),
        check_vma=False,
    )
```

```python
import functools

import jax
import jax.numpy as jnp
from jax import lax
from jax.experimental import pallas as pl
from jax.experimental.pallas import tpu as pltpu
from jax.sharding import Mesh
from jax.sharding import PartitionSpec as P

SEQ = ("x", "y", "c")
ALL = ("x", "y", "c", "z")
NORM_EPS = 1e-05
HEADS = 48
INNER = 3072
CONV = 3328


def scaled_rows(values, gain_vector):
    return values * lax.rsqrt(jnp.mean(values * values, -1, keepdims=True) + NORM_EPS) * gain_vector


def glu_back(acts_pair, hidden_back):
    half_width = acts_pair.shape[-1] // 2
    gate_part = acts_pair[..., :half_width]
    up_part = acts_pair[..., half_width:]
    sigmoid_gate = jax.nn.sigmoid(gate_part)
    gate_grad = hidden_back * up_part * sigmoid_gate * (1.0 + gate_part * (1.0 - sigmoid_gate))
    up_grad = hidden_back * gate_part * sigmoid_gate
    return jnp.concatenate([gate_grad, up_grad], -1).astype(jnp.bfloat16)


MESH_ID = pl.DeviceIdType.MESH
RS_ORDERS = (("x", "y", "z"), ("y", "z", "x"), ("z", "x", "y"))
RS_COUNTS = (9, 9, 8)
RS_FIRST = (0, 9, 18)
RS_SLOTS = 26
RS_COLS = 256
RS_LAGS = (0, 2, 4, 6, 8)
RS_TIMES = max(RS_COUNTS) + RS_LAGS[-1]
NEIGHBOURS = [("c", 1)] + [(axis, o) for axis in ("x", "y", "z") for o in (1, 2, 3)]


def ring(axis, offset):
    size = lax.axis_size(axis)
    return lax.rem(lax.axis_index(axis) + offset + size, size)


def greet(targets):
    barrier = pltpu.get_barrier_semaphore()
    for target in targets:
        pl.semaphore_signal(barrier, inc=1, device_id=target, device_id_type=MESH_ID)
    pl.semaphore_wait(barrier, len(targets))


def greet_neighbours():
    greet([{axis: ring(axis, o)} for axis, o in NEIGHBOURS])


def remote(src, dst, send_sem, recv_sem, target):
    return pltpu.make_async_remote_copy(
        src_ref=src,
        dst_ref=dst,
        send_sem=send_sem,
        recv_sem=recv_sem,
        device_id=target,
        device_id_type=MESH_ID,
    )


def dot32(left, right):
    return jnp.dot(left, right, preferred_element_type=jnp.float32)


def grad_sum_scratch(rows):
    half, block, low = rows // 2, rows // 8, jnp.bfloat16
    sems = lambda *shape: [pltpu.SemaphoreType.DMA(shape)] * 2
    return [
        pltpu.VMEM((RS_SLOTS, half, RS_COLS), low),
        pltpu.VMEM((RS_SLOTS, 4, block // 2, RS_COLS), low),
        pltpu.VMEM((RS_SLOTS, 2, block // 2, RS_COLS), low),
        pltpu.VMEM((RS_SLOTS, 3, block // 4, RS_COLS), low),
        pltpu.VMEM((RS_SLOTS, 4, 16, RS_COLS), low),
        pltpu.VMEM((RS_SLOTS, 3, 16, RS_COLS), low),
        pltpu.VMEM((3, block // 4 + 8, RS_COLS), jnp.float32),
        *sems(RS_SLOTS, 4), *sems(RS_SLOTS, 2), *sems(RS_SLOTS, 3), *sems(RS_SLOTS, 3),
    ]


def share_factors(lefts_ref, left_in, left_both, rights, sems):
    me, half = lax.axis_index("c"), left_in.shape[1]
    copies = [
        remote(
            lefts_ref.at[:, pl.ds(pl.multiple_of((1 - me) * half, half), half)], left_in, sems[0].at[0], sems[1].at[0], {"c": 1 - me}
        ),
        remote(rights.at[:TILE], rights.at[TILE:], sems[0].at[1], sems[1].at[1], {"c": 1 - me}),
    ]
    for copy in copies:
        copy.start()

    def receive():
        left_both[:, :, :TILE] = lefts_ref[:, pl.ds(pl.multiple_of(me * half, half), half), :]
        for copy in copies:
            copy.wait()
        left_both[:, :, TILE:] = left_in[...]

    return receive


def share_scratch(lefts):
    count, rows, depth = lefts.shape
    return [
        pltpu.VMEM((count, rows // 2, depth), lefts.dtype),
        pltpu.VMEM((count, rows // 2, 2 * depth), lefts.dtype),
        pltpu.VMEM((2 * depth, RS_SLOTS * RS_COLS), lefts.dtype),
        pltpu.SemaphoreType.DMA((2,)),
        pltpu.SemaphoreType.DMA((2,)),
    ]


def grad_sum_steps(scratch, product, store):
    core_in, near, far, second_in, third_out, third_in, lines = scratch[:7]
    near_ss, near_rs, far_ss, far_rs, second_ss, second_rs, third_ss, third_rs = scratch[7:]
    half = core_in.shape[1]
    block = half // 4
    edge = block // 2
    small = block // 4
    unit = third_out.shape[2]
    kept = small // 4
    lines[...] = jnp.zeros_like(lines)

    def near_copies(part, k):
        slot = RS_FIRST[part] + k
        axis = RS_ORDERS[part][0]
        after, before, across = ring(axis, 1), ring(axis, -1), ring(axis, 2)
        plan = ((before, 0, before), (after, edge, after), (across, 0, after), (across, edge, before))
        return [
            remote(
                core_in.at[slot, pl.ds(which * block + offset, edge)], near.at[slot, n],
                near_ss.at[slot, n], near_rs.at[slot, n], {axis: target},
            )
            for n, (which, offset, target) in enumerate(plan)
        ]

    def far_copies(part, k):
        slot = RS_FIRST[part] + k
        axis = RS_ORDERS[part][0]
        return [
            remote(
                near.at[slot, 2 + n], far.at[slot, n],
                far_ss.at[slot, n], far_rs.at[slot, n], {axis: ring(axis, o)},
            )
            for n, o in enumerate((1, -1))
        ]

    def second_copies(part, k):
        slot = RS_FIRST[part] + k
        axis = RS_ORDERS[part][1]
        copies = []
        for o in (1, 2, 3):
            target = ring(axis, o)
            copies.append(
                remote(
                    near.at[slot, target // 2, pl.ds(lax.rem(target, 2) * small, small)],
                    second_in.at[slot, o - 1],
                    second_ss.at[slot, o - 1], second_rs.at[slot, o - 1], {axis: target},
                )
            )
        return copies

    def third_copies(part, k):
        slot = RS_FIRST[part] + k
        axis = RS_ORDERS[part][2]
        return [
            remote(
                third_out.at[slot, ring(axis, o)], third_in.at[slot, o - 1],
                third_ss.at[slot, o - 1], third_rs.at[slot, o - 1], {axis: ring(axis, o)},
            )
            for o in (1, 2, 3)
        ]

    def stage_near(part, k):
        core_in[RS_FIRST[part] + k] = product(part, k).astype(jnp.bfloat16)
        for copy in near_copies(part, k):
            copy.start()

    def load(ref, *where):
        return ref[where].astype(jnp.float32)

    def stage_far(part, k):
        slot = RS_FIRST[part] + k
        axis = RS_ORDERS[part][0]
        copies = near_copies(part, k)
        for n, (which, offset) in enumerate(((ring(axis, 1), 0), (ring(axis, -1), edge))):
            copies[2 + n].wait_recv()
            rows = pl.ds(pl.multiple_of(which * block + offset, edge), edge)
            near[slot, 2 + n] = (load(near, slot, 2 + n) + load(core_in, slot, rows)).astype(jnp.bfloat16)
        for copy in far_copies(part, k):
            copy.start()

    def stage_second(part, k):
        slot = RS_FIRST[part] + k
        me = lax.axis_index(RS_ORDERS[part][0])
        copies, far_in = near_copies(part, k), far_copies(part, k)
        for n in range(2):
            copies[n].wait_recv()
            far_in[n].wait_recv()
            rows = pl.ds(pl.multiple_of(me * block + n * edge, edge), edge)
            near[slot, n] = (
                load(near, slot, n) + load(far, slot, n) + load(core_in, slot, rows)
            ).astype(jnp.bfloat16)
        for copy in second_copies(part, k):
            copy.start()

    def stage_third(part, k):
        slot = RS_FIRST[part] + k
        me = lax.axis_index(RS_ORDERS[part][1])
        for copy in second_copies(part, k):
            copy.wait_recv()
        rows = pl.ds(pl.multiple_of(lax.rem(me, 2) * small, small), small)
        lines[part, :small] = load(near, slot, me // 2, rows) + (
            load(second_in, slot, 0) + load(second_in, slot, 1) + load(second_in, slot, 2)
        )
        for j in range(4):
            third_out[slot, j] = lines[part, kept * j : kept * j + unit].astype(jnp.bfloat16)
        for copy in third_copies(part, k):
            copy.start()

    def stage_last(part, k):
        slot = RS_FIRST[part] + k
        for copy in third_copies(part, k):
            copy.wait_recv()
        me = lax.axis_index(RS_ORDERS[part][2])
        total = load(third_out, slot, me) + (
            load(third_in, slot, 0) + load(third_in, slot, 1) + load(third_in, slot, 2)
        )
        store(part, k, total)

    stages = (stage_near, stage_far, stage_second, stage_third, stage_last)

    def step(t):
        for lag, stage in zip(RS_LAGS, stages):
            k = t - lag
            for count in sorted(set(RS_COUNTS)):
                @pl.when((k >= 0) & (k < count))
                def _():
                    for part in range(3):
                        if RS_COUNTS[part] == count:
                            stage(part, k)

    def finish():
        for part in range(3):
            def wait_sent(k, carry, part=part):
                for copies in (near_copies, far_copies, second_copies, third_copies):
                    for copy in copies(part, k):
                        copy.wait_send()
                return carry

            lax.fori_loop(0, RS_COUNTS[part], wait_sent, 0)

    return step, finish


def grad_sum_kernel(
    tail_back_ref, rim_ref, gain_ref, tail_ref, taps_ref, gated_gain_ref, post_ref, heads_ref, router_ref,
    main_ref, gate_far, conv_far, lefts_far, tokens_far, middle_far,
    out_ref, small_ref, tokens_back_far, *scratch
):
    gate_ref, conv_ref, lefts_ref, tokens_ref, middle_ref, load_sem, tokens_back_ref, save_sem, *scratch = scratch
    save = pltpu.make_async_copy(tokens_back_ref, tokens_back_far, save_sem.at[0])
    loads = [
        pltpu.make_async_copy(far, near, load_sem.at[i])
        for i, (far, near) in enumerate(
            zip((gate_far, conv_far, lefts_far, tokens_far, middle_far), (gate_ref, conv_ref, lefts_ref, tokens_ref, middle_ref))
        )
    ]
    for copy in loads:
        copy.start()
    *sum_scratch, left_in, left_both, back_ref, share_ss, share_rs, total, weights, weight_sem, pack, pack_in, pack_work, pack_others, pack_ss, pack_rs = scratch
    me_core = lax.axis_index("c")
    other = 1 - me_core
    blocks = main_ref.shape[1] // weights.shape[2]

    def fetch(j):
        rows = weights.shape[2]
        return [
            pltpu.make_async_copy(
                main_ref.at[i, pl.ds(pl.multiple_of(j * rows, 16), rows)],
                weights.at[lax.rem(j, 2), i],
                weight_sem.at[lax.rem(j, 2), i],
            )
            for i in range(4)
        ]

    for copy in fetch(0) + fetch(1):
        copy.start()
    greet_neighbours()
    inner, conv = gate_ref.shape[1], conv_ref.shape[1]
    for copy in loads[:3]:
        copy.wait()
    back_ref[:TILE, :inner] = gate_ref[...]
    back_ref[:TILE, inner : inner + conv] = short(conv_ref[...])
    rim = jnp.concatenate([jnp.zeros((8, conv), jnp.float32), rim_ref[...]], 0)
    back_ref[TILE - 16 : TILE, inner : inner + conv] = short(conv_ref[TILE - 16 :] + rim)
    back_ref[:TILE, inner + conv : inner + conv + TILE] = short(tail_back_ref[...])
    rest = back_ref.shape[1] - inner - conv - TILE
    back_ref[:TILE, inner + conv + TILE :] = jnp.zeros((TILE, rest), jnp.bfloat16)
    receive = share_factors(lefts_ref, left_in, left_both, back_ref, (share_ss, share_rs))
    taps_width, wide = taps_ref.shape[1], pack.shape[1] // 2

    def project_step(j):
        for copy in fetch(j):
            copy.wait()
        rows, width = weights.shape[2:]
        here = back_ref[:TILE, pl.ds(pl.multiple_of(j * rows, TILE), rows)]
        for i in range(4):
            total[:, i * width : (i + 1) * width] += dot32(here, weights[lax.rem(j, 2), i])

        @pl.when(j + 2 < blocks)
        def _():
            for copy in fetch(j + 2):
                copy.start()

    def project_end():
        for copy in loads[3:]:
            copy.wait()
        values = tokens_ref[...].astype(jnp.float32)
        scale = lax.rsqrt(jnp.mean(values * values, 1, keepdims=True) + NORM_EPS)
        back = total[...]
        spread = back * gain_ref[...]
        shift = jnp.mean(spread * values, 1, keepdims=True) * scale * scale * scale
        tokens_back_ref[...] = middle_ref[...] + spread * scale - values * shift
        save.start()
        model = tokens_ref.shape[1]
        pack[:, :taps_width] = taps_ref[...]
        pack[5:6, : gated_gain_ref.shape[1]] = gated_gain_ref[0:1]
        pack[6:7, :model] = jnp.sum(back * values * scale, 0, keepdims=True)
        pack[6:7, model : 2 * model] = post_ref[...]
        for i in range(3):
            pack[7:8, TILE * i : TILE * (i + 1)] = heads_ref[i : i + 1]
        pack[:, taps_width:] = router_ref[...]

    width = weights.shape[3]
    for i in range(4):
        total[:, i * width : (i + 1) * width] = dot32(short(tail_back_ref[...]), tail_ref[i])

    def pack_half(ref, which):
        return ref.at[:, pl.ds(pl.multiple_of(which * wide, 128), wide)]

    def pack_core(last):
        if last:
            return remote(pack_work.at[3], pack_half(small_ref, me_core), pack_ss.at[4, 0], pack_rs.at[4, 0], {"c": other})
        return remote(pack_half(pack, other), pack_in, pack_ss.at[0, 0], pack_rs.at[0, 0], {"c": other})

    def pack_copies(s):
        axis = ("x", "y", "z")[s - 1]
        return [
            remote(pack_work.at[s - 1], pack_others.at[s - 1, o - 1], pack_ss.at[s, o], pack_rs.at[s, o], {axis: ring(axis, o)})
            for o in (1, 2, 3)
        ]

    def pack_step(s):
        if s == 0:
            project_end()
            pack_core(False).start()
        if s == 1:
            pack_core(False).wait_recv()
            pack_work[0] = pack[:, pl.ds(pl.multiple_of(me_core * wide, 128), wide)] + pack_in[...]
        if s in (2, 3, 4):
            for copy in pack_copies(s - 1):
                copy.wait_recv()
            pack_work[s - 1] = pack_work[s - 2] + (
                pack_others[s - 2, 0] + pack_others[s - 2, 1] + pack_others[s - 2, 2]
            )
        if s in (1, 2, 3):
            for copy in pack_copies(s):
                copy.start()
        if s == 4:
            pack_core(True).start()
            small_ref[:, pl.ds(pl.multiple_of(me_core * wide, 128), wide)] = pack_work[3]
        if s == 5:
            pack_core(True).wait_recv()
            pack_core(True).wait_send()
            pack_core(False).wait_send()
            for n in (1, 2, 3):
                for copy in pack_copies(n):
                    copy.wait_send()

    def product(part, k):
        chunk = pl.ds(pl.multiple_of((RS_FIRST[part] + k) * RS_COLS, RS_COLS), RS_COLS)
        return dot32(left_both[part], back_ref[:, chunk])

    whole = out_ref.shape[1] // RS_COLS
    rows = out_ref.shape[0]

    def store(part, k, total):
        chunk = RS_FIRST[part] + k

        @pl.when(chunk < whole)
        def _():
            out_ref[:, pl.ds(pl.multiple_of(chunk * RS_COLS, RS_COLS), RS_COLS)] = total[:rows]

        if part == 2:
            @pl.when(chunk == whole)
            def _():
                out_ref[:, whole * RS_COLS :] = total[:rows, : out_ref.shape[1] - whole * RS_COLS]

    step, finish = grad_sum_steps(sum_scratch, product, store)
    receive()

    def run(t, carry):
        step(t)

        @pl.when(t < blocks)
        def _():
            project_step(t)

        for s in range(6):
            @pl.when(t == blocks + s)
            def _():
                pack_step(s)

        return carry

    lax.fori_loop(0, RS_TIMES, run, 0)
    finish()
    save.wait()


def grad_sum(lefts, gate, conv, tail_back, rim, tokens, gain, middle, tails, taps, gated_gain, post, heads, router, main, columns):
    rows = lefts.shape[1]
    wide = taps.shape[1] + router.shape[1]
    slots, model = tokens.shape
    space = pl.BlockSpec(memory_space=pltpu.VMEM)
    block = main.shape[1] // 5
    return pl.pallas_call(
        grad_sum_kernel,
        out_shape=(
            jax.ShapeDtypeStruct((rows // 128, columns), jnp.float32),
            jax.ShapeDtypeStruct((8, wide), jnp.float32),
            jax.ShapeDtypeStruct((slots, model), jnp.float32),
        ),
        in_specs=[space] * 9 + [pl.BlockSpec(memory_space=pl.ANY)] * 6,
        out_specs=(space, space, pl.BlockSpec(memory_space=pl.ANY)),
        scratch_shapes=[pltpu.VMEM(a.shape, a.dtype) for a in (gate, conv, lefts, tokens, middle)]
        + [pltpu.SemaphoreType.DMA((5,)), pltpu.VMEM((slots, model), jnp.float32), pltpu.SemaphoreType.DMA((1,))]
        + grad_sum_scratch(rows)
        + [
            *share_scratch(lefts),
            pltpu.VMEM((slots, model), jnp.float32),
            pltpu.VMEM((2, 4, block, main.shape[2]), jnp.bfloat16),
            pltpu.SemaphoreType.DMA((2, 4)),
            pltpu.VMEM((8, wide), jnp.float32),
            pltpu.VMEM((8, wide // 2), jnp.float32),
            pltpu.VMEM((4, 8, wide // 2), jnp.float32),
            pltpu.VMEM((3, 3, 8, wide // 2), jnp.float32),
            pltpu.SemaphoreType.DMA((5, 4)),
            pltpu.SemaphoreType.DMA((5, 4)),
        ],
        compiler_params=pltpu.CompilerParams(
            collective_id=0, has_side_effects=True, vmem_limit_bytes=60 * 2**20
        ),
        name="grad_sum",
    )(tail_back, rim, gain, tails, taps, gated_gain, post, heads, router, main, gate, conv, lefts, tokens, middle)


def owner_moves(order, stride, offset, rows):
    moves = []
    for to in range(128):
        digits = {"c": to // 64}
        for axis, at in zip(order, (to // 16 % 4, to // 4 % 4, to % 4)):
            digits[axis] = at
        owner = ((digits["x"] * 4 + digits["y"]) * 2 + digits["c"]) * 4 + digits["z"]
        source, target = owner * stride + offset, to * 12
        if moves and moves[-1][0] + moves[-1][2] == source and moves[-1][1] + moves[-1][2] == target:
            moves[-1][2] += rows
        else:
            moves.append([source, target, rows])
    return moves


def lefts_kernel(first_ref, second_ref, gated_ref, hidden_ref, early_ref, late_ref, turned, sorted_rows):
    def turn(ref):
        for j in range(ref.shape[1] // TILE):
            turned[j * TILE : (j + 1) * TILE] = ref[:, j * TILE : (j + 1) * TILE].astype(jnp.float32).T

    def place(out_ref, at, order, stride, offset, rows):
        if rows < 12:
            sorted_rows[...] = jnp.zeros_like(sorted_rows)
        for source, target, size in owner_moves(order, stride, offset, rows):
            sorted_rows[target : target + size] = turned[source : source + size]
        out_ref[at] = sorted_rows[...].astype(jnp.bfloat16)

    turn(first_ref)
    for part in range(3):
        place(late_ref, part, RS_ORDERS[part], 12, 0, 12)
    turn(second_ref)
    place(early_ref, 0, RS_ORDERS[0], 12, 0, 12)
    turn(hidden_ref)
    for at, part in ((1, 0), (3, 1), (5, 2)):
        place(early_ref, at, RS_ORDERS[part], 8, 0, 8)
    turn(gated_ref)
    place(early_ref, 2, RS_ORDERS[1], 24, 0, 12)
    place(early_ref, 4, RS_ORDERS[2], 24, 12, 12)


def plane_others():
    x, y = lax.axis_index("x"), lax.axis_index("y")
    found = []
    for dx in range(4):
        for dy in range(4):
            if dx + dy:
                tx, ty = lax.rem(x + dx, 4), lax.rem(y + dy, 4)
                found.append((dx * 4 + dy, tx * 4 + ty, {"x": tx, "y": ty}))
    return found


def line_neighbour(ahead):
    x, y, c = lax.axis_index("x"), lax.axis_index("y"), lax.axis_index("c")
    chip = lax.rem(x * 4 + y + (c if ahead else c + 15), 16)
    return {"x": chip // 4, "y": lax.rem(chip, 4), "c": 1 - c}


def greet_plane():
    c = lax.axis_index("c")
    chip = lax.rem(lax.axis_index("x") * 4 + lax.axis_index("y") + 2 * c + 15, 16)
    greet(
        [{"c": 1 - c}, {"x": chip // 4, "y": lax.rem(chip, 4), "c": 1 - c}]
        + [{"z": ring("z", o)} for o in (1, 2, 3)]
        + [where for unused, unused_too, where in plane_others()]
    )


def state_exchange(reverse, state_ref, totals_ref, rows_ref, out_ref, all_rows, rows_sum, tick, *refs):
    pair_in, pair_totals, outgoing, got, back, mine, hand, ps, pr, ss, rs, bs, br, zs, zr = refs
    x, y, c, z = (lax.axis_index(a) for a in ALL)
    chip = x * 4 + y
    half = pair_in.shape[0]
    groups, size = back.shape[1:3]
    others = plane_others()
    mine_at, theirs_at = c * half, (1 - c) * half

    def pair_copies():
        return [
            remote(state_ref.at[pl.ds(theirs_at, half)], pair_in, ps.at[0], pr.at[0], {"c": 1 - c}),
            remote(totals_ref, pair_totals, ps.at[1], pr.at[1], {"c": 1 - c}),
        ]

    def out_copy(at, target, where):
        return remote(outgoing.at[target], got.at[chip], ss.at[at], rs.at[at], where)

    def back_copy(at, target, where):
        return remote(back.at[target], mine.at[pl.ds(groups * chip, groups)], bs.at[at], br.at[at], where)

    def hand_copy():
        return remote(hand, out_ref.at[pl.ds(mine_at, half)], ps.at[2], pr.at[2], {"c": 1 - c})

    row_copies = []
    for o in (1, 3, 2):
        source = rows_ref.at[ring("z", o)] if reverse else rows_ref
        target = all_rows.at[o - 1] if reverse else all_rows.at[z]
        row_copies.append(remote(source, target, zs.at[o], zr.at[o], {"z": ring("z", o)}))
    for copy in pair_copies():
        copy.start()
    for copy in row_copies:
        copy.start()
    own_rows = None if reverse else pltpu.make_async_copy(rows_ref, all_rows.at[z], zs.at[0])
    if not reverse:
        own_rows.start()
    tick(0)
    for copy in pair_copies():
        copy.wait_recv()
    first = jnp.where(c == 0, totals_ref[...], pair_totals[...])
    second = jnp.where(c == 0, pair_totals[...], totals_ref[...])
    inner, outer = (first, second) if reverse else (second, first)
    lanes = lax.broadcasted_iota(jnp.int32, (8, TILE), 1) - c * (half // 2)

    def decay(logs, head):
        return jnp.exp(jnp.sum(jnp.where(lanes[: logs.shape[0]] == head, logs, 0.0), 1, keepdims=True))[:1]

    def states(g):
        own, other = state_ref[mine_at + g].astype(jnp.float32), pair_in[g].astype(jnp.float32)
        return jnp.where(c == 0, own, other), jnp.where(c == 0, other, own)

    total = (first + second)[:1]
    high = total.astype(jnp.bfloat16).astype(jnp.float32)
    middle = (total - high).astype(jnp.bfloat16).astype(jnp.float32)
    row = lax.broadcasted_iota(jnp.int32, (16, TILE), 0)
    split = jnp.where(row == 0, high, jnp.where(row == 1, middle, jnp.where(row == 2, total - high - middle, 0.0)))
    split = split.astype(jnp.bfloat16)

    def combine(m, carry):
        for i in range(groups):
            g = groups * m + i
            early, late = states(g)
            rate = decay(inner, g // 2)
            pair = early + rate * late if reverse else rate * early + late
            outgoing[m, i * size : (i + 1) * size] = pair.astype(jnp.bfloat16)
        outgoing[m, groups * size :] = split
        return carry

    lax.fori_loop(0, 16, combine, 0)
    for d in others:
        out_copy(*d).start()
    got[chip] = outgoing[chip]
    tick(1)
    for d in others:
        out_copy(*d).wait_recv()

    def advance(step, carried):
        p = 15 - step if reverse else step
        logs = jnp.sum(got[p, groups * size :].astype(jnp.float32), 0, keepdims=True)
        new = []
        for i in range(groups):
            back[p, i] = carried[i].astype(back.dtype)
            here = got[p, i * size : (i + 1) * size].astype(jnp.float32)
            new.append(carried[i] * decay(logs, (groups * chip + i) // 2) + here)
        return tuple(new)

    lax.fori_loop(0, 16, advance, (jnp.zeros((size, TILE), jnp.float32),) * groups)
    for d in others:
        back_copy(*d).start()
    mine[pl.ds(groups * chip, groups)] = back[chip]
    tick(2)
    for d in others:
        back_copy(*d).wait_recv()

    def spread(h, carry):
        rate = decay(outer, h)
        for i in range(2):
            g = 2 * h + i
            early, late = states(g)
            near = mine[g].astype(jnp.float32)
            beyond = rate * near + (late if reverse else early)
            swap = (c == 1) if reverse else (c == 0)
            out_ref[mine_at + g] = jnp.where(swap, near, beyond).astype(out_ref.dtype)
            hand[g] = jnp.where(swap, beyond, near).astype(hand.dtype)
        return carry

    lax.fori_loop(0, half // 2, spread, 0)
    hand_copy().start()
    tick(3)
    for copy in row_copies:
        copy.wait()
    if not reverse:
        own_rows.wait()
    if reverse:
        add_parts(rows_ref, z, all_rows, rows_sum)
    hand_copy().wait()
    for copy in pair_copies():
        copy.wait_send()
    for d in others:
        out_copy(*d).wait_send()
        back_copy(*d).wait_send()


def add_parts(ref, me, got, out):
    def rows_at(j, carry):
        rows = pl.ds(pl.multiple_of(j * 32, 32), 32)
        total = ref[me, rows].astype(jnp.float32)
        for o in range(3):
            total = total + got[o, rows].astype(jnp.float32)
        out[rows] = total
        return carry

    lax.fori_loop(0, out.shape[0] // 32, rows_at, 0)


def scan_scratch():
    low, sem = jnp.bfloat16, pltpu.SemaphoreType.DMA
    return [
        pltpu.VMEM((48, 32, TILE), low),
        pltpu.VMEM((8, TILE), jnp.float32),
        pltpu.VMEM((16, 112, TILE), low),
        pltpu.VMEM((16, 112, TILE), low),
        pltpu.VMEM((16, 3, 32, TILE), low),
        pltpu.VMEM((48, 32, TILE), low),
        pltpu.VMEM((48, 32, TILE), low),
        sem((3,)), sem((3,)), sem((16,)), sem((16,)), sem((16,)), sem((16,)), sem((4,)), sem((4,)),
    ]


def middle_kernel(
    normed_ref, tokens_ref, gain_ref, router_ref, chosen_ref, up_ref, out_far, in_far, down_far,
    *refs
):
    outs, refs = refs[:6], refs[6:]
    all_rows, all_gates, out_w, in_w, down_w, *refs = refs
    inside, refs = refs[:6], refs[6:]
    middle_ref, second_ref, base_ref, back_ref, hidden_ref, acts_ref = inside
    save_sem, load_sem, row_ss, row_rs, gate_ss, gate_rs = refs
    saves = [pltpu.make_async_copy(near, far, save_sem.at[i]) for i, (near, far) in enumerate(zip(inside, outs))]
    z = lax.axis_index("z")
    own_rows = pltpu.make_async_copy(second_ref, all_rows.at[z], save_sem.at[6])
    loads = []
    for far, near, parts in ((out_far, out_w, 4), (in_far, in_w, 3), (down_far, down_w, 2)):
        rows = near.shape[0] // parts
        for i in range(parts):
            here = pl.ds(i * rows, rows)
            loads.append(pltpu.make_async_copy(far.at[here], near.at[here], load_sem.at[len(loads)]))
    for copy in loads:
        copy.start()
    greet([{"z": ring("z", o)} for o in (1, 2, 3)])
    depth = normed_ref.shape[1] // 4
    middle = tokens_ref[...].astype(jnp.float32)
    for i in range(4):
        loads[i].wait()
        here = slice(i * depth, (i + 1) * depth)
        middle = middle + dot32(normed_ref[:, here], out_w[here])
    middle_ref[...] = middle
    saves[0].start()
    scale = lax.rsqrt(jnp.mean(middle * middle, 1, keepdims=True) + NORM_EPS)
    second_ref[...] = short(middle * scale * gain_ref[...])
    saves[1].start()
    own_rows.start()

    def row_copy(o):
        return remote(second_ref, all_rows.at[z], row_ss.at[o], row_rs.at[o], {"z": ring("z", o)})

    def row_forward(o):
        half = all_rows.shape[1] // 2
        block = all_rows.at[lax.rem(z + 4 - o, 4), pl.ds(0 if o == 1 else half, half)]
        return remote(block, block, row_ss.at[3 + o], row_rs.at[3 + o], {"z": ring("z", o)})

    def gate_copy(o):
        return remote(all_gates.at[z], all_gates.at[z], gate_ss.at[o], gate_rs.at[o], {"z": ring("z", o)})

    for o in (1, 3):
        row_copy(o).start()
    logits = dot_nt(router_ref[...], second_ref[...])
    masked = jnp.where(chosen_ref[...] > 0.0, logits, -jnp.inf)
    powers = jnp.exp(masked - jnp.max(masked, 0, keepdims=True))
    all_gates[z] = powers / jnp.sum(powers, 0, keepdims=True)
    for o in (1, 3, 2):
        gate_copy(o).start()
    width = hidden_ref.shape[1]
    block = 256
    for copy in loads[4:]:
        copy.wait()
    second = second_ref[...]
    for j in range(0, width, block):
        gate = dot32(second, in_w[:, j : j + block])
        up = dot32(second, in_w[:, width + j : width + j + block])
        sig = jax.nn.sigmoid(gate)
        hidden_ref[:, j : j + block] = short(gate * sig * up)
        back = dot_nt(up_ref[...], down_w[j : j + block])
        acts_ref[:, j : j + block] = short(back * up * sig * (1.0 + gate * (1.0 - sig)))
        acts_ref[:, width + j : width + j + block] = short(back * gate * sig)
    saves[4].start()
    saves[5].start()
    for o in (1, 3):
        row_copy(o).wait_recv()
        row_forward(o).start()
    model = middle_ref.shape[1]
    for j in range(0, model, 2 * block):
        here = slice(j, j + 2 * block)
        base_ref[:, here] = middle_ref[:, here] + dot32(hidden_ref[...], down_w[:, here])
        back_ref[:, here] = dot_nt(acts_ref[...], in_w[here])
    saves[2].start()
    saves[3].start()
    for o in (1, 3):
        row_copy(o).wait_send()
        row_forward(o).wait()
    for o in (1, 3, 2):
        gate_copy(o).wait()
    for copy in saves:
        copy.wait()
    own_rows.wait()


def middle_part(normed, tokens, gain, router, chosen, upstream, out_w, in_w, down_w):
    space, away = pl.BlockSpec(memory_space=pltpu.VMEM), pl.BlockSpec(memory_space=pl.ANY)
    slots, model = tokens.shape
    f32, low, sem = jnp.float32, jnp.bfloat16, pltpu.SemaphoreType.DMA
    outs = [
        ((slots, model), f32), ((slots, model), low), ((slots, model), f32), ((slots, model), f32),
        ((slots, down_w.shape[0]), low), ((slots, in_w.shape[1]), low), ((4, slots, model), low), ((4, *chosen.shape), f32),
    ]
    return pl.pallas_call(
        middle_kernel,
        out_shape=tuple(jax.ShapeDtypeStruct(s, d) for s, d in outs),
        in_specs=[space] * 6 + [away] * 3,
        out_specs=(away,) * 7 + (space,),
        scratch_shapes=[pltpu.VMEM(w.shape, w.dtype) for w in (out_w, in_w, down_w)]
        + [pltpu.VMEM(s, d) for s, d in outs[:6]]
        + [sem((7,)), sem((9,)), sem((7,)), sem((7,)), sem((4,)), sem((4,))],
        compiler_params=pltpu.CompilerParams(
            collective_id=5, has_side_effects=True, vmem_limit_bytes=60 * 2**20
        ),
        name="middle",
    )(normed, tokens, gain, router, chosen, upstream, out_w, in_w, down_w)


EXPERT_ORDERS = (("x", "y"), ("y", "x"))
EXPERT_STEPS = 6
EXPERT_COLS = 256


def expert_sum_kernel(
    picks_ref, gates_ref, gain_ref, back_far, *refs
):
    far, refs = refs[:9], refs[9:]
    weights_far, out_ref, middle_out, mix_out, post_back, router_back, normed_out, *refs = refs
    (middle_back, mix_ref, normed_back, back_ref), refs = refs[:4], refs[4:]
    near_refs, refs = refs[:9], refs[9:]
    rows_ref, acts_ref, hidden_ref, grads_ref, middle_ref, shared_ref, up_ref, second_ref, router_ref = near_refs
    expert_sum_body(
        list(zip(far, near_refs)),
        rows_ref, acts_ref, hidden_ref, grads_ref, back_ref, picks_ref,
        middle_ref, shared_ref, up_ref, second_ref, gates_ref, router_ref, gain_ref, weights_far,
        out_ref, middle_back, mix_ref, post_back, router_back, normed_back, back_far, middle_out, mix_out, normed_out, *refs,
    )


def expert_sum_body(
    far_near,
    rows_ref, acts_ref, hidden_ref, grads_ref, back_ref, picks_ref,
    middle_ref, shared_ref, up_ref, second_ref, gates_ref, router_ref, gain_ref, weights_far,
    out_ref, middle_back, mix_ref, post_back, router_back, normed_back, back_far, middle_out, mix_out, normed_out,
    stage_sem, save_sem, weights, load_sem, back_sum, picks_all,
    core_out, core_in, near, far, second_in, got, turned_rows, turned_hidden,
    core_ss, core_rs, near_ss, near_rs, far_ss, far_rs, second_ss, second_rs, zs, zr,
):
    me_core = lax.axis_index("c")
    me_z = lax.axis_index("z")
    other = 1 - me_core
    half = core_out.shape[2]
    block = half // 4
    edge = block // 2
    small = block // 4
    third = small // 3
    cols = EXPERT_COLS
    quarter = weights.shape[0] // 4
    loads = [
        pltpu.make_async_copy(weights_far.at[pl.ds(i * quarter, quarter)], weights.at[pl.ds(i * quarter, quarter)], load_sem.at[i])
        for i in range(4)
    ]
    staged = [pltpu.make_async_copy(far, here, stage_sem.at[i]) for i, (far, here) in enumerate(far_near)]
    staged.append(pltpu.make_async_copy(back_far, back_ref, stage_sem.at[9]))
    saves = [
        pltpu.make_async_copy(here, far, save_sem.at[i])
        for i, (here, far) in enumerate(((middle_back, middle_out), (mix_ref, mix_out), (normed_back, normed_out)))
    ]
    for copy in staged + loads:
        copy.start()
    greet_neighbours()

    sums = []
    for n, ref in enumerate((back_far,)):
        for o in (1, 3, 2):
            sums.append(
                remote(ref.at[ring("z", o)], got.at[n, o - 1], zs.at[n, o], zr.at[n, o], {"z": ring("z", o)})
            )
    for o in (1, 3, 2):
        sums.append(
            remote(picks_ref.at[ring("z", o)], picks_all.at[me_z], zs.at[2, o], zr.at[2, o], {"z": ring("z", o)})
        )
    for copy in sums:
        copy.start()
    picks_all[me_z] = picks_ref[me_z]
    for copy in staged[:4]:
        copy.wait()
    for j in range(rows_ref.shape[1] // TILE):
        turned_rows[j * TILE : (j + 1) * TILE] = rows_ref[:, j * TILE : (j + 1) * TILE].T
    for part in range(2):
        for j in range(hidden_ref.shape[2] // TILE):
            turned_hidden[part, j * TILE : (j + 1) * TILE] = hidden_ref[part, :, j * TILE : (j + 1) * TILE].T

    def plane_rows(part, which, load, size):
        blocks = []
        for j in range(4):
            for i in range(4):
                spot = (j * 4 + i if part == 0 else i * 4 + j) * 2 + which
                blocks.append(load(pl.ds(pl.multiple_of(spot * size, 16), size)))
        return jnp.concatenate(blocks, 0)

    def core_copy(part, k):
        slot = part * EXPERT_STEPS + k
        return remote(
            core_out.at[lax.rem(k, 2), part], core_in.at[slot],
            core_ss.at[slot], core_rs.at[slot], {"c": other},
        )

    def near_copies(part, k):
        slot = part * EXPERT_STEPS + k
        axis = EXPERT_ORDERS[part][0]
        after, before, across = ring(axis, 1), ring(axis, -1), ring(axis, 2)
        plan = ((before, 0, before), (after, edge, after), (across, 0, after), (across, edge, before))
        return [
            remote(
                core_in.at[slot, pl.ds(which * block + offset, edge)], near.at[slot, n],
                near_ss.at[slot, n], near_rs.at[slot, n], {axis: target},
            )
            for n, (which, offset, target) in enumerate(plan)
        ]

    def far_copies(part, k):
        slot = part * EXPERT_STEPS + k
        axis = EXPERT_ORDERS[part][0]
        return [
            remote(
                near.at[slot, 2 + n], far.at[slot, n],
                far_ss.at[slot, n], far_rs.at[slot, n], {axis: ring(axis, o)},
            )
            for n, o in enumerate((1, -1))
        ]

    def second_copies(part, k):
        slot = part * EXPERT_STEPS + k
        axis = EXPERT_ORDERS[part][1]
        copies = []
        for o in (1, 2, 3):
            target = ring(axis, o)
            copies.append(
                remote(
                    near.at[slot, target // 2, pl.ds(lax.rem(target, 2) * small, small)],
                    second_in.at[slot, o - 1],
                    second_ss.at[slot, o - 1], second_rs.at[slot, o - 1], {axis: target},
                )
            )
        return copies

    def load(ref, *where):
        return ref[where].astype(jnp.float32)

    def products(part, k, which_half, store):
        @pl.when(k < 4)
        def _():
            right = acts_ref[part, :, pl.ds(pl.multiple_of(k * cols, cols), cols)]

            left = plane_rows(part, which_half, lambda rows: turned_rows[rows], small)
            store(0, half, dot32(left, right))

        @pl.when(k >= 4)
        def _():
            left = plane_rows(part, which_half, lambda rows: turned_hidden[part, rows], third)
            for t in range(3):
                right = grads_ref[part, :, pl.ds(pl.multiple_of(t * 2 * cols + (k - 4) * cols, cols), cols)]
                product = dot32(left, right)
                for i in range(16):
                    store(i * small + t * third, third, product[i * third : (i + 1) * third])

    def stage_product(part, k):
        @pl.when(k >= 2)
        def _():
            core_copy(part, k - 2).wait_send()

        def store(at, size, value):
            core_out[lax.rem(k, 2), part, pl.ds(at, size), :] = value.astype(jnp.bfloat16)

        products(part, k, other, store)
        core_copy(part, k).start()

    def stage_near(part, k):
        slot = part * EXPERT_STEPS + k
        core_copy(part, k).wait_recv()

        def store(at, size, value):
            rows = pl.ds(at, size)
            core_in[slot, rows, :] = (value + load(core_in, slot, rows)).astype(jnp.bfloat16)

        products(part, k, me_core, store)
        for copy in near_copies(part, k):
            copy.start()

    def stage_far(part, k):
        slot = part * EXPERT_STEPS + k
        axis = EXPERT_ORDERS[part][0]
        copies = near_copies(part, k)
        for n, (which, offset) in enumerate(((ring(axis, 1), 0), (ring(axis, -1), edge))):
            copies[2 + n].wait_recv()
            rows = pl.ds(pl.multiple_of(which * block + offset, edge), edge)
            near[slot, 2 + n] = (load(near, slot, 2 + n) + load(core_in, slot, rows)).astype(jnp.bfloat16)
        for copy in far_copies(part, k):
            copy.start()

    def stage_second(part, k):
        slot = part * EXPERT_STEPS + k
        me = lax.axis_index(EXPERT_ORDERS[part][0])
        copies, far_in = near_copies(part, k), far_copies(part, k)
        for n in range(2):
            copies[n].wait_recv()
            far_in[n].wait_recv()
            rows = pl.ds(pl.multiple_of(me * block + n * edge, edge), edge)
            near[slot, n] = (
                load(near, slot, n) + load(far, slot, n) + load(core_in, slot, rows)
            ).astype(jnp.bfloat16)
        for copy in second_copies(part, k):
            copy.start()

    def stage_last(part, k):
        slot = part * EXPERT_STEPS + k
        me = lax.axis_index(EXPERT_ORDERS[part][1])
        for copy in second_copies(part, k):
            copy.wait_recv()
        rows = pl.ds(pl.multiple_of(lax.rem(me, 2) * small, small), small)
        out_ref[part, :, pl.ds(pl.multiple_of(k * cols, cols), cols)] = load(near, slot, me // 2, rows) + (
            load(second_in, slot, 0) + load(second_in, slot, 1) + load(second_in, slot, 2)
        )

    stages = (stage_product, stage_near, stage_far, stage_second, stage_last)

    def way_back():
        for copy in sums + staged[4:]:
            copy.wait()
        add_parts(back_ref, me_z, got.at[0], back_sum)
        gates = gates_ref[me_z]
        picked = jnp.concatenate([picks_all[i, 0:2] for i in range(4)], 0)
        logits_back = gates * (picked - jnp.sum(gates * picked, 0, keepdims=True))
        padded = jnp.concatenate([logits_back, jnp.zeros((TILE - 8, TILE), jnp.float32)], 0)
        router_back[...] = dot32(short(padded), second_ref[...])[:8]
        middle = middle_ref[...]
        scale = lax.rsqrt(jnp.mean(middle * middle, 1, keepdims=True) + NORM_EPS)
        back = shared_ref[...] + back_sum[...] + dot32(short(padded.T), router_ref[...])
        post_back[...] = jnp.sum(back * middle * scale, 0, keepdims=True)
        spread = back * gain_ref[...]
        shift = jnp.mean(spread * middle, 1, keepdims=True) * scale * scale * scale
        total = spread * scale - middle * shift + up_ref[...].astype(jnp.float32)
        middle_back[...] = total
        mix_ref[...] = short(total)
        saves[0].start()
        saves[1].start()
        turned = short(total.T)
        for i in range(4):
            loads[i].wait()
            here = slice(i * quarter, (i + 1) * quarter)
            normed_back[:, here] = dot32(weights[here], turned).T
        saves[2].start()

    def step(t, carry):
        @pl.when(t == 5)
        def _():
            way_back()

        for lag, stage in enumerate(stages):
            k = t - lag

            @pl.when((k >= 0) & (k < EXPERT_STEPS))
            def _():
                for part in range(2):
                    stage(part, k)

        return carry

    lax.fori_loop(0, EXPERT_STEPS + len(stages) - 1, step, 0)

    def finish(k, carry):
        for part in range(2):
            @pl.when(k >= EXPERT_STEPS - 2)
            def _():
                core_copy(part, k).wait_send()

            for copies in (near_copies, far_copies, second_copies):
                for copy in copies(part, k):
                    copy.wait_send()
        return carry

    lax.fori_loop(0, EXPERT_STEPS, finish, 0)
    for copy in saves:
        copy.wait()


def expert_sum(rows, acts, hidden, grads, back, picks, middle, shared, upstream, second, gates, router, gain, weights):
    slots, cols, half = 2 * EXPERT_STEPS, EXPERT_COLS, rows.shape[1] // 2
    block = half // 4
    low, f32 = jnp.bfloat16, jnp.float32
    sem = pltpu.SemaphoreType.DMA
    sems = lambda *shape: [sem(shape)] * 2
    space, away = pl.BlockSpec(memory_space=pltpu.VMEM), pl.BlockSpec(memory_space=pl.ANY)
    depth, model = middle.shape
    staged = [rows, acts, hidden, grads, middle, shared, upstream, second, router]
    outs = [
        ((2, block // 4, EXPERT_STEPS * cols), f32), ((depth, model), f32), ((depth, model), low),
        ((1, model), f32), ((8, model), f32), ((depth, weights.shape[0]), f32),
    ]
    return pl.pallas_call(
        expert_sum_kernel,
        out_shape=tuple(jax.ShapeDtypeStruct(s, d) for s, d in outs),
        in_specs=[space] * 3 + [away] * 11,
        out_specs=(space, away, away, space, space, away),
        scratch_shapes=[
            *[pltpu.VMEM(*outs[i]) for i in (1, 2, 5)],
            pltpu.VMEM(back.shape, back.dtype),
            *[pltpu.VMEM(a.shape, a.dtype) for a in staged],
            sem((10,)),
            sem((3,)),
            pltpu.VMEM(weights.shape, low),
            sem((4,)),
            pltpu.VMEM((depth, model), f32),
            pltpu.VMEM(picks.shape, f32),
            pltpu.VMEM((2, 2, half, cols), low),
            pltpu.VMEM((slots, half, cols), low),
            pltpu.VMEM((slots, 4, block // 2, cols), low),
            pltpu.VMEM((slots, 2, block // 2, cols), low),
            pltpu.VMEM((slots, 3, block // 4, cols), low),
            pltpu.VMEM((1, 3, *back.shape[1:]), low),
            pltpu.VMEM(rows.shape[::-1], low),
            pltpu.VMEM((2, *hidden.shape[:0:-1]), low),
            *sems(slots), *sems(slots, 4), *sems(slots, 2), *sems(slots, 3), *sems(3, 4),
        ],
        compiler_params=pltpu.CompilerParams(
            collective_id=4, has_side_effects=True, vmem_limit_bytes=60 * 2**20
        ),
        name="expert_sum",
    )(picks, gates, gain, back, *staged, weights)


def gather_sems(count):
    sem = lambda *shape: [pltpu.SemaphoreType.DMA(shape)] * 2
    return sem(count, 4) + sem(count, 8) + sem(count, 4, 4) + sem(count, 4, 8) + sem(count, 4, 5)


def gather_steps(shards, fulls, by_rows, main, sems):
    unit_ss, unit_rs, deep_ss, deep_rs, first_ss, first_rs, second_ss, second_rs, core_ss, core_rs = sems
    x, y, c, z = (lax.axis_index(a) for a in ALL)
    first_at = (1 - c) * x + c * y
    second_at = c * x + (1 - c) * y

    def along_first(o):
        return {"x": lax.rem(x + (1 - c) * o, 4), "y": lax.rem(y + c * o, 4)}

    def along_second(o):
        return {"x": lax.rem(x + c * o, 4), "y": lax.rem(y + (1 - c) * o, 4)}

    def sizes(n):
        if main and n == 0:
            total = fulls[0].shape[1]
            spread = total * 16 // 25
            return total // 2, spread // 2, spread // 32
        total = shards[n].shape[0]
        spread = total if total % 384 else total * 2 // 3
        if n in by_rows:
            return total // 2, spread // 2, spread // 32
        return total, spread, spread // 16

    def place(n, deep, offset):
        total, spread, unit = sizes(n)
        if n in by_rows:
            return (2 * spread + c * (total - spread) if deep else c * spread) + offset
        return (spread if deep else 0) + offset

    def window(n, shard, deep, offset, length):
        rows, width = shards[n].shape
        at = place(n, deep, offset)
        if main and n == 0:
            return fulls[0].at[shard, pl.ds(pl.multiple_of(at, 16), length)]
        rows = pl.ds(pl.multiple_of(at + shard * rows, 16), length)
        if n in by_rows:
            return fulls[n].at[rows]
        return fulls[n].at[rows, pl.ds(pl.multiple_of(c * (width // 2), 128), width // 2)]

    def own_window(n, deep, offset, length):
        width = shards[n].shape[1]
        rows = pl.ds(pl.multiple_of(place(n, deep, offset), 16), length)
        if n in by_rows:
            return shards[n].at[rows]
        return shards[n].at[rows, pl.ds(pl.multiple_of(c * (width // 2), 128), width // 2)]

    def came_from(o):
        return lax.rem(z - o + 4, 4)

    def unit_copy(n, o):
        unit = sizes(n)[2]
        at = (second_at * 4 + first_at) * unit
        return remote(
            own_window(n, False, at, unit), window(n, z, False, at, unit), unit_ss.at[n, o], unit_rs.at[n, o], {"z": ring("z", o)}
        )

    def deep_copy(n, o):
        total, spread, unit = sizes(n)
        return remote(
            own_window(n, True, 0, total - spread), window(n, z, True, 0, total - spread),
            deep_ss.at[n, o], deep_rs.at[n, o], {"z": ring("z", o)},
        )

    def deep_forward(n, o):
        total, spread, unit = sizes(n)
        edge = (total - spread) // 2
        block = window(n, came_from(o), True, 0 if o == 1 else edge, edge)
        return remote(block, block, deep_ss.at[n, 3 + o], deep_rs.at[n, 3 + o], {"z": ring("z", o)})

    def first_copy(n, o, step):
        unit = sizes(n)[2]
        block = window(n, came_from(o), False, (second_at * 4 + first_at) * unit, unit)
        return remote(block, block, first_ss.at[n, o, step], first_rs.at[n, o, step], along_first(step))

    def second_copy(n, o, step):
        unit = sizes(n)[2]
        block = window(n, came_from(o), False, second_at * 4 * unit, 4 * unit)
        return remote(block, block, second_ss.at[n, o, step], second_rs.at[n, o, step], along_second(step))

    def second_forward(n, o, step):
        unit = sizes(n)[2]
        source = lax.rem(second_at + 4 - step, 4)
        at = source * 4 * unit + (0 if step == 1 else 2 * unit)
        block = window(n, came_from(o), False, at, 2 * unit)
        return remote(block, block, second_ss.at[n, o, 4 + step], second_rs.at[n, o, 4 + step], along_second(step))

    def core_copy(n, o, which):
        total, spread, unit = sizes(n)
        shard = came_from(o)
        if which == 4:
            block = window(n, shard, True, 0, total - spread)
        else:
            block = window(n, shard, False, lax.rem(second_at + 4 - which, 4) * 4 * unit, 4 * unit)
        return remote(block, block, core_ss.at[n, o, which], core_rs.at[n, o, which], {"c": 1 - c})

    def core_copies(n, o):
        return [core_copy(n, o, which) for which in ((0, 1, 3, 2, 4) if n in deep else (0, 1, 3, 2))]

    arrays = range(len(shards))
    deep = [n for n in arrays if sizes(n)[0] > sizes(n)[1]]
    sides, offsets = (1, 3), (1, 3, 2)

    def begin():
        for n in arrays:
            for o in offsets:
                unit_copy(n, o).start()
        for n in deep:
            for o in sides:
                deep_copy(n, o).start()

    def go_first():
        for n in arrays:
            for o in offsets:
                unit_copy(n, o).wait_recv()
                for step in offsets:
                    first_copy(n, o, step).start()

    def go_second():
        for n in arrays:
            for o in offsets:
                for step in offsets:
                    first_copy(n, o, step).wait_recv()
                for step in sides:
                    second_copy(n, o, step).start()
                core_copy(n, o, 0).start()

    def go_deep():
        for n in deep:
            for o in sides:
                deep_copy(n, o).wait_recv()
                deep_forward(n, o).start()
                core_copy(n, o, 4).start()

    def go_forward():
        for n in arrays:
            for o in offsets:
                for step in sides:
                    second_copy(n, o, step).wait_recv()
                    second_forward(n, o, step).start()
                    core_copy(n, o, step).start()

    def go_core():
        for n in arrays:
            for o in offsets:
                for step in sides:
                    second_forward(n, o, step).wait_recv()
                core_copy(n, o, 2).start()
            if n in deep:
                for o in sides:
                    deep_forward(n, o).wait_recv()
                core_copy(n, 2, 4).start()

    def arrived(n, o):
        for copy in core_copies(n, o):
            copy.wait_recv()

    def finish():
        for n in arrays:
            for o in offsets:
                for copy in core_copies(n, o):
                    copy.wait_send()
                unit_copy(n, o).wait_send()
                for step in offsets:
                    first_copy(n, o, step).wait_send()
                for step in sides:
                    second_copy(n, o, step).wait_send()
                    second_forward(n, o, step).wait_send()
            if n in deep:
                for o in sides:
                    deep_copy(n, o).wait_send()
                    deep_forward(n, o).wait_send()

    return dict(
        begin=begin, first=go_first, second=go_second, deep=go_deep, forward=go_forward, core=go_core,
        arrived=arrived, finish=finish, came_from=came_from,
    )


def project_kernel(
    tokens_ref, gain_ref, tail_ref, shard_ref, main_out, norm_far, proj_far, tail_out, tails_ref,
    kept, main, turned, norm_ref, proj_ref, out_sem, save_sem, load_sem, tail_ss, tail_rs, *sems
):
    z = lax.axis_index("z")
    rows, width = main.shape[1:]
    load = pltpu.make_async_copy(shard_ref.at[pl.ds(0, rows)], main.at[z], load_sem.at[0])
    load.start()
    greet_neighbours()
    steps = gather_steps([shard_ref], [main], (0,), True, sems)
    steps["begin"]()
    tails = [
        remote(tail_ref, tails_ref.at[z], tail_ss.at[o], tail_rs.at[o], {"z": ring("z", o)}) for o in (1, 3, 2)
    ]
    for copy in tails:
        copy.start()
    tails_ref[z] = tail_ref[...]

    def save(shard):
        return pltpu.make_async_copy(main.at[shard], main_out.at[shard], save_sem.at[shard])

    values = tokens_ref[...].astype(jnp.float32)
    scale = lax.rsqrt(jnp.mean(values * values, 1, keepdims=True) + NORM_EPS)
    normed = values * scale * gain_ref[...]
    norm_ref[...] = short(normed)
    save_norm = pltpu.make_async_copy(norm_ref, norm_far, out_sem.at[0])
    save_norm.start()
    kept[...] = short(normed.T)
    steps["first"]()
    block = PROJ_BLOCK

    def add(shard, fresh):
        right = kept[pl.ds(pl.multiple_of(shard * width, TILE), width)]

        def rows_at(j, carry):
            here = pl.ds(pl.multiple_of(j * block, block), block)
            product = dot32(main[shard, here], right)
            turned[here] = product if fresh else turned[here] + product
            return carry

        lax.fori_loop(0, rows // block, rows_at, 0)

    steps["second"]()
    load.wait()
    add(z, True)
    save(z).start()
    steps["deep"]()
    for copy in tails:
        copy.wait()
    total = dot32(tails_ref[0], kept[:width])
    for i in range(1, 4):
        total = total + dot32(tails_ref[i], kept[i * width : (i + 1) * width])
    tail_out[...] = total.T
    steps["forward"]()
    steps["core"]()
    for o in (1, 3):
        steps["arrived"](0, o)
        shard = steps["came_from"](o)
        save(shard).start()
        add(shard, False)
    steps["arrived"](0, 2)
    shard = steps["came_from"](2)
    save(shard).start()
    right = kept[pl.ds(pl.multiple_of(shard * width, TILE), width)]

    def save_block(j):
        here = pl.ds(pl.multiple_of(j * block, block), block)
        return pltpu.make_async_copy(proj_ref.at[:, here], proj_far.at[:, here], out_sem.at[1 + j])

    def last(j, carry):
        here = pl.ds(pl.multiple_of(j * block, block), block)
        proj_ref[:, here] = (turned[here] + dot32(main[shard, here], right)).T
        save_block(j).start()
        return carry

    lax.fori_loop(0, rows // block, last, 0)
    save_norm.wait()
    for j in range(rows // block):
        save_block(j).wait()
    steps["finish"]()
    for i in range(4):
        save(i).wait()


def project(tokens, gain, tail, shard, main_rows):
    slots, model = tokens.shape
    width = shard.shape[1]
    space, away = pl.BlockSpec(memory_space=pltpu.VMEM), pl.BlockSpec(memory_space=pl.ANY)
    sem = pltpu.SemaphoreType.DMA
    return pl.pallas_call(
        project_kernel,
        out_shape=(
            jax.ShapeDtypeStruct((4, main_rows, width), jnp.bfloat16),
            jax.ShapeDtypeStruct((slots, model), jnp.bfloat16),
            jax.ShapeDtypeStruct((slots, main_rows), jnp.float32),
            jax.ShapeDtypeStruct((slots, tail.shape[0]), jnp.float32),
            jax.ShapeDtypeStruct((4, *tail.shape), jnp.bfloat16),
        ),
        in_specs=[space, space, space, away],
        out_specs=(away, away, away, space, space),
        scratch_shapes=[
            pltpu.VMEM((model, slots), jnp.bfloat16),
            pltpu.VMEM((4, main_rows, width), jnp.bfloat16),
            pltpu.VMEM((main_rows, slots), jnp.float32),
            pltpu.VMEM((slots, model), jnp.bfloat16),
            pltpu.VMEM((slots, main_rows), jnp.float32),
            sem((1 + main_rows // PROJ_BLOCK,)),
            sem((4,)), sem((1,)), sem((4,)), sem((4,)),
        ]
        + gather_sems(1),
        compiler_params=pltpu.CompilerParams(
            collective_id=6, has_side_effects=True, vmem_limit_bytes=60 * 2**20
        ),
        name="project",
    )(tokens, gain, tail, shard)


TILE = 128
HIGH = lax.Precision.HIGHEST


def tile_at(j):
    return pl.ds(pl.multiple_of(j * TILE, TILE), TILE)


def dot_nt(left, right):
    return lax.dot_general(left, right, (((1,), (1,)), ((), ())), preferred_element_type=jnp.float32)


def short(values):
    return values.astype(jnp.bfloat16)


def lane_ids():
    return lax.broadcasted_iota(jnp.int32, (TILE, TILE), 1)


def row_ids():
    return lax.broadcasted_iota(jnp.int32, (TILE, TILE), 0)


def head_steps(tail_ref, heads_ref):
    raw = tail_ref[...] + heads_ref[1:2]
    used = lane_ids() < HEADS
    small = jnp.exp(-jnp.abs(raw))
    tail = jnp.where(small < 1e-3, small * (1.0 - small * (0.5 - small / 3.0)), jnp.log(1.0 + small))
    soft = jnp.maximum(raw, 0.0) + tail
    step = jnp.where(used, soft, 0.0)
    return raw, step, jnp.where(used, -jnp.exp(heads_ref[0:1]) * step, 0.0)


def head_columns(values, pair):
    moved = pltpu.roll(values, lax.rem(TILE - 2 * pair, TILE), 1)
    return moved[:, 0:1], moved[:, 1:2]


def both_heads(columns):
    return jnp.where(lane_ids() < TILE // 2, columns[0], columns[1])


def taps_of(ext, cw_ref, lanes):
    summed = cw_ref[4:5, lanes]
    for k in range(4):
        summed = summed + cw_ref[k : k + 1, lanes] * ext[5 + k : 5 + k + TILE]
    return summed


def fill_ext(ext, halo_ref, proj_ref, j):
    ext[0:8] = halo_ref[:, tile_at(j)]
    ext[8 : 8 + TILE] = proj_ref[:, pl.ds(pl.multiple_of(INNER + j * TILE, TILE), TILE)]


def mixer_in_part(ticks, halo_copy, proj_ref, tail_ref, halo_ref, cw_ref, heads_ref, mixed_ref, state_ref, totals_ref, run_ref, step_ref, ext):
    unused_raw, step, log_decay = head_steps(tail_ref, heads_ref)
    lower = (row_ids() >= lane_ids()).astype(jnp.float32)
    run = jnp.dot(lower, log_decay, precision=HIGH, preferred_element_type=jnp.float32)
    run_ref[...] = run
    step_ref[...] = step
    last = run[TILE - 1 : TILE]
    totals_ref[...] = jnp.broadcast_to(last, totals_ref.shape)
    weight = jnp.exp(last - run) * step

    halo_copy.wait()
    ticks[0]()
    spot = lax.axis_index("x") * 8 + lax.axis_index("y") * 2 + lax.axis_index("c")

    @pl.when(spot == 0)
    def _():
        halo_ref[...] = jnp.zeros_like(halo_ref)

    def conv(j, carry):
        fill_ext(ext, halo_ref, proj_ref, j)
        u = taps_of(ext, cw_ref, tile_at(j))
        mixed_ref[:, tile_at(j)] = u * jax.nn.sigmoid(u)
        return carry

    lax.fori_loop(0, CONV // TILE, conv, 0)
    ticks[1]()
    in_map = short(mixed_ref[:, INNER : INNER + TILE])

    def state(p, carry):
        scaled = mixed_ref[:, tile_at(p)] * both_heads(head_columns(weight, p))
        state_ref[pl.ds(4 * p, 4)] = short(dot32(short(scaled.T), in_map)).reshape(4, 32, TILE)
        return carry

    lax.fori_loop(0, HEADS // 2, state, 0, unroll=2)


def decays_of(column, row, lower):
    return jnp.where(lower, jnp.exp(jnp.minimum(column - row, 0.0)), 0.0)


def mixer_out_part(proj_ref, mixed_ref, run_ref, step_ref, carried_ref, wide_ref, normed_ref, scanned_ref, gated, rows):
    run = run_ref[...]
    rows[0] = run.T
    rows[1] = step_ref[...].T
    lower = row_ids() >= lane_ids()
    in_map = mixed_ref[:, INNER : INNER + TILE]
    out_map = mixed_ref[:, INNER + TILE : INNER + 2 * TILE]
    kernel = lax.dot_general(out_map, in_map, (((1,), (1,)), ((), ())), precision=HIGH, preferred_element_type=jnp.float32)
    out_low = short(out_map)

    def pair(p, squares):
        values = mixed_ref[:, tile_at(p)]
        values_low = short(values)
        columns = head_columns(run, p)
        parts = []
        for h in range(2):
            decays = decays_of(columns[h], rows[0, pl.ds(2 * p + h, 1)], lower)
            weights = kernel * decays * rows[1, pl.ds(2 * p + h, 1)]
            parts.append(dot32(short(weights), values_low))
        result = jnp.where(lane_ids() < TILE // 2, parts[0], parts[1])
        result = result + jnp.exp(both_heads(columns)) * dot_nt(out_low, carried_ref[pl.ds(4 * p, 4)].reshape(TILE, TILE))
        result = result + wide_ref[0:1, tile_at(p)] * values
        scanned_ref[:, tile_at(p)] = result
        gate = proj_ref[:, tile_at(p)]
        g = result * (gate * jax.nn.sigmoid(gate))
        gated[:, tile_at(p)] = g
        return squares + g * g

    squares = lax.fori_loop(0, HEADS // 2, pair, jnp.zeros((TILE, TILE), jnp.float32), unroll=2)
    scale = lax.rsqrt(jnp.sum(squares, 1, keepdims=True) / INNER + NORM_EPS)

    def norm(p, carry):
        normed_ref[:, tile_at(p)] = short(gated[:, tile_at(p)] * scale * wide_ref[1:2, tile_at(p)])
        return carry

    lax.fori_loop(0, HEADS // 2, norm, 0, unroll=2)


def mixer_kernel(
    tail_ref, cw_ref, heads_ref, wide_ref, rows_ref, proj_far, *refs
):
    shards, refs = refs[:3], refs[3:]
    (mixed_far, totals_ref, run_ref, step_ref, halo_ref, carried_far, normed_ref, scanned_far, all_rows), refs = refs[:9], refs[9:]
    fulls, refs = refs[:3], refs[3:]
    edge, state_ref, ext, gated, rows, mixed_ref, scanned_ref, carried_ref, proj_ref, proj_sem, halo_ss, halo_rs, load_sem, save_sem, out_sem, *refs = refs
    staged, refs = refs[:3], refs[3:]
    scan_refs, sems = refs[: len(scan_scratch())], refs[len(scan_scratch()) :]
    z = lax.axis_index("z")
    loads = [pltpu.make_async_copy(shards[n], staged[n], load_sem.at[n]) for n in range(3)]
    views = [
        ref.at[at : at + 64, columns]
        for columns in (slice(INNER, INNER + CONV), slice(0, INNER))
        for at in (0, 64)
        for ref in (proj_far, proj_ref)
    ]
    proj_loads = [pltpu.make_async_copy(views[2 * i], views[2 * i + 1], proj_sem.at[i]) for i in range(4)]
    for copy in proj_loads + loads:
        copy.start()
    greet_plane()
    proj_loads[0].wait()
    proj_loads[1].wait()
    edge[...] = proj_ref[TILE - 8 :, INNER : INNER + CONV]
    halo_copy = remote(edge, halo_ref, halo_ss.at[0], halo_rs.at[0], line_neighbour(True))
    halo_copy.start()
    steps = gather_steps(shards, fulls, (0,), False, sems)
    steps["begin"]()
    mixer_in_part((steps["first"], steps["second"]), halo_copy, proj_ref, tail_ref, halo_ref, cw_ref, heads_ref, mixed_ref, state_ref, totals_ref, run_ref, step_ref, ext)
    save_mixed = pltpu.make_async_copy(mixed_ref, mixed_far, out_sem.at[0])
    save_mixed.start()
    saves = []
    for n in range(3):
        loads[n].wait()
        total = shards[n].shape[0]
        saves.append(
            pltpu.make_async_copy(
                staged[n], fulls[n].at[pl.ds(pl.multiple_of(z * total, 16), total)], save_sem.at[n]
            )
        )
        saves[-1].start()

    def tick(n):
        if n == 0:
            steps["deep"]()
        if n == 2:
            steps["forward"]()
        if n == 3:
            steps["core"]()

    state_exchange(False, state_ref, totals_ref, rows_ref, carried_ref, all_rows, None, tick, *scan_refs)
    save_carried = pltpu.make_async_copy(carried_ref, carried_far, out_sem.at[2])
    save_carried.start()
    proj_loads[2].wait()
    proj_loads[3].wait()
    mixer_out_part(proj_ref, mixed_ref, run_ref, step_ref, carried_ref, wide_ref, normed_ref, scanned_ref, gated, rows)
    save_scanned = pltpu.make_async_copy(scanned_ref, scanned_far, out_sem.at[1])
    save_scanned.start()
    for n in range(3):
        saves[n].wait()
        for o in (1, 3, 2):
            steps["arrived"](n, o)
    steps["finish"]()
    save_mixed.wait()
    save_scanned.wait()
    save_carried.wait()


def mixer(projected, tail_values, taps, heads, wide, rows, shards):
    space, away = pl.BlockSpec(memory_space=pltpu.VMEM), pl.BlockSpec(memory_space=pl.ANY)
    f32, low, sem = jnp.float32, jnp.bfloat16, pltpu.SemaphoreType.DMA
    square = (TILE, TILE)
    outs = [
        ((TILE, CONV), f32), ((8, TILE), f32), (square, f32), (square, f32), ((8, CONV), f32),
        ((96, 32, TILE), low), ((TILE, INNER), low), ((TILE, INNER), f32), ((4, *rows.shape), low),
    ]
    fulls = [((4 * s.shape[0], s.shape[1]), low) for s in shards]
    return pl.pallas_call(
        mixer_kernel,
        out_shape=tuple(jax.ShapeDtypeStruct(s, d) for s, d in outs + fulls),
        in_specs=[space] * 5 + [away] * 4,
        out_specs=tuple(away if i in (0, 5, 7, 8) else space for i in range(len(outs))) + (away,) * 3,
        scratch_shapes=[
            pltpu.VMEM((8, CONV), f32),
            pltpu.VMEM((96, 32, TILE), low),
            pltpu.VMEM((TILE + 8, TILE), f32),
            pltpu.VMEM((TILE, INNER), f32),
            pltpu.VMEM((2, *square), f32),
            pltpu.VMEM((TILE, CONV), f32),
            pltpu.VMEM((TILE, INNER), f32),
            pltpu.VMEM((96, 32, TILE), low),
            pltpu.VMEM(projected.shape, f32),
            sem((4,)),
            sem((1,)), sem((1,)), sem((3,)), sem((3,)), sem((3,)),
            *[pltpu.VMEM(s.shape, s.dtype) for s in shards],
        ]
        + scan_scratch()
        + gather_sems(3),
        compiler_params=pltpu.CompilerParams(
            collective_id=1, has_side_effects=True, vmem_limit_bytes=60 * 2**20
        ),
        name="mixer",
    )(tail_values, taps, heads, wide, rows, projected, *shards)


def gate_back_part(tick, proj_ref, mixed_ref, scanned_ref, back_ref, run_ref, wide_ref, result_ref, gate_ref, gain_ref, state_ref, gated):
    run = run_ref[...]
    out_map = short(mixed_ref[:, INNER + TILE : INNER + 2 * TILE])

    def first(p, sums):
        gate = proj_ref[:, tile_at(p)]
        g = scanned_ref[:, tile_at(p)] * (gate * jax.nn.sigmoid(gate))
        gated[:, tile_at(p)] = g
        back = back_ref[:, tile_at(p)] * wide_ref[1:2, tile_at(p)]
        return sums[0] + g * g, sums[1] + g * back

    zero = jnp.zeros((TILE, TILE), jnp.float32)
    squares, products = lax.fori_loop(0, HEADS // 2, first, (zero, zero), unroll=2)
    scale = lax.rsqrt(jnp.sum(squares, 1, keepdims=True) / INNER + NORM_EPS)
    shift = jnp.sum(products, 1, keepdims=True) * scale * scale * scale / INNER

    tick()

    def second(p, carry):
        lanes = tile_at(p)
        gate = proj_ref[:, lanes]
        sig = jax.nn.sigmoid(gate)
        g = gated[:, lanes]
        back = back_ref[:, lanes]
        gain_ref[:, lanes] = jnp.broadcast_to(jnp.sum(back * g * scale, 0, keepdims=True), (8, TILE))
        g_back = back * wide_ref[1:2, lanes] * scale - g * shift
        result_back = g_back * (gate * sig)
        result_ref[:, lanes] = result_back
        gate_ref[:, lanes] = short(g_back * scanned_ref[:, lanes] * sig * (1.0 + gate * (1.0 - sig)))
        moved = result_back * jnp.exp(both_heads(head_columns(run, p)))
        state_ref[pl.ds(4 * p, 4)] = short(dot32(short(moved.T), out_map)).reshape(4, 32, TILE)
        return carry

    lax.fori_loop(0, HEADS // 2, second, 0, unroll=2)


def mixer_back_kernel(
    tail_ref, halo_ref, cw_ref, heads_ref, run_ref, step_ref, wide_ref, totals_ref, valid_ref, *refs
):
    away, refs = refs[:11], refs[11:]
    (rim_in_ref, taps_ref, step_back_ref, heads_back_ref, shared_in_ref, out_ref, shared_out_ref,
    gate_far, gain_ref, block_ref, conv_far,
    gate_ref, parts_sum, save_sem, result_ref, gated, rim_ref, rows, column_sums, row_sums, kernel_back, maps_back, mixed_back, ext, padded, left_in, left_both, rights, share_ss, share_rs,
    state_ref, leaving_ref, parts_in, rim_ss, rim_rs, load_sem, conv_ref), refs = refs[:37], refs[37:]
    here, refs = refs[:11], refs[11:]
    scan_refs, sum_scratch = refs[: len(scan_scratch())], refs[len(scan_scratch()) :]
    loads = [pltpu.make_async_copy(far, near, load_sem.at[i]) for i, (far, near) in enumerate(zip(away, here))]
    for copy in loads:
        copy.start()
    lefts_ref, acts_ref, mix_ref, up_ref, proj_ref, scanned_ref, back_ref, mixed_ref, parts_ref, carried_ref, base_ref = here
    greet_plane()
    for copy in loads[:4]:
        copy.wait()
    model = mix_ref.shape[1]
    plain = [acts_ref.shape[1] // RS_COLS, model // RS_COLS, model // RS_COLS]
    up_at = [0, RS_COUNTS[0] - plain[0], RS_COUNTS[0] + RS_COUNTS[1] - plain[0] - plain[1]]
    for part, ref in enumerate((acts_ref, mix_ref, mix_ref)):
        at, end = RS_FIRST[part] * RS_COLS, (RS_FIRST[part] + RS_COUNTS[part]) * RS_COLS
        rights[:TILE, at : at + ref.shape[1]] = ref[...]
        at = at + ref.shape[1]
        rights[:TILE, at:end] = up_ref[:, up_at[part] * RS_COLS : up_at[part] * RS_COLS + end - at]
    receive = share_factors(lefts_ref, left_in, left_both, rights, (share_ss, share_rs))

    def product(part, k):
        chunk = pl.ds(pl.multiple_of((RS_FIRST[part] + k) * RS_COLS, RS_COLS), RS_COLS)
        return dot32(left_both[2 * part + k // plain[part]], rights[:, chunk])

    def store(part, k, total):
        @pl.when(k < plain[part])
        def _():
            lanes = pl.ds(pl.multiple_of(k * RS_COLS, RS_COLS), RS_COLS)
            if part == 0:
                shared_in_ref[:, lanes] = total[:12]
            else:
                out_ref[12 * part - 12 : 12 * part, lanes] = total[:12]

        @pl.when(k >= plain[part])
        def _():
            lanes = pl.ds(pl.multiple_of((k - plain[part] + up_at[part]) * RS_COLS, RS_COLS), RS_COLS)
            shared_out_ref[:, lanes] = total[:8]

    sum_step, sum_finish = grad_sum_steps(sum_scratch, product, store)

    for copy in loads[4:8]:
        copy.wait()
    receive()
    sum_step(0)
    gate_back_part(
        lambda: sum_step(1), proj_ref, mixed_ref, scanned_ref, back_ref, run_ref, wide_ref, result_ref, gate_ref, gain_ref,
        state_ref, gated,
    )
    save_gate = pltpu.make_async_copy(gate_ref, gate_far, save_sem.at[0])
    save_gate.start()
    sum_step(2)
    loads[8].wait()
    def tick_scan(n):
        sum_step(3 + n)

    state_exchange(
        True, state_ref, totals_ref, parts_ref, leaving_ref, parts_in, parts_sum, tick_scan, *scan_refs
    )
    run, step = run_ref[...], step_ref[...]
    rows[0] = run.T
    rows[1] = step.T
    lanes_id, rows_id = lane_ids(), row_ids()
    lower = rows_id >= lanes_id
    left_half = lanes_id < TILE // 2
    half_line = lax.broadcasted_iota(jnp.int32, (1, TILE), 1) // (TILE // 2)
    in_map = mixed_ref[:, INNER : INNER + TILE]
    out_map = mixed_ref[:, INNER + TILE : INNER + 2 * TILE]
    kernel = lax.dot_general(out_map, in_map, (((1,), (1,)), ((), ())), precision=HIGH, preferred_element_type=jnp.float32)
    in_low, out_low = short(in_map), short(out_map)
    last = run[TILE - 1 : TILE]
    fade = jnp.exp(last - run)
    weight = fade * step
    column_sums[...] = jnp.zeros_like(column_sums)
    row_sums[...] = jnp.zeros_like(row_sums)
    kernel_back[...] = jnp.zeros_like(kernel_back)
    maps_back[...] = jnp.zeros_like(maps_back)

    loads[9].wait()
    loads[10].wait()
    block_ref[...] = short(jnp.where(valid_ref[...] > 0.0, base_ref[...] + parts_sum[...], 0.0))

    def pair(p, carry):
        @pl.when((lax.rem(p, 2) == 0) & (p < 20))
        def _():
            sum_step(7 + p // 2)

        lanes = tile_at(p)
        values, back = mixed_ref[:, lanes], result_ref[:, lanes]
        values_low, back_low = short(values), short(back)
        columns = head_columns(run, p)
        which = 2 * p + (rows_id >= TILE // 2).astype(jnp.int32)
        spread = (lanes_id == which).astype(jnp.bfloat16)
        parts = []
        for h in range(2):
            at = pl.ds(2 * p + h, 1)
            decays = decays_of(columns[h], rows[0, at], lower)
            plain = kernel * decays
            steps = rows[1, at]
            weights = plain * steps
            mine = jnp.where(left_half, back, 0.0) if h == 0 else jnp.where(left_half, 0.0, back)
            weights_back = dot_nt(short(mine), values_low)
            kernel_back[...] += weights_back * (decays * steps)
            loose = weights_back * plain
            pulled = short(loose * steps)
            column_sums[0] += dot32(pulled, (lanes_id == 2 * p + h).astype(jnp.bfloat16))
            row_sums[0, at] = jnp.sum(pulled.astype(jnp.float32), 0, keepdims=True)
            row_sums[1, at] = jnp.sum(loose, 0, keepdims=True)
            parts.append(dot32(short(weights.T), back_low))
        values_back = jnp.where(left_half, parts[0], parts[1]) + wide_ref[0:1, lanes] * back
        carried = carried_ref[pl.ds(4 * p, 4)].reshape(TILE, TILE)
        leaving = leaving_ref[pl.ds(4 * p, 4)].reshape(TILE, TILE)
        moved = back * jnp.exp(both_heads(columns))
        moved_low = short(moved)
        seen = dot_nt(out_low, carried)
        column_sums[0] += dot32(short(moved * seen), spread)
        maps_back[1] += dot32(moved_low, carried)
        weight_pair = both_heads(head_columns(weight, p))
        pulled_state = dot_nt(in_low, leaving)
        values_back = values_back + weight_pair * pulled_state
        maps_back[0] += dot32(short(values * weight_pair), leaving)
        column_sums[1] += dot32(short(values * pulled_state), spread)
        mixed_back[:, lanes] = values_back
        skip_part = jnp.sum(back * values, 0, keepdims=True)
        kept = jnp.sum(carried.astype(jnp.float32) * leaving.astype(jnp.float32), 1, keepdims=True)
        for h in range(2):
            half = slice(h * TILE // 2, (h + 1) * TILE // 2)
            row_sums[2, pl.ds(2 * p + h, 1)] = jnp.broadcast_to(
                jnp.sum(jnp.where(half_line == h, skip_part, 0.0), 1, keepdims=True), (1, TILE)
            )
            row_sums[3, pl.ds(2 * p + h, 1)] = jnp.broadcast_to(
                jnp.sum(kept[half], 0, keepdims=True), (1, TILE)
            )
        return carry

    lax.fori_loop(0, HEADS // 2, pair, 0)

    used = lanes_id < HEADS
    loose_columns = row_sums[1].T
    weight_back = column_sums[1]
    run_back = column_sums[0] - row_sums[0].T - weight * weight_back
    skip_back, decay_back = row_sums[2].T, row_sums[3].T
    last_back = jnp.sum(weight * weight_back, 0, keepdims=True) + jnp.exp(last) * decay_back[0:1]
    run_back = run_back + jnp.where(rows_id == TILE - 1, last_back, 0.0)
    upper = (lanes_id >= rows_id).astype(jnp.float32)
    log_back = jnp.dot(upper, run_back, precision=HIGH, preferred_element_type=jnp.float32)
    raw, unused_step, log_decay = head_steps(tail_ref, heads_ref)
    rate = jnp.exp(heads_ref[0:1])
    step_back = loose_columns + fade * weight_back - rate * log_back
    raw_back = jnp.where(used, step_back * jax.nn.sigmoid(raw), 0.0)
    step_back_ref[...] = raw_back
    rate_back = jnp.sum(jnp.where(used, log_back * log_decay, 0.0), 0, keepdims=True)
    bias_back = jnp.sum(raw_back, 0, keepdims=True)
    at_row = lax.broadcasted_iota(jnp.int32, (8, TILE), 0)
    heads_back_ref[...] = jnp.where(
        at_row == 0, rate_back, jnp.where(at_row == 1, bias_back, jnp.where(at_row == 2, skip_back[0:1], 0.0))
    )
    both = kernel_back[...]
    mixed_back[:, INNER : INNER + TILE] = maps_back[0] + dot32(short(both.T), out_low)
    mixed_back[:, INNER + TILE : INNER + 2 * TILE] = maps_back[1] + dot32(short(both), in_low)
    padded[0:8] = jnp.zeros((8, TILE), jnp.float32)
    padded[8 + TILE : 16 + TILE] = jnp.zeros((8, TILE), jnp.float32)

    def conv(j, carry):
        lanes = tile_at(j)
        fill_ext(ext, halo_ref, proj_ref, j)
        u = taps_of(ext, cw_ref, lanes)
        sig = jax.nn.sigmoid(u)
        back = mixed_back[:, lanes] * sig * (1.0 + u * (1.0 - sig))
        padded[8 : 8 + TILE] = back
        taps_ref[4:5, lanes] = jnp.sum(back, 0, keepdims=True)
        total = jnp.zeros((TILE, TILE), jnp.float32)
        rim = jnp.zeros((8, TILE), jnp.float32)
        for k in range(4):
            tap = cw_ref[k : k + 1, lanes]
            taps_ref[k : k + 1, lanes] = jnp.sum(back * ext[5 + k : 5 + k + TILE], 0, keepdims=True)
            total = total + tap * padded[11 - k : 11 - k + TILE]
            rim = rim + tap * padded[3 - k : 11 - k]
        conv_ref[:, lanes] = total
        rim_ref[:, lanes] = rim
        return carry

    lax.fori_loop(0, CONV // TILE, conv, 0)
    rim_copy = remote(rim_ref, rim_in_ref, rim_ss.at[0], rim_rs.at[0], line_neighbour(False))
    rim_copy.start()
    save_conv = pltpu.make_async_copy(conv_ref, conv_far, save_sem.at[1])
    save_conv.start()
    sum_finish()
    rim_copy.wait()
    save_gate.wait()
    save_conv.wait()
    spot = lax.axis_index("x") * 8 + lax.axis_index("y") * 2 + lax.axis_index("c")

    @pl.when(spot == 31)
    def _():
        rim_in_ref[...] = jnp.zeros_like(rim_in_ref)


def tile_call(kernel, outs, scratch, name, *args, collective=None, away=0, away_outs=()):
    space = pl.BlockSpec(memory_space=pltpu.VMEM)
    far = pl.BlockSpec(memory_space=pl.ANY)
    params = dict(vmem_limit_bytes=40 * 2**20)
    if collective is not None:
        params = dict(vmem_limit_bytes=60 * 2**20, collective_id=collective, has_side_effects=True)
    return pl.pallas_call(
        kernel,
        out_shape=tuple(jax.ShapeDtypeStruct(s, d) for s, d in outs),
        in_specs=[space] * (len(args) - away) + [far] * away,
        out_specs=tuple(far if i in away_outs else space for i in range(len(outs))),
        scratch_shapes=[pltpu.VMEM(s, jnp.float32) if isinstance(s, tuple) else s for s in scratch],
        compiler_params=pltpu.CompilerParams(**params),
        name=name,
    )(*args)


PROJ_BLOCK = 640


def local(
    tokens,
    cotangent,
    lengths,
    routes,
    norm_gain,
    w_in,
    conv_weight,
    conv_bias,
    a_log,
    dt_bias,
    skip_scale,
    gated_gain,
    w_out,
    post_gain,
    w_router,
    shared_in,
    shared_out,
    expert_in,
    expert_out,
):
    low = jnp.bfloat16
    tokens, cotangent, routes = tokens[0], cotangent[0], routes[0]
    slot_count, model_width = tokens.shape
    inner_width = gated_gain.shape[0]
    conv_width = conv_bias.shape[0]
    head_count = a_log.shape[0]
    tap_count = conv_weight.shape[0]
    expert_count = w_router.shape[1]
    residual = tokens.astype(jnp.float32)
    positions = lax.axis_index(SEQ) * slot_count + jnp.arange(slot_count)
    valid = positions < lengths[0]
    upstream_low = jnp.where(valid[:, None], cotangent, jnp.zeros_like(cotangent))
    upstream = upstream_low.astype(jnp.float32)
    main_rows = inner_width + conv_width
    turned = w_in.T
    tail_shard = jnp.concatenate(
        [
            turned[main_rows:],
            w_router.T,
            jnp.zeros((TILE - head_count - expert_count, turned.shape[1]), low),
        ],
        0,
    )
    full_in, first_norm, projected, tail_values, tails = project(
        tokens, norm_gain[None], tail_shard, turned, main_rows
    )
    full_router = jnp.swapaxes(tails[:, head_count : head_count + expert_count], 0, 1)
    full_router = full_router.reshape(expert_count, model_width)

    taps = jnp.concatenate([conv_weight, conv_bias[None], jnp.zeros((3, conv_width), jnp.float32)], 0)
    heads = jnp.pad(jnp.stack([a_log, dt_bias]), ((0, 6), (0, TILE - head_count)))
    wide = jnp.stack([jnp.repeat(skip_scale, inner_width // head_count), gated_gain])
    square = (TILE, TILE)
    mixed, totals, running, steps, halo, carried, normed_low, scanned, all_upstream, full_out, full_shared_in, full_shared_out = mixer(
        projected, tail_values, taps, heads, wide, upstream_low, [w_out, shared_in, shared_out]
    )
    chosen = jnp.any(routes[:, :, None] == jnp.arange(expert_count)[None, None, :], 1)
    middle, second_norm, base_out, shared_second, shared_hidden, shared_act_grad, all_rows, all_gates = middle_part(
        normed_low, tokens, post_gain[None], full_router, chosen.T.astype(jnp.float32), upstream_low,
        full_out, full_shared_in, full_shared_out,
    )
    rows = all_rows.reshape(-1, model_width)
    back_rows = all_upstream.reshape(-1, model_width)
    owned = expert_in.shape[0]
    first_owned = lax.axis_index("z") * owned
    gates = lax.dynamic_slice_in_dim(all_gates, first_owned, owned, 1)
    gates = jnp.swapaxes(gates, 0, 1).reshape(owned, -1)
    hidden_width = expert_out.shape[1]
    acts = jnp.einsum("td,edf->etf", rows, expert_in, preferred_element_type=jnp.float32)
    hidden = (jax.nn.silu(acts[..., :hidden_width]) * acts[..., hidden_width:]).astype(low)
    output = jnp.einsum("etf,efd->etd", hidden, expert_out, preferred_element_type=jnp.float32)
    output = output.astype(low).astype(jnp.float32)
    part = jnp.sum(gates[..., None] * output, 0).astype(low)
    back_wide = back_rows.astype(jnp.float32)
    picks = jnp.sum(output * back_wide[None], -1)
    out_grad = (gates[..., None] * back_wide[None]).astype(low)
    hidden_back = jnp.einsum("etd,efd->etf", out_grad, expert_out, preferred_element_type=jnp.float32)
    act_grad = glu_back(acts, hidden_back)
    back = jnp.einsum("etf,edf->td", act_grad, expert_in, preferred_element_type=jnp.float32).astype(low)
    picks = jnp.swapaxes(picks.reshape(owned, 4, slot_count), 0, 1)
    picks = jnp.pad(picks, ((0, 0), (0, 8 - owned), (0, 0)))
    expert_parts, middle_back, mix_low, grad_post_gain, router_back, normed_back = expert_sum(
        rows,
        act_grad,
        hidden,
        out_grad,
        back.reshape(4, slot_count, model_width),
        picks,
        middle,
        shared_second,
        upstream_low,
        second_norm,
        all_gates,
        jnp.pad(full_router, ((0, TILE - expert_count), (0, 0))),
        post_gain[None],
        full_out,
    )
    act_width = act_grad.shape[2]
    grad_expert_in = expert_parts[:, :, :act_width]
    grad_expert_out = expert_parts[:, :, act_width:].reshape(owned, 3, -1, model_width // 3)
    grad_expert_out = jnp.swapaxes(grad_expert_out, 1, 2).reshape(owned, -1, model_width)

    shared_width = full_shared_out.shape[0]
    early_lefts, late_lefts = tile_call(
        lefts_kernel,
        [((6, model_width, TILE), low), ((3, model_width, TILE), low)],
        [(inner_width, TILE), (model_width, TILE)],
        "lefts",
        first_norm, second_norm, normed_low, shared_hidden,
    )
    large = [
        early_lefts, shared_act_grad, mix_low, upstream_low, projected, scanned, normed_back, mixed,
        part.reshape(4, slot_count, model_width), carried, base_out,
    ]
    (
        rim_back, taps_back, steps_back, heads_back, shared_in_part, w_out_part, shared_out_part,
        gate_back, gain_back, block_out, conv_part,
    ) = tile_call(
        mixer_back_kernel,
        [
            ((8, conv_width), jnp.float32), ((8, conv_width), jnp.float32),
            (square, jnp.float32), ((8, TILE), jnp.float32), ((12, 2 * shared_width), jnp.float32),
            ((24, model_width), jnp.float32), ((8, model_width), jnp.float32),
            ((TILE, inner_width), low), ((8, inner_width), jnp.float32), ((TILE, model_width), low),
            ((TILE, conv_width), jnp.float32),
        ],
        [
            pltpu.VMEM((TILE, inner_width), low), (TILE, model_width), pltpu.SemaphoreType.DMA((2,)),
            (TILE, inner_width), (TILE, inner_width), (8, conv_width),
            (2, *square), (2, *square), (4, *square), square, (2, *square),
            (TILE, conv_width), (TILE + 8, TILE), (TILE + 16, TILE),
            *share_scratch(early_lefts),
            pltpu.VMEM((96, 32, TILE), low),
            pltpu.VMEM((96, 32, TILE), low),
            pltpu.VMEM((3, TILE, model_width), low),
            pltpu.SemaphoreType.DMA((1,)),
            pltpu.SemaphoreType.DMA((1,)),
            pltpu.SemaphoreType.DMA((11,)),
            (TILE, conv_width),
        ]
        + [pltpu.VMEM(a.shape, a.dtype) for a in large]
        + scan_scratch()
        + grad_sum_scratch(model_width),
        "mixer_back",
        tail_values, halo, taps, heads, running, steps, wide, totals,
        valid[:, None].astype(jnp.float32), *large,
        collective=7,
        away=len(large),
        away_outs=(7, 10),
    )
    w_in_part, small, grad_tokens = grad_sum(
        late_lefts, gate_back, conv_part, steps_back, rim_back, tokens, norm_gain[None], middle_back, tails,
        taps_back, gain_back, grad_post_gain, heads_back, router_back, full_in, w_in.shape[1]
    )
    owner = lax.axis_index(ALL)

    def owned_part(row, rows, start, width):
        size = width // 128
        return lax.dynamic_slice(small, (row, start + owner * size), (rows, size))

    return (
        block_out[None],
        grad_tokens[None],
        owned_part(6, 1, 0, model_width)[0],
        w_in_part,
        owned_part(0, 4, 0, conv_width),
        owned_part(4, 1, 0, conv_width)[0],
        small[7, :head_count],
        small[7, TILE : TILE + head_count],
        small[7, 2 * TILE : 2 * TILE + head_count],
        owned_part(5, 1, 0, inner_width)[0],
        w_out_part,
        owned_part(6, 1, model_width, model_width)[0],
        owned_part(0, 8, conv_width, model_width).T,
        shared_in_part,
        shared_out_part,
        grad_expert_in,
        grad_expert_out,
    )


def solution(mesh):
    split = Mesh(mesh.devices.reshape(4, 4, 2, 4), ALL)
    placed = (
        P("z", SEQ, None),
        P("z", SEQ, None),
        P("z"),
        P("z", SEQ, None),
        P(),
        P("z", None),
        P(),
        P(),
        P(),
        P(),
        P(),
        P(),
        P("z", None),
        P(),
        P("z", None),
        P("z", None),
        P("z", None),
        P("z", None, None),
        P("z", None, None),
    )
    return jax.shard_map(
        local,
        mesh=split,
        in_specs=placed,
        out_specs=(
            P("z", SEQ, None),
            P("z", SEQ, None),
            P(ALL),
            P(ALL, None),
            P(None, ALL),
            P(ALL),
            P(),
            P(),
            P(),
            P(ALL),
            P(ALL, None),
            P(ALL),
            P(ALL, None),
            P(ALL, None),
            P(ALL, None),
            P("z", SEQ, None),
            P("z", SEQ, None),
        ),
        check_vma=False,
    )
```

```python
import functools

import jax
import jax.numpy as jnp
from jax import lax
from jax.experimental import pallas as pl
from jax.experimental.pallas import tpu as pltpu
from jax.sharding import Mesh
from jax.sharding import PartitionSpec as P

SEQ = ("x", "y", "c")
ALL = ("x", "y", "c", "z")
NORM_EPS = 1e-05
HEADS = 48
INNER = 3072
CONV = 3328


def scaled_rows(values, gain_vector):
    return values * lax.rsqrt(jnp.mean(values * values, -1, keepdims=True) + NORM_EPS) * gain_vector


def glu_back(acts_pair, hidden_back):
    half_width = acts_pair.shape[-1] // 2
    gate_part = acts_pair[..., :half_width]
    up_part = acts_pair[..., half_width:]
    sigmoid_gate = jax.nn.sigmoid(gate_part)
    gate_grad = hidden_back * up_part * sigmoid_gate * (1.0 + gate_part * (1.0 - sigmoid_gate))
    up_grad = hidden_back * gate_part * sigmoid_gate
    return jnp.concatenate([gate_grad, up_grad], -1).astype(jnp.bfloat16)


MESH_ID = pl.DeviceIdType.MESH
RS_ORDERS = (("x", "y", "z"), ("y", "z", "x"), ("z", "x", "y"))
RS_COUNTS = (9, 9, 8)
RS_FIRST = (0, 9, 18)
RS_SLOTS = 26
RS_COLS = 256
RS_LAGS = (0, 2, 4, 6, 8)
RS_TIMES = max(RS_COUNTS) + RS_LAGS[-1]
NEIGHBOURS = [("c", 1)] + [(axis, o) for axis in ("x", "y", "z") for o in (1, 2, 3)]


def ring(axis, offset):
    size = lax.axis_size(axis)
    return lax.rem(lax.axis_index(axis) + offset + size, size)


def greet(targets):
    barrier = pltpu.get_barrier_semaphore()
    for target in targets:
        pl.semaphore_signal(barrier, inc=1, device_id=target, device_id_type=MESH_ID)
    pl.semaphore_wait(barrier, len(targets))


def greet_neighbours():
    greet([{axis: ring(axis, o)} for axis, o in NEIGHBOURS])


def remote(src, dst, send_sem, recv_sem, target):
    return pltpu.make_async_remote_copy(
        src_ref=src,
        dst_ref=dst,
        send_sem=send_sem,
        recv_sem=recv_sem,
        device_id=target,
        device_id_type=MESH_ID,
    )


def dot32(left, right):
    return jnp.dot(left, right, preferred_element_type=jnp.float32)


def grad_sum_scratch(rows):
    half, block, low = rows // 2, rows // 8, jnp.bfloat16
    sems = lambda *shape: [pltpu.SemaphoreType.DMA(shape)] * 2
    return [
        pltpu.VMEM((RS_SLOTS, half, RS_COLS), low),
        pltpu.VMEM((RS_SLOTS, 4, block // 2, RS_COLS), low),
        pltpu.VMEM((RS_SLOTS, 2, block // 2, RS_COLS), low),
        pltpu.VMEM((RS_SLOTS, 3, block // 4, RS_COLS), low),
        pltpu.VMEM((RS_SLOTS, 4, 16, RS_COLS), low),
        pltpu.VMEM((RS_SLOTS, 3, 16, RS_COLS), low),
        pltpu.VMEM((3, block // 4 + 8, RS_COLS), jnp.float32),
        *sems(RS_SLOTS, 4), *sems(RS_SLOTS, 2), *sems(RS_SLOTS, 3), *sems(RS_SLOTS, 3),
    ]


def share_factors(lefts_ref, left_in, left_both, rights, sems):
    me, half = lax.axis_index("c"), left_in.shape[1]
    copies = [
        remote(
            lefts_ref.at[:, pl.ds(pl.multiple_of((1 - me) * half, half), half)], left_in, sems[0].at[0], sems[1].at[0], {"c": 1 - me}
        ),
        remote(rights.at[:TILE], rights.at[TILE:], sems[0].at[1], sems[1].at[1], {"c": 1 - me}),
    ]
    for copy in copies:
        copy.start()

    def receive():
        left_both[:, :, :TILE] = lefts_ref[:, pl.ds(pl.multiple_of(me * half, half), half), :]
        for copy in copies:
            copy.wait()
        left_both[:, :, TILE:] = left_in[...]

    return receive


def share_scratch(lefts):
    count, rows, depth = lefts.shape
    return [
        pltpu.VMEM((count, rows // 2, depth), lefts.dtype),
        pltpu.VMEM((count, rows // 2, 2 * depth), lefts.dtype),
        pltpu.VMEM((2 * depth, RS_SLOTS * RS_COLS), lefts.dtype),
        pltpu.SemaphoreType.DMA((2,)),
        pltpu.SemaphoreType.DMA((2,)),
    ]


def grad_sum_steps(scratch, product, store):
    core_in, near, far, second_in, third_out, third_in, lines = scratch[:7]
    near_ss, near_rs, far_ss, far_rs, second_ss, second_rs, third_ss, third_rs = scratch[7:]
    half = core_in.shape[1]
    block = half // 4
    edge = block // 2
    small = block // 4
    unit = third_out.shape[2]
    kept = small // 4
    lines[...] = jnp.zeros_like(lines)

    def near_copies(part, k):
        slot = RS_FIRST[part] + k
        axis = RS_ORDERS[part][0]
        after, before, across = ring(axis, 1), ring(axis, -1), ring(axis, 2)
        plan = ((before, 0, before), (after, edge, after), (across, 0, after), (across, edge, before))
        return [
            remote(
                core_in.at[slot, pl.ds(which * block + offset, edge)], near.at[slot, n],
                near_ss.at[slot, n], near_rs.at[slot, n], {axis: target},
            )
            for n, (which, offset, target) in enumerate(plan)
        ]

    def far_copies(part, k):
        slot = RS_FIRST[part] + k
        axis = RS_ORDERS[part][0]
        return [
            remote(
                near.at[slot, 2 + n], far.at[slot, n],
                far_ss.at[slot, n], far_rs.at[slot, n], {axis: ring(axis, o)},
            )
            for n, o in enumerate((1, -1))
        ]

    def second_copies(part, k):
        slot = RS_FIRST[part] + k
        axis = RS_ORDERS[part][1]
        copies = []
        for o in (1, 2, 3):
            target = ring(axis, o)
            copies.append(
                remote(
                    near.at[slot, target // 2, pl.ds(lax.rem(target, 2) * small, small)],
                    second_in.at[slot, o - 1],
                    second_ss.at[slot, o - 1], second_rs.at[slot, o - 1], {axis: target},
                )
            )
        return copies

    def third_copies(part, k):
        slot = RS_FIRST[part] + k
        axis = RS_ORDERS[part][2]
        return [
            remote(
                third_out.at[slot, ring(axis, o)], third_in.at[slot, o - 1],
                third_ss.at[slot, o - 1], third_rs.at[slot, o - 1], {axis: ring(axis, o)},
            )
            for o in (1, 2, 3)
        ]

    def stage_near(part, k):
        core_in[RS_FIRST[part] + k] = product(part, k).astype(jnp.bfloat16)
        for copy in near_copies(part, k):
            copy.start()

    def load(ref, *where):
        return ref[where].astype(jnp.float32)

    def stage_far(part, k):
        slot = RS_FIRST[part] + k
        axis = RS_ORDERS[part][0]
        copies = near_copies(part, k)
        for n, (which, offset) in enumerate(((ring(axis, 1), 0), (ring(axis, -1), edge))):
            copies[2 + n].wait_recv()
            rows = pl.ds(pl.multiple_of(which * block + offset, edge), edge)
            near[slot, 2 + n] = (load(near, slot, 2 + n) + load(core_in, slot, rows)).astype(jnp.bfloat16)
        for copy in far_copies(part, k):
            copy.start()

    def stage_second(part, k):
        slot = RS_FIRST[part] + k
        me = lax.axis_index(RS_ORDERS[part][0])
        copies, far_in = near_copies(part, k), far_copies(part, k)
        for n in range(2):
            copies[n].wait_recv()
            far_in[n].wait_recv()
            rows = pl.ds(pl.multiple_of(me * block + n * edge, edge), edge)
            near[slot, n] = (
                load(near, slot, n) + load(far, slot, n) + load(core_in, slot, rows)
            ).astype(jnp.bfloat16)
        for copy in second_copies(part, k):
            copy.start()

    def stage_third(part, k):
        slot = RS_FIRST[part] + k
        me = lax.axis_index(RS_ORDERS[part][1])
        for copy in second_copies(part, k):
            copy.wait_recv()
        rows = pl.ds(pl.multiple_of(lax.rem(me, 2) * small, small), small)
        lines[part, :small] = load(near, slot, me // 2, rows) + (
            load(second_in, slot, 0) + load(second_in, slot, 1) + load(second_in, slot, 2)
        )
        for j in range(4):
            third_out[slot, j] = lines[part, kept * j : kept * j + unit].astype(jnp.bfloat16)
        for copy in third_copies(part, k):
            copy.start()

    def stage_last(part, k):
        slot = RS_FIRST[part] + k
        for copy in third_copies(part, k):
            copy.wait_recv()
        me = lax.axis_index(RS_ORDERS[part][2])
        total = load(third_out, slot, me) + (
            load(third_in, slot, 0) + load(third_in, slot, 1) + load(third_in, slot, 2)
        )
        store(part, k, total)

    stages = (stage_near, stage_far, stage_second, stage_third, stage_last)

    def step(t):
        for lag, stage in zip(RS_LAGS, stages):
            k = t - lag
            for count in sorted(set(RS_COUNTS)):
                @pl.when((k >= 0) & (k < count))
                def _():
                    for part in range(3):
                        if RS_COUNTS[part] == count:
                            stage(part, k)

    def finish():
        for part in range(3):
            def wait_sent(k, carry, part=part):
                for copies in (near_copies, far_copies, second_copies, third_copies):
                    for copy in copies(part, k):
                        copy.wait_send()
                return carry

            lax.fori_loop(0, RS_COUNTS[part], wait_sent, 0)

    return step, finish


def grad_sum_kernel(
    tail_back_ref, rim_ref, gain_ref, tail_ref, taps_ref, gated_gain_ref, post_ref, heads_ref, router_ref,
    main_ref, gate_far, conv_far, lefts_far, tokens_far, middle_far,
    out_ref, small_ref, tokens_back_far, *scratch
):
    gate_ref, conv_ref, lefts_ref, tokens_ref, middle_ref, load_sem, tokens_back_ref, save_sem, *scratch = scratch
    save = pltpu.make_async_copy(tokens_back_ref, tokens_back_far, save_sem.at[0])
    loads = [
        pltpu.make_async_copy(far, near, load_sem.at[i])
        for i, (far, near) in enumerate(
            zip((gate_far, conv_far, lefts_far, tokens_far, middle_far), (gate_ref, conv_ref, lefts_ref, tokens_ref, middle_ref))
        )
    ]
    for copy in loads:
        copy.start()
    *sum_scratch, left_in, left_both, back_ref, share_ss, share_rs, total, weights, weight_sem, pack, pack_in, pack_work, pack_others, pack_ss, pack_rs = scratch
    me_core = lax.axis_index("c")
    other = 1 - me_core
    blocks = main_ref.shape[1] // weights.shape[2]

    def fetch(j):
        rows = weights.shape[2]
        return [
            pltpu.make_async_copy(
                main_ref.at[i, pl.ds(pl.multiple_of(j * rows, 16), rows)],
                weights.at[lax.rem(j, 2), i],
                weight_sem.at[lax.rem(j, 2), i],
            )
            for i in range(4)
        ]

    for copy in fetch(0) + fetch(1):
        copy.start()
    greet_neighbours()
    inner, conv = gate_ref.shape[1], conv_ref.shape[1]
    for copy in loads[:3]:
        copy.wait()
    back_ref[:TILE, :inner] = gate_ref[...]
    back_ref[:TILE, inner : inner + conv] = short(conv_ref[...])
    rim = jnp.concatenate([jnp.zeros((8, conv), jnp.float32), rim_ref[...]], 0)
    back_ref[TILE - 16 : TILE, inner : inner + conv] = short(conv_ref[TILE - 16 :] + rim)
    back_ref[:TILE, inner + conv : inner + conv + TILE] = short(tail_back_ref[...])
    rest = back_ref.shape[1] - inner - conv - TILE
    back_ref[:TILE, inner + conv + TILE :] = jnp.zeros((TILE, rest), jnp.bfloat16)
    receive = share_factors(lefts_ref, left_in, left_both, back_ref, (share_ss, share_rs))
    taps_width, wide = taps_ref.shape[1], pack.shape[1] // 2

    def project_step(j):
        for copy in fetch(j):
            copy.wait()
        rows, width = weights.shape[2:]
        here = back_ref[:TILE, pl.ds(pl.multiple_of(j * rows, TILE), rows)]
        for i in range(4):
            total[:, i * width : (i + 1) * width] += dot32(here, weights[lax.rem(j, 2), i])

        @pl.when(j + 2 < blocks)
        def _():
            for copy in fetch(j + 2):
                copy.start()

    def project_end():
        for copy in loads[3:]:
            copy.wait()
        values = tokens_ref[...].astype(jnp.float32)
        scale = lax.rsqrt(jnp.mean(values * values, 1, keepdims=True) + NORM_EPS)
        back = total[...]
        spread = back * gain_ref[...]
        shift = jnp.mean(spread * values, 1, keepdims=True) * scale * scale * scale
        tokens_back_ref[...] = middle_ref[...] + spread * scale - values * shift
        save.start()
        model = tokens_ref.shape[1]
        pack[:, :taps_width] = taps_ref[...]
        pack[5:6, : gated_gain_ref.shape[1]] = gated_gain_ref[0:1]
        pack[6:7, :model] = jnp.sum(back * values * scale, 0, keepdims=True)
        pack[6:7, model : 2 * model] = post_ref[...]
        for i in range(3):
            pack[7:8, TILE * i : TILE * (i + 1)] = heads_ref[i : i + 1]
        pack[:, taps_width:] = router_ref[...]

    width = weights.shape[3]
    for i in range(4):
        total[:, i * width : (i + 1) * width] = dot32(short(tail_back_ref[...]), tail_ref[i])

    def pack_half(ref, which):
        return ref.at[:, pl.ds(pl.multiple_of(which * wide, 128), wide)]

    def pack_core(last):
        if last:
            return remote(pack_work.at[3], pack_half(small_ref, me_core), pack_ss.at[4, 0], pack_rs.at[4, 0], {"c": other})
        return remote(pack_half(pack, other), pack_in, pack_ss.at[0, 0], pack_rs.at[0, 0], {"c": other})

    def pack_copies(s):
        axis = ("x", "y", "z")[s - 1]
        return [
            remote(pack_work.at[s - 1], pack_others.at[s - 1, o - 1], pack_ss.at[s, o], pack_rs.at[s, o], {axis: ring(axis, o)})
            for o in (1, 2, 3)
        ]

    def pack_step(s):
        if s == 0:
            project_end()
            pack_core(False).start()
        if s == 1:
            pack_core(False).wait_recv()
            pack_work[0] = pack[:, pl.ds(pl.multiple_of(me_core * wide, 128), wide)] + pack_in[...]
        if s in (2, 3, 4):
            for copy in pack_copies(s - 1):
                copy.wait_recv()
            pack_work[s - 1] = pack_work[s - 2] + (
                pack_others[s - 2, 0] + pack_others[s - 2, 1] + pack_others[s - 2, 2]
            )
        if s in (1, 2, 3):
            for copy in pack_copies(s):
                copy.start()
        if s == 4:
            pack_core(True).start()
            small_ref[:, pl.ds(pl.multiple_of(me_core * wide, 128), wide)] = pack_work[3]
        if s == 5:
            pack_core(True).wait_recv()
            pack_core(True).wait_send()
            pack_core(False).wait_send()
            for n in (1, 2, 3):
                for copy in pack_copies(n):
                    copy.wait_send()

    def product(part, k):
        chunk = pl.ds(pl.multiple_of((RS_FIRST[part] + k) * RS_COLS, RS_COLS), RS_COLS)
        return dot32(left_both[part], back_ref[:, chunk])

    whole = out_ref.shape[1] // RS_COLS
    rows = out_ref.shape[0]

    def store(part, k, total):
        chunk = RS_FIRST[part] + k

        @pl.when(chunk < whole)
        def _():
            out_ref[:, pl.ds(pl.multiple_of(chunk * RS_COLS, RS_COLS), RS_COLS)] = total[:rows]

        if part == 2:
            @pl.when(chunk == whole)
            def _():
                out_ref[:, whole * RS_COLS :] = total[:rows, : out_ref.shape[1] - whole * RS_COLS]

    step, finish = grad_sum_steps(sum_scratch, product, store)
    receive()

    def run(t, carry):
        step(t)

        @pl.when(t < blocks)
        def _():
            project_step(t)

        for s in range(6):
            @pl.when(t == blocks + s)
            def _():
                pack_step(s)

        return carry

    lax.fori_loop(0, RS_TIMES, run, 0)
    finish()
    save.wait()


def grad_sum(lefts, gate, conv, tail_back, rim, tokens, gain, middle, tails, taps, gated_gain, post, heads, router, main, columns):
    rows = lefts.shape[1]
    wide = taps.shape[1] + router.shape[1]
    slots, model = tokens.shape
    space = pl.BlockSpec(memory_space=pltpu.VMEM)
    block = main.shape[1] // 5
    return pl.pallas_call(
        grad_sum_kernel,
        out_shape=(
            jax.ShapeDtypeStruct((rows // 128, columns), jnp.float32),
            jax.ShapeDtypeStruct((8, wide), jnp.float32),
            jax.ShapeDtypeStruct((slots, model), jnp.float32),
        ),
        in_specs=[space] * 9 + [pl.BlockSpec(memory_space=pl.ANY)] * 6,
        out_specs=(space, space, pl.BlockSpec(memory_space=pl.ANY)),
        scratch_shapes=[pltpu.VMEM(a.shape, a.dtype) for a in (gate, conv, lefts, tokens, middle)]
        + [pltpu.SemaphoreType.DMA((5,)), pltpu.VMEM((slots, model), jnp.float32), pltpu.SemaphoreType.DMA((1,))]
        + grad_sum_scratch(rows)
        + [
            *share_scratch(lefts),
            pltpu.VMEM((slots, model), jnp.float32),
            pltpu.VMEM((2, 4, block, main.shape[2]), jnp.bfloat16),
            pltpu.SemaphoreType.DMA((2, 4)),
            pltpu.VMEM((8, wide), jnp.float32),
            pltpu.VMEM((8, wide // 2), jnp.float32),
            pltpu.VMEM((4, 8, wide // 2), jnp.float32),
            pltpu.VMEM((3, 3, 8, wide // 2), jnp.float32),
            pltpu.SemaphoreType.DMA((5, 4)),
            pltpu.SemaphoreType.DMA((5, 4)),
        ],
        compiler_params=pltpu.CompilerParams(
            collective_id=0, has_side_effects=True, vmem_limit_bytes=60 * 2**20
        ),
        name="grad_sum",
    )(tail_back, rim, gain, tails, taps, gated_gain, post, heads, router, main, gate, conv, lefts, tokens, middle)


def owner_moves(order, stride, offset, rows):
    moves = []
    for to in range(128):
        digits = {"c": to // 64}
        for axis, at in zip(order, (to // 16 % 4, to // 4 % 4, to % 4)):
            digits[axis] = at
        owner = ((digits["x"] * 4 + digits["y"]) * 2 + digits["c"]) * 4 + digits["z"]
        source, target = owner * stride + offset, to * 12
        if moves and moves[-1][0] + moves[-1][2] == source and moves[-1][1] + moves[-1][2] == target:
            moves[-1][2] += rows
        else:
            moves.append([source, target, rows])
    return moves


def lefts_kernel(first_ref, second_ref, gated_ref, hidden_ref, early_ref, late_ref, turned, sorted_rows):
    def turn(ref):
        for j in range(ref.shape[1] // TILE):
            turned[j * TILE : (j + 1) * TILE] = ref[:, j * TILE : (j + 1) * TILE].astype(jnp.float32).T

    def place(out_ref, at, order, stride, offset, rows):
        if rows < 12:
            sorted_rows[...] = jnp.zeros_like(sorted_rows)
        for source, target, size in owner_moves(order, stride, offset, rows):
            sorted_rows[target : target + size] = turned[source : source + size]
        out_ref[at] = sorted_rows[...].astype(jnp.bfloat16)

    turn(first_ref)
    for part in range(3):
        place(late_ref, part, RS_ORDERS[part], 12, 0, 12)
    turn(second_ref)
    place(early_ref, 0, RS_ORDERS[0], 12, 0, 12)
    turn(hidden_ref)
    for at, part in ((1, 0), (3, 1), (5, 2)):
        place(early_ref, at, RS_ORDERS[part], 8, 0, 8)
    turn(gated_ref)
    place(early_ref, 2, RS_ORDERS[1], 24, 0, 12)
    place(early_ref, 4, RS_ORDERS[2], 24, 12, 12)


def plane_others():
    x, y = lax.axis_index("x"), lax.axis_index("y")
    found = []
    for dx in range(4):
        for dy in range(4):
            if dx + dy:
                tx, ty = lax.rem(x + dx, 4), lax.rem(y + dy, 4)
                found.append((dx * 4 + dy, tx * 4 + ty, {"x": tx, "y": ty}))
    return found


def line_neighbour(ahead):
    x, y, c = lax.axis_index("x"), lax.axis_index("y"), lax.axis_index("c")
    chip = lax.rem(x * 4 + y + (c if ahead else c + 15), 16)
    return {"x": chip // 4, "y": lax.rem(chip, 4), "c": 1 - c}


def greet_plane():
    c = lax.axis_index("c")
    chip = lax.rem(lax.axis_index("x") * 4 + lax.axis_index("y") + 2 * c + 15, 16)
    greet(
        [{"c": 1 - c}, {"x": chip // 4, "y": lax.rem(chip, 4), "c": 1 - c}]
        + [{"z": ring("z", o)} for o in (1, 2, 3)]
        + [where for unused, unused_too, where in plane_others()]
    )


def state_exchange(reverse, state_ref, totals_ref, rows_ref, out_ref, all_rows, rows_sum, tick, *refs):
    pair_in, pair_totals, outgoing, got, back, mine, hand, ps, pr, ss, rs, bs, br, zs, zr = refs
    x, y, c, z = (lax.axis_index(a) for a in ALL)
    chip = x * 4 + y
    half = pair_in.shape[0]
    groups, size = back.shape[1:3]
    others = plane_others()
    mine_at, theirs_at = c * half, (1 - c) * half

    def pair_copies():
        return [
            remote(state_ref.at[pl.ds(theirs_at, half)], pair_in, ps.at[0], pr.at[0], {"c": 1 - c}),
            remote(totals_ref, pair_totals, ps.at[1], pr.at[1], {"c": 1 - c}),
        ]

    def out_copy(at, target, where):
        return remote(outgoing.at[target], got.at[chip], ss.at[at], rs.at[at], where)

    def back_copy(at, target, where):
        return remote(back.at[target], mine.at[pl.ds(groups * chip, groups)], bs.at[at], br.at[at], where)

    def hand_copy():
        return remote(hand, out_ref.at[pl.ds(mine_at, half)], ps.at[2], pr.at[2], {"c": 1 - c})

    row_copies = []
    for o in (1, 3, 2):
        source = rows_ref.at[ring("z", o)] if reverse else rows_ref
        target = all_rows.at[o - 1] if reverse else all_rows.at[z]
        row_copies.append(remote(source, target, zs.at[o], zr.at[o], {"z": ring("z", o)}))
    for copy in pair_copies():
        copy.start()
    for copy in row_copies:
        copy.start()
    own_rows = None if reverse else pltpu.make_async_copy(rows_ref, all_rows.at[z], zs.at[0])
    if not reverse:
        own_rows.start()
    tick(0)
    for copy in pair_copies():
        copy.wait_recv()
    first = jnp.where(c == 0, totals_ref[...], pair_totals[...])
    second = jnp.where(c == 0, pair_totals[...], totals_ref[...])
    inner, outer = (first, second) if reverse else (second, first)
    lanes = lax.broadcasted_iota(jnp.int32, (8, TILE), 1) - c * (half // 2)

    def decay(logs, head):
        return jnp.exp(jnp.sum(jnp.where(lanes[: logs.shape[0]] == head, logs, 0.0), 1, keepdims=True))[:1]

    def states(g):
        own, other = state_ref[mine_at + g].astype(jnp.float32), pair_in[g].astype(jnp.float32)
        return jnp.where(c == 0, own, other), jnp.where(c == 0, other, own)

    total = (first + second)[:1]
    high = total.astype(jnp.bfloat16).astype(jnp.float32)
    middle = (total - high).astype(jnp.bfloat16).astype(jnp.float32)
    row = lax.broadcasted_iota(jnp.int32, (16, TILE), 0)
    split = jnp.where(row == 0, high, jnp.where(row == 1, middle, jnp.where(row == 2, total - high - middle, 0.0)))
    split = split.astype(jnp.bfloat16)

    def combine(m, carry):
        for i in range(groups):
            g = groups * m + i
            early, late = states(g)
            rate = decay(inner, g // 2)
            pair = early + rate * late if reverse else rate * early + late
            outgoing[m, i * size : (i + 1) * size] = pair.astype(jnp.bfloat16)
        outgoing[m, groups * size :] = split
        return carry

    lax.fori_loop(0, 16, combine, 0)
    for d in others:
        out_copy(*d).start()
    got[chip] = outgoing[chip]
    tick(1)
    for d in others:
        out_copy(*d).wait_recv()

    def advance(step, carried):
        p = 15 - step if reverse else step
        logs = jnp.sum(got[p, groups * size :].astype(jnp.float32), 0, keepdims=True)
        new = []
        for i in range(groups):
            back[p, i] = carried[i].astype(back.dtype)
            here = got[p, i * size : (i + 1) * size].astype(jnp.float32)
            new.append(carried[i] * decay(logs, (groups * chip + i) // 2) + here)
        return tuple(new)

    lax.fori_loop(0, 16, advance, (jnp.zeros((size, TILE), jnp.float32),) * groups)
    for d in others:
        back_copy(*d).start()
    mine[pl.ds(groups * chip, groups)] = back[chip]
    tick(2)
    for d in others:
        back_copy(*d).wait_recv()

    def spread(h, carry):
        rate = decay(outer, h)
        for i in range(2):
            g = 2 * h + i
            early, late = states(g)
            near = mine[g].astype(jnp.float32)
            beyond = rate * near + (late if reverse else early)
            swap = (c == 1) if reverse else (c == 0)
            out_ref[mine_at + g] = jnp.where(swap, near, beyond).astype(out_ref.dtype)
            hand[g] = jnp.where(swap, beyond, near).astype(hand.dtype)
        return carry

    lax.fori_loop(0, half // 2, spread, 0)
    hand_copy().start()
    tick(3)
    for copy in row_copies:
        copy.wait()
    if not reverse:
        own_rows.wait()
    if reverse:
        add_parts(rows_ref, z, all_rows, rows_sum)
    hand_copy().wait()
    for copy in pair_copies():
        copy.wait_send()
    for d in others:
        out_copy(*d).wait_send()
        back_copy(*d).wait_send()


def add_parts(ref, me, got, out):
    def rows_at(j, carry):
        rows = pl.ds(pl.multiple_of(j * 32, 32), 32)
        total = ref[me, rows].astype(jnp.float32)
        for o in range(3):
            total = total + got[o, rows].astype(jnp.float32)
        out[rows] = total
        return carry

    lax.fori_loop(0, out.shape[0] // 32, rows_at, 0)


def scan_scratch():
    low, sem = jnp.bfloat16, pltpu.SemaphoreType.DMA
    return [
        pltpu.VMEM((48, 32, TILE), low),
        pltpu.VMEM((8, TILE), jnp.float32),
        pltpu.VMEM((16, 112, TILE), low),
        pltpu.VMEM((16, 112, TILE), low),
        pltpu.VMEM((16, 3, 32, TILE), low),
        pltpu.VMEM((48, 32, TILE), low),
        pltpu.VMEM((48, 32, TILE), low),
        sem((3,)), sem((3,)), sem((16,)), sem((16,)), sem((16,)), sem((16,)), sem((4,)), sem((4,)),
    ]


def middle_kernel(
    normed_ref, tokens_ref, gain_ref, router_ref, chosen_ref, up_ref, out_far, in_far, down_far,
    *refs
):
    outs, refs = refs[:6], refs[6:]
    all_rows, all_gates, out_w, in_w, down_w, *refs = refs
    inside, refs = refs[:6], refs[6:]
    middle_ref, second_ref, base_ref, back_ref, hidden_ref, acts_ref = inside
    save_sem, load_sem, row_ss, row_rs, gate_ss, gate_rs = refs
    saves = [pltpu.make_async_copy(near, far, save_sem.at[i]) for i, (near, far) in enumerate(zip(inside, outs))]
    z = lax.axis_index("z")
    own_rows = pltpu.make_async_copy(second_ref, all_rows.at[z], save_sem.at[6])
    loads = []
    for far, near, parts in ((out_far, out_w, 4), (in_far, in_w, 3), (down_far, down_w, 2)):
        rows = near.shape[0] // parts
        for i in range(parts):
            here = pl.ds(i * rows, rows)
            loads.append(pltpu.make_async_copy(far.at[here], near.at[here], load_sem.at[len(loads)]))
    for copy in loads:
        copy.start()
    greet([{"z": ring("z", o)} for o in (1, 2, 3)])
    depth = normed_ref.shape[1] // 4
    middle = tokens_ref[...].astype(jnp.float32)
    for i in range(4):
        loads[i].wait()
        here = slice(i * depth, (i + 1) * depth)
        middle = middle + dot32(normed_ref[:, here], out_w[here])
    middle_ref[...] = middle
    saves[0].start()
    scale = lax.rsqrt(jnp.mean(middle * middle, 1, keepdims=True) + NORM_EPS)
    second_ref[...] = short(middle * scale * gain_ref[...])
    saves[1].start()
    own_rows.start()

    def row_copy(o):
        return remote(second_ref, all_rows.at[z], row_ss.at[o], row_rs.at[o], {"z": ring("z", o)})

    def row_forward(o):
        half = all_rows.shape[1] // 2
        block = all_rows.at[lax.rem(z + 4 - o, 4), pl.ds(0 if o == 1 else half, half)]
        return remote(block, block, row_ss.at[3 + o], row_rs.at[3 + o], {"z": ring("z", o)})

    def gate_copy(o):
        return remote(all_gates.at[z], all_gates.at[z], gate_ss.at[o], gate_rs.at[o], {"z": ring("z", o)})

    for o in (1, 3):
        row_copy(o).start()
    logits = dot_nt(router_ref[...], second_ref[...])
    masked = jnp.where(chosen_ref[...] > 0.0, logits, -jnp.inf)
    powers = jnp.exp(masked - jnp.max(masked, 0, keepdims=True))
    all_gates[z] = powers / jnp.sum(powers, 0, keepdims=True)
    for o in (1, 3, 2):
        gate_copy(o).start()
    width = hidden_ref.shape[1]
    block = 256
    for copy in loads[4:]:
        copy.wait()
    second = second_ref[...]
    for j in range(0, width, block):
        gate = dot32(second, in_w[:, j : j + block])
        up = dot32(second, in_w[:, width + j : width + j + block])
        sig = jax.nn.sigmoid(gate)
        hidden_ref[:, j : j + block] = short(gate * sig * up)
        back = dot_nt(up_ref[...], down_w[j : j + block])
        acts_ref[:, j : j + block] = short(back * up * sig * (1.0 + gate * (1.0 - sig)))
        acts_ref[:, width + j : width + j + block] = short(back * gate * sig)
    saves[4].start()
    saves[5].start()
    for o in (1, 3):
        row_copy(o).wait_recv()
        row_forward(o).start()
    model = middle_ref.shape[1]
    for j in range(0, model, 2 * block):
        here = slice(j, j + 2 * block)
        base_ref[:, here] = middle_ref[:, here] + dot32(hidden_ref[...], down_w[:, here])
        back_ref[:, here] = dot_nt(acts_ref[...], in_w[here])
    saves[2].start()
    saves[3].start()
    for o in (1, 3):
        row_copy(o).wait_send()
        row_forward(o).wait()
    for o in (1, 3, 2):
        gate_copy(o).wait()
    for copy in saves:
        copy.wait()
    own_rows.wait()


def middle_part(normed, tokens, gain, router, chosen, upstream, out_w, in_w, down_w):
    space, away = pl.BlockSpec(memory_space=pltpu.VMEM), pl.BlockSpec(memory_space=pl.ANY)
    slots, model = tokens.shape
    f32, low, sem = jnp.float32, jnp.bfloat16, pltpu.SemaphoreType.DMA
    outs = [
        ((slots, model), f32), ((slots, model), low), ((slots, model), f32), ((slots, model), f32),
        ((slots, down_w.shape[0]), low), ((slots, in_w.shape[1]), low), ((4, slots, model), low), ((4, *chosen.shape), f32),
    ]
    return pl.pallas_call(
        middle_kernel,
        out_shape=tuple(jax.ShapeDtypeStruct(s, d) for s, d in outs),
        in_specs=[space] * 6 + [away] * 3,
        out_specs=(away,) * 7 + (space,),
        scratch_shapes=[pltpu.VMEM(w.shape, w.dtype) for w in (out_w, in_w, down_w)]
        + [pltpu.VMEM(s, d) for s, d in outs[:6]]
        + [sem((7,)), sem((9,)), sem((7,)), sem((7,)), sem((4,)), sem((4,))],
        compiler_params=pltpu.CompilerParams(
            collective_id=5, has_side_effects=True, vmem_limit_bytes=60 * 2**20
        ),
        name="middle",
    )(normed, tokens, gain, router, chosen, upstream, out_w, in_w, down_w)


EXPERT_ORDERS = (("x", "y"), ("y", "x"))
EXPERT_STEPS = 6
EXPERT_COLS = 256


def expert_sum_kernel(
    picks_ref, gates_ref, gain_ref, back_far, *refs
):
    far, refs = refs[:9], refs[9:]
    weights_far, out_ref, middle_out, mix_out, post_back, router_back, normed_out, *refs = refs
    (middle_back, mix_ref, normed_back, back_ref), refs = refs[:4], refs[4:]
    near_refs, refs = refs[:9], refs[9:]
    rows_ref, acts_ref, hidden_ref, grads_ref, middle_ref, shared_ref, up_ref, second_ref, router_ref = near_refs
    expert_sum_body(
        list(zip(far, near_refs)),
        rows_ref, acts_ref, hidden_ref, grads_ref, back_ref, picks_ref,
        middle_ref, shared_ref, up_ref, second_ref, gates_ref, router_ref, gain_ref, weights_far,
        out_ref, middle_back, mix_ref, post_back, router_back, normed_back, back_far, middle_out, mix_out, normed_out, *refs,
    )


def expert_sum_body(
    far_near,
    rows_ref, acts_ref, hidden_ref, grads_ref, back_ref, picks_ref,
    middle_ref, shared_ref, up_ref, second_ref, gates_ref, router_ref, gain_ref, weights_far,
    out_ref, middle_back, mix_ref, post_back, router_back, normed_back, back_far, middle_out, mix_out, normed_out,
    stage_sem, save_sem, turned_mix, weights, load_sem, back_sum, picks_all,
    core_out, core_in, near, far, second_in, got, turned_rows, turned_hidden,
    core_ss, core_rs, near_ss, near_rs, far_ss, far_rs, second_ss, second_rs, zs, zr,
):
    me_core = lax.axis_index("c")
    me_z = lax.axis_index("z")
    other = 1 - me_core
    half = core_out.shape[2]
    block = half // 4
    edge = block // 2
    small = block // 4
    third = small // 3
    cols = EXPERT_COLS
    quarter = weights.shape[0] // 4
    loads = [
        pltpu.make_async_copy(weights_far.at[pl.ds(i * quarter, quarter)], weights.at[pl.ds(i * quarter, quarter)], load_sem.at[i])
        for i in range(4)
    ]
    staged = [pltpu.make_async_copy(far, here, stage_sem.at[i]) for i, (far, here) in enumerate(far_near)]
    staged.append(pltpu.make_async_copy(back_far, back_ref, stage_sem.at[9]))
    saves = [
        pltpu.make_async_copy(here, far, save_sem.at[i])
        for i, (here, far) in enumerate(((middle_back, middle_out), (mix_ref, mix_out), (normed_back, normed_out)))
    ]
    for copy in staged + loads:
        copy.start()
    greet_neighbours()

    sums = []
    for n, ref in enumerate((back_far,)):
        for o in (1, 3, 2):
            sums.append(
                remote(ref.at[ring("z", o)], got.at[n, o - 1], zs.at[n, o], zr.at[n, o], {"z": ring("z", o)})
            )
    for o in (1, 3, 2):
        sums.append(
            remote(picks_ref.at[ring("z", o)], picks_all.at[me_z], zs.at[2, o], zr.at[2, o], {"z": ring("z", o)})
        )
    for copy in sums:
        copy.start()
    picks_all[me_z] = picks_ref[me_z]
    for copy in staged[:4]:
        copy.wait()
    for j in range(rows_ref.shape[1] // TILE):
        turned_rows[j * TILE : (j + 1) * TILE] = rows_ref[:, j * TILE : (j + 1) * TILE].T
    for part in range(2):
        for j in range(hidden_ref.shape[2] // TILE):
            turned_hidden[part, j * TILE : (j + 1) * TILE] = hidden_ref[part, :, j * TILE : (j + 1) * TILE].T

    def plane_rows(part, which, load, size):
        blocks = []
        for j in range(4):
            for i in range(4):
                spot = (j * 4 + i if part == 0 else i * 4 + j) * 2 + which
                blocks.append(load(pl.ds(pl.multiple_of(spot * size, 16), size)))
        return jnp.concatenate(blocks, 0)

    def core_copy(part, k):
        slot = part * EXPERT_STEPS + k
        return remote(
            core_out.at[lax.rem(k, 2), part], core_in.at[slot],
            core_ss.at[slot], core_rs.at[slot], {"c": other},
        )

    def near_copies(part, k):
        slot = part * EXPERT_STEPS + k
        axis = EXPERT_ORDERS[part][0]
        after, before, across = ring(axis, 1), ring(axis, -1), ring(axis, 2)
        plan = ((before, 0, before), (after, edge, after), (across, 0, after), (across, edge, before))
        return [
            remote(
                core_in.at[slot, pl.ds(which * block + offset, edge)], near.at[slot, n],
                near_ss.at[slot, n], near_rs.at[slot, n], {axis: target},
            )
            for n, (which, offset, target) in enumerate(plan)
        ]

    def far_copies(part, k):
        slot = part * EXPERT_STEPS + k
        axis = EXPERT_ORDERS[part][0]
        return [
            remote(
                near.at[slot, 2 + n], far.at[slot, n],
                far_ss.at[slot, n], far_rs.at[slot, n], {axis: ring(axis, o)},
            )
            for n, o in enumerate((1, -1))
        ]

    def second_copies(part, k):
        slot = part * EXPERT_STEPS + k
        axis = EXPERT_ORDERS[part][1]
        copies = []
        for o in (1, 2, 3):
            target = ring(axis, o)
            copies.append(
                remote(
                    near.at[slot, target // 2, pl.ds(lax.rem(target, 2) * small, small)],
                    second_in.at[slot, o - 1],
                    second_ss.at[slot, o - 1], second_rs.at[slot, o - 1], {axis: target},
                )
            )
        return copies

    def load(ref, *where):
        return ref[where].astype(jnp.float32)

    def products(part, k, which_half, store):
        @pl.when(k < 4)
        def _():
            right = acts_ref[part, :, pl.ds(pl.multiple_of(k * cols, cols), cols)]

            left = plane_rows(part, which_half, lambda rows: turned_rows[rows], small)
            store(0, half, dot32(left, right))

        @pl.when(k >= 4)
        def _():
            left = plane_rows(part, which_half, lambda rows: turned_hidden[part, rows], third)
            for t in range(3):
                right = grads_ref[part, :, pl.ds(pl.multiple_of(t * 2 * cols + (k - 4) * cols, cols), cols)]
                product = dot32(left, right)
                for i in range(16):
                    store(i * small + t * third, third, product[i * third : (i + 1) * third])

    def stage_product(part, k):
        @pl.when(k >= 2)
        def _():
            core_copy(part, k - 2).wait_send()

        def store(at, size, value):
            core_out[lax.rem(k, 2), part, pl.ds(at, size), :] = value.astype(jnp.bfloat16)

        products(part, k, other, store)
        core_copy(part, k).start()

    def stage_near(part, k):
        slot = part * EXPERT_STEPS + k
        core_copy(part, k).wait_recv()

        def store(at, size, value):
            rows = pl.ds(at, size)
            core_in[slot, rows, :] = (value + load(core_in, slot, rows)).astype(jnp.bfloat16)

        products(part, k, me_core, store)
        for copy in near_copies(part, k):
            copy.start()

    def stage_far(part, k):
        slot = part * EXPERT_STEPS + k
        axis = EXPERT_ORDERS[part][0]
        copies = near_copies(part, k)
        for n, (which, offset) in enumerate(((ring(axis, 1), 0), (ring(axis, -1), edge))):
            copies[2 + n].wait_recv()
            rows = pl.ds(pl.multiple_of(which * block + offset, edge), edge)
            near[slot, 2 + n] = (load(near, slot, 2 + n) + load(core_in, slot, rows)).astype(jnp.bfloat16)
        for copy in far_copies(part, k):
            copy.start()

    def stage_second(part, k):
        slot = part * EXPERT_STEPS + k
        me = lax.axis_index(EXPERT_ORDERS[part][0])
        copies, far_in = near_copies(part, k), far_copies(part, k)
        for n in range(2):
            copies[n].wait_recv()
            far_in[n].wait_recv()
            rows = pl.ds(pl.multiple_of(me * block + n * edge, edge), edge)
            near[slot, n] = (
                load(near, slot, n) + load(far, slot, n) + load(core_in, slot, rows)
            ).astype(jnp.bfloat16)
        for copy in second_copies(part, k):
            copy.start()

    def stage_last(part, k):
        slot = part * EXPERT_STEPS + k
        me = lax.axis_index(EXPERT_ORDERS[part][1])
        for copy in second_copies(part, k):
            copy.wait_recv()
        rows = pl.ds(pl.multiple_of(lax.rem(me, 2) * small, small), small)
        out_ref[part, :, pl.ds(pl.multiple_of(k * cols, cols), cols)] = load(near, slot, me // 2, rows) + (
            load(second_in, slot, 0) + load(second_in, slot, 1) + load(second_in, slot, 2)
        )

    stages = (stage_product, stage_near, stage_far, stage_second, stage_last)

    def way_back():
        for copy in sums + staged[4:]:
            copy.wait()
        add_parts(back_ref, me_z, got.at[0], back_sum)
        gates = gates_ref[me_z]
        picked = jnp.concatenate([picks_all[i, 0:2] for i in range(4)], 0)
        logits_back = gates * (picked - jnp.sum(gates * picked, 0, keepdims=True))
        padded = jnp.concatenate([logits_back, jnp.zeros((TILE - 8, TILE), jnp.float32)], 0)
        router_back[...] = dot32(short(padded), second_ref[...])[:8]
        middle = middle_ref[...]
        scale = lax.rsqrt(jnp.mean(middle * middle, 1, keepdims=True) + NORM_EPS)
        back = shared_ref[...] + back_sum[...] + dot32(short(padded.T), router_ref[...])
        post_back[...] = jnp.sum(back * middle * scale, 0, keepdims=True)
        spread = back * gain_ref[...]
        shift = jnp.mean(spread * middle, 1, keepdims=True) * scale * scale * scale
        total = spread * scale - middle * shift + up_ref[...].astype(jnp.float32)
        middle_back[...] = total
        mix_ref[...] = short(total)
        saves[0].start()
        saves[1].start()
        turned_mix[...] = short(total.T)

    def way_back_rows(i):
        loads[i].wait()
        here = slice(i * quarter, (i + 1) * quarter)
        normed_back[:, here] = dot32(weights[here], turned_mix[...]).T
        if i == 3:
            saves[2].start()

    def step(t, carry):
        @pl.when(t == 4)
        def _():
            way_back()

        for i in range(4):
            @pl.when(t == 5 + i)
            def _():
                way_back_rows(i)

        for lag, stage in enumerate(stages):
            k = t - lag

            @pl.when((k >= 0) & (k < EXPERT_STEPS))
            def _():
                for part in range(2):
                    stage(part, k)

        return carry

    lax.fori_loop(0, EXPERT_STEPS + len(stages) - 1, step, 0)

    def finish(k, carry):
        for part in range(2):
            @pl.when(k >= EXPERT_STEPS - 2)
            def _():
                core_copy(part, k).wait_send()

            for copies in (near_copies, far_copies, second_copies):
                for copy in copies(part, k):
                    copy.wait_send()
        return carry

    lax.fori_loop(0, EXPERT_STEPS, finish, 0)
    for copy in saves:
        copy.wait()


def expert_sum(rows, acts, hidden, grads, back, picks, middle, shared, upstream, second, gates, router, gain, weights):
    slots, cols, half = 2 * EXPERT_STEPS, EXPERT_COLS, rows.shape[1] // 2
    block = half // 4
    low, f32 = jnp.bfloat16, jnp.float32
    sem = pltpu.SemaphoreType.DMA
    sems = lambda *shape: [sem(shape)] * 2
    space, away = pl.BlockSpec(memory_space=pltpu.VMEM), pl.BlockSpec(memory_space=pl.ANY)
    depth, model = middle.shape
    staged = [rows, acts, hidden, grads, middle, shared, upstream, second, router]
    outs = [
        ((2, block // 4, EXPERT_STEPS * cols), f32), ((depth, model), f32), ((depth, model), low),
        ((1, model), f32), ((8, model), f32), ((depth, weights.shape[0]), f32),
    ]
    return pl.pallas_call(
        expert_sum_kernel,
        out_shape=tuple(jax.ShapeDtypeStruct(s, d) for s, d in outs),
        in_specs=[space] * 3 + [away] * 11,
        out_specs=(space, away, away, space, space, away),
        scratch_shapes=[
            *[pltpu.VMEM(*outs[i]) for i in (1, 2, 5)],
            pltpu.VMEM(back.shape, back.dtype),
            *[pltpu.VMEM(a.shape, a.dtype) for a in staged],
            sem((10,)),
            sem((3,)),
            pltpu.VMEM((model, depth), low),
            pltpu.VMEM(weights.shape, low),
            sem((4,)),
            pltpu.VMEM((depth, model), f32),
            pltpu.VMEM(picks.shape, f32),
            pltpu.VMEM((2, 2, half, cols), low),
            pltpu.VMEM((slots, half, cols), low),
            pltpu.VMEM((slots, 4, block // 2, cols), low),
            pltpu.VMEM((slots, 2, block // 2, cols), low),
            pltpu.VMEM((slots, 3, block // 4, cols), low),
            pltpu.VMEM((1, 3, *back.shape[1:]), low),
            pltpu.VMEM(rows.shape[::-1], low),
            pltpu.VMEM((2, *hidden.shape[:0:-1]), low),
            *sems(slots), *sems(slots, 4), *sems(slots, 2), *sems(slots, 3), *sems(3, 4),
        ],
        compiler_params=pltpu.CompilerParams(
            collective_id=4, has_side_effects=True, vmem_limit_bytes=60 * 2**20
        ),
        name="expert_sum",
    )(picks, gates, gain, back, *staged, weights)


def gather_sems(count):
    sem = lambda *shape: [pltpu.SemaphoreType.DMA(shape)] * 2
    return sem(count, 4) + sem(count, 8) + sem(count, 4, 4) + sem(count, 4, 8) + sem(count, 4, 5)


def gather_steps(shards, fulls, by_rows, main, sems):
    unit_ss, unit_rs, deep_ss, deep_rs, first_ss, first_rs, second_ss, second_rs, core_ss, core_rs = sems
    x, y, c, z = (lax.axis_index(a) for a in ALL)
    first_at = (1 - c) * x + c * y
    second_at = c * x + (1 - c) * y

    def along_first(o):
        return {"x": lax.rem(x + (1 - c) * o, 4), "y": lax.rem(y + c * o, 4)}

    def along_second(o):
        return {"x": lax.rem(x + c * o, 4), "y": lax.rem(y + (1 - c) * o, 4)}

    def sizes(n):
        if main and n == 0:
            total = fulls[0].shape[1]
            spread = total * 16 // 25
            return total // 2, spread // 2, spread // 32
        total = shards[n].shape[0]
        spread = total if total % 384 else total * 2 // 3
        if n in by_rows:
            return total // 2, spread // 2, spread // 32
        return total, spread, spread // 16

    def place(n, deep, offset):
        total, spread, unit = sizes(n)
        if n in by_rows:
            return (2 * spread + c * (total - spread) if deep else c * spread) + offset
        return (spread if deep else 0) + offset

    def window(n, shard, deep, offset, length):
        rows, width = shards[n].shape
        at = place(n, deep, offset)
        if main and n == 0:
            return fulls[0].at[shard, pl.ds(pl.multiple_of(at, 16), length)]
        rows = pl.ds(pl.multiple_of(at + shard * rows, 16), length)
        if n in by_rows:
            return fulls[n].at[rows]
        return fulls[n].at[rows, pl.ds(pl.multiple_of(c * (width // 2), 128), width // 2)]

    def own_window(n, deep, offset, length):
        width = shards[n].shape[1]
        rows = pl.ds(pl.multiple_of(place(n, deep, offset), 16), length)
        if n in by_rows:
            return shards[n].at[rows]
        return shards[n].at[rows, pl.ds(pl.multiple_of(c * (width // 2), 128), width // 2)]

    def came_from(o):
        return lax.rem(z - o + 4, 4)

    def unit_copy(n, o):
        unit = sizes(n)[2]
        at = (second_at * 4 + first_at) * unit
        return remote(
            own_window(n, False, at, unit), window(n, z, False, at, unit), unit_ss.at[n, o], unit_rs.at[n, o], {"z": ring("z", o)}
        )

    def deep_copy(n, o):
        total, spread, unit = sizes(n)
        return remote(
            own_window(n, True, 0, total - spread), window(n, z, True, 0, total - spread),
            deep_ss.at[n, o], deep_rs.at[n, o], {"z": ring("z", o)},
        )

    def deep_forward(n, o):
        total, spread, unit = sizes(n)
        edge = (total - spread) // 2
        block = window(n, came_from(o), True, 0 if o == 1 else edge, edge)
        return remote(block, block, deep_ss.at[n, 3 + o], deep_rs.at[n, 3 + o], {"z": ring("z", o)})

    def first_copy(n, o, step):
        unit = sizes(n)[2]
        block = window(n, came_from(o), False, (second_at * 4 + first_at) * unit, unit)
        return remote(block, block, first_ss.at[n, o, step], first_rs.at[n, o, step], along_first(step))

    def second_copy(n, o, step):
        unit = sizes(n)[2]
        block = window(n, came_from(o), False, second_at * 4 * unit, 4 * unit)
        return remote(block, block, second_ss.at[n, o, step], second_rs.at[n, o, step], along_second(step))

    def second_forward(n, o, step):
        unit = sizes(n)[2]
        source = lax.rem(second_at + 4 - step, 4)
        at = source * 4 * unit + (0 if step == 1 else 2 * unit)
        block = window(n, came_from(o), False, at, 2 * unit)
        return remote(block, block, second_ss.at[n, o, 4 + step], second_rs.at[n, o, 4 + step], along_second(step))

    def core_copy(n, o, which):
        total, spread, unit = sizes(n)
        shard = came_from(o)
        if which == 4:
            block = window(n, shard, True, 0, total - spread)
        else:
            block = window(n, shard, False, lax.rem(second_at + 4 - which, 4) * 4 * unit, 4 * unit)
        return remote(block, block, core_ss.at[n, o, which], core_rs.at[n, o, which], {"c": 1 - c})

    def core_copies(n, o):
        return [core_copy(n, o, which) for which in ((0, 1, 3, 2, 4) if n in deep else (0, 1, 3, 2))]

    arrays = range(len(shards))
    deep = [n for n in arrays if sizes(n)[0] > sizes(n)[1]]
    sides, offsets = (1, 3), (1, 3, 2)

    def begin():
        for n in arrays:
            for o in offsets:
                unit_copy(n, o).start()
        for n in deep:
            for o in sides:
                deep_copy(n, o).start()

    def go_first():
        for n in arrays:
            for o in offsets:
                unit_copy(n, o).wait_recv()
                for step in offsets:
                    first_copy(n, o, step).start()

    def go_second():
        for n in arrays:
            for o in offsets:
                for step in offsets:
                    first_copy(n, o, step).wait_recv()
                for step in sides:
                    second_copy(n, o, step).start()
                core_copy(n, o, 0).start()

    def go_deep():
        for n in deep:
            for o in sides:
                deep_copy(n, o).wait_recv()
                deep_forward(n, o).start()
                core_copy(n, o, 4).start()

    def go_forward():
        for n in arrays:
            for o in offsets:
                for step in sides:
                    second_copy(n, o, step).wait_recv()
                    second_forward(n, o, step).start()
                    core_copy(n, o, step).start()

    def go_core():
        for n in arrays:
            for o in offsets:
                for step in sides:
                    second_forward(n, o, step).wait_recv()
                core_copy(n, o, 2).start()
            if n in deep:
                for o in sides:
                    deep_forward(n, o).wait_recv()
                core_copy(n, 2, 4).start()

    def arrived(n, o):
        for copy in core_copies(n, o):
            copy.wait_recv()

    def finish():
        for n in arrays:
            for o in offsets:
                for copy in core_copies(n, o):
                    copy.wait_send()
                unit_copy(n, o).wait_send()
                for step in offsets:
                    first_copy(n, o, step).wait_send()
                for step in sides:
                    second_copy(n, o, step).wait_send()
                    second_forward(n, o, step).wait_send()
            if n in deep:
                for o in sides:
                    deep_copy(n, o).wait_send()
                    deep_forward(n, o).wait_send()

    return dict(
        begin=begin, first=go_first, second=go_second, deep=go_deep, forward=go_forward, core=go_core,
        arrived=arrived, finish=finish, came_from=came_from,
    )


def project_kernel(
    tokens_ref, gain_ref, tail_ref, shard_ref, main_out, norm_far, proj_far, tail_out, tails_ref,
    kept, main, turned, norm_ref, proj_ref, out_sem, save_sem, load_sem, tail_ss, tail_rs, *sems
):
    z = lax.axis_index("z")
    rows, width = main.shape[1:]
    load = pltpu.make_async_copy(shard_ref.at[pl.ds(0, rows)], main.at[z], load_sem.at[0])
    load.start()
    greet_neighbours()
    steps = gather_steps([shard_ref], [main], (0,), True, sems)
    steps["begin"]()
    tails = [
        remote(tail_ref, tails_ref.at[z], tail_ss.at[o], tail_rs.at[o], {"z": ring("z", o)}) for o in (1, 3, 2)
    ]
    for copy in tails:
        copy.start()
    tails_ref[z] = tail_ref[...]

    def save(shard):
        return pltpu.make_async_copy(main.at[shard], main_out.at[shard], save_sem.at[shard])

    values = tokens_ref[...].astype(jnp.float32)
    scale = lax.rsqrt(jnp.mean(values * values, 1, keepdims=True) + NORM_EPS)
    normed = values * scale * gain_ref[...]
    norm_ref[...] = short(normed)
    save_norm = pltpu.make_async_copy(norm_ref, norm_far, out_sem.at[0])
    save_norm.start()
    kept[...] = short(normed.T)
    steps["first"]()
    block = PROJ_BLOCK

    def add(shard, fresh):
        right = kept[pl.ds(pl.multiple_of(shard * width, TILE), width)]

        def rows_at(j, carry):
            here = pl.ds(pl.multiple_of(j * block, block), block)
            product = dot32(main[shard, here], right)
            turned[here] = product if fresh else turned[here] + product
            return carry

        lax.fori_loop(0, rows // block, rows_at, 0)

    steps["second"]()
    load.wait()
    add(z, True)
    save(z).start()
    steps["deep"]()
    for copy in tails:
        copy.wait()
    total = dot32(tails_ref[0], kept[:width])
    for i in range(1, 4):
        total = total + dot32(tails_ref[i], kept[i * width : (i + 1) * width])
    tail_out[...] = total.T
    steps["forward"]()
    steps["core"]()
    for o in (1, 3):
        steps["arrived"](0, o)
        shard = steps["came_from"](o)
        save(shard).start()
        add(shard, False)
    steps["arrived"](0, 2)
    shard = steps["came_from"](2)
    save(shard).start()
    right = kept[pl.ds(pl.multiple_of(shard * width, TILE), width)]

    def save_block(j):
        here = pl.ds(pl.multiple_of(j * block, block), block)
        return pltpu.make_async_copy(proj_ref.at[:, here], proj_far.at[:, here], out_sem.at[1 + j])

    def last(j, carry):
        here = pl.ds(pl.multiple_of(j * block, block), block)
        proj_ref[:, here] = (turned[here] + dot32(main[shard, here], right)).T
        save_block(j).start()
        return carry

    lax.fori_loop(0, rows // block, last, 0)
    save_norm.wait()
    for j in range(rows // block):
        save_block(j).wait()
    steps["finish"]()
    for i in range(4):
        save(i).wait()


def project(tokens, gain, tail, shard, main_rows):
    slots, model = tokens.shape
    width = shard.shape[1]
    space, away = pl.BlockSpec(memory_space=pltpu.VMEM), pl.BlockSpec(memory_space=pl.ANY)
    sem = pltpu.SemaphoreType.DMA
    return pl.pallas_call(
        project_kernel,
        out_shape=(
            jax.ShapeDtypeStruct((4, main_rows, width), jnp.bfloat16),
            jax.ShapeDtypeStruct((slots, model), jnp.bfloat16),
            jax.ShapeDtypeStruct((slots, main_rows), jnp.float32),
            jax.ShapeDtypeStruct((slots, tail.shape[0]), jnp.float32),
            jax.ShapeDtypeStruct((4, *tail.shape), jnp.bfloat16),
        ),
        in_specs=[space, space, space, away],
        out_specs=(away, away, away, space, space),
        scratch_shapes=[
            pltpu.VMEM((model, slots), jnp.bfloat16),
            pltpu.VMEM((4, main_rows, width), jnp.bfloat16),
            pltpu.VMEM((main_rows, slots), jnp.float32),
            pltpu.VMEM((slots, model), jnp.bfloat16),
            pltpu.VMEM((slots, main_rows), jnp.float32),
            sem((1 + main_rows // PROJ_BLOCK,)),
            sem((4,)), sem((1,)), sem((4,)), sem((4,)),
        ]
        + gather_sems(1),
        compiler_params=pltpu.CompilerParams(
            collective_id=6, has_side_effects=True, vmem_limit_bytes=60 * 2**20
        ),
        name="project",
    )(tokens, gain, tail, shard)


TILE = 128
HIGH = lax.Precision.HIGHEST


def tile_at(j):
    return pl.ds(pl.multiple_of(j * TILE, TILE), TILE)


def dot_nt(left, right):
    return lax.dot_general(left, right, (((1,), (1,)), ((), ())), preferred_element_type=jnp.float32)


def short(values):
    return values.astype(jnp.bfloat16)


def lane_ids():
    return lax.broadcasted_iota(jnp.int32, (TILE, TILE), 1)


def row_ids():
    return lax.broadcasted_iota(jnp.int32, (TILE, TILE), 0)


def head_steps(tail_ref, heads_ref):
    raw = tail_ref[...] + heads_ref[1:2]
    used = lane_ids() < HEADS
    small = jnp.exp(-jnp.abs(raw))
    tail = jnp.where(small < 1e-3, small * (1.0 - small * (0.5 - small / 3.0)), jnp.log(1.0 + small))
    soft = jnp.maximum(raw, 0.0) + tail
    step = jnp.where(used, soft, 0.0)
    return raw, step, jnp.where(used, -jnp.exp(heads_ref[0:1]) * step, 0.0)


def head_columns(values, pair):
    moved = pltpu.roll(values, lax.rem(TILE - 2 * pair, TILE), 1)
    return moved[:, 0:1], moved[:, 1:2]


def both_heads(columns):
    return jnp.where(lane_ids() < TILE // 2, columns[0], columns[1])


def taps_of(ext, cw_ref, lanes):
    summed = cw_ref[4:5, lanes]
    for k in range(4):
        summed = summed + cw_ref[k : k + 1, lanes] * ext[5 + k : 5 + k + TILE]
    return summed


def fill_ext(ext, halo_ref, proj_ref, j):
    ext[0:8] = halo_ref[:, tile_at(j)]
    ext[8 : 8 + TILE] = proj_ref[:, pl.ds(pl.multiple_of(INNER + j * TILE, TILE), TILE)]


def mixer_in_part(ticks, halo_copy, proj_ref, tail_ref, halo_ref, cw_ref, heads_ref, mixed_ref, state_ref, totals_ref, run_ref, step_ref, ext):
    unused_raw, step, log_decay = head_steps(tail_ref, heads_ref)
    lower = (row_ids() >= lane_ids()).astype(jnp.float32)
    run = jnp.dot(lower, log_decay, precision=HIGH, preferred_element_type=jnp.float32)
    run_ref[...] = run
    step_ref[...] = step
    last = run[TILE - 1 : TILE]
    totals_ref[...] = jnp.broadcast_to(last, totals_ref.shape)
    weight = jnp.exp(last - run) * step

    halo_copy.wait()
    ticks[0]()
    spot = lax.axis_index("x") * 8 + lax.axis_index("y") * 2 + lax.axis_index("c")

    @pl.when(spot == 0)
    def _():
        halo_ref[...] = jnp.zeros_like(halo_ref)

    def conv(j, carry):
        fill_ext(ext, halo_ref, proj_ref, j)
        u = taps_of(ext, cw_ref, tile_at(j))
        mixed_ref[:, tile_at(j)] = u * jax.nn.sigmoid(u)
        return carry

    lax.fori_loop(0, CONV // TILE, conv, 0)
    ticks[1]()
    in_map = short(mixed_ref[:, INNER : INNER + TILE])

    def state(p, carry):
        scaled = mixed_ref[:, tile_at(p)] * both_heads(head_columns(weight, p))
        state_ref[pl.ds(4 * p, 4)] = short(dot32(short(scaled.T), in_map)).reshape(4, 32, TILE)
        return carry

    lax.fori_loop(0, HEADS // 2, state, 0, unroll=2)


def decays_of(column, row, lower):
    return jnp.where(lower, jnp.exp(jnp.minimum(column - row, 0.0)), 0.0)


def mixer_out_part(proj_ref, mixed_ref, run_ref, step_ref, carried_ref, wide_ref, normed_ref, scanned_ref, gated, rows):
    run = run_ref[...]
    rows[0] = run.T
    rows[1] = step_ref[...].T
    lower = row_ids() >= lane_ids()
    in_map = mixed_ref[:, INNER : INNER + TILE]
    out_map = mixed_ref[:, INNER + TILE : INNER + 2 * TILE]
    kernel = lax.dot_general(out_map, in_map, (((1,), (1,)), ((), ())), precision=HIGH, preferred_element_type=jnp.float32)
    out_low = short(out_map)

    def pair(p, squares):
        values = mixed_ref[:, tile_at(p)]
        values_low = short(values)
        columns = head_columns(run, p)
        parts = []
        for h in range(2):
            decays = decays_of(columns[h], rows[0, pl.ds(2 * p + h, 1)], lower)
            weights = kernel * decays * rows[1, pl.ds(2 * p + h, 1)]
            parts.append(dot32(short(weights), values_low))
        result = jnp.where(lane_ids() < TILE // 2, parts[0], parts[1])
        result = result + jnp.exp(both_heads(columns)) * dot_nt(out_low, carried_ref[pl.ds(4 * p, 4)].reshape(TILE, TILE))
        result = result + wide_ref[0:1, tile_at(p)] * values
        scanned_ref[:, tile_at(p)] = result
        gate = proj_ref[:, tile_at(p)]
        g = result * (gate * jax.nn.sigmoid(gate))
        gated[:, tile_at(p)] = g
        return squares + g * g

    squares = lax.fori_loop(0, HEADS // 2, pair, jnp.zeros((TILE, TILE), jnp.float32), unroll=2)
    scale = lax.rsqrt(jnp.sum(squares, 1, keepdims=True) / INNER + NORM_EPS)

    def norm(p, carry):
        normed_ref[:, tile_at(p)] = short(gated[:, tile_at(p)] * scale * wide_ref[1:2, tile_at(p)])
        return carry

    lax.fori_loop(0, HEADS // 2, norm, 0, unroll=2)


def mixer_kernel(
    tail_ref, cw_ref, heads_ref, wide_ref, rows_ref, proj_far, *refs
):
    shards, refs = refs[:3], refs[3:]
    (mixed_far, totals_ref, run_ref, step_ref, halo_ref, carried_far, normed_ref, scanned_far, all_rows), refs = refs[:9], refs[9:]
    fulls, refs = refs[:3], refs[3:]
    edge, state_ref, ext, gated, rows, mixed_ref, scanned_ref, carried_ref, proj_ref, proj_sem, halo_ss, halo_rs, load_sem, save_sem, out_sem, *refs = refs
    staged, refs = refs[:3], refs[3:]
    scan_refs, sems = refs[: len(scan_scratch())], refs[len(scan_scratch()) :]
    z = lax.axis_index("z")
    loads = [pltpu.make_async_copy(shards[n], staged[n], load_sem.at[n]) for n in range(3)]
    views = [
        ref.at[at : at + 64, columns]
        for columns in (slice(INNER, INNER + CONV), slice(0, INNER))
        for at in (0, 64)
        for ref in (proj_far, proj_ref)
    ]
    proj_loads = [pltpu.make_async_copy(views[2 * i], views[2 * i + 1], proj_sem.at[i]) for i in range(4)]
    for copy in proj_loads + loads:
        copy.start()
    greet_plane()
    proj_loads[0].wait()
    proj_loads[1].wait()
    edge[...] = proj_ref[TILE - 8 :, INNER : INNER + CONV]
    halo_copy = remote(edge, halo_ref, halo_ss.at[0], halo_rs.at[0], line_neighbour(True))
    halo_copy.start()
    steps = gather_steps(shards, fulls, (0,), False, sems)
    steps["begin"]()
    mixer_in_part((steps["first"], steps["second"]), halo_copy, proj_ref, tail_ref, halo_ref, cw_ref, heads_ref, mixed_ref, state_ref, totals_ref, run_ref, step_ref, ext)
    save_mixed = pltpu.make_async_copy(mixed_ref, mixed_far, out_sem.at[0])
    save_mixed.start()
    saves = []
    for n in range(3):
        loads[n].wait()
        total = shards[n].shape[0]
        saves.append(
            pltpu.make_async_copy(
                staged[n], fulls[n].at[pl.ds(pl.multiple_of(z * total, 16), total)], save_sem.at[n]
            )
        )
        saves[-1].start()

    def tick(n):
        if n == 0:
            steps["deep"]()
        if n == 2:
            steps["forward"]()
        if n == 3:
            steps["core"]()

    state_exchange(False, state_ref, totals_ref, rows_ref, carried_ref, all_rows, None, tick, *scan_refs)
    save_carried = pltpu.make_async_copy(carried_ref, carried_far, out_sem.at[2])
    save_carried.start()
    proj_loads[2].wait()
    proj_loads[3].wait()
    mixer_out_part(proj_ref, mixed_ref, run_ref, step_ref, carried_ref, wide_ref, normed_ref, scanned_ref, gated, rows)
    save_scanned = pltpu.make_async_copy(scanned_ref, scanned_far, out_sem.at[1])
    save_scanned.start()
    for n in range(3):
        saves[n].wait()
        for o in (1, 3, 2):
            steps["arrived"](n, o)
    steps["finish"]()
    save_mixed.wait()
    save_scanned.wait()
    save_carried.wait()


def mixer(projected, tail_values, taps, heads, wide, rows, shards):
    space, away = pl.BlockSpec(memory_space=pltpu.VMEM), pl.BlockSpec(memory_space=pl.ANY)
    f32, low, sem = jnp.float32, jnp.bfloat16, pltpu.SemaphoreType.DMA
    square = (TILE, TILE)
    outs = [
        ((TILE, CONV), f32), ((8, TILE), f32), (square, f32), (square, f32), ((8, CONV), f32),
        ((96, 32, TILE), low), ((TILE, INNER), low), ((TILE, INNER), f32), ((4, *rows.shape), low),
    ]
    fulls = [((4 * s.shape[0], s.shape[1]), low) for s in shards]
    return pl.pallas_call(
        mixer_kernel,
        out_shape=tuple(jax.ShapeDtypeStruct(s, d) for s, d in outs + fulls),
        in_specs=[space] * 5 + [away] * 4,
        out_specs=tuple(away if i in (0, 5, 7, 8) else space for i in range(len(outs))) + (away,) * 3,
        scratch_shapes=[
            pltpu.VMEM((8, CONV), f32),
            pltpu.VMEM((96, 32, TILE), low),
            pltpu.VMEM((TILE + 8, TILE), f32),
            pltpu.VMEM((TILE, INNER), f32),
            pltpu.VMEM((2, *square), f32),
            pltpu.VMEM((TILE, CONV), f32),
            pltpu.VMEM((TILE, INNER), f32),
            pltpu.VMEM((96, 32, TILE), low),
            pltpu.VMEM(projected.shape, f32),
            sem((4,)),
            sem((1,)), sem((1,)), sem((3,)), sem((3,)), sem((3,)),
            *[pltpu.VMEM(s.shape, s.dtype) for s in shards],
        ]
        + scan_scratch()
        + gather_sems(3),
        compiler_params=pltpu.CompilerParams(
            collective_id=1, has_side_effects=True, vmem_limit_bytes=60 * 2**20
        ),
        name="mixer",
    )(tail_values, taps, heads, wide, rows, projected, *shards)


def gate_back_part(tick, proj_ref, mixed_ref, scanned_ref, back_ref, run_ref, wide_ref, result_ref, gate_ref, gain_ref, state_ref, gated):
    run = run_ref[...]
    out_map = short(mixed_ref[:, INNER + TILE : INNER + 2 * TILE])

    def first(p, sums):
        gate = proj_ref[:, tile_at(p)]
        g = scanned_ref[:, tile_at(p)] * (gate * jax.nn.sigmoid(gate))
        gated[:, tile_at(p)] = g
        back = back_ref[:, tile_at(p)] * wide_ref[1:2, tile_at(p)]
        return sums[0] + g * g, sums[1] + g * back

    zero = jnp.zeros((TILE, TILE), jnp.float32)
    squares, products = lax.fori_loop(0, HEADS // 2, first, (zero, zero), unroll=2)
    scale = lax.rsqrt(jnp.sum(squares, 1, keepdims=True) / INNER + NORM_EPS)
    shift = jnp.sum(products, 1, keepdims=True) * scale * scale * scale / INNER

    tick()

    def second(p, carry):
        lanes = tile_at(p)
        gate = proj_ref[:, lanes]
        sig = jax.nn.sigmoid(gate)
        g = gated[:, lanes]
        back = back_ref[:, lanes]
        gain_ref[:, lanes] = jnp.broadcast_to(jnp.sum(back * g * scale, 0, keepdims=True), (8, TILE))
        g_back = back * wide_ref[1:2, lanes] * scale - g * shift
        result_back = g_back * (gate * sig)
        result_ref[:, lanes] = result_back
        gate_ref[:, lanes] = short(g_back * scanned_ref[:, lanes] * sig * (1.0 + gate * (1.0 - sig)))
        moved = result_back * jnp.exp(both_heads(head_columns(run, p)))
        state_ref[pl.ds(4 * p, 4)] = short(dot32(short(moved.T), out_map)).reshape(4, 32, TILE)
        return carry

    lax.fori_loop(0, HEADS // 2, second, 0, unroll=2)


def mixer_back_kernel(
    tail_ref, halo_ref, cw_ref, heads_ref, run_ref, step_ref, wide_ref, totals_ref, valid_ref, *refs
):
    away, refs = refs[:11], refs[11:]
    (rim_in_ref, taps_ref, step_back_ref, heads_back_ref, shared_in_ref, out_ref, shared_out_ref,
    gate_far, gain_ref, block_ref, conv_far,
    gate_ref, parts_sum, save_sem, result_ref, gated, rim_ref, rows, column_sums, row_sums, kernel_back, maps_back, mixed_back, ext, padded, left_in, left_both, rights, share_ss, share_rs,
    state_ref, leaving_ref, parts_in, rim_ss, rim_rs, load_sem, conv_ref), refs = refs[:37], refs[37:]
    here, refs = refs[:11], refs[11:]
    scan_refs, sum_scratch = refs[: len(scan_scratch())], refs[len(scan_scratch()) :]
    loads = [pltpu.make_async_copy(far, near, load_sem.at[i]) for i, (far, near) in enumerate(zip(away, here))]
    for copy in loads:
        copy.start()
    lefts_ref, acts_ref, mix_ref, up_ref, proj_ref, scanned_ref, back_ref, mixed_ref, parts_ref, carried_ref, base_ref = here
    greet_plane()
    for copy in loads[:4]:
        copy.wait()
    model = mix_ref.shape[1]
    plain = [acts_ref.shape[1] // RS_COLS, model // RS_COLS, model // RS_COLS]
    up_at = [0, RS_COUNTS[0] - plain[0], RS_COUNTS[0] + RS_COUNTS[1] - plain[0] - plain[1]]
    for part, ref in enumerate((acts_ref, mix_ref, mix_ref)):
        at, end = RS_FIRST[part] * RS_COLS, (RS_FIRST[part] + RS_COUNTS[part]) * RS_COLS
        rights[:TILE, at : at + ref.shape[1]] = ref[...]
        at = at + ref.shape[1]
        rights[:TILE, at:end] = up_ref[:, up_at[part] * RS_COLS : up_at[part] * RS_COLS + end - at]
    receive = share_factors(lefts_ref, left_in, left_both, rights, (share_ss, share_rs))

    def product(part, k):
        chunk = pl.ds(pl.multiple_of((RS_FIRST[part] + k) * RS_COLS, RS_COLS), RS_COLS)
        return dot32(left_both[2 * part + k // plain[part]], rights[:, chunk])

    def store(part, k, total):
        @pl.when(k < plain[part])
        def _():
            lanes = pl.ds(pl.multiple_of(k * RS_COLS, RS_COLS), RS_COLS)
            if part == 0:
                shared_in_ref[:, lanes] = total[:12]
            else:
                out_ref[12 * part - 12 : 12 * part, lanes] = total[:12]

        @pl.when(k >= plain[part])
        def _():
            lanes = pl.ds(pl.multiple_of((k - plain[part] + up_at[part]) * RS_COLS, RS_COLS), RS_COLS)
            shared_out_ref[:, lanes] = total[:8]

    sum_step, sum_finish = grad_sum_steps(sum_scratch, product, store)

    for copy in loads[4:8]:
        copy.wait()
    receive()
    sum_step(0)
    gate_back_part(
        lambda: sum_step(1), proj_ref, mixed_ref, scanned_ref, back_ref, run_ref, wide_ref, result_ref, gate_ref, gain_ref,
        state_ref, gated,
    )
    save_gate = pltpu.make_async_copy(gate_ref, gate_far, save_sem.at[0])
    save_gate.start()
    sum_step(2)
    loads[8].wait()
    def tick_scan(n):
        sum_step(3 + n)

    state_exchange(
        True, state_ref, totals_ref, parts_ref, leaving_ref, parts_in, parts_sum, tick_scan, *scan_refs
    )
    run, step = run_ref[...], step_ref[...]
    rows[0] = run.T
    rows[1] = step.T
    lanes_id, rows_id = lane_ids(), row_ids()
    lower = rows_id >= lanes_id
    left_half = lanes_id < TILE // 2
    half_line = lax.broadcasted_iota(jnp.int32, (1, TILE), 1) // (TILE // 2)
    in_map = mixed_ref[:, INNER : INNER + TILE]
    out_map = mixed_ref[:, INNER + TILE : INNER + 2 * TILE]
    kernel = lax.dot_general(out_map, in_map, (((1,), (1,)), ((), ())), precision=HIGH, preferred_element_type=jnp.float32)
    in_low, out_low = short(in_map), short(out_map)
    last = run[TILE - 1 : TILE]
    fade = jnp.exp(last - run)
    weight = fade * step
    column_sums[...] = jnp.zeros_like(column_sums)
    row_sums[...] = jnp.zeros_like(row_sums)
    kernel_back[...] = jnp.zeros_like(kernel_back)
    maps_back[...] = jnp.zeros_like(maps_back)

    loads[9].wait()
    loads[10].wait()
    block_ref[...] = short(jnp.where(valid_ref[...] > 0.0, base_ref[...] + parts_sum[...], 0.0))

    def pair(p, carry):
        @pl.when((lax.rem(p, 2) == 0) & (p < 20))
        def _():
            sum_step(7 + p // 2)

        lanes = tile_at(p)
        values, back = mixed_ref[:, lanes], result_ref[:, lanes]
        values_low, back_low = short(values), short(back)
        columns = head_columns(run, p)
        which = 2 * p + (rows_id >= TILE // 2).astype(jnp.int32)
        spread = (lanes_id == which).astype(jnp.bfloat16)
        parts = []
        for h in range(2):
            at = pl.ds(2 * p + h, 1)
            decays = decays_of(columns[h], rows[0, at], lower)
            plain = kernel * decays
            steps = rows[1, at]
            weights = plain * steps
            mine = jnp.where(left_half, back, 0.0) if h == 0 else jnp.where(left_half, 0.0, back)
            weights_back = dot_nt(short(mine), values_low)
            kernel_back[...] += weights_back * (decays * steps)
            loose = weights_back * plain
            pulled = short(loose * steps)
            column_sums[0] += dot32(pulled, (lanes_id == 2 * p + h).astype(jnp.bfloat16))
            row_sums[0, at] = jnp.sum(pulled.astype(jnp.float32), 0, keepdims=True)
            row_sums[1, at] = jnp.sum(loose, 0, keepdims=True)
            parts.append(dot32(short(weights.T), back_low))
        values_back = jnp.where(left_half, parts[0], parts[1]) + wide_ref[0:1, lanes] * back
        carried = carried_ref[pl.ds(4 * p, 4)].reshape(TILE, TILE)
        leaving = leaving_ref[pl.ds(4 * p, 4)].reshape(TILE, TILE)
        moved = back * jnp.exp(both_heads(columns))
        moved_low = short(moved)
        seen = dot_nt(out_low, carried)
        column_sums[0] += dot32(short(moved * seen), spread)
        maps_back[1] += dot32(moved_low, carried)
        weight_pair = both_heads(head_columns(weight, p))
        pulled_state = dot_nt(in_low, leaving)
        values_back = values_back + weight_pair * pulled_state
        maps_back[0] += dot32(short(values * weight_pair), leaving)
        column_sums[1] += dot32(short(values * pulled_state), spread)
        mixed_back[:, lanes] = values_back
        skip_part = jnp.sum(back * values, 0, keepdims=True)
        kept = jnp.sum(carried.astype(jnp.float32) * leaving.astype(jnp.float32), 1, keepdims=True)
        for h in range(2):
            half = slice(h * TILE // 2, (h + 1) * TILE // 2)
            row_sums[2, pl.ds(2 * p + h, 1)] = jnp.broadcast_to(
                jnp.sum(jnp.where(half_line == h, skip_part, 0.0), 1, keepdims=True), (1, TILE)
            )
            row_sums[3, pl.ds(2 * p + h, 1)] = jnp.broadcast_to(
                jnp.sum(kept[half], 0, keepdims=True), (1, TILE)
            )
        return carry

    lax.fori_loop(0, HEADS // 2, pair, 0)

    used = lanes_id < HEADS
    loose_columns = row_sums[1].T
    weight_back = column_sums[1]
    run_back = column_sums[0] - row_sums[0].T - weight * weight_back
    skip_back, decay_back = row_sums[2].T, row_sums[3].T
    last_back = jnp.sum(weight * weight_back, 0, keepdims=True) + jnp.exp(last) * decay_back[0:1]
    run_back = run_back + jnp.where(rows_id == TILE - 1, last_back, 0.0)
    upper = (lanes_id >= rows_id).astype(jnp.float32)
    log_back = jnp.dot(upper, run_back, precision=HIGH, preferred_element_type=jnp.float32)
    raw, unused_step, log_decay = head_steps(tail_ref, heads_ref)
    rate = jnp.exp(heads_ref[0:1])
    step_back = loose_columns + fade * weight_back - rate * log_back
    raw_back = jnp.where(used, step_back * jax.nn.sigmoid(raw), 0.0)
    step_back_ref[...] = raw_back
    rate_back = jnp.sum(jnp.where(used, log_back * log_decay, 0.0), 0, keepdims=True)
    bias_back = jnp.sum(raw_back, 0, keepdims=True)
    at_row = lax.broadcasted_iota(jnp.int32, (8, TILE), 0)
    heads_back_ref[...] = jnp.where(
        at_row == 0, rate_back, jnp.where(at_row == 1, bias_back, jnp.where(at_row == 2, skip_back[0:1], 0.0))
    )
    both = kernel_back[...]
    mixed_back[:, INNER : INNER + TILE] = maps_back[0] + dot32(short(both.T), out_low)
    mixed_back[:, INNER + TILE : INNER + 2 * TILE] = maps_back[1] + dot32(short(both), in_low)
    padded[0:8] = jnp.zeros((8, TILE), jnp.float32)
    padded[8 + TILE : 16 + TILE] = jnp.zeros((8, TILE), jnp.float32)

    def conv(j, carry):
        lanes = tile_at(j)
        fill_ext(ext, halo_ref, proj_ref, j)
        u = taps_of(ext, cw_ref, lanes)
        sig = jax.nn.sigmoid(u)
        back = mixed_back[:, lanes] * sig * (1.0 + u * (1.0 - sig))
        padded[8 : 8 + TILE] = back
        taps_ref[4:5, lanes] = jnp.sum(back, 0, keepdims=True)
        total = jnp.zeros((TILE, TILE), jnp.float32)
        rim = jnp.zeros((8, TILE), jnp.float32)
        for k in range(4):
            tap = cw_ref[k : k + 1, lanes]
            taps_ref[k : k + 1, lanes] = jnp.sum(back * ext[5 + k : 5 + k + TILE], 0, keepdims=True)
            total = total + tap * padded[11 - k : 11 - k + TILE]
            rim = rim + tap * padded[3 - k : 11 - k]
        conv_ref[:, lanes] = total
        rim_ref[:, lanes] = rim
        return carry

    lax.fori_loop(0, CONV // TILE, conv, 0)
    rim_copy = remote(rim_ref, rim_in_ref, rim_ss.at[0], rim_rs.at[0], line_neighbour(False))
    rim_copy.start()
    save_conv = pltpu.make_async_copy(conv_ref, conv_far, save_sem.at[1])
    save_conv.start()
    sum_finish()
    rim_copy.wait()
    save_gate.wait()
    save_conv.wait()
    spot = lax.axis_index("x") * 8 + lax.axis_index("y") * 2 + lax.axis_index("c")

    @pl.when(spot == 31)
    def _():
        rim_in_ref[...] = jnp.zeros_like(rim_in_ref)


def tile_call(kernel, outs, scratch, name, *args, collective=None, away=0, away_outs=()):
    space = pl.BlockSpec(memory_space=pltpu.VMEM)
    far = pl.BlockSpec(memory_space=pl.ANY)
    params = dict(vmem_limit_bytes=40 * 2**20)
    if collective is not None:
        params = dict(vmem_limit_bytes=60 * 2**20, collective_id=collective, has_side_effects=True)
    return pl.pallas_call(
        kernel,
        out_shape=tuple(jax.ShapeDtypeStruct(s, d) for s, d in outs),
        in_specs=[space] * (len(args) - away) + [far] * away,
        out_specs=tuple(far if i in away_outs else space for i in range(len(outs))),
        scratch_shapes=[pltpu.VMEM(s, jnp.float32) if isinstance(s, tuple) else s for s in scratch],
        compiler_params=pltpu.CompilerParams(**params),
        name=name,
    )(*args)


PROJ_BLOCK = 640


def local(
    tokens,
    cotangent,
    lengths,
    routes,
    norm_gain,
    w_in,
    conv_weight,
    conv_bias,
    a_log,
    dt_bias,
    skip_scale,
    gated_gain,
    w_out,
    post_gain,
    w_router,
    shared_in,
    shared_out,
    expert_in,
    expert_out,
):
    low = jnp.bfloat16
    tokens, cotangent, routes = tokens[0], cotangent[0], routes[0]
    slot_count, model_width = tokens.shape
    inner_width = gated_gain.shape[0]
    conv_width = conv_bias.shape[0]
    head_count = a_log.shape[0]
    tap_count = conv_weight.shape[0]
    expert_count = w_router.shape[1]
    residual = tokens.astype(jnp.float32)
    positions = lax.axis_index(SEQ) * slot_count + jnp.arange(slot_count)
    valid = positions < lengths[0]
    upstream_low = jnp.where(valid[:, None], cotangent, jnp.zeros_like(cotangent))
    upstream = upstream_low.astype(jnp.float32)
    main_rows = inner_width + conv_width
    turned = w_in.T
    tail_shard = jnp.concatenate(
        [
            turned[main_rows:],
            w_router.T,
            jnp.zeros((TILE - head_count - expert_count, turned.shape[1]), low),
        ],
        0,
    )
    full_in, first_norm, projected, tail_values, tails = project(
        tokens, norm_gain[None], tail_shard, turned, main_rows
    )
    full_router = jnp.swapaxes(tails[:, head_count : head_count + expert_count], 0, 1)
    full_router = full_router.reshape(expert_count, model_width)

    taps = jnp.concatenate([conv_weight, conv_bias[None], jnp.zeros((3, conv_width), jnp.float32)], 0)
    heads = jnp.pad(jnp.stack([a_log, dt_bias]), ((0, 6), (0, TILE - head_count)))
    wide = jnp.stack([jnp.repeat(skip_scale, inner_width // head_count), gated_gain])
    square = (TILE, TILE)
    mixed, totals, running, steps, halo, carried, normed_low, scanned, all_upstream, full_out, full_shared_in, full_shared_out = mixer(
        projected, tail_values, taps, heads, wide, upstream_low, [w_out, shared_in, shared_out]
    )
    chosen = jnp.any(routes[:, :, None] == jnp.arange(expert_count)[None, None, :], 1)
    middle, second_norm, base_out, shared_second, shared_hidden, shared_act_grad, all_rows, all_gates = middle_part(
        normed_low, tokens, post_gain[None], full_router, chosen.T.astype(jnp.float32), upstream_low,
        full_out, full_shared_in, full_shared_out,
    )
    rows = all_rows.reshape(-1, model_width)
    back_rows = all_upstream.reshape(-1, model_width)
    owned = expert_in.shape[0]
    first_owned = lax.axis_index("z") * owned
    gates = lax.dynamic_slice_in_dim(all_gates, first_owned, owned, 1)
    gates = jnp.swapaxes(gates, 0, 1).reshape(owned, -1)
    hidden_width = expert_out.shape[1]
    acts = jnp.einsum("td,edf->etf", rows, expert_in, preferred_element_type=jnp.float32)
    hidden = (jax.nn.silu(acts[..., :hidden_width]) * acts[..., hidden_width:]).astype(low)
    output = jnp.einsum("etf,efd->etd", hidden, expert_out, preferred_element_type=jnp.float32)
    output = output.astype(low).astype(jnp.float32)
    part = jnp.sum(gates[..., None] * output, 0).astype(low)
    back_wide = back_rows.astype(jnp.float32)
    picks = jnp.sum(output * back_wide[None], -1)
    out_grad = (gates[..., None] * back_wide[None]).astype(low)
    hidden_back = jnp.einsum("etd,efd->etf", out_grad, expert_out, preferred_element_type=jnp.float32)
    act_grad = glu_back(acts, hidden_back)
    back = jnp.einsum("etf,edf->td", act_grad, expert_in, preferred_element_type=jnp.float32).astype(low)
    picks = jnp.swapaxes(picks.reshape(owned, 4, slot_count), 0, 1)
    picks = jnp.pad(picks, ((0, 0), (0, 8 - owned), (0, 0)))
    expert_parts, middle_back, mix_low, grad_post_gain, router_back, normed_back = expert_sum(
        rows,
        act_grad,
        hidden,
        out_grad,
        back.reshape(4, slot_count, model_width),
        picks,
        middle,
        shared_second,
        upstream_low,
        second_norm,
        all_gates,
        jnp.pad(full_router, ((0, TILE - expert_count), (0, 0))),
        post_gain[None],
        full_out,
    )
    act_width = act_grad.shape[2]
    grad_expert_in = expert_parts[:, :, :act_width]
    grad_expert_out = expert_parts[:, :, act_width:].reshape(owned, 3, -1, model_width // 3)
    grad_expert_out = jnp.swapaxes(grad_expert_out, 1, 2).reshape(owned, -1, model_width)

    shared_width = full_shared_out.shape[0]
    early_lefts, late_lefts = tile_call(
        lefts_kernel,
        [((6, model_width, TILE), low), ((3, model_width, TILE), low)],
        [(inner_width, TILE), (model_width, TILE)],
        "lefts",
        first_norm, second_norm, normed_low, shared_hidden,
    )
    large = [
        early_lefts, shared_act_grad, mix_low, upstream_low, projected, scanned, normed_back, mixed,
        part.reshape(4, slot_count, model_width), carried, base_out,
    ]
    (
        rim_back, taps_back, steps_back, heads_back, shared_in_part, w_out_part, shared_out_part,
        gate_back, gain_back, block_out, conv_part,
    ) = tile_call(
        mixer_back_kernel,
        [
            ((8, conv_width), jnp.float32), ((8, conv_width), jnp.float32),
            (square, jnp.float32), ((8, TILE), jnp.float32), ((12, 2 * shared_width), jnp.float32),
            ((24, model_width), jnp.float32), ((8, model_width), jnp.float32),
            ((TILE, inner_width), low), ((8, inner_width), jnp.float32), ((TILE, model_width), low),
            ((TILE, conv_width), jnp.float32),
        ],
        [
            pltpu.VMEM((TILE, inner_width), low), (TILE, model_width), pltpu.SemaphoreType.DMA((2,)),
            (TILE, inner_width), (TILE, inner_width), (8, conv_width),
            (2, *square), (2, *square), (4, *square), square, (2, *square),
            (TILE, conv_width), (TILE + 8, TILE), (TILE + 16, TILE),
            *share_scratch(early_lefts),
            pltpu.VMEM((96, 32, TILE), low),
            pltpu.VMEM((96, 32, TILE), low),
            pltpu.VMEM((3, TILE, model_width), low),
            pltpu.SemaphoreType.DMA((1,)),
            pltpu.SemaphoreType.DMA((1,)),
            pltpu.SemaphoreType.DMA((11,)),
            (TILE, conv_width),
        ]
        + [pltpu.VMEM(a.shape, a.dtype) for a in large]
        + scan_scratch()
        + grad_sum_scratch(model_width),
        "mixer_back",
        tail_values, halo, taps, heads, running, steps, wide, totals,
        valid[:, None].astype(jnp.float32), *large,
        collective=7,
        away=len(large),
        away_outs=(7, 10),
    )
    w_in_part, small, grad_tokens = grad_sum(
        late_lefts, gate_back, conv_part, steps_back, rim_back, tokens, norm_gain[None], middle_back, tails,
        taps_back, gain_back, grad_post_gain, heads_back, router_back, full_in, w_in.shape[1]
    )
    owner = lax.axis_index(ALL)

    def owned_part(row, rows, start, width):
        size = width // 128
        return lax.dynamic_slice(small, (row, start + owner * size), (rows, size))

    return (
        block_out[None],
        grad_tokens[None],
        owned_part(6, 1, 0, model_width)[0],
        w_in_part,
        owned_part(0, 4, 0, conv_width),
        owned_part(4, 1, 0, conv_width)[0],
        small[7, :head_count],
        small[7, TILE : TILE + head_count],
        small[7, 2 * TILE : 2 * TILE + head_count],
        owned_part(5, 1, 0, inner_width)[0],
        w_out_part,
        owned_part(6, 1, model_width, model_width)[0],
        owned_part(0, 8, conv_width, model_width).T,
        shared_in_part,
        shared_out_part,
        grad_expert_in,
        grad_expert_out,
    )


def solution(mesh):
    split = Mesh(mesh.devices.reshape(4, 4, 2, 4), ALL)
    placed = (
        P("z", SEQ, None),
        P("z", SEQ, None),
        P("z"),
        P("z", SEQ, None),
        P(),
        P("z", None),
        P(),
        P(),
        P(),
        P(),
        P(),
        P(),
        P("z", None),
        P(),
        P("z", None),
        P("z", None),
        P("z", None),
        P("z", None, None),
        P("z", None, None),
    )
    return jax.shard_map(
        local,
        mesh=split,
        in_specs=placed,
        out_specs=(
            P("z", SEQ, None),
            P("z", SEQ, None),
            P(ALL),
            P(ALL, None),
            P(None, ALL),
            P(ALL),
            P(),
            P(),
            P(),
            P(ALL),
            P(ALL, None),
            P(ALL),
            P(ALL, None),
            P(ALL, None),
            P(ALL, None),
            P("z", SEQ, None),
            P("z", SEQ, None),
        ),
        check_vma=False,
    )
```
